32 devices in a mesh: range: 32 (over z, y, x, core).
Axes of the slice: x: 2, y: 2, z: 4, core: 2. Of those that a mesh axis runs over, the one named last changes fastest.
Arguments:
- raw: bfloat16 [2, 64, 32, 8192], P(None, None, None, 'range'), may hold values from -40 to 40
- replica: bfloat16 [2, 128], replicated, may hold values from -1 to 1
- det_bin: int32 [1024], P('range'), may hold values from 0 to 31
- det_block: int32 [1024], P('range'), may hold values from 0 to 1
- det_beam: int32 [1024], P('range'), may hold values from 0 to 7
- det_owner: int32 [1024, 1], P('range'), may hold values from 0 to 31; in each aligned block of 32 rows (0 to 31, 32 to 63, ...) at most 2 rows name the same one
Outputs:
- tracked: float32 [2048, 256], P('range')
The draws below stay inside these ranges and needn't reach their ends.
Inputs may be any that keep to these rules, and one draw needn't show every extreme that they name: `det_owner`: in each slab's detections no owner appears more than 2 times; some owner appears exactly 2 times.
All inputs are finite; a program needn't handle non-finite values.
Results may differ from the reference program's by a relative error of at most 0.025.
Values may be sent and summed in bfloat16 or wider, within the bound.
No kernel may reach another device: no remote copies, remote signals or barrier semaphores. Data moves between devices by JAX's collectives and lax.ppermute only.
A program may use at most 256 MiB of HBM per device.

```python
import math
import jax
import jax.numpy as jnp
import numpy as np
from jax import lax

C = 64
P_SIZE = 32
TAPS = 128
BLOCK = 128
G_DEV = 256
BEAMS = 8
CAP = 2
DET_DEV = 32
NDET = 1024
NG = 8192
N_RANGE = 32


def draw_raw(key, part):
    keys = jax.random.split(jax.random.fold_in(key, 17), 4)
    slabs = NG // G_DEV
    slab_of = jnp.arange(NG).astype(jnp.int32) // G_DEV
    phases = jax.random.uniform(keys[0], (slabs,), minval=-1.0, maxval=1.0)
    freqs = jax.random.uniform(keys[1], (slabs,), minval=0.0, maxval=float(P_SIZE))
    gain = jax.random.truncated_normal(keys[2], -4.0, 4.0, (2, NG))
    noise = jax.random.truncated_normal(keys[3], -6.0, 6.0, (2, C, P_SIZE, NG))
    chan = jnp.arange(C).astype(jnp.float32)[:, None, None]
    pulse = jnp.arange(P_SIZE).astype(jnp.float32)[None, :, None]
    angle = math.pi * phases[slab_of][None, None, :] * chan + 2.0 * math.pi / P_SIZE * freqs[slab_of][None, None, :] * pulse
    cosine = jnp.cos(angle)
    sine = jnp.sin(angle)
    real_part = 4.0 * (gain[0] * cosine - gain[1] * sine)
    imag_part = 4.0 * (gain[0] * sine + gain[1] * cosine)
    return (noise + jnp.stack([real_part, imag_part], 0)).astype(jnp.bfloat16)


def plant(result, key, least, top_value):
    spot = [jax.random.randint(jax.random.fold_in(key, axis), (), 0, length) for axis, length in enumerate(result.shape)]
    widest = result.shape.index(max(result.shape))
    beside = spot[:widest] + [(spot[widest] + 1) % result.shape[widest]] + spot[widest + 1:]
    return result.at[tuple(spot)].set(least).at[tuple(beside)].set(top_value)


def assign_block(key, own, number, rows, count, top, limit, slope):
    ranking = jax.random.permutation(key, count)
    packed, usual = shares(count, rows * top, limit, slope, True), shares(count, rows * top, limit, slope, False)
    places = jnp.arange(count)

    def named(sizes, turn):
        used = int((sizes > 0).sum())
        fixed = max(1, used // 4)
        passed = fixed + (places - fixed + turn * (used - fixed)) % max(1, count - fixed)
        return jnp.zeros((count,), jnp.int32).at[ranking[jnp.where(places < fixed, places, passed)]].set(jnp.asarray(sizes, jnp.int32))

    sizes = jnp.where(number % 4 == 0, named(packed, number // 4), named(usual, number - number // 4 - 1))
    mixed = jax.random.permutation(jax.random.fold_in(own, 3), count)
    donor, taker = mixed[0:count // 2 * 2:2], mixed[1:count // 2 * 2:2]
    slack = jnp.minimum(sizes[donor] - 1, limit - sizes[taker]) // 2
    slack = jnp.where((donor == ranking[0]) | (taker == ranking[0]) | (sizes[taker] == 0), 0, jnp.maximum(slack, 0))
    passed = jax.random.randint(jax.random.fold_in(own, 4), (count // 2,), 0, 1 << 20) % (slack + 1)
    sizes = sizes.at[donor].add(-passed).at[taker].add(passed)
    items = jnp.searchsorted(jnp.cumsum(sizes), jnp.arange(rows * top), side="right").astype(jnp.int32)
    table = items.reshape(top, rows).T
    table = table[jax.random.permutation(jax.random.fold_in(own, 1), rows)]
    turn = jax.random.randint(jax.random.fold_in(own, 2), (rows, 1), 0, top)
    return jnp.take_along_axis(table, (jnp.arange(top)[None, :] + turn) % top, axis=1)


def shares(number_of, total, limit, skew, full):
    loads = [(1 << 20) // math.isqrt(grade ** skew) + 1 for grade in range(1, number_of + 1)]
    largest = limit if full else min(limit, max(-(-total // number_of), total * loads[0] // sum(loads)))
    least = 1 if total - largest >= number_of - 1 else 0
    holding, rest = [largest] + [least] * (number_of - 1), total - largest - least * (number_of - 1)
    while rest > 0:
        candidates = [i for i in range(1, number_of) if holding[i] < largest] or [i for i in range(1, number_of) if holding[i] < limit]
        whole, budget = sum([loads[i] for i in candidates]), rest
        for i in candidates:
            more = min(limit - holding[i], max(1, budget * loads[i] // whole), rest)
            holding[i] = holding[i] + more
            rest = rest - more
    return np.array(holding)


def scatter_about(stream_key, extent, width, limit, kind=jnp.bfloat16):
    values = width * jax.random.normal(stream_key, extent, jnp.float32)
    return jnp.clip(values, min=-limit, max=limit).astype(kind)


def setup_inputs(seed: int = 0) -> dict:
    arg_keys = jax.random.split(jax.random.key(seed), 7)
    raw = draw_raw(jax.random.fold_in(arg_keys[6], 71), 0)
    replica = scatter_about(arg_keys[1], (2, TAPS), ((2 * TAPS) ** -0.5), 1.0)
    det_bin = plant(jax.random.randint(arg_keys[2], (NDET,), 0, P_SIZE), jax.random.fold_in(arg_keys[2], 1), 0, P_SIZE - 1).astype(jnp.int32)
    det_block = plant(jax.random.randint(arg_keys[3], (NDET,), 0, G_DEV // BLOCK), jax.random.fold_in(arg_keys[3], 1), 0, (G_DEV // BLOCK) - 1).astype(jnp.int32)
    det_beam = plant(jax.random.randint(arg_keys[4], (NDET,), 0, BEAMS), jax.random.fold_in(arg_keys[4], 1), 0, BEAMS - 1).astype(jnp.int32)
    det_owner_keys = jax.random.split(jax.random.fold_in(arg_keys[5], 1), NDET // DET_DEV)
    det_owner_turns = jax.random.permutation(jax.random.fold_in(arg_keys[5], 3), NDET // DET_DEV)
    det_owner = jax.vmap(lambda own, number: assign_block(jax.random.fold_in(arg_keys[5], 2), own, number, DET_DEV, N_RANGE, 1, CAP, 2))(det_owner_keys, det_owner_turns).reshape((NDET, 1))
    return {"raw": raw, "replica": replica, "det_bin": det_bin, "det_block": det_block, "det_beam": det_beam, "det_owner": det_owner}


def toeplitz(replica):
    taps = replica.shape[1]
    zero = jnp.zeros((2, taps), replica.dtype)
    padded = jnp.concatenate([zero, replica, zero], axis=1)

    def column(shift):
        return lax.dynamic_slice_in_dim(padded, (taps - shift).astype(jnp.int32), 2 * taps, 1)
    cols = jax.vmap(column)(jnp.arange(taps).astype(jnp.int32))
    real_part = cols[:, 0, :].T
    imag_part = cols[:, 1, :].T
    return jnp.stack([jnp.stack([real_part, -imag_part], 1), jnp.stack([imag_part, real_part], 1)], 0)

def dft_table(pulses):
    index = jnp.arange(pulses).astype(jnp.int32)
    angle = 2.0 * math.pi / pulses * (index[:, None] * index[None, :] % pulses).astype(jnp.float32)
    cosine = jnp.cos(angle)
    sine = jnp.sin(angle)
    table = jnp.stack([jnp.stack([cosine, -sine], 1), jnp.stack([sine, cosine], 1)], 0)
    return (table * pulses ** (-0.5)).astype(jnp.bfloat16)

def compress(extended, replica):
    taps = replica.shape[1]
    gates = extended.shape[3] - taps
    shape = extended.shape[:3] + (gates // taps, taps)
    current = extended[..., :gates].reshape(shape)
    following = extended[..., taps:].reshape(shape)
    paired = jnp.concatenate([current, following], axis=4).astype(jnp.float32)
    kernel = toeplitz(replica).astype(jnp.float32)
    out = jnp.einsum('icpbn,inom->ocpbm', paired, kernel, precision=lax.Precision.HIGHEST)
    return out.reshape(extended.shape[:3] + (gates,)).astype(jnp.bfloat16)

def doppler(compressed):
    table = dft_table(compressed.shape[2]).astype(jnp.float32)
    out = jnp.einsum('icpg,ipod->docg', compressed.astype(jnp.float32), table, precision=lax.Precision.HIGHEST)
    return out.astype(jnp.bfloat16)

def cross_blocks(spectra):
    bins, _, chans, gates = spectra.shape
    flat = spectra.reshape(bins, 2 * chans, gates).astype(jnp.float32)
    parts = []
    for delta in range(3):
        parts.append(jnp.einsum('erg,esg->ers', flat, jnp.roll(flat, -delta, 0), precision=lax.Precision.HIGHEST))
    return jnp.stack(parts, 0)

def to_complex(blocks):
    bins = blocks.shape[1]
    chans = blocks.shape[2] // 2
    split = blocks.reshape(3, bins, 2, chans, 2, chans)
    real_part = split[:, :, 0, :, 0, :] + split[:, :, 1, :, 1, :]
    imag_part = split[:, :, 1, :, 0, :] - split[:, :, 0, :, 1, :]
    return jnp.stack([real_part, imag_part], 2)

def weights(cross, total, beams, chosen):
    cross = cross / jnp.float32(total)
    bins = cross.shape[1]
    chans = cross.shape[3]
    count = chosen.shape[0]
    rows_real = []
    rows_imag = []
    for left in range(3):
        row_real = []
        row_imag = []
        for right in range(3):
            if right >= left:
                picked = cross[right - left][(chosen - 1 + left) % bins]
                row_real.append(picked[:, 0])
                row_imag.append(picked[:, 1])
            else:
                picked = cross[left - right][(chosen - 1 + right) % bins]
                row_real.append(jnp.swapaxes(picked[:, 0], 1, 2))
                row_imag.append(-jnp.swapaxes(picked[:, 1], 1, 2))
        rows_real.append(jnp.concatenate(row_real, 2))
        rows_imag.append(jnp.concatenate(row_imag, 2))
    cov_real = jnp.concatenate(rows_real, 1)
    cov_imag = jnp.concatenate(rows_imag, 1)
    embedded = jnp.concatenate([jnp.concatenate([cov_real, -cov_imag], 2), jnp.concatenate([cov_imag, cov_real], 2)], 1)
    lower = jnp.linalg.cholesky(embedded)
    chan_index = jnp.arange(chans).astype(jnp.float32)
    sines = -0.8 + 1.6 * jnp.arange(beams).astype(jnp.float32) / (beams - 1)
    angle = math.pi * chan_index[:, None] * sines[None, :]
    empty = jnp.zeros((chans, beams), jnp.float32)
    steer = jnp.concatenate([empty, jnp.cos(angle), empty, empty, jnp.sin(angle), empty], 0)
    steer = jnp.broadcast_to(steer, (count,) + steer.shape)
    middle = lax.linalg.triangular_solve(lower, steer, left_side=True, lower=True)
    solved = lax.linalg.triangular_solve(lower, middle, left_side=True, lower=True, transpose_a=True)
    quad = lax.optimization_barrier(jnp.sum(steer * solved, axis=1))
    return (solved / jnp.sqrt(quad)[:, None, :]).astype(jnp.bfloat16)

def beam_blocks(spectra, weight, det_bin, det_block, det_beam, block):
    bins, _, chans, _ = spectra.shape

    def single(bin_id, block_id, beam_id):
        start = (block_id * block).astype(jnp.int32)
        zero = jnp.int32(0)
        pieces = []
        for offset in range(3):
            band = ((bin_id - 1 + offset) % bins).astype(jnp.int32)
            pieces.append(lax.dynamic_slice(spectra, (band, zero, zero, start), (1, 2, chans, block)))
        window = jnp.concatenate(pieces, 0).astype(jnp.float32)
        vector = weight[bin_id, :, beam_id].reshape(2, 3, chans).astype(jnp.float32)
        hp = lax.Precision.HIGHEST
        real_out = jnp.einsum('oc,ocg->g', vector[0], window[:, 0], precision=hp) + jnp.einsum('oc,ocg->g', vector[1], window[:, 1], precision=hp)
        imag_out = jnp.einsum('oc,ocg->g', vector[0], window[:, 1], precision=hp) - jnp.einsum('oc,ocg->g', vector[1], window[:, 0], precision=hp)
        return jnp.concatenate([real_out, imag_out], 0)
    return jax.vmap(single)(det_bin, det_block, det_beam)

def reference(raw, replica, det_bin, det_block, det_beam, det_owner):
    slabs = N_RANGE
    padded = jnp.concatenate([raw, jnp.zeros((2, C, P_SIZE, TAPS), raw.dtype)], axis=3)

    def advance(total, slab):
        extended = lax.dynamic_slice_in_dim(padded, slab * G_DEV, G_DEV + TAPS, 3)
        spectra = doppler(compress(extended, replica))
        return (total + cross_blocks(spectra), spectra)
    start = jnp.zeros((3, P_SIZE, 2 * C, 2 * C), jnp.float32)
    blocks, spectra_all = lax.scan(advance, start, jnp.arange(slabs).astype(jnp.int32))
    weight = weights(to_complex(blocks), NG, BEAMS, jnp.arange(P_SIZE).astype(jnp.int32))
    beams = jax.vmap(lambda s, a, b, c: beam_blocks(s, weight, a, b, c, BLOCK))(spectra_all, det_bin.reshape(slabs, -1), det_block.reshape(slabs, -1), det_beam.reshape(slabs, -1))
    owners = det_owner[:, 0].reshape(slabs, -1)
    index = jnp.arange(owners.shape[1]).astype(jnp.int32)
    earlier = (owners[:, None, :] == owners[:, :, None]) & (index[None, None, :] < index[None, :, None])
    ranks = lax.optimization_barrier(jnp.sum(earlier.astype(jnp.int32), axis=2))
    source = jnp.arange(slabs).astype(jnp.int32)[:, None]
    target = owners * (owners.shape[1] * CAP) + source * CAP + ranks
    tracked = jnp.zeros((NDET * CAP, 2 * BLOCK), jnp.float32)
    return tracked.at[target.reshape(-1)].set(beams.reshape(-1, 2 * BLOCK))
```

```python
import functools
import math

import jax
import jax.numpy as jnp
import ml_dtypes
import numpy as np
from jax import lax
from jax.experimental import pallas as pl
from jax.experimental.pallas import tpu as pltpu
from jax.sharding import PartitionSpec as P

BLOCK = 128
BEAMS = 8
CAP = 2
UNITS = 5

F32 = jnp.float32
BF16 = jnp.bfloat16
VMEM = pltpu.VMEM
MIB = 1024 * 1024
NT = (((1,), (1,)), ((), ()))


def vmem_spec():
    return pl.BlockSpec(memory_space=VMEM)


def smem_spec():
    return pl.BlockSpec(memory_space=pltpu.SMEM)


def params(mib=48):
    return pltpu.CompilerParams(vmem_limit_bytes=mib * MIB)


def dot(a, b):
    return jnp.dot(a, b, preferred_element_type=F32)


def dot_nt(a, b, precision=None):
    return lax.dot_general(a, b, NT, precision=precision, preferred_element_type=F32)


def iota(shape, axis):
    return lax.broadcasted_iota(jnp.int32, shape, axis)


def taps_kernel(rep_ref, out_ref):
    taps = rep_ref.shape[1]
    base = rep_ref[...].astype(F32)
    row = iota((taps, 2 * taps), 0)
    parts = []
    for i in range(2):
        line = jnp.concatenate([base[i : i + 1], jnp.zeros((1, taps), F32)], axis=1)
        skew = jnp.broadcast_to(line, (taps, 2 * taps))
        bit = 1
        while bit < taps:
            skew = jnp.where((row & bit) != 0, pltpu.roll(skew, bit, 1), skew)
            bit *= 2
        parts.append(skew.T)
    real_part, imag_part = parts
    out_ref[0] = jnp.concatenate([real_part, -imag_part], axis=1).astype(BF16)
    out_ref[1] = jnp.concatenate([imag_part, real_part], axis=1).astype(BF16)


def correlation_matrix(replica):
    taps = replica.shape[1]
    return pl.pallas_call(
        taps_kernel,
        out_shape=jax.ShapeDtypeStruct((2, 2 * taps, 2 * taps), BF16),
        in_specs=[vmem_spec()],
        out_specs=vmem_spec(),
        compiler_params=params(),
    )(replica)


def doppler_matrix(pulses, group):
    index = np.arange(pulses)
    angle = 2.0 * math.pi / pulses * (index[:, None] * index[None, :] % pulses)
    cosine = np.cos(angle) * pulses**-0.5
    sine = np.sin(angle) * pulses**-0.5
    table = np.stack([np.stack([cosine, -sine], 1), np.stack([sine, cosine], 1)], 0)
    full = np.einsum("ipod,ce->dociep", table, np.eye(group))
    shape = (pulses * 2 * group, 2 * group * pulses)
    return full.reshape(shape).astype(ml_dtypes.bfloat16)


def spectra_body(first, second, taps_ref, dft_ref, out_ref):
    bins, _, chans, gates = out_ref.shape
    total = None
    for i in range(2):
        window = jnp.concatenate([first(i), second(i)], axis=1)
        term = dot(window, taps_ref[i])
        total = term if total is None else total + term
    compressed = total.astype(BF16)
    rows = compressed.shape[0]
    half = rows // 2
    pieces = []
    for h in range(2):
        part = compressed[h * half : (h + 1) * half]
        stacked = jnp.concatenate([part[:, :gates], part[:, gates:]], axis=0)
        piece = dot(dft_ref[...], stacked)
        pieces.append(piece.reshape(bins * 2, chans // 2, gates))
    joined = jnp.concatenate(pieces, axis=1).astype(BF16)
    out_ref[...] = joined.reshape(bins, 2, chans, gates)


def spectra_first_kernel(raw_ref, taps_ref, dft_ref, out_ref):
    spectra_body(
        lambda i: raw_ref[i, :, :BLOCK],
        lambda i: raw_ref[i, :, BLOCK:],
        taps_ref, dft_ref, out_ref,
    )


def spectra_last_kernel(raw_ref, halo_ref, taps_ref, dft_ref, out_ref):
    spectra_body(lambda i: raw_ref[i], lambda i: halo_ref[i], taps_ref, dft_ref, out_ref)


def spectra_block(raw, halo, matrix, table, pulses):
    group = 16
    rows, gates = raw.shape[1:]
    chans = rows // pulses
    const = [
        pl.BlockSpec(matrix.shape, lambda j: (0, 0, 0)),
        pl.BlockSpec(table.shape, lambda j: (0, 0)),
    ]
    if halo is None:
        kernel = spectra_first_kernel
        data = [raw]
        specs = [pl.BlockSpec((2, group * pulses, gates), lambda j: (0, j, 0))]
    else:
        kernel = spectra_last_kernel
        data = [raw, halo]
        specs = [
            pl.BlockSpec((2, group * pulses, BLOCK), lambda j: (0, j, 1)),
            pl.BlockSpec((2, group * pulses, BLOCK), lambda j: (0, j, 0)),
        ]
    return pl.pallas_call(
        kernel,
        grid=(chans // group,),
        out_shape=jax.ShapeDtypeStruct((pulses, 2, chans, BLOCK), BF16),
        in_specs=specs + const,
        out_specs=pl.BlockSpec((pulses, 2, group, BLOCK), lambda j: (0, 0, j, 0)),
        compiler_params=params(),
    )(*data, matrix, table)


def cross_kernel(base_ref, s0_ref, s1_ref, out_ref):
    bins, _, chans, gates = s0_ref.shape
    units = out_ref.shape[0]
    wanted = units // UNITS
    base = base_ref[0]
    lower = iota((chans, chans), 0) >= iota((chans, chans), 1)
    half = chans // 2

    def parts(e):
        where = lax.rem(base + e - 1 + 2 * bins, bins)
        real_part = jnp.concatenate([s0_ref[where, 0], s1_ref[where, 0]], axis=1)
        imag_part = jnp.concatenate([s0_ref[where, 1], s1_ref[where, 1]], axis=1)
        return real_part, imag_part

    def packed(block):
        swapped = pltpu.roll(block, chans, 1)
        mixed = jnp.where(lower, block[:, :chans], swapped[:, :chans])
        return jnp.concatenate([mixed[:half], mixed[half:]], axis=1)

    def pair(e):
        each = [parts(e + k) for k in range(4)]
        left_real = jnp.concatenate([p[0] for p in each], axis=0)
        left_imag = jnp.concatenate([p[1] for p in each], axis=0)
        right_real = jnp.concatenate([each[0][0], -each[0][1], each[1][0], -each[1][1]], axis=0)
        right_imag = jnp.concatenate([each[0][1], each[0][0], each[1][1], each[1][0]], axis=0)
        return dot_nt(left_real, right_real) + dot_nt(left_imag, right_imag)

    def write(unit, block, chunks):
        out_ref[unit] = packed(block[:chans])
        for k in range(chunks):
            out_ref[unit + 1 + k] = block[chans + k * half : chans + (k + 1) * half]

    @pl.loop(0, wanted // 2)
    def _(step):
        e = step * 2
        both = pair(e)
        write(e * UNITS, both[: 3 * chans, : 2 * chans], 4)
        write((e + 1) * UNITS, both[chans:, 2 * chans :], 4)

    both = pair(wanted - 1)
    write((wanted - 1) * UNITS, both[: 3 * chans, : 2 * chans], 4)
    out_ref[wanted * UNITS] = packed(both[chans : 2 * chans, 2 * chans :])


def cross_units(base, s0, s1, count):
    bins, _, chans, _ = s0.shape
    units = (count + 1) * UNITS + 1
    return pl.pallas_call(
        cross_kernel,
        out_shape=jax.ShapeDtypeStruct((units, chans // 2, 2 * chans), F32),
        in_specs=[smem_spec(), vmem_spec(), vmem_spec()],
        out_specs=vmem_spec(),
        compiler_params=params(),
    )(base, s0, s1)


def partner_sum(value, axis, bit):
    count = lax.axis_size(axis)
    return lax.ppermute(value, axis, [(i, i ^ bit) for i in range(count)])


def turn(value):
    half = value.shape[1] // 2
    rolled = pltpu.roll(value, half, 1)
    return jnp.where(iota(value.shape, 1) < half, -rolled, rolled)


def embed(value):
    return jnp.concatenate([value, turn(value)], axis=0)


def mul(a, b):
    return jnp.dot(a, embed(b), precision=lax.Precision.HIGHEST, preferred_element_type=F32)


def mul_conj(a, b):
    half = a.shape[1] // 2
    stacked = jnp.concatenate([a, -turn(a)], axis=0)
    both = dot_nt(stacked, b, lax.Precision.HIGHEST)
    rows = a.shape[0]
    return jnp.concatenate([both[:rows], both[rows:]], axis=1)


def invert(work_ref):
    chans, width = work_ref.shape
    sub = 8
    tiles = [work_ref[t * sub : (t + 1) * sub, :] for t in range(chans // sub)]
    lane = iota((sub, width), 1)
    row = iota((sub, width), 0)
    first_half = lane < chans

    def spin(value):
        rolled = pltpu.roll(value, chans, 1)
        return jnp.where(first_half, -rolled, rolled)

    def column(value, k):
        return jnp.broadcast_to(value[:, k : k + 1], (sub, width))

    for k in range(0, chans, 2):
        t, r = divmod(k, sub)
        line0 = jnp.broadcast_to(tiles[t][r : r + 1, :], (sub, width))
        line1 = jnp.broadcast_to(tiles[t][r + 1 : r + 2, :], (sub, width))
        a = column(line0, k)
        b_re = column(line0, k + 1)
        b_im = column(line0, chans + k + 1)
        d = column(line1, k + 1)
        inv = 1.0 / (a * d - (b_re * b_re + b_im * b_im))
        cleared = (lane == k) | (lane == k + 1) | (lane == chans + k) | (lane == chans + k + 1)
        u0 = jnp.where(cleared, jnp.where(lane == k, 1.0, 0.0), line0)
        u1 = jnp.where(cleared, jnp.where(lane == k + 1, 1.0, 0.0), line1)
        j0, j1 = spin(u0), spin(u1)
        a, d, b_re, b_im = a * inv, d * inv, b_re * inv, b_im * inv
        n0 = d * u0 - b_re * u1 - b_im * j1
        n1 = a * u1 - b_re * u0 + b_im * j0
        m0 = d * j0 - b_re * j1 + b_im * u1
        m1 = a * j1 - b_re * j0 - b_im * u0
        fresh = []
        for s, tile in enumerate(tiles):
            c0r, c0i = column(tile, k), column(tile, chans + k)
            c1r, c1i = column(tile, k + 1), column(tile, chans + k + 1)
            update = (c0r * n0 + c0i * m0) + (c1r * n1 + c1i * m1)
            value = jnp.where(cleared, 0.0, tile) - update
            if s == t:
                value = jnp.where(row == r, n0, jnp.where(row == r + 1, n1, value))
            fresh.append(value)
        tiles = fresh
    for t, tile in enumerate(tiles):
        work_ref[t * sub : (t + 1) * sub, :] = tile


def solve_kernel(total, keep_ref, recv_ref, steer_ref, out_ref, work, diag, low, mids):
    chans = work.shape[0]
    scale = F32(1.0 / total)

    def block(unit, count):
        pieces = [
            (keep_ref[unit + k] + recv_ref[unit + k]) * scale for k in range(count)
        ]
        return pieces[0] if count == 1 else jnp.concatenate(pieces, axis=0)

    def unpacked(unit):
        piece = block(unit, 1)
        swapped = pltpu.roll(piece, chans, 1)
        return jnp.concatenate([piece, swapped], axis=0)[:, :chans]

    def hermitian(mixed, across):
        i, j = iota(mixed.shape, 0), iota(mixed.shape, 1)
        real_part = jnp.where(i >= j, mixed, across)
        imag_part = jnp.where(i < j, mixed, jnp.where(i > j, -across, 0.0))
        return jnp.concatenate([real_part, imag_part], axis=1)

    m_left, m_mid, m_right = unpacked(0), unpacked(UNITS), unpacked(2 * UNITS)
    ml = block(1, 2)
    rl = block(3, 2)
    rm = block(UNITS + 1, 2)
    square = jnp.concatenate(
        [jnp.concatenate([m_left, m_mid], axis=1), jnp.concatenate([m_right, m_right], axis=1)],
        axis=0,
    ).T
    work[...] = hermitian(m_left, square[:chans, :chans])
    diag[0] = hermitian(m_right, square[:chans, chans:])
    diag[1] = hermitian(m_mid, square[chans:, :chans])
    flipped = jnp.concatenate([rm, rm], axis=0).T
    mr = jnp.concatenate([flipped[:chans, :chans], -flipped[chans:, :chans]], axis=1)
    low[0] = rl
    low[1] = ml
    mids[0] = mr

    @pl.loop(0, 3)
    def _(stage):
        invert(work)

        @pl.when(stage == 0)
        def _():
            inverse = work[...]
            both = mul(jnp.concatenate([low[0], low[1]], axis=0), inverse)
            pr, qm = both[:chans], both[chans:]
            work[...] = diag[0] - mul_conj(pr, low[0])
            mids[0] = mids[0] - mul_conj(qm, low[0])
            diag[1] = diag[1] - mul_conj(qm, low[1])
            low[0] = pr
            low[1] = qm

        @pl.when(stage == 1)
        def _():
            v = mul(mids[0], work[...])
            work[...] = diag[1] - mul_conj(v, mids[0])
            mids[0] = v

        @pl.when(stage == 2)
        def _():
            steer = steer_ref[...]
            y_mid = mul(steer, work[...])
            quad = jnp.sum(steer * y_mid, axis=1, keepdims=True)
            y_mid = y_mid / jnp.sqrt(quad)
            y_right = -mul(y_mid, mids[0])
            y_left = -(mul(y_right, low[0]) + mul(y_mid, low[1]))
            y = jnp.concatenate([y_left, y_mid, y_right], axis=1)
            real_lane = lax.rem(iota(y.shape, 1), 2 * chans) < chans
            out_ref[...] = jnp.where(real_lane, y, -y).astype(BF16)


def solve(keep, recv, total, chans):
    index = np.arange(chans)
    sines = -0.8 + 1.6 * np.arange(BEAMS) / (BEAMS - 1)
    angle = math.pi * sines[:, None] * index[None, :]
    steer = np.concatenate([np.cos(angle), -np.sin(angle)], axis=1).astype(np.float32)
    wide = 2 * chans
    return pl.pallas_call(
        functools.partial(solve_kernel, total),
        out_shape=jax.ShapeDtypeStruct((BEAMS, 3 * wide), BF16),
        in_specs=[vmem_spec()] * 3,
        out_specs=vmem_spec(),
        scratch_shapes=[
            pltpu.VMEM((chans, wide), F32),
            pltpu.VMEM((2, chans, wide), F32),
            pltpu.VMEM((2, chans, wide), F32),
            pltpu.VMEM((1, chans, wide), F32),
        ],
        compiler_params=params(),
    )(keep, recv, steer)


def beam_kernel(bin_ref, block_ref, beam_ref, owner_ref, s0_ref, s1_ref, w_ref, out_ref,
                both_ref, rows_ref, seen_ref):
    bins, wide, gates = s0_ref.shape
    half = wide // 2
    bits = bins.bit_length() - 1
    devices = seen_ref.shape[0]
    count = bin_ref.shape[0]
    rows_ref[...] = jnp.zeros_like(rows_ref)

    @pl.loop(0, devices)
    def _(i):
        seen_ref[i] = 0

    w = w_ref[...].astype(F32)
    for k in range(3):
        part = w[:, k * wide : (k + 1) * wide]
        both_ref[:, 0:BEAMS, k * wide : (k + 1) * wide] = part.reshape(bins, BEAMS, wide)
        both_ref[:, BEAMS:, k * wide : (k + 1) * wide] = turn(part).reshape(bins, BEAMS, wide)

    def detection(j, carry):
        bin_id = bin_ref[j]
        beam_id = beam_ref[j]
        owner = owner_ref[j]
        rank = seen_ref[owner]
        seen_ref[owner] = rank + 1
        place = jnp.int32(0)
        for bit in range(bits):
            place = place | (((bin_id >> bit) & 1) << (bits - 1 - bit))
        left = both_ref[place].astype(BF16)
        bands = [lax.rem(bin_id + bins - 1 + k, bins) for k in range(3)]
        first = block_ref[j] == 0
        window = jnp.concatenate(
            [jnp.where(first, s0_ref[b], s1_ref[b]) for b in bands], axis=0
        )
        both = dot(left, window)
        line = jnp.concatenate([both[:BEAMS], both[BEAMS:]], axis=1)
        chosen = jnp.where(iota(line.shape, 0) == beam_id, line, 0.0)
        row = owner * CAP + rank
        rows_ref[pl.ds(row, 1), :] = jnp.sum(chosen, axis=0, keepdims=True)
        return carry

    lax.fori_loop(0, count, detection, 0, unroll=4)
    out_ref[...] = rows_ref[...].astype(BF16)


def beam_rows(det_bin, det_block, det_beam, owners, s0, s1, weight, devices):
    bins, wide, gates = s0.shape
    return pl.pallas_call(
        beam_kernel,
        out_shape=jax.ShapeDtypeStruct((devices * CAP, 2 * gates), BF16),
        in_specs=[smem_spec()] * 4 + [vmem_spec()] * 3,
        out_specs=vmem_spec(),
        scratch_shapes=[
            pltpu.VMEM((bins, 2 * BEAMS, 3 * wide), F32),
            pltpu.VMEM((devices * CAP, 2 * gates), F32),
            pltpu.SMEM((devices,), jnp.int32),
        ],
        compiler_params=params(),
    )(det_bin, det_block, det_beam, owners, s0, s1, weight)


def on_device(raw, replica, det_bin, det_block, det_beam, det_owner):
    devices = lax.axis_size("range")
    myself = lax.axis_index("range")
    taps = replica.shape[1]
    _, chans, pulses, gates = raw.shape
    bins = pulses
    flat = raw.reshape(2, chans * pulses, gates)
    halo = lax.ppermute(
        flat[..., :taps], "range", [(source, source - 1) for source in range(1, devices)]
    )
    matrix = correlation_matrix(replica)
    table = doppler_matrix(pulses, 8)
    s0 = spectra_block(flat, None, matrix, table, pulses)
    s1 = spectra_block(flat, halo, matrix, table, pulses)

    stages = bins.bit_length() - 1
    count = bins // 2
    bit = myself & 1
    send = cross_units(jnp.reshape((1 - bit) * count, (1,)), s0, s1, count)
    recv = partner_sum(send, "range", 1)
    keep = cross_units(jnp.reshape(bit * count, (1,)), s0, s1, count)
    for stage in range(1, stages):
        count //= 2
        size = (count + 1) * UNITS + 1
        bit = (myself >> stage) & 1

        def part(start):
            return lax.dynamic_slice_in_dim(keep, start, size, 0) + lax.dynamic_slice_in_dim(
                recv, start, size, 0
            )

        send = part((1 - bit) * count * UNITS)
        fresh = partner_sum(send, "range", 1 << stage)
        keep = part(bit * count * UNITS)
        recv = fresh
    for stage in range(stages, devices.bit_length() - 1):
        keep = keep + recv
        recv = partner_sum(keep, "range", 1 << stage)

    mine = solve(keep, recv, gates * devices, chans)
    groups = [list(range(first, first + bins)) for first in range(0, devices, bins)]
    weight = lax.all_gather(
        mine, "range", axis=0, tiled=True, axis_index_groups=groups if len(groups) > 1 else None
    )
    outgoing = beam_rows(
        det_bin, det_block, det_beam, det_owner[:, 0],
        s0.reshape(bins, 2 * chans, BLOCK), s1.reshape(bins, 2 * chans, BLOCK), weight, devices,
    )
    incoming = lax.all_to_all(
        outgoing.reshape(devices, CAP, 2 * BLOCK), "range", split_axis=0, concat_axis=0, tiled=True
    )
    return incoming.astype(F32).reshape(devices * CAP, 2 * BLOCK)


def solution(mesh):
    in_specs = (
        P(None, None, None, "range"),
        P(),
        P("range"),
        P("range"),
        P("range"),
        P("range", None),
    )
    out_specs = P("range", None)
    return jax.shard_map(
        on_device, mesh=mesh, in_specs=in_specs, out_specs=out_specs, check_vma=False
    )
```

```python
import functools
import math

import jax
import jax.numpy as jnp
import ml_dtypes
import numpy as np
from jax import lax
from jax.experimental import pallas as pl
from jax.experimental.pallas import tpu as pltpu
from jax.sharding import PartitionSpec as P

BLOCK = 128
BEAMS = 8
CAP = 2

F32 = jnp.float32
BF16 = jnp.bfloat16
VMEM = pltpu.VMEM
MIB = 1024 * 1024
NT = (((1,), (1,)), ((), ()))


def vmem_spec():
    return pl.BlockSpec(memory_space=VMEM)


def smem_spec():
    return pl.BlockSpec(memory_space=pltpu.SMEM)


def hbm_spec():
    return pl.BlockSpec(memory_space=pltpu.HBM)


def params(mib=16):
    return pltpu.CompilerParams(vmem_limit_bytes=mib * MIB)


def dot(a, b):
    return jnp.dot(a, b, preferred_element_type=F32)


def dot_nt(a, b, precision=None):
    return lax.dot_general(a, b, NT, precision=precision, preferred_element_type=F32)


def iota(shape, axis):
    return lax.broadcasted_iota(jnp.int32, shape, axis)


def halo_kernel(raw_ref, out_ref, sem):
    copy = pltpu.make_async_copy(raw_ref.at[:, :, :BLOCK], out_ref, sem)
    copy.start()
    copy.wait()


def first_gates(raw):
    return pl.pallas_call(
        halo_kernel,
        out_shape=jax.ShapeDtypeStruct(raw.shape[:2] + (BLOCK,), BF16),
        in_specs=[hbm_spec()],
        out_specs=vmem_spec(),
        scratch_shapes=[pltpu.SemaphoreType.DMA],
        compiler_params=params(),
    )(raw)


def correlation_matrix(rep_ref, out_ref):
    taps = rep_ref.shape[1]
    base = rep_ref[...].astype(F32)
    row = iota((taps, 2 * taps), 0)
    parts = []
    for i in range(2):
        line = jnp.concatenate([base[i : i + 1], jnp.zeros((1, taps), F32)], axis=1)
        skew = jnp.broadcast_to(line, (taps, 2 * taps))
        bit = 1
        while bit < taps:
            skew = jnp.where((row & bit) != 0, pltpu.roll(skew, bit, 1), skew)
            bit *= 2
        parts.append(skew.T)
    real_part, imag_part = parts
    out_ref[0] = jnp.concatenate([real_part, -imag_part], axis=1).astype(BF16)
    out_ref[1] = jnp.concatenate([imag_part, real_part], axis=1).astype(BF16)


def doppler_matrix(pulses, group):
    index = np.arange(pulses)
    angle = 2.0 * math.pi / pulses * (index[:, None] * index[None, :] % pulses)
    cosine = np.cos(angle) * pulses**-0.5
    sine = np.sin(angle) * pulses**-0.5
    table = np.stack([np.stack([cosine, -sine], 1), np.stack([sine, cosine], 1)], 0)
    full = np.einsum("ipod,ce->dociep", table, np.eye(group))
    shape = (pulses * 2 * group, 2 * group * pulses)
    return full.reshape(shape).astype(ml_dtypes.bfloat16)


def doppler_rows(total, dft):
    compressed = total.astype(BF16)
    rows, wide = compressed.shape
    half, gates = rows // 2, wide // 2
    stacked = jnp.concatenate(
        [
            jnp.concatenate([compressed[:half, :gates], compressed[half:, :gates]], axis=1),
            jnp.concatenate([compressed[:half, gates:], compressed[half:, gates:]], axis=1),
        ],
        axis=0,
    )
    both = dot(dft, stacked)
    lines = both.shape[0] // 8
    joined = jnp.concatenate(
        [both[:, :gates].reshape(lines, 8, gates), both[:, gates:].reshape(lines, 8, gates)],
        axis=1,
    )
    return joined.astype(BF16)


GROUP = 16


def spectra_first_kernel(raw_ref, rep_ref, dft_ref, s_ref, local_ref, taps_ref, buf, sems):
    bins, _, chans, gates = s_ref.shape
    size = GROUP * bins
    copies = [
        pltpu.make_async_copy(
            raw_ref.at[:, j * size : (j + 1) * size, :],
            buf.at[:, j * size : (j + 1) * size, :],
            sems.at[j],
        )
        for j in range(chans // GROUP)
    ]
    for copy in copies:
        copy.start()
    correlation_matrix(rep_ref, taps_ref)
    for j, copy in enumerate(copies):
        copy.wait()
        rows = slice(j * size, (j + 1) * size)
        total = dot(buf[0, rows, :], taps_ref[0]) + dot(buf[1, rows, :], taps_ref[1])
        out = doppler_rows(total, dft_ref[...])
        s_ref[:, :, j * GROUP : (j + 1) * GROUP, :] = out.reshape(bins, 2, GROUP, gates)
        later = jnp.concatenate([buf[0, rows, gates:], buf[1, rows, gates:]], axis=1)
        near = jnp.concatenate([taps_ref[0, :gates, :], taps_ref[1, :gates, :]], axis=0)
        local_ref[rows, :] = dot(later, near)


def spectra_last_kernel(local_ref, halo_ref, taps_ref, dft_ref, s_ref):
    bins, _, chans, gates = s_ref.shape
    size = GROUP * bins
    for j in range(chans // GROUP):
        rows = slice(j * size, (j + 1) * size)
        later = jnp.concatenate([halo_ref[0, rows, :], halo_ref[1, rows, :]], axis=1)
        far = jnp.concatenate([taps_ref[0, gates:, :], taps_ref[1, gates:, :]], axis=0)
        out = doppler_rows(local_ref[rows, :] + dot(later, far), dft_ref[...])
        s_ref[:, :, j * GROUP : (j + 1) * GROUP, :] = out.reshape(bins, 2, GROUP, gates)


def spectra_first(raw, replica, table, pulses):
    _, rows, gates = raw.shape
    chans = rows // pulses
    taps = replica.shape[1]
    return pl.pallas_call(
        spectra_first_kernel,
        out_shape=[
            jax.ShapeDtypeStruct((pulses, 2, chans, BLOCK), BF16),
            jax.ShapeDtypeStruct((rows, 2 * BLOCK), F32),
            jax.ShapeDtypeStruct((2, 2 * taps, 2 * taps), BF16),
        ],
        in_specs=[hbm_spec(), vmem_spec(), vmem_spec()],
        out_specs=[vmem_spec()] * 3,
        scratch_shapes=[
            pltpu.VMEM(raw.shape, BF16),
            pltpu.SemaphoreType.DMA((chans // GROUP,)),
        ],
        compiler_params=params(),
    )(raw, replica, table)


def spectra_last(local, halo, matrix, table, pulses):
    rows = local.shape[0]
    return pl.pallas_call(
        spectra_last_kernel,
        out_shape=jax.ShapeDtypeStruct((pulses, 2, rows // pulses, BLOCK), BF16),
        in_specs=[vmem_spec()] * 4,
        out_specs=vmem_spec(),
        compiler_params=params(),
    )(local, halo, matrix, table)


def cross_body(base, s_ref, before_ref, out_ref):
    bins, _, chans, gates = s_ref.shape
    lower = iota((chans, chans), 0) >= iota((chans, chans), 1)
    half = chans // 2

    def packed(block):
        swapped = pltpu.roll(block, chans, 1)
        mixed = jnp.where(lower, block[:, :chans], swapped[:, :chans])
        return jnp.concatenate([mixed[:half], mixed[half:]], axis=1)

    def write(e, block):
        value = jnp.concatenate([packed(block[:chans]), block[chans:]], axis=0)
        if before_ref is not None:
            value = value + before_ref[base + e]
        out_ref[e] = value

    @pl.loop(0, out_ref.shape[0] // 2)
    def _(step):
        e = step * 2
        each = []
        for k in range(4):
            where = lax.rem(base + e + k, bins)
            each.append((s_ref[where, 0], s_ref[where, 1]))
        left = jnp.concatenate(
            [jnp.concatenate([re, im], axis=1) for re, im in each], axis=0
        )
        right = jnp.concatenate(
            [
                jnp.concatenate(pieces, axis=1)
                for re, im in each[:2]
                for pieces in ((re, im), (-im, re))
            ],
            axis=0,
        )
        both = dot_nt(left, right)
        write(e, both[: 3 * chans, : 2 * chans])
        write(e + 1, both[chans:, 2 * chans :])


def cross_first_kernel(s_ref, out_ref):
    cross_body(0, s_ref, None, out_ref)


def cross_last_kernel(base_ref, s_ref, before_ref, out_ref):
    cross_body(base_ref[0], s_ref, before_ref, out_ref)


def cross_first(spectra):
    bins, _, chans, _ = spectra.shape
    return pl.pallas_call(
        cross_first_kernel,
        out_shape=jax.ShapeDtypeStruct((bins, 5 * chans // 2, 2 * chans), F32),
        in_specs=[vmem_spec()],
        out_specs=vmem_spec(),
        compiler_params=params(),
    )(spectra)


def cross_last(base, spectra, before):
    bins = spectra.shape[0]
    return pl.pallas_call(
        cross_last_kernel,
        out_shape=jax.ShapeDtypeStruct((bins // 2,) + before.shape[1:], F32),
        in_specs=[smem_spec(), vmem_spec(), vmem_spec()],
        out_specs=vmem_spec(),
        compiler_params=params(),
    )(jnp.reshape(base, (1,)), spectra, before)


def partner(value, bit):
    count = lax.axis_size("range")
    return lax.ppermute(value, "range", [(i, i ^ bit) for i in range(count)])


def bin_of(index):
    low = index & 31
    return ((low & 1) << 4) | ((low & 2) << 2) | (low & 4) | (low >> 3)


def index_of(bin_id):
    return (bin_id >> 4) | ((bin_id >> 2) & 2) | (bin_id & 4) | ((bin_id & 3) << 3)


def plane_kernel(place_ref, keep_ref, core_ref, a_ref, b_ref):
    x, y = place_ref[0], place_ref[1]
    half = keep_ref.shape[1] // 2
    for k in range(8):
        e = (1 - x) * 8 + k
        a_ref[k] = keep_ref[e, :half] + core_ref[e, :half]
        e = (k // 4) * 8 + (1 - y) * 4 + k % 4
        b_ref[k] = keep_ref[e, half:] + core_ref[e, half:]


def cross_plane_kernel(place_ref, keep_ref, core_ref, a1_ref, b1_ref, a_ref, b_ref):
    x, y = place_ref[0], place_ref[1]
    half = keep_ref.shape[1] // 2
    for k in range(4):
        e = x * 8 + (1 - y) * 4 + k
        a_ref[k] = keep_ref[e, :half] + core_ref[e, :half] + a1_ref[(1 - y) * 4 + k]
        e = (1 - x) * 8 + y * 4 + k
        b_ref[k] = keep_ref[e, half:] + core_ref[e, half:] + b1_ref[(1 - x) * 4 + k]


def line_sum(place_ref, keep_ref, core_ref, a1_ref, b1_ref, a2_ref, b2_ref, z):
    x, y = place_ref[0], place_ref[1]
    half = keep_ref.shape[1] // 2
    e = x * 8 + y * 4 + z
    upper = keep_ref[e, :half] + core_ref[e, :half] + a1_ref[y * 4 + z] + a2_ref[z]
    lower = keep_ref[e, half:] + core_ref[e, half:] + b1_ref[x * 4 + z] + b2_ref[z]
    return upper, lower


def line_kernel(place_ref, *refs):
    outs = refs[6:]
    half = refs[0].shape[1] // 2
    for k, out_ref in enumerate(outs):
        upper, lower = line_sum(place_ref, *refs[:6], place_ref[2] ^ (k + 1))
        out_ref[:half] = upper
        out_ref[half:] = lower


def own_kernel(place_ref, *refs):
    z1_ref, z2_ref, z3_ref, out_ref = refs[6:]
    half = refs[0].shape[1] // 2
    upper, lower = line_sum(place_ref, *refs[:6], place_ref[2])
    out_ref[:half] = upper + z1_ref[:half] + (z2_ref[:half] + z3_ref[:half])
    out_ref[half:] = lower + z1_ref[half:] + (z2_ref[half:] + z3_ref[half:])


def summed(kernel, place, data, shapes):
    return pl.pallas_call(
        kernel,
        out_shape=[jax.ShapeDtypeStruct(shape, F32) for shape in shapes],
        in_specs=[smem_spec()] + [vmem_spec()] * len(data),
        out_specs=[vmem_spec()] * len(shapes),
        compiler_params=params(),
    )(place, *data)


def bin_sums(keep, core, myself):
    _, rows, wide = keep.shape
    half = rows // 2
    place = jnp.stack([(myself >> 1) & 1, (myself >> 2) & 1, (myself >> 3) & 3])
    data = [keep, core]
    a, b = summed(plane_kernel, place, data, [(8, half, wide)] * 2)
    data += [partner(a, 2), partner(b, 4)]
    a, b = summed(cross_plane_kernel, place, data, [(4, half, wide)] * 2)
    data += [partner(a, 4), partner(b, 2)]
    sends = summed(line_kernel, place, data, [(rows, wide)] * 3)
    data += [partner(value, (k + 1) * 8) for k, value in enumerate(sends)]
    own = summed(own_kernel, place, data, [(rows, wide)])[0]
    bit = 32
    while bit < lax.axis_size("range"):
        own = own + partner(own, bit)
        bit *= 2
    return own


def from_bin(value, offset):
    count = lax.axis_size("range")
    pairs = []
    for i in range(count):
        target = index_of((bin_of(i) - offset) % 32) | (i & ~31)
        pairs.append((i, target))
    return lax.ppermute(value, "range", pairs)


def turn(value):
    half = value.shape[1] // 2
    rolled = pltpu.roll(value, half, 1)
    return jnp.where(iota(value.shape, 1) < half, -rolled, rolled)


def embed(value):
    return jnp.concatenate([value, turn(value)], axis=0)


def mul(a, b):
    return jnp.dot(a, embed(b), precision=lax.Precision.HIGHEST, preferred_element_type=F32)


def mul_conj(a, b):
    half = a.shape[1] // 2
    stacked = jnp.concatenate([a, -turn(a)], axis=0)
    both = dot_nt(stacked, b, lax.Precision.HIGHEST)
    rows = a.shape[0]
    return jnp.concatenate([both[:rows], both[rows:]], axis=1)


def invert(work_ref):
    chans, width = work_ref.shape
    sub = 8
    tiles = [work_ref[t * sub : (t + 1) * sub, :] for t in range(chans // sub)]
    lane = iota((sub, width), 1)
    row = iota((sub, width), 0)
    first_half = lane < chans

    def spin(value):
        rolled = pltpu.roll(value, chans, 1)
        return jnp.where(first_half, -rolled, rolled)

    def column(value, k):
        return jnp.broadcast_to(value[:, k : k + 1], (sub, width))

    for k in range(0, chans, 2):
        t, r = divmod(k, sub)
        line0 = jnp.broadcast_to(tiles[t][r : r + 1, :], (sub, width))
        line1 = jnp.broadcast_to(tiles[t][r + 1 : r + 2, :], (sub, width))
        a = column(line0, k)
        b_re = column(line0, k + 1)
        b_im = column(line0, chans + k + 1)
        d = column(line1, k + 1)
        inv = 1.0 / (a * d - (b_re * b_re + b_im * b_im))
        cleared = (lane == k) | (lane == k + 1) | (lane == chans + k) | (lane == chans + k + 1)
        u0 = jnp.where(cleared, jnp.where(lane == k, 1.0, 0.0), line0)
        u1 = jnp.where(cleared, jnp.where(lane == k + 1, 1.0, 0.0), line1)
        j0, j1 = spin(u0), spin(u1)
        a, d, b_re, b_im = a * inv, d * inv, b_re * inv, b_im * inv
        n0 = d * u0 - b_re * u1 - b_im * j1
        n1 = a * u1 - b_re * u0 + b_im * j0
        m0 = d * j0 - b_re * j1 + b_im * u1
        m1 = a * j1 - b_re * j0 - b_im * u0
        fresh = []
        for s, tile in enumerate(tiles):
            c0r, c0i = column(tile, k), column(tile, chans + k)
            c1r, c1i = column(tile, k + 1), column(tile, chans + k + 1)
            update = (c0r * n0 + c0i * m0) + (c1r * n1 + c1i * m1)
            value = jnp.where(cleared, 0.0, tile) - update
            if s == t:
                value = jnp.where(row == r, n0, jnp.where(row == r + 1, n1, value))
            fresh.append(value)
        tiles = fresh
    for t, tile in enumerate(tiles):
        work_ref[t * sub : (t + 1) * sub, :] = tile


def solve_kernel(total, own_ref, left_ref, right_ref, steer_ref, out_ref, work, diag, low, mids):
    chans = work.shape[0]
    scale = F32(1.0 / total)
    half = chans // 2

    def unpacked(ref):
        piece = ref[:half] * scale
        swapped = pltpu.roll(piece, chans, 1)
        return jnp.concatenate([piece, swapped], axis=0)[:, :chans]

    def hermitian(mixed, across):
        i, j = iota(mixed.shape, 0), iota(mixed.shape, 1)
        real_part = jnp.where(i >= j, mixed, across)
        imag_part = jnp.where(i < j, mixed, jnp.where(i > j, -across, 0.0))
        return jnp.concatenate([real_part, imag_part], axis=1)

    m_left, m_mid, m_right = unpacked(left_ref), unpacked(own_ref), unpacked(right_ref)
    ml = left_ref[half : half + chans] * scale
    rl = left_ref[half + chans :] * scale
    rm = own_ref[half : half + chans] * scale
    square = jnp.concatenate(
        [jnp.concatenate([m_left, m_mid], axis=1), jnp.concatenate([m_right, m_right], axis=1)],
        axis=0,
    ).T
    work[...] = hermitian(m_left, square[:chans, :chans])
    diag[0] = hermitian(m_right, square[:chans, chans:])
    diag[1] = hermitian(m_mid, square[chans:, :chans])
    flipped = jnp.concatenate([rm, rm], axis=0).T
    mr = jnp.concatenate([flipped[:chans, :chans], -flipped[chans:, :chans]], axis=1)
    low[0] = rl
    low[1] = ml
    mids[0] = mr

    @pl.loop(0, 3)
    def _(stage):
        invert(work)

        @pl.when(stage == 0)
        def _():
            inverse = work[...]
            both = mul(jnp.concatenate([low[0], low[1]], axis=0), inverse)
            pr, qm = both[:chans], both[chans:]
            work[...] = diag[0] - mul_conj(pr, low[0])
            mids[0] = mids[0] - mul_conj(qm, low[0])
            diag[1] = diag[1] - mul_conj(qm, low[1])
            low[0] = pr
            low[1] = qm

        @pl.when(stage == 1)
        def _():
            v = mul(mids[0], work[...])
            work[...] = diag[1] - mul_conj(v, mids[0])
            mids[0] = v

        @pl.when(stage == 2)
        def _():
            steer = steer_ref[...]
            y_mid = mul(steer, work[...])
            quad = jnp.sum(steer * y_mid, axis=1, keepdims=True)
            y_mid = y_mid / jnp.sqrt(quad)
            y_right = -mul(y_mid, mids[0])
            y_left = -(mul(y_right, low[0]) + mul(y_mid, low[1]))
            y = jnp.concatenate([y_left, y_mid, y_right], axis=1)
            real_lane = lax.rem(iota(y.shape, 1), 2 * chans) < chans
            mine = jnp.where(real_lane, y, -y).astype(BF16)
            for k in range(out_ref.shape[0]):
                out_ref[k] = mine


def solve(own, left, right, total, chans, copies):
    index = np.arange(chans)
    sines = -0.8 + 1.6 * np.arange(BEAMS) / (BEAMS - 1)
    angle = math.pi * sines[:, None] * index[None, :]
    steer = np.concatenate([np.cos(angle), -np.sin(angle)], axis=1).astype(np.float32)
    wide = 2 * chans
    return pl.pallas_call(
        functools.partial(solve_kernel, total),
        out_shape=jax.ShapeDtypeStruct((copies, BEAMS, 3 * wide), BF16),
        in_specs=[vmem_spec()] * 4,
        out_specs=vmem_spec(),
        scratch_shapes=[
            pltpu.VMEM((chans, wide), F32),
            pltpu.VMEM((2, chans, wide), F32),
            pltpu.VMEM((2, chans, wide), F32),
            pltpu.VMEM((1, chans, wide), F32),
        ],
        compiler_params=params(),
    )(own, left, right, steer)


def beam_kernel(bin_ref, block_ref, beam_ref, owner_ref, s0_ref, s1_ref, w_ref, out_ref,
                both_ref, rows_ref, seen_ref):
    bins, wide, gates = s0_ref.shape
    devices = seen_ref.shape[0]
    count = bin_ref.shape[0]
    rows_ref[...] = jnp.zeros_like(rows_ref)

    @pl.loop(0, devices)
    def _(i):
        seen_ref[i] = 0

    w = w_ref[...].astype(F32)
    for k in range(3):
        part = w[:, k * wide : (k + 1) * wide]
        both_ref[:, 0:BEAMS, k * wide : (k + 1) * wide] = part.reshape(bins, BEAMS, wide)
        both_ref[:, BEAMS:, k * wide : (k + 1) * wide] = turn(part).reshape(bins, BEAMS, wide)

    def detection(j, carry):
        bin_id = bin_ref[j]
        beam_id = beam_ref[j]
        owner = owner_ref[j]
        rank = seen_ref[owner]
        seen_ref[owner] = rank + 1
        left = both_ref[index_of(bin_id)].astype(BF16)
        bands = [lax.rem(bin_id + bins - 1 + k, bins) for k in range(3)]
        first = block_ref[j] == 0
        window = jnp.concatenate(
            [jnp.where(first, s0_ref[b], s1_ref[b]) for b in bands], axis=0
        )
        both = dot(left, window)
        line = jnp.concatenate([both[:BEAMS], both[BEAMS:]], axis=1)
        chosen = jnp.where(iota(line.shape, 0) == beam_id, line, 0.0)
        row = owner * CAP + rank
        rows_ref[pl.ds(row, 1), :] = jnp.sum(chosen, axis=0, keepdims=True)
        return carry

    lax.fori_loop(0, count, detection, 0, unroll=4)
    out_ref[...] = rows_ref[...].astype(BF16)


def beam_rows(det_bin, det_block, det_beam, owners, s0, s1, weight, devices):
    bins, wide, gates = s0.shape
    return pl.pallas_call(
        beam_kernel,
        out_shape=jax.ShapeDtypeStruct((devices * CAP, 2 * gates), BF16),
        in_specs=[smem_spec()] * 4 + [vmem_spec()] * 3,
        out_specs=vmem_spec(),
        scratch_shapes=[
            pltpu.VMEM((bins, 2 * BEAMS, 3 * wide), F32),
            pltpu.VMEM((devices * CAP, 2 * gates), F32),
            pltpu.SMEM((devices,), jnp.int32),
        ],
        compiler_params=params(),
    )(det_bin, det_block, det_beam, owners, s0, s1, weight)


def on_device(raw, replica, det_bin, det_block, det_beam, det_owner):
    devices = lax.axis_size("range")
    myself = lax.axis_index("range")
    _, chans, pulses, gates = raw.shape
    bins = pulses
    flat = raw.reshape(2, chans * pulses, gates)
    halo = lax.ppermute(
        first_gates(flat), "range", [(source, source - 1) for source in range(1, devices)]
    )
    table = doppler_matrix(pulses, 8)
    s0, local, matrix = spectra_first(flat, replica, table, pulses)
    first = cross_first(s0)
    s1 = spectra_last(local, halo, matrix, table, pulses)
    core = myself & 1
    core_sum = partner(cross_last((1 - core) * (bins // 2), s1, first), 1)
    keep = cross_last(core * (bins // 2), s1, first)
    own = bin_sums(keep, core_sum, myself)
    left = from_bin(own, -1)
    right = from_bin(own[: chans // 2], 1)

    mine = solve(own, left, right, gates * devices, chans, bins)
    groups = [list(range(first, first + bins)) for first in range(0, devices, bins)]
    weight = lax.all_to_all(
        mine, "range", split_axis=0, concat_axis=0, tiled=True,
        axis_index_groups=groups if len(groups) > 1 else None,
    ).reshape(bins * BEAMS, mine.shape[2])
    outgoing = beam_rows(
        det_bin, det_block, det_beam, det_owner[:, 0],
        s0.reshape(bins, 2 * chans, BLOCK), s1.reshape(bins, 2 * chans, BLOCK), weight, devices,
    )
    incoming = lax.all_to_all(
        outgoing.reshape(devices, CAP, 2 * BLOCK), "range", split_axis=0, concat_axis=0, tiled=True
    )
    return incoming.astype(F32).reshape(devices * CAP, 2 * BLOCK)


def solution(mesh):
    in_specs = (
        P(None, None, None, "range"),
        P(),
        P("range"),
        P("range"),
        P("range"),
        P("range", None),
    )
    out_specs = P("range", None)
    return jax.shard_map(
        on_device, mesh=mesh, in_specs=in_specs, out_specs=out_specs, check_vma=False
    )
```

```python
import functools
import math

import jax
import jax.numpy as jnp
import ml_dtypes
import numpy as np
from jax import lax
from jax.experimental import pallas as pl
from jax.experimental.pallas import tpu as pltpu
from jax.sharding import PartitionSpec as P

BLOCK = 128
BEAMS = 8
CAP = 2

F32 = jnp.float32
BF16 = jnp.bfloat16
VMEM = pltpu.VMEM
MIB = 1024 * 1024
NT = (((1,), (1,)), ((), ()))


def vmem_spec():
    return pl.BlockSpec(memory_space=VMEM)


def smem_spec():
    return pl.BlockSpec(memory_space=pltpu.SMEM)


def hbm_spec():
    return pl.BlockSpec(memory_space=pltpu.HBM)


def params(mib=16):
    return pltpu.CompilerParams(vmem_limit_bytes=mib * MIB)


def dot(a, b):
    return jnp.dot(a, b, preferred_element_type=F32)


def dot_nt(a, b, precision=None):
    return lax.dot_general(a, b, NT, precision=precision, preferred_element_type=F32)


def iota(shape, axis):
    return lax.broadcasted_iota(jnp.int32, shape, axis)


def halo_kernel(raw_ref, out_ref, sem):
    copy = pltpu.make_async_copy(raw_ref.at[:, :, :BLOCK], out_ref, sem)
    copy.start()
    copy.wait()


def first_gates(raw):
    return pl.pallas_call(
        halo_kernel,
        out_shape=jax.ShapeDtypeStruct(raw.shape[:2] + (BLOCK,), BF16),
        in_specs=[hbm_spec()],
        out_specs=vmem_spec(),
        scratch_shapes=[pltpu.SemaphoreType.DMA],
        compiler_params=params(63),
    )(raw)


def correlation_matrix(rep_ref, out_ref):
    taps = rep_ref.shape[1]
    base = rep_ref[...].astype(F32)
    row = iota((taps, 2 * taps), 0)
    parts = []
    for i in range(2):
        line = jnp.concatenate([base[i : i + 1], jnp.zeros((1, taps), F32)], axis=1)
        skew = jnp.broadcast_to(line, (taps, 2 * taps))
        bit = 1
        while bit < taps:
            skew = jnp.where((row & bit) != 0, pltpu.roll(skew, bit, 1), skew)
            bit *= 2
        parts.append(skew.T)
    real_part, imag_part = parts
    out_ref[0] = jnp.concatenate([real_part, -imag_part], axis=1).astype(BF16)
    out_ref[1] = jnp.concatenate([imag_part, real_part], axis=1).astype(BF16)


def doppler_matrix(pulses, group):
    index = np.arange(pulses)
    angle = 2.0 * math.pi / pulses * (index[:, None] * index[None, :] % pulses)
    cosine = np.cos(angle) * pulses**-0.5
    sine = np.sin(angle) * pulses**-0.5
    table = np.stack([np.stack([cosine, -sine], 1), np.stack([sine, cosine], 1)], 0)
    full = np.einsum("ipod,ce->dociep", table, np.eye(group))
    shape = (pulses * 2 * group, 2 * group * pulses)
    return full.reshape(shape).astype(ml_dtypes.bfloat16)


def doppler_rows(total, dft):
    compressed = total.astype(BF16)
    rows, wide = compressed.shape
    half, gates = rows // 2, wide // 2
    stacked = jnp.concatenate(
        [
            jnp.concatenate([compressed[:half, :gates], compressed[half:, :gates]], axis=1),
            jnp.concatenate([compressed[:half, gates:], compressed[half:, gates:]], axis=1),
        ],
        axis=0,
    )
    both = dot(dft, stacked)
    lines = both.shape[0] // 8
    joined = jnp.concatenate(
        [both[:, :gates].reshape(lines, 8, gates), both[:, gates:].reshape(lines, 8, gates)],
        axis=1,
    )
    return joined.astype(BF16)


GROUP = 16


def spectra_first_kernel(raw_ref, rep_ref, dft_ref, s_ref, local_ref, taps_ref, buf, sems):
    bins, _, chans, gates = s_ref.shape
    size = GROUP * bins
    copies = [
        pltpu.make_async_copy(
            raw_ref.at[:, j * size : (j + 1) * size, :],
            buf.at[:, j * size : (j + 1) * size, :],
            sems.at[j],
        )
        for j in range(chans // GROUP)
    ]
    for copy in copies:
        copy.start()
    correlation_matrix(rep_ref, taps_ref)
    for j, copy in enumerate(copies):
        copy.wait()
        rows = slice(j * size, (j + 1) * size)
        total = dot(buf[0, rows, :], taps_ref[0]) + dot(buf[1, rows, :], taps_ref[1])
        out = doppler_rows(total, dft_ref[...])
        s_ref[:, :, j * GROUP : (j + 1) * GROUP, :] = out.reshape(bins, 2, GROUP, gates)
        later = jnp.concatenate([buf[0, rows, gates:], buf[1, rows, gates:]], axis=1)
        near = jnp.concatenate([taps_ref[0, :gates, :], taps_ref[1, :gates, :]], axis=0)
        local_ref[rows, :] = dot(later, near)


def spectra_last_kernel(local_ref, halo_ref, taps_ref, dft_ref, s_ref):
    bins, _, chans, gates = s_ref.shape
    size = GROUP * bins
    for j in range(chans // GROUP):
        rows = slice(j * size, (j + 1) * size)
        later = jnp.concatenate([halo_ref[0, rows, :], halo_ref[1, rows, :]], axis=1)
        far = jnp.concatenate([taps_ref[0, gates:, :], taps_ref[1, gates:, :]], axis=0)
        out = doppler_rows(local_ref[rows, :] + dot(later, far), dft_ref[...])
        s_ref[:, :, j * GROUP : (j + 1) * GROUP, :] = out.reshape(bins, 2, GROUP, gates)


def spectra_first(raw, replica, table, pulses):
    _, rows, gates = raw.shape
    chans = rows // pulses
    taps = replica.shape[1]
    return pl.pallas_call(
        spectra_first_kernel,
        out_shape=[
            jax.ShapeDtypeStruct((pulses, 2, chans, BLOCK), BF16),
            jax.ShapeDtypeStruct((rows, 2 * BLOCK), F32),
            jax.ShapeDtypeStruct((2, 2 * taps, 2 * taps), BF16),
        ],
        in_specs=[hbm_spec(), vmem_spec(), vmem_spec()],
        out_specs=[vmem_spec()] * 3,
        scratch_shapes=[
            pltpu.VMEM(raw.shape, BF16),
            pltpu.SemaphoreType.DMA((chans // GROUP,)),
        ],
        compiler_params=params(),
    )(raw, replica, table)


def spectra_last(local, halo, matrix, table, pulses):
    rows = local.shape[0]
    return pl.pallas_call(
        spectra_last_kernel,
        out_shape=jax.ShapeDtypeStruct((pulses, 2, rows // pulses, BLOCK), BF16),
        in_specs=[vmem_spec()] * 4,
        out_specs=vmem_spec(),
        compiler_params=params(),
    )(local, halo, matrix, table)


def cross_body(base, s_ref, before_ref, out_ref):
    bins, _, chans, gates = s_ref.shape
    lower = iota((chans, chans), 0) >= iota((chans, chans), 1)
    half = chans // 2

    def packed(block):
        swapped = pltpu.roll(block, chans, 1)
        mixed = jnp.where(lower, block[:, :chans], swapped[:, :chans])
        return jnp.concatenate([mixed[:half], mixed[half:]], axis=1)

    def write(e, block):
        value = jnp.concatenate([packed(block[:chans]), block[chans:]], axis=0)
        if before_ref is not None:
            value = value + before_ref[base + e]
        out_ref[e] = value

    @pl.loop(0, out_ref.shape[0] // 2, unroll=2)
    def _(step):
        e = step * 2
        each = []
        for k in range(4):
            where = lax.rem(base + e + k, bins)
            each.append((s_ref[where, 0], s_ref[where, 1]))
        left = jnp.concatenate(
            [jnp.concatenate([re, im], axis=1) for re, im in each], axis=0
        )
        right = jnp.concatenate(
            [
                jnp.concatenate(pieces, axis=1)
                for re, im in each[:2]
                for pieces in ((re, im), (-im, re))
            ],
            axis=0,
        )
        both = dot_nt(left, right)
        write(e, both[: 3 * chans, : 2 * chans])
        write(e + 1, both[chans:, 2 * chans :])


def cross_first_kernel(s_ref, out_ref):
    cross_body(0, s_ref, None, out_ref)


def cross_last_kernel(mine, s_ref, before_ref, out_ref):
    core = lax.axis_index("range") & 1
    base = (core if mine else 1 - core) * out_ref.shape[0]
    cross_body(base, s_ref, before_ref, out_ref)


def cross_first(spectra):
    bins, _, chans, _ = spectra.shape
    return pl.pallas_call(
        cross_first_kernel,
        out_shape=jax.ShapeDtypeStruct((bins, 5 * chans // 2, 2 * chans), F32),
        in_specs=[vmem_spec()],
        out_specs=vmem_spec(),
        compiler_params=params(),
    )(spectra)


def cross_last(mine, spectra, before):
    bins = spectra.shape[0]
    return pl.pallas_call(
        functools.partial(cross_last_kernel, mine),
        out_shape=jax.ShapeDtypeStruct((bins // 2,) + before.shape[1:], F32),
        in_specs=[vmem_spec(), vmem_spec()],
        out_specs=vmem_spec(),
        compiler_params=params(),
    )(spectra, before)


def partner(value, bit):
    count = lax.axis_size("range")
    return lax.ppermute(value, "range", [(i, i ^ bit) for i in range(count)])


def bin_of(index):
    low = index & 31
    return ((low & 1) << 4) | ((low & 2) << 2) | (low & 4) | (low >> 3)


def index_of(bin_id):
    return (bin_id >> 4) | ((bin_id >> 2) & 2) | (bin_id & 4) | ((bin_id & 3) << 3)


def place():
    index = lax.axis_index("range")
    return (index >> 1) & 1, (index >> 2) & 1, (index >> 3) & 3


def plane_kernel(keep_ref, core_ref, a_ref, b_ref):
    x, y, _ = place()
    half = keep_ref.shape[1] // 2
    for k in range(8):
        e = (1 - x) * 8 + k
        a_ref[k] = keep_ref[e, :half] + core_ref[e, :half]
        e = (k // 4) * 8 + (1 - y) * 4 + k % 4
        b_ref[k] = keep_ref[e, half:] + core_ref[e, half:]


def cross_plane_kernel(keep_ref, core_ref, a1_ref, b1_ref, a_ref, b_ref):
    x, y, _ = place()
    half = keep_ref.shape[1] // 2
    for k in range(4):
        e = x * 8 + (1 - y) * 4 + k
        a_ref[k] = keep_ref[e, :half] + core_ref[e, :half] + a1_ref[(1 - y) * 4 + k]
        e = (1 - x) * 8 + y * 4 + k
        b_ref[k] = keep_ref[e, half:] + core_ref[e, half:] + b1_ref[(1 - x) * 4 + k]


def line_sum(keep_ref, core_ref, a1_ref, b1_ref, a2_ref, b2_ref, z):
    x, y, _ = place()
    half = keep_ref.shape[1] // 2
    e = x * 8 + y * 4 + z
    upper = keep_ref[e, :half] + core_ref[e, :half] + a1_ref[y * 4 + z] + a2_ref[z]
    lower = keep_ref[e, half:] + core_ref[e, half:] + b1_ref[x * 4 + z] + b2_ref[z]
    return upper, lower


def line_kernel(*refs):
    z = place()[2]
    outs = refs[6:]
    half = refs[0].shape[1] // 2
    for k, out_ref in enumerate(outs):
        upper, lower = line_sum(*refs[:6], z ^ (k + 1))
        out_ref[:half] = upper
        out_ref[half:] = lower


def own_kernel(*refs):
    z1_ref, z2_ref, z3_ref, out_ref, packed_ref = refs[6:]
    half = refs[0].shape[1] // 2
    upper, lower = line_sum(*refs[:6], place()[2])
    upper = upper + z1_ref[:half] + (z2_ref[:half] + z3_ref[:half])
    out_ref[:half] = upper
    packed_ref[...] = upper[: packed_ref.shape[0]]
    out_ref[half:] = lower + z1_ref[half:] + (z2_ref[half:] + z3_ref[half:])


def summed(kernel, data, shapes):
    return pl.pallas_call(
        kernel,
        out_shape=[jax.ShapeDtypeStruct(shape, F32) for shape in shapes],
        in_specs=[vmem_spec()] * len(data),
        out_specs=[vmem_spec()] * len(shapes),
        compiler_params=params(),
    )(*data)


def bin_sums(keep, core):
    _, rows, wide = keep.shape
    half = rows // 2
    data = [keep, core]
    a, b = summed(plane_kernel, data, [(8, half, wide)] * 2)
    data += [partner(a, 2), partner(b, 4)]
    a, b = summed(cross_plane_kernel, data, [(4, half, wide)] * 2)
    data += [partner(a, 4), partner(b, 2)]
    sends = summed(line_kernel, data, [(rows, wide)] * 3)
    data += [partner(value, (k + 1) * 8) for k, value in enumerate(sends)]
    own, packed = summed(own_kernel, data, [(rows, wide), (rows // 5, wide)])
    bit = 32
    while bit < lax.axis_size("range"):
        own = own + partner(own, bit)
        packed = packed + partner(packed, bit)
        bit *= 2
    return own, packed


def from_bin(value, offset):
    count = lax.axis_size("range")
    pairs = []
    for i in range(count):
        target = index_of((bin_of(i) - offset) % 32) | (i & ~31)
        pairs.append((i, target))
    return lax.ppermute(value, "range", pairs)


def turn(value):
    half = value.shape[1] // 2
    rolled = pltpu.roll(value, half, 1)
    return jnp.where(iota(value.shape, 1) < half, -rolled, rolled)


def embed(value):
    return jnp.concatenate([value, turn(value)], axis=0)


def mul(a, b):
    return jnp.dot(a, embed(b), precision=lax.Precision.HIGHEST, preferred_element_type=F32)


def mul_conj(a, b):
    half = a.shape[1] // 2
    stacked = jnp.concatenate([a, -turn(a)], axis=0)
    both = dot_nt(stacked, b, lax.Precision.HIGHEST)
    rows = a.shape[0]
    return jnp.concatenate([both[:rows], both[rows:]], axis=1)


def conj_mul(a, b):
    half = a.shape[1] // 2
    both = lax.dot_general(
        a, b, (((0,), (0,)), ((), ())),
        precision=lax.Precision.HIGHEST, preferred_element_type=F32,
    )
    return both[:half] - turn(both[half:])


def pivot_inverse(p):
    def times(x, y):
        return x[0] * y[0] - x[1] * y[1], x[0] * y[1] + x[1] * y[0]

    def conj(x):
        return x[0], -x[1]

    def plus(x, y):
        return x[0] + y[0], x[1] + y[1]

    def scaled(x, s):
        return x[0] * s, x[1] * s

    def square(x):
        return x[0] * x[0] + x[1] * x[1]

    def two(a, b, d):
        inv = 1.0 / (a * d - square(b))
        return d * inv, scaled(b, -inv), a * inv

    a, d = p[0][0], p[1][1]
    b = p[0][1]
    ea, eb, ed = two(a, b, d)
    f = [[p[0][2], p[0][3]], [p[1][2], p[1][3]]]
    w = [
        [plus(scaled(f[0][j], ea), times(eb, f[1][j])) for j in range(2)],
        [plus(times(conj(eb), f[0][j]), scaled(f[1][j], ed)) for j in range(2)],
    ]

    def inner(i, j):
        return plus(times(conj(f[0][i]), w[0][j]), times(conj(f[1][i]), w[1][j]))

    ha = p[2][2] - inner(0, 0)[0]
    hd = p[3][3] - inner(1, 1)[0]
    cross = inner(0, 1)
    hb = (p[2][3][0] - cross[0], p[2][3][1] - cross[1])
    ga, gb, gd = two(ha, hb, hd)
    v = [
        [
            plus(scaled(w[i][0], ga), times(w[i][1], conj(gb))),
            plus(times(w[i][0], gb), scaled(w[i][1], gd)),
        ]
        for i in range(2)
    ]
    top = [
        [plus(times(v[i][0], conj(w[j][0])), times(v[i][1], conj(w[j][1]))) for j in range(2)]
        for i in range(2)
    ]
    zero = None
    out = [[None] * 4 for _ in range(4)]
    out[0][0] = (ea + top[0][0][0], zero)
    out[1][1] = (ed + top[1][1][0], zero)
    out[0][1] = plus(eb, top[0][1])
    out[2][2], out[3][3], out[2][3] = (ga, zero), (gd, zero), gb
    for i in range(2):
        for j in range(2):
            out[i][2 + j] = (-v[i][j][0], -v[i][j][1])
    for i in range(4):
        for j in range(i):
            out[i][j] = conj(out[j][i])
    return out


def invert(matrix):
    chans, width = matrix.shape
    sub = 8
    tiles = [matrix[t * sub : (t + 1) * sub, :] for t in range(chans // sub)]
    lane = iota((sub, width), 1)
    row = iota((sub, width), 0)
    first_half = lane < chans

    def spin(value):
        rolled = pltpu.roll(value, chans, 1)
        return jnp.where(first_half, -rolled, rolled)

    def column(value, k):
        return jnp.broadcast_to(value[:, k : k + 1], (sub, width))

    def combine(terms):
        while len(terms) > 1:
            terms = [
                terms[i] + terms[i + 1] if i + 1 < len(terms) else terms[i]
                for i in range(0, len(terms), 2)
            ]
        return terms[0]

    for k in range(0, chans, 4):
        t, r = divmod(k, sub)
        lines = [jnp.broadcast_to(tiles[t][r + i : r + i + 1, :], (sub, width)) for i in range(4)]
        pivot = [[None] * 4 for _ in range(4)]
        for i in range(4):
            pivot[i][i] = column(lines[i], k + i)
            for j in range(i + 1, 4):
                pivot[i][j] = column(lines[i], k + j), column(lines[i], chans + k + j)
        low = jnp.bitwise_and(lane, chans - 1)
        cleared = (low >= k) & (low < k + 4)
        unit = [
            jnp.where(cleared, jnp.where(lane == k + i, 1.0, 0.0), lines[i]) for i in range(4)
        ]
        spun = [spin(u) for u in unit]
        p = pivot_inverse(pivot)
        fresh_lines, fresh_spun = [], []
        for i in range(4):
            terms, other = [], []
            for j in range(4):
                re, im = p[i][j]
                terms.append(re * unit[j])
                other.append(re * spun[j])
                if im is not None:
                    terms.append(im * spun[j])
                    other.append(-(im * unit[j]))
            fresh_lines.append(combine(terms))
            fresh_spun.append(combine(other))
        fresh = []
        for s, tile in enumerate(tiles):
            terms = []
            for i in range(4):
                terms.append(column(tile, k + i) * fresh_lines[i])
                terms.append(column(tile, chans + k + i) * fresh_spun[i])
            value = jnp.where(cleared, 0.0, tile) - combine(terms)
            if s == t:
                for i in range(4):
                    value = jnp.where(row == r + i, fresh_lines[i], value)
            fresh.append(value)
        tiles = fresh
    return jnp.concatenate(tiles, axis=0)


def unpacked(ref, scale):
    half, wide = ref.shape[0], ref.shape[1]
    piece = ref[...] * scale
    swapped = pltpu.roll(piece, wide // 2, 1)
    return jnp.concatenate([piece, swapped], axis=0)[:, : wide // 2]


def hermitian(mixed, across):
    i, j = iota(mixed.shape, 0), iota(mixed.shape, 1)
    real_part = jnp.where(i >= j, mixed, across)
    imag_part = jnp.where(i < j, mixed, jnp.where(i > j, -across, 0.0))
    return jnp.concatenate([real_part, imag_part], axis=1)


def middle_kernel(total, packed_ref, steer_ref, inv_ref, t_ref):
    chans = inv_ref.shape[0]
    mixed = unpacked(packed_ref, F32(1.0 / total))
    twice = jnp.concatenate([mixed, mixed], axis=1)
    across = jnp.concatenate([twice, twice], axis=0).T[:chans, :chans]
    inverse = invert(hermitian(mixed, across))
    inv_ref[...] = inverse
    t_ref[...] = mul(steer_ref[...], inverse)


def outer_kernel(total, own_ref, left_ref, right_ref, steer_ref, inv_ref, t_ref, out_ref,
                 work, keep):
    chans = inv_ref.shape[0]
    scale = F32(1.0 / total)
    half = chans // 2
    m_left = unpacked(left_ref.at[:half], scale)
    m_right = unpacked(right_ref, scale)
    ml = left_ref[half : half + chans] * scale
    rl = left_ref[half + chans :] * scale
    rm = own_ref[half : half + chans] * scale
    pair = jnp.concatenate([m_left, m_right], axis=1)
    square = jnp.concatenate([pair, pair], axis=0).T
    inv_mid = inv_ref[...]
    t = t_ref[...]
    h = mul(inv_mid, ml)
    g = mul(rm, inv_mid)
    work[...] = hermitian(m_left, square[:chans, :chans]) - conj_mul(ml, h)
    s_rl = rl - mul(rm, h)
    s_rr = hermitian(m_right, square[chans:, :chans]) - mul_conj(g, rm)
    rhs_left = -mul(t, ml)
    rhs_right = -mul_conj(t, rm)
    keep[0] = s_rl
    keep[1] = s_rr
    keep[2] = h
    keep[3] = g
    keep[4, 0:BEAMS] = rhs_left
    keep[4, BEAMS : 2 * BEAMS] = rhs_right

    @pl.loop(0, 2)
    def _(stage):
        work[...] = invert(work[...])

        @pl.when(stage == 0)
        def _():
            inverse = work[...]
            s_rl = keep[0]
            both = mul(jnp.concatenate([s_rl, keep[4, 0:BEAMS]], axis=0), inverse)
            k, y_left = both[:chans], both[chans:]
            work[...] = keep[1] - mul_conj(k, s_rl)
            keep[0] = k
            keep[4, BEAMS : 2 * BEAMS] = keep[4, BEAMS : 2 * BEAMS] - mul_conj(y_left, s_rl)
            keep[4, 0:BEAMS] = y_left
            keep[4, 2 * BEAMS : 3 * BEAMS] = t_ref[...] - mul_conj(y_left, keep[2])
            keep[3] = keep[3] - mul_conj(k, keep[2])

        @pl.when(stage == 1)
        def _():
            y_right = mul(keep[4, BEAMS : 2 * BEAMS], work[...])
            y_left = keep[4, 0:BEAMS] - mul(y_right, keep[0])
            y_mid = keep[4, 2 * BEAMS : 3 * BEAMS] - mul(y_right, keep[3])
            quad = jnp.sum(steer_ref[...] * y_mid, axis=1, keepdims=True)
            y = jnp.concatenate([y_left, y_mid, y_right], axis=1) / jnp.sqrt(quad)
            real_lane = lax.rem(iota(y.shape, 1), 2 * chans) < chans
            mine = jnp.where(real_lane, y, -y).astype(BF16)
            for c in range(out_ref.shape[0]):
                out_ref[c] = mine


def steering(chans):
    index = np.arange(chans)
    sines = -0.8 + 1.6 * np.arange(BEAMS) / (BEAMS - 1)
    angle = math.pi * sines[:, None] * index[None, :]
    return np.concatenate([np.cos(angle), -np.sin(angle)], axis=1).astype(np.float32)


def solve_middle(packed, steer, total):
    half, wide = packed.shape
    return pl.pallas_call(
        functools.partial(middle_kernel, total),
        out_shape=[
            jax.ShapeDtypeStruct((2 * half, wide), F32),
            jax.ShapeDtypeStruct((BEAMS, wide), F32),
        ],
        in_specs=[vmem_spec()] * 2,
        out_specs=[vmem_spec()] * 2,
        compiler_params=params(),
    )(packed, steer)


def solve_outer(own, left, right, steer, inverse, t, total, copies):
    chans, wide = inverse.shape
    return pl.pallas_call(
        functools.partial(outer_kernel, total),
        out_shape=jax.ShapeDtypeStruct((copies, BEAMS, 3 * wide), BF16),
        in_specs=[vmem_spec()] * 6,
        out_specs=vmem_spec(),
        scratch_shapes=[pltpu.VMEM((chans, wide), F32), pltpu.VMEM((5, chans, wide), F32)],
        compiler_params=params(),
    )(own, left, right, steer, inverse, t)


def beam_kernel(bin_ref, block_ref, beam_ref, owner_ref, s0_ref, s1_ref, w_ref, out_ref,
                both_ref, rows_ref, seen_ref):
    bins, wide, gates = s0_ref.shape
    devices = seen_ref.shape[0]
    count = bin_ref.shape[0]
    rows_ref[...] = jnp.zeros_like(rows_ref)

    @pl.loop(0, devices)
    def _(i):
        seen_ref[i] = 0

    w = w_ref[...].astype(F32)
    for k in range(3):
        part = w[:, k * wide : (k + 1) * wide]
        both_ref[:, 0:BEAMS, k * wide : (k + 1) * wide] = part.reshape(bins, BEAMS, wide)
        both_ref[:, BEAMS:, k * wide : (k + 1) * wide] = turn(part).reshape(bins, BEAMS, wide)

    def detection(j, carry):
        bin_id = bin_ref[j]
        beam_id = beam_ref[j]
        owner = owner_ref[j]
        rank = seen_ref[owner]
        seen_ref[owner] = rank + 1
        left = both_ref[index_of(bin_id)].astype(BF16)
        bands = [lax.rem(bin_id + bins - 1 + k, bins) for k in range(3)]
        first = block_ref[j] == 0
        window = jnp.concatenate(
            [jnp.where(first, s0_ref[b], s1_ref[b]) for b in bands], axis=0
        )
        both = dot(left, window)
        line = jnp.concatenate([both[:BEAMS], both[BEAMS:]], axis=1)
        chosen = jnp.where(iota(line.shape, 0) == beam_id, line, 0.0)
        row = owner * CAP + rank
        rows_ref[pl.ds(row, 1), :] = jnp.sum(chosen, axis=0, keepdims=True)
        return carry

    lax.fori_loop(0, count, detection, 0, unroll=4)
    out_ref[...] = rows_ref[...].astype(BF16)


def beam_rows(det_bin, det_block, det_beam, owners, s0, s1, weight, devices):
    bins, wide, gates = s0.shape
    return pl.pallas_call(
        beam_kernel,
        out_shape=jax.ShapeDtypeStruct((devices * CAP, 2 * gates), BF16),
        in_specs=[smem_spec()] * 4 + [vmem_spec()] * 3,
        out_specs=vmem_spec(),
        scratch_shapes=[
            pltpu.VMEM((bins, 2 * BEAMS, 3 * wide), F32),
            pltpu.VMEM((devices * CAP, 2 * gates), F32),
            pltpu.SMEM((devices,), jnp.int32),
        ],
        compiler_params=params(),
    )(det_bin, det_block, det_beam, owners, s0, s1, weight)


def on_device(raw, replica, det_bin, det_block, det_beam, det_owner):
    devices = lax.axis_size("range")
    _, chans, pulses, gates = raw.shape
    bins = pulses
    flat = raw.reshape(2, chans * pulses, gates)
    halo = lax.ppermute(
        first_gates(flat), "range", [(source, source - 1) for source in range(1, devices)]
    )
    table = doppler_matrix(pulses, 8)
    s0, local, matrix = spectra_first(flat, replica, table, pulses)
    first = cross_first(s0)
    s1 = spectra_last(local, halo, matrix, table, pulses)
    core_sum = partner(cross_last(False, s1, first), 1)
    keep = cross_last(True, s1, first)
    own, packed = bin_sums(keep, core_sum)
    total = gates * devices
    steer = steering(chans)
    left = from_bin(own, -1)
    right = from_bin(packed, 1)
    inverse, t = solve_middle(packed, steer, total)
    mine = solve_outer(own, left, right, steer, inverse, t, total, bins)
    groups = [list(range(first, first + bins)) for first in range(0, devices, bins)]
    weight = lax.all_to_all(
        mine, "range", split_axis=0, concat_axis=0, tiled=True,
        axis_index_groups=groups if len(groups) > 1 else None,
    ).reshape(bins * BEAMS, mine.shape[2])
    outgoing = beam_rows(
        det_bin, det_block, det_beam, det_owner[:, 0],
        s0.reshape(bins, 2 * chans, BLOCK), s1.reshape(bins, 2 * chans, BLOCK), weight, devices,
    )
    incoming = lax.all_to_all(
        outgoing.reshape(devices, CAP, 2 * BLOCK), "range", split_axis=0, concat_axis=0, tiled=True
    )
    return incoming.astype(F32).reshape(devices * CAP, 2 * BLOCK)


def solution(mesh):
    in_specs = (
        P(None, None, None, "range"),
        P(),
        P("range"),
        P("range"),
        P("range"),
        P("range", None),
    )
    out_specs = P("range", None)
    return jax.shard_map(
        on_device, mesh=mesh, in_specs=in_specs, out_specs=out_specs, check_vma=False
    )
```

```python
import functools
import math

import jax
import jax.numpy as jnp
import ml_dtypes
import numpy as np
from jax import lax
from jax.experimental import pallas as pl
from jax.experimental.pallas import tpu as pltpu
from jax.sharding import PartitionSpec as P

BLOCK = 128
BEAMS = 8
CAP = 2

F32 = jnp.float32
BF16 = jnp.bfloat16
VMEM = pltpu.VMEM
MIB = 1024 * 1024
NT = (((1,), (1,)), ((), ()))


def vmem_spec():
    return pl.BlockSpec(memory_space=VMEM)


def smem_spec():
    return pl.BlockSpec(memory_space=pltpu.SMEM)


def hbm_spec():
    return pl.BlockSpec(memory_space=pltpu.HBM)


def params(mib=16):
    return pltpu.CompilerParams(vmem_limit_bytes=mib * MIB)


def dot(a, b):
    return jnp.dot(a, b, preferred_element_type=F32)


def dot_nt(a, b, precision=None):
    return lax.dot_general(a, b, NT, precision=precision, preferred_element_type=F32)


def iota(shape, axis):
    return lax.broadcasted_iota(jnp.int32, shape, axis)


def halo_kernel(raw_ref, out_ref, sems):
    parts = sems.shape[0]
    size = out_ref.shape[1] // parts
    copies = [
        pltpu.make_async_copy(
            raw_ref.at[:, j * size : (j + 1) * size, :BLOCK],
            out_ref.at[:, j * size : (j + 1) * size, :],
            sems.at[j],
        )
        for j in range(parts)
    ]
    for copy in copies:
        copy.start()
    for copy in copies:
        copy.wait()


def first_gates(raw):
    return pl.pallas_call(
        halo_kernel,
        out_shape=jax.ShapeDtypeStruct(raw.shape[:2] + (BLOCK,), BF16),
        in_specs=[hbm_spec()],
        out_specs=vmem_spec(),
        scratch_shapes=[pltpu.SemaphoreType.DMA((8,))],
        compiler_params=params(63),
    )(raw)


def correlation_matrix(rep_ref, out_ref):
    taps = rep_ref.shape[1]
    base = rep_ref[...].astype(F32)
    row = iota((taps, 2 * taps), 0)
    parts = []
    for i in range(2):
        line = jnp.concatenate([base[i : i + 1], jnp.zeros((1, taps), F32)], axis=1)
        skew = jnp.broadcast_to(line, (taps, 2 * taps))
        bit = 1
        while bit < taps:
            skew = jnp.where((row & bit) != 0, pltpu.roll(skew, bit, 1), skew)
            bit *= 2
        parts.append(skew.T)
    real_part, imag_part = parts
    out_ref[0] = jnp.concatenate([real_part, -imag_part], axis=1).astype(BF16)
    out_ref[1] = jnp.concatenate([imag_part, real_part], axis=1).astype(BF16)


def doppler_matrix(pulses, group):
    index = np.arange(pulses)
    angle = 2.0 * math.pi / pulses * (index[:, None] * index[None, :] % pulses)
    cosine = np.cos(angle) * pulses**-0.5
    sine = np.sin(angle) * pulses**-0.5
    table = np.stack([np.stack([cosine, -sine], 1), np.stack([sine, cosine], 1)], 0)
    full = np.einsum("ipod,ce->dociep", table, np.eye(group))
    shape = (pulses * 2 * group, 2 * group * pulses)
    return full.reshape(shape).astype(ml_dtypes.bfloat16)


def doppler_rows(total, dft):
    compressed = total.astype(BF16)
    rows, wide = compressed.shape
    half, gates = rows // 2, wide // 2
    stacked = jnp.concatenate(
        [
            jnp.concatenate([compressed[:half, :gates], compressed[half:, :gates]], axis=1),
            jnp.concatenate([compressed[:half, gates:], compressed[half:, gates:]], axis=1),
        ],
        axis=0,
    )
    both = dot(dft, stacked)
    lines = both.shape[0] // 8
    joined = jnp.concatenate(
        [both[:, :gates].reshape(lines, 8, gates), both[:, gates:].reshape(lines, 8, gates)],
        axis=1,
    )
    return joined.astype(BF16)


GROUP = 16


def spectra_first_kernel(raw_ref, rep_ref, dft_ref, s_ref, local_ref, taps_ref, buf, sems):
    bins, _, chans, gates = s_ref.shape
    size = GROUP * bins
    copies = [
        pltpu.make_async_copy(
            raw_ref.at[:, j * size : (j + 1) * size, :],
            buf.at[:, j * size : (j + 1) * size, :],
            sems.at[j],
        )
        for j in range(chans // GROUP)
    ]
    for copy in copies:
        copy.start()
    correlation_matrix(rep_ref, taps_ref)
    for j, copy in enumerate(copies):
        copy.wait()
        rows = slice(j * size, (j + 1) * size)
        total = dot(buf[0, rows, :], taps_ref[0]) + dot(buf[1, rows, :], taps_ref[1])
        out = doppler_rows(total, dft_ref[...])
        s_ref[:, :, j * GROUP : (j + 1) * GROUP, :] = out.reshape(bins, 2, GROUP, gates)
        later = jnp.concatenate([buf[0, rows, gates:], buf[1, rows, gates:]], axis=1)
        near = jnp.concatenate([taps_ref[0, :gates, :], taps_ref[1, :gates, :]], axis=0)
        local_ref[rows, :] = dot(later, near)


def spectra_last_kernel(local_ref, halo_ref, taps_ref, dft_ref, s_ref):
    bins, _, chans, gates = s_ref.shape
    size = GROUP * bins
    for j in range(chans // GROUP):
        rows = slice(j * size, (j + 1) * size)
        later = jnp.concatenate([halo_ref[0, rows, :], halo_ref[1, rows, :]], axis=1)
        far = jnp.concatenate([taps_ref[0, gates:, :], taps_ref[1, gates:, :]], axis=0)
        out = doppler_rows(local_ref[rows, :] + dot(later, far), dft_ref[...])
        s_ref[:, :, j * GROUP : (j + 1) * GROUP, :] = out.reshape(bins, 2, GROUP, gates)


def spectra_first(raw, replica, table, pulses):
    _, rows, gates = raw.shape
    chans = rows // pulses
    taps = replica.shape[1]
    return pl.pallas_call(
        spectra_first_kernel,
        out_shape=[
            jax.ShapeDtypeStruct((pulses, 2, chans, BLOCK), BF16),
            jax.ShapeDtypeStruct((rows, 2 * BLOCK), F32),
            jax.ShapeDtypeStruct((2, 2 * taps, 2 * taps), BF16),
        ],
        in_specs=[hbm_spec(), vmem_spec(), vmem_spec()],
        out_specs=[vmem_spec()] * 3,
        scratch_shapes=[
            pltpu.VMEM(raw.shape, BF16),
            pltpu.SemaphoreType.DMA((chans // GROUP,)),
        ],
        compiler_params=params(),
    )(raw, replica, table)


def spectra_last(local, halo, matrix, table, pulses):
    rows = local.shape[0]
    return pl.pallas_call(
        spectra_last_kernel,
        out_shape=jax.ShapeDtypeStruct((pulses, 2, rows // pulses, BLOCK), BF16),
        in_specs=[vmem_spec()] * 4,
        out_specs=vmem_spec(),
        compiler_params=params(),
    )(local, halo, matrix, table)


def cross_body(base, s_ref, before_ref, out_ref):
    bins, _, chans, gates = s_ref.shape
    lower = iota((chans, chans), 0) >= iota((chans, chans), 1)
    half = chans // 2

    def packed(block):
        swapped = pltpu.roll(block, chans, 1)
        mixed = jnp.where(lower, block[:, :chans], swapped[:, :chans])
        return jnp.concatenate([mixed[:half], mixed[half:]], axis=1)

    def write(e, block):
        value = jnp.concatenate([packed(block[:chans]), block[chans:]], axis=0)
        if before_ref is not None:
            value = value + before_ref[base + e]
        out_ref[e] = value

    @pl.loop(0, out_ref.shape[0] // 2, unroll=2)
    def _(step):
        e = step * 2
        each = []
        for k in range(4):
            where = lax.rem(base + e + k, bins)
            each.append((s_ref[where, 0], s_ref[where, 1]))
        left = jnp.concatenate(
            [jnp.concatenate([re, im], axis=1) for re, im in each], axis=0
        )
        right = jnp.concatenate(
            [
                jnp.concatenate(pieces, axis=1)
                for re, im in each[:2]
                for pieces in ((re, im), (-im, re))
            ],
            axis=0,
        )
        both = dot_nt(left, right)
        write(e, both[: 3 * chans, : 2 * chans])
        write(e + 1, both[chans:, 2 * chans :])


def cross_first_kernel(s_ref, out_ref):
    cross_body(0, s_ref, None, out_ref)


def cross_last_kernel(mine, s_ref, before_ref, out_ref):
    core = lax.axis_index("range") & 1
    base = (core if mine else 1 - core) * out_ref.shape[0]
    cross_body(base, s_ref, before_ref, out_ref)


def cross_first(spectra):
    bins, _, chans, _ = spectra.shape
    return pl.pallas_call(
        cross_first_kernel,
        out_shape=jax.ShapeDtypeStruct((bins, 5 * chans // 2, 2 * chans), F32),
        in_specs=[vmem_spec()],
        out_specs=vmem_spec(),
        compiler_params=params(),
    )(spectra)


def cross_last(mine, spectra, before):
    bins = spectra.shape[0]
    return pl.pallas_call(
        functools.partial(cross_last_kernel, mine),
        out_shape=jax.ShapeDtypeStruct((bins // 2,) + before.shape[1:], F32),
        in_specs=[vmem_spec(), vmem_spec()],
        out_specs=vmem_spec(),
        compiler_params=params(),
    )(spectra, before)


X, Y, Z0, Z1 = 0, 1, 2, 3
DEVICE_BIT = (2, 4, 8, 16)
BIN_BIT = (8, 4, 1, 2)
ORDERS = ((X, Y, Z0, Z1), (Y, Z0, X, Z1), (Z0, X, Y, Z1))


def partner(value, bit):
    count = lax.axis_size("range")
    return lax.ppermute(value, "range", [(i, i ^ bit) for i in range(count)])


def bin_of(index):
    low = index & 31
    return ((low & 1) << 4) | ((low & 2) << 2) | (low & 4) | (low >> 3)


def index_of(bin_id):
    return (bin_id >> 4) | ((bin_id >> 2) & 2) | (bin_id & 4) | ((bin_id & 3) << 3)


def row_parts(rows):
    third = -(-rows // 24) * 8
    return ((0, third), (third, 2 * third), (2 * third, rows))


def gathered(keep_ref, core_ref, received, order, span, bits):
    first, last = span
    e = sum(bits[axis] * BIN_BIT[axis] for axis in range(4))
    value = keep_ref[e, first:last] + core_ref[e, first:last]
    for stage, ref in enumerate(received):
        place = 0
        for axis in order[stage + 1 :]:
            place = place * 2 + bits[axis]
        value = value + ref[place]
    return value


def stage_kernel(stage, rows, *refs):
    spans = row_parts(rows)
    keep_ref, core_ref = refs[:2]
    received = [refs[2 + p * stage : 2 + (p + 1) * stage] for p in range(3)]
    outs = refs[2 + 3 * stage :]
    index = lax.axis_index("range")
    mine = [(index // DEVICE_BIT[axis]) & 1 for axis in range(4)]
    for p, order in enumerate(ORDERS):
        later = order[stage + 1 :]
        for k in range(1 << len(later)):
            bits = list(mine)
            bits[order[stage]] = 1 - mine[order[stage]]
            for i, axis in enumerate(later):
                bits[axis] = (k >> (len(later) - 1 - i)) & 1
            outs[p][k] = gathered(keep_ref, core_ref, received[p], order, spans[p], bits)


def own_kernel(rows, *refs):
    spans = row_parts(rows)
    received = [refs[2 + 4 * p : 6 + 4 * p] for p in range(3)]
    out_ref, packed_ref = refs[14:]
    index = lax.axis_index("range")
    mine = [(index // DEVICE_BIT[axis]) & 1 for axis in range(4)]
    for p, order in enumerate(ORDERS):
        first, last = spans[p]
        value = gathered(refs[0], refs[1], received[p], order, spans[p], mine)
        out_ref[first:last] = value
        if p == 0:
            packed_ref[...] = value[: packed_ref.shape[0]]


def summed(kernel, data, shapes):
    return pl.pallas_call(
        kernel,
        out_shape=[jax.ShapeDtypeStruct(shape, F32) for shape in shapes],
        in_specs=[vmem_spec()] * len(data),
        out_specs=[vmem_spec()] * len(shapes),
        compiler_params=params(),
    )(*data)


def bin_sums(keep, core):
    _, rows, wide = keep.shape
    received = [[], [], []]
    for stage in range(4):
        data = [keep, core] + received[0] + received[1] + received[2]
        shapes = [(8 >> stage, last - first, wide) for first, last in row_parts(rows)]
        sends = summed(functools.partial(stage_kernel, stage, rows), data, shapes)
        for p, value in enumerate(sends):
            received[p] = received[p] + [partner(value, DEVICE_BIT[ORDERS[p][stage]])]
    data = [keep, core] + received[0] + received[1] + received[2]
    own, packed = summed(
        functools.partial(own_kernel, rows), data, [(rows, wide), (rows // 5, wide)]
    )
    bit = 32
    while bit < lax.axis_size("range"):
        own = own + partner(own, bit)
        packed = packed + partner(packed, bit)
        bit *= 2
    return own, packed


def from_bin(value, offset):
    count = lax.axis_size("range")
    pairs = []
    for i in range(count):
        target = index_of((bin_of(i) - offset) % 32) | (i & ~31)
        pairs.append((i, target))
    return lax.ppermute(value, "range", pairs)


def turn(value):
    half = value.shape[1] // 2
    rolled = pltpu.roll(value, half, 1)
    return jnp.where(iota(value.shape, 1) < half, -rolled, rolled)


def embed(value):
    return jnp.concatenate([value, turn(value)], axis=0)


def mul(a, b):
    return jnp.dot(a, embed(b), precision=lax.Precision.HIGHEST, preferred_element_type=F32)


def mul_conj(a, b):
    half = a.shape[1] // 2
    stacked = jnp.concatenate([a, -turn(a)], axis=0)
    both = dot_nt(stacked, b, lax.Precision.HIGHEST)
    rows = a.shape[0]
    return jnp.concatenate([both[:rows], both[rows:]], axis=1)


def conj_mul(a, b):
    half = a.shape[1] // 2
    both = lax.dot_general(
        a, b, (((0,), (0,)), ((), ())),
        precision=lax.Precision.HIGHEST, preferred_element_type=F32,
    )
    return both[:half] - turn(both[half:])


def reciprocal(x):
    value = pl.reciprocal(x, approx=True)
    for _ in range(2):
        value = value * (2.0 - x * value)
    return value


def pivot_inverse(p):
    def times(x, y):
        return x[0] * y[0] - x[1] * y[1], x[0] * y[1] + x[1] * y[0]

    def conj(x):
        return x[0], -x[1]

    def plus(x, y):
        return x[0] + y[0], x[1] + y[1]

    def scaled(x, s):
        return x[0] * s, x[1] * s

    def square(x):
        return x[0] * x[0] + x[1] * x[1]

    def two(a, b, d):
        inv = reciprocal(a * d - square(b))
        return d * inv, scaled(b, -inv), a * inv

    a, d = p[0][0], p[1][1]
    b = p[0][1]
    ea, eb, ed = two(a, b, d)
    f = [[p[0][2], p[0][3]], [p[1][2], p[1][3]]]
    w = [
        [plus(scaled(f[0][j], ea), times(eb, f[1][j])) for j in range(2)],
        [plus(times(conj(eb), f[0][j]), scaled(f[1][j], ed)) for j in range(2)],
    ]

    def inner(i, j):
        return plus(times(conj(f[0][i]), w[0][j]), times(conj(f[1][i]), w[1][j]))

    ha = p[2][2] - inner(0, 0)[0]
    hd = p[3][3] - inner(1, 1)[0]
    cross = inner(0, 1)
    hb = (p[2][3][0] - cross[0], p[2][3][1] - cross[1])
    ga, gb, gd = two(ha, hb, hd)
    v = [
        [
            plus(scaled(w[i][0], ga), times(w[i][1], conj(gb))),
            plus(times(w[i][0], gb), scaled(w[i][1], gd)),
        ]
        for i in range(2)
    ]
    top = [
        [plus(times(v[i][0], conj(w[j][0])), times(v[i][1], conj(w[j][1]))) for j in range(2)]
        for i in range(2)
    ]
    zero = None
    out = [[None] * 4 for _ in range(4)]
    out[0][0] = (ea + top[0][0][0], zero)
    out[1][1] = (ed + top[1][1][0], zero)
    out[0][1] = plus(eb, top[0][1])
    out[2][2], out[3][3], out[2][3] = (ga, zero), (gd, zero), gb
    for i in range(2):
        for j in range(2):
            out[i][2 + j] = (-v[i][j][0], -v[i][j][1])
    for i in range(4):
        for j in range(i):
            out[i][j] = conj(out[j][i])
    return out


def invert(matrix):
    chans, width = matrix.shape
    sub = 8
    tiles = [matrix[t * sub : (t + 1) * sub, :] for t in range(chans // sub)]
    lane = iota((sub, width), 1)
    row = iota((sub, width), 0)
    first_half = lane < chans

    def spin(value):
        rolled = pltpu.roll(value, chans, 1)
        return jnp.where(first_half, -rolled, rolled)

    def column(value, k):
        return jnp.broadcast_to(value[:, k : k + 1], (sub, width))

    def combine(terms):
        while len(terms) > 1:
            terms = [
                terms[i] + terms[i + 1] if i + 1 < len(terms) else terms[i]
                for i in range(0, len(terms), 2)
            ]
        return terms[0]

    for k in range(0, chans, 4):
        t, r = divmod(k, sub)
        lines = [jnp.broadcast_to(tiles[t][r + i : r + i + 1, :], (sub, width)) for i in range(4)]
        pivot = [[None] * 4 for _ in range(4)]
        for i in range(4):
            pivot[i][i] = column(lines[i], k + i)
            for j in range(i + 1, 4):
                pivot[i][j] = column(lines[i], k + j), column(lines[i], chans + k + j)
        low = jnp.bitwise_and(lane, chans - 1)
        cleared = (low >= k) & (low < k + 4)
        unit = [
            jnp.where(cleared, jnp.where(lane == k + i, 1.0, 0.0), lines[i]) for i in range(4)
        ]
        spun = [spin(u) for u in unit]
        p = pivot_inverse(pivot)
        fresh_lines, fresh_spun = [], []
        for i in range(4):
            terms, other = [], []
            for j in range(4):
                re, im = p[i][j]
                terms.append(re * unit[j])
                other.append(re * spun[j])
                if im is not None:
                    terms.append(im * spun[j])
                    other.append(-(im * unit[j]))
            fresh_lines.append(combine(terms))
            fresh_spun.append(combine(other))
        fresh = []
        for s, tile in enumerate(tiles):
            terms = []
            for i in range(4):
                terms.append(column(tile, k + i) * fresh_lines[i])
                terms.append(column(tile, chans + k + i) * fresh_spun[i])
            value = jnp.where(cleared, 0.0, tile) - combine(terms)
            if s == t:
                for i in range(4):
                    value = jnp.where(row == r + i, fresh_lines[i], value)
            fresh.append(value)
        tiles = fresh
    return jnp.concatenate(tiles, axis=0)


def unpacked(ref, scale):
    half, wide = ref.shape[0], ref.shape[1]
    piece = ref[...] * scale
    swapped = pltpu.roll(piece, wide // 2, 1)
    return jnp.concatenate([piece, swapped], axis=0)[:, : wide // 2]


def hermitian(mixed, across):
    i, j = iota(mixed.shape, 0), iota(mixed.shape, 1)
    real_part = jnp.where(i >= j, mixed, across)
    imag_part = jnp.where(i < j, mixed, jnp.where(i > j, -across, 0.0))
    return jnp.concatenate([real_part, imag_part], axis=1)


def middle_kernel(total, packed_ref, steer_ref, inv_ref, t_ref):
    chans = inv_ref.shape[0]
    mixed = unpacked(packed_ref, F32(1.0 / total))
    twice = jnp.concatenate([mixed, mixed], axis=1)
    across = jnp.concatenate([twice, twice], axis=0).T[:chans, :chans]
    inverse = invert(hermitian(mixed, across))
    inv_ref[...] = inverse
    t_ref[...] = mul(steer_ref[...], inverse)


def outer_kernel(total, own_ref, left_ref, right_ref, steer_ref, inv_ref, t_ref, out_ref,
                 work, keep):
    chans = inv_ref.shape[0]
    scale = F32(1.0 / total)
    half = chans // 2
    m_left = unpacked(left_ref.at[:half], scale)
    m_right = unpacked(right_ref, scale)
    ml = left_ref[half : half + chans] * scale
    rl = left_ref[half + chans :] * scale
    rm = own_ref[half : half + chans] * scale
    pair = jnp.concatenate([m_left, m_right], axis=1)
    square = jnp.concatenate([pair, pair], axis=0).T
    inv_mid = inv_ref[...]
    t = t_ref[...]
    h = mul(inv_mid, ml)
    g = mul(rm, inv_mid)
    work[...] = hermitian(m_left, square[:chans, :chans]) - conj_mul(ml, h)
    s_rl = rl - mul(rm, h)
    s_rr = hermitian(m_right, square[chans:, :chans]) - mul_conj(g, rm)
    rhs_left = -mul(t, ml)
    rhs_right = -mul_conj(t, rm)
    keep[0] = s_rl
    keep[1] = s_rr
    keep[2] = h
    keep[3] = g
    keep[4, 0:BEAMS] = rhs_left
    keep[4, BEAMS : 2 * BEAMS] = rhs_right

    @pl.loop(0, 2)
    def _(stage):
        work[...] = invert(work[...])

        @pl.when(stage == 0)
        def _():
            inverse = work[...]
            s_rl = keep[0]
            both = mul(jnp.concatenate([s_rl, keep[4, 0:BEAMS]], axis=0), inverse)
            k, y_left = both[:chans], both[chans:]
            work[...] = keep[1] - mul_conj(k, s_rl)
            keep[0] = k
            keep[4, BEAMS : 2 * BEAMS] = keep[4, BEAMS : 2 * BEAMS] - mul_conj(y_left, s_rl)
            keep[4, 0:BEAMS] = y_left
            keep[4, 2 * BEAMS : 3 * BEAMS] = t_ref[...] - mul_conj(y_left, keep[2])
            keep[3] = keep[3] - mul_conj(k, keep[2])

        @pl.when(stage == 1)
        def _():
            y_right = mul(keep[4, BEAMS : 2 * BEAMS], work[...])
            y_left = keep[4, 0:BEAMS] - mul(y_right, keep[0])
            y_mid = keep[4, 2 * BEAMS : 3 * BEAMS] - mul(y_right, keep[3])
            quad = jnp.sum(steer_ref[...] * y_mid, axis=1, keepdims=True)
            y = jnp.concatenate([y_left, y_mid, y_right], axis=1) / jnp.sqrt(quad)
            real_lane = lax.rem(iota(y.shape, 1), 2 * chans) < chans
            mine = jnp.where(real_lane, y, -y).astype(BF16)
            for c in range(out_ref.shape[0]):
                out_ref[c] = mine


def steering(chans):
    index = np.arange(chans)
    sines = -0.8 + 1.6 * np.arange(BEAMS) / (BEAMS - 1)
    angle = math.pi * sines[:, None] * index[None, :]
    return np.concatenate([np.cos(angle), -np.sin(angle)], axis=1).astype(np.float32)


def solve_middle(packed, steer, total):
    half, wide = packed.shape
    return pl.pallas_call(
        functools.partial(middle_kernel, total),
        out_shape=[
            jax.ShapeDtypeStruct((2 * half, wide), F32),
            jax.ShapeDtypeStruct((BEAMS, wide), F32),
        ],
        in_specs=[vmem_spec()] * 2,
        out_specs=[vmem_spec()] * 2,
        compiler_params=params(),
    )(packed, steer)


def solve_outer(own, left, right, steer, inverse, t, total, copies):
    chans, wide = inverse.shape
    return pl.pallas_call(
        functools.partial(outer_kernel, total),
        out_shape=jax.ShapeDtypeStruct((copies, BEAMS, 3 * wide), BF16),
        in_specs=[vmem_spec()] * 6,
        out_specs=vmem_spec(),
        scratch_shapes=[pltpu.VMEM((chans, wide), F32), pltpu.VMEM((5, chans, wide), F32)],
        compiler_params=params(),
    )(own, left, right, steer, inverse, t)


def beam_kernel(bin_ref, block_ref, beam_ref, owner_ref, s0_ref, s1_ref, w_ref, out_ref,
                both_ref, rows_ref, seen_ref):
    bins, wide, gates = s0_ref.shape
    devices = seen_ref.shape[0]
    count = bin_ref.shape[0]
    rows_ref[...] = jnp.zeros_like(rows_ref)

    @pl.loop(0, devices)
    def _(i):
        seen_ref[i] = 0

    w = w_ref[...].astype(F32)
    for k in range(3):
        part = w[:, k * wide : (k + 1) * wide]
        both_ref[:, 0:BEAMS, k * wide : (k + 1) * wide] = part.reshape(bins, BEAMS, wide)
        both_ref[:, BEAMS:, k * wide : (k + 1) * wide] = turn(part).reshape(bins, BEAMS, wide)

    def detection(j, carry):
        bin_id = bin_ref[j]
        beam_id = beam_ref[j]
        owner = owner_ref[j]
        rank = seen_ref[owner]
        seen_ref[owner] = rank + 1
        left = both_ref[index_of(bin_id)].astype(BF16)
        bands = [lax.rem(bin_id + bins - 1 + k, bins) for k in range(3)]
        first = block_ref[j] == 0
        window = jnp.concatenate(
            [jnp.where(first, s0_ref[b], s1_ref[b]) for b in bands], axis=0
        )
        both = dot(left, window)
        line = jnp.concatenate([both[:BEAMS], both[BEAMS:]], axis=1)
        chosen = jnp.where(iota(line.shape, 0) == beam_id, line, 0.0)
        row = owner * CAP + rank
        rows_ref[pl.ds(row, 1), :] = jnp.sum(chosen, axis=0, keepdims=True)
        return carry

    lax.fori_loop(0, count, detection, 0, unroll=16)
    out_ref[...] = rows_ref[...].astype(BF16)


def beam_rows(det_bin, det_block, det_beam, owners, s0, s1, weight, devices):
    bins, wide, gates = s0.shape
    return pl.pallas_call(
        beam_kernel,
        out_shape=jax.ShapeDtypeStruct((devices * CAP, 2 * gates), BF16),
        in_specs=[smem_spec()] * 4 + [vmem_spec()] * 3,
        out_specs=vmem_spec(),
        scratch_shapes=[
            pltpu.VMEM((bins, 2 * BEAMS, 3 * wide), F32),
            pltpu.VMEM((devices * CAP, 2 * gates), F32),
            pltpu.SMEM((devices,), jnp.int32),
        ],
        compiler_params=params(),
    )(det_bin, det_block, det_beam, owners, s0, s1, weight)


def on_device(raw, replica, det_bin, det_block, det_beam, det_owner):
    devices = lax.axis_size("range")
    _, chans, pulses, gates = raw.shape
    bins = pulses
    flat = raw.reshape(2, chans * pulses, gates)
    halo = lax.ppermute(
        first_gates(flat), "range", [(source, source - 1) for source in range(1, devices)]
    )
    table = doppler_matrix(pulses, 8)
    s0, local, matrix = spectra_first(flat, replica, table, pulses)
    first = cross_first(s0)
    s1 = spectra_last(local, halo, matrix, table, pulses)
    core_sum = partner(cross_last(False, s1, first), 1)
    keep = cross_last(True, s1, first)
    own, packed = bin_sums(keep, core_sum)
    total = gates * devices
    steer = steering(chans)
    left = from_bin(own, -1)
    right = from_bin(packed, 1)
    inverse, t = solve_middle(packed, steer, total)
    mine = solve_outer(own, left, right, steer, inverse, t, total, bins)
    groups = [list(range(first, first + bins)) for first in range(0, devices, bins)]
    weight = lax.all_to_all(
        mine, "range", split_axis=0, concat_axis=0, tiled=True,
        axis_index_groups=groups if len(groups) > 1 else None,
    ).reshape(bins * BEAMS, mine.shape[2])
    outgoing = beam_rows(
        det_bin, det_block, det_beam, det_owner[:, 0],
        s0.reshape(bins, 2 * chans, BLOCK), s1.reshape(bins, 2 * chans, BLOCK), weight, devices,
    )
    incoming = lax.all_to_all(
        outgoing.reshape(devices, CAP, 2 * BLOCK), "range", split_axis=0, concat_axis=0, tiled=True
    )
    return incoming.astype(F32).reshape(devices * CAP, 2 * BLOCK)


def solution(mesh):
    in_specs = (
        P(None, None, None, "range"),
        P(),
        P("range"),
        P("range"),
        P("range"),
        P("range", None),
    )
    out_specs = P("range", None)
    return jax.shard_map(
        on_device, mesh=mesh, in_specs=in_specs, out_specs=out_specs, check_vma=False
    )
```

```python
import functools
import math

import jax
import jax.numpy as jnp
import ml_dtypes
import numpy as np
from jax import lax
from jax.experimental import pallas as pl
from jax.experimental.pallas import tpu as pltpu
from jax.sharding import PartitionSpec as P

BLOCK = 128
BEAMS = 8
CAP = 2

F32 = jnp.float32
BF16 = jnp.bfloat16
VMEM = pltpu.VMEM
MIB = 1024 * 1024
NT = (((1,), (1,)), ((), ()))


def vmem_spec():
    return pl.BlockSpec(memory_space=VMEM)


def smem_spec():
    return pl.BlockSpec(memory_space=pltpu.SMEM)


def hbm_spec():
    return pl.BlockSpec(memory_space=pltpu.HBM)


def params(mib=16):
    return pltpu.CompilerParams(vmem_limit_bytes=mib * MIB)


def dot(a, b):
    return jnp.dot(a, b, preferred_element_type=F32)


def dot_nt(a, b, precision=None):
    return lax.dot_general(a, b, NT, precision=precision, preferred_element_type=F32)


def iota(shape, axis):
    return lax.broadcasted_iota(jnp.int32, shape, axis)


def halo_kernel(raw_ref, out_ref, sems):
    parts = sems.shape[0]
    size = out_ref.shape[1] // parts
    copies = [
        pltpu.make_async_copy(
            raw_ref.at[:, j * size : (j + 1) * size, :BLOCK],
            out_ref.at[:, j * size : (j + 1) * size, :],
            sems.at[j],
        )
        for j in range(parts)
    ]
    for copy in copies:
        copy.start()
    for copy in copies:
        copy.wait()


def first_gates(raw):
    return pl.pallas_call(
        halo_kernel,
        out_shape=jax.ShapeDtypeStruct(raw.shape[:2] + (BLOCK,), BF16),
        in_specs=[hbm_spec()],
        out_specs=vmem_spec(),
        scratch_shapes=[pltpu.SemaphoreType.DMA((8,))],
        compiler_params=params(63),
    )(raw)


def correlation_matrix(rep_ref, out_ref):
    taps = rep_ref.shape[1]
    base = rep_ref[...].astype(F32)
    row = iota((taps, 2 * taps), 0)
    parts = []
    for i in range(2):
        line = jnp.concatenate([base[i : i + 1], jnp.zeros((1, taps), F32)], axis=1)
        skew = jnp.broadcast_to(line, (taps, 2 * taps))
        bit = 1
        while bit < taps:
            skew = jnp.where((row & bit) != 0, pltpu.roll(skew, bit, 1), skew)
            bit *= 2
        parts.append(skew.T)
    real_part, imag_part = parts
    out_ref[0] = jnp.concatenate([real_part, -imag_part], axis=1).astype(BF16)
    out_ref[1] = jnp.concatenate([imag_part, real_part], axis=1).astype(BF16)


def doppler_matrix(pulses, group):
    index = np.arange(pulses)
    angle = 2.0 * math.pi / pulses * (index[:, None] * index[None, :] % pulses)
    cosine = np.cos(angle) * pulses**-0.5
    sine = np.sin(angle) * pulses**-0.5
    table = np.stack([np.stack([cosine, -sine], 1), np.stack([sine, cosine], 1)], 0)
    full = np.einsum("ipod,ce->dociep", table, np.eye(group))
    shape = (pulses * 2 * group, 2 * group * pulses)
    return full.reshape(shape).astype(ml_dtypes.bfloat16)


def doppler_rows(total, dft):
    compressed = total.astype(BF16)
    rows, wide = compressed.shape
    half, gates = rows // 2, wide // 2
    stacked = jnp.concatenate(
        [
            jnp.concatenate([compressed[:half, :gates], compressed[half:, :gates]], axis=1),
            jnp.concatenate([compressed[:half, gates:], compressed[half:, gates:]], axis=1),
        ],
        axis=0,
    )
    both = dot(dft, stacked)
    lines = both.shape[0] // 8
    joined = jnp.concatenate(
        [both[:, :gates].reshape(lines, 8, gates), both[:, gates:].reshape(lines, 8, gates)],
        axis=1,
    )
    return joined.astype(BF16)


GROUP = 16


def spectra_first_kernel(raw_ref, rep_ref, dft_ref, s_ref, local_ref, taps_ref, buf, sems):
    bins, _, chans, gates = s_ref.shape
    size = GROUP * bins
    copies = [
        pltpu.make_async_copy(
            raw_ref.at[:, j * size : (j + 1) * size, :],
            buf.at[:, j * size : (j + 1) * size, :],
            sems.at[j],
        )
        for j in range(chans // GROUP)
    ]
    for copy in copies:
        copy.start()
    correlation_matrix(rep_ref, taps_ref)
    for j, copy in enumerate(copies):
        copy.wait()
        rows = slice(j * size, (j + 1) * size)
        total = dot(buf[0, rows, :], taps_ref[0]) + dot(buf[1, rows, :], taps_ref[1])
        out = doppler_rows(total, dft_ref[...])
        s_ref[:, :, j * GROUP : (j + 1) * GROUP, :] = out.reshape(bins, 2, GROUP, gates)
        later = jnp.concatenate([buf[0, rows, gates:], buf[1, rows, gates:]], axis=1)
        near = jnp.concatenate([taps_ref[0, :gates, :], taps_ref[1, :gates, :]], axis=0)
        local_ref[rows, :] = dot(later, near)


def spectra_last_kernel(local_ref, halo_ref, taps_ref, dft_ref, s_ref):
    bins, _, chans, gates = s_ref.shape
    size = GROUP * bins
    for j in range(chans // GROUP):
        rows = slice(j * size, (j + 1) * size)
        later = jnp.concatenate([halo_ref[0, rows, :], halo_ref[1, rows, :]], axis=1)
        far = jnp.concatenate([taps_ref[0, gates:, :], taps_ref[1, gates:, :]], axis=0)
        out = doppler_rows(local_ref[rows, :] + dot(later, far), dft_ref[...])
        s_ref[:, :, j * GROUP : (j + 1) * GROUP, :] = out.reshape(bins, 2, GROUP, gates)


def spectra_first(raw, replica, table, pulses):
    _, rows, gates = raw.shape
    chans = rows // pulses
    taps = replica.shape[1]
    return pl.pallas_call(
        spectra_first_kernel,
        out_shape=[
            jax.ShapeDtypeStruct((pulses, 2, chans, BLOCK), BF16),
            jax.ShapeDtypeStruct((rows, 2 * BLOCK), F32),
            jax.ShapeDtypeStruct((2, 2 * taps, 2 * taps), BF16),
        ],
        in_specs=[hbm_spec(), vmem_spec(), vmem_spec()],
        out_specs=[vmem_spec()] * 3,
        scratch_shapes=[
            pltpu.VMEM(raw.shape, BF16),
            pltpu.SemaphoreType.DMA((chans // GROUP,)),
        ],
        compiler_params=params(),
    )(raw, replica, table)


def spectra_last(local, halo, matrix, table, pulses):
    rows = local.shape[0]
    return pl.pallas_call(
        spectra_last_kernel,
        out_shape=jax.ShapeDtypeStruct((pulses, 2, rows // pulses, BLOCK), BF16),
        in_specs=[vmem_spec()] * 4,
        out_specs=vmem_spec(),
        compiler_params=params(),
    )(local, halo, matrix, table)


def cross_body(base, s_ref, before_ref, out_ref):
    bins, _, chans, gates = s_ref.shape
    lower = iota((chans, chans), 0) >= iota((chans, chans), 1)
    half = chans // 2

    def packed(block):
        swapped = pltpu.roll(block, chans, 1)
        mixed = jnp.where(lower, block[:, :chans], swapped[:, :chans])
        return jnp.concatenate([mixed[:half], mixed[half:]], axis=1)

    def write(e, block):
        value = jnp.concatenate([packed(block[:chans]), block[chans:]], axis=0)
        if before_ref is not None:
            value = value + before_ref[base + e]
        out_ref[e] = value

    @pl.loop(0, out_ref.shape[0] // 2, unroll=2)
    def _(step):
        e = step * 2
        each = []
        for k in range(4):
            where = lax.rem(base + e + k, bins)
            each.append((s_ref[where, 0], s_ref[where, 1]))
        left = jnp.concatenate(
            [jnp.concatenate([re, im], axis=1) for re, im in each], axis=0
        )
        right = jnp.concatenate(
            [
                jnp.concatenate(pieces, axis=1)
                for re, im in each[:2]
                for pieces in ((re, im), (-im, re))
            ],
            axis=0,
        )
        both = dot_nt(left, right)
        write(e, both[: 3 * chans, : 2 * chans])
        write(e + 1, both[chans:, 2 * chans :])


def cross_first_kernel(s_ref, out_ref):
    cross_body(0, s_ref, None, out_ref)


def cross_last_kernel(mine, s_ref, before_ref, out_ref):
    core = lax.axis_index("range") & 1
    base = (core if mine else 1 - core) * out_ref.shape[0]
    cross_body(base, s_ref, before_ref, out_ref)


def cross_first(spectra):
    bins, _, chans, _ = spectra.shape
    return pl.pallas_call(
        cross_first_kernel,
        out_shape=jax.ShapeDtypeStruct((bins, 5 * chans // 2, 2 * chans), F32),
        in_specs=[vmem_spec()],
        out_specs=vmem_spec(),
        compiler_params=params(),
    )(spectra)


def cross_last(mine, spectra, before):
    bins = spectra.shape[0]
    return pl.pallas_call(
        functools.partial(cross_last_kernel, mine),
        out_shape=jax.ShapeDtypeStruct((bins // 2,) + before.shape[1:], F32),
        in_specs=[vmem_spec(), vmem_spec()],
        out_specs=vmem_spec(),
        compiler_params=params(),
    )(spectra, before)


X, Y, Z0, Z1 = 0, 1, 2, 3
DEVICE_BIT = (2, 4, 8, 16)
ORDERS = ((X, Y, Z0, Z1), (Y, X, Z1, Z0))


def partner(value, bits):
    count = lax.axis_size("range")
    return lax.ppermute(value, "range", [(i, i ^ bits[i & 1]) for i in range(count)])


def slot_of(core, x, y, z):
    return (4 * z + ((2 * y + (x ^ y)) ^ (3 * (z & 1)))) ^ (15 * core)


def bin_of(index):
    core = index & 1
    return core * 16 + slot_of(core, (index >> 1) & 1, (index >> 2) & 1, (index >> 3) & 3)


def index_of(bin_id):
    core = bin_id >> 4
    path = (bin_id & 15) ^ (15 * core)
    z = path >> 2
    turned = (path & 3) ^ (3 * (z & 1))
    y = turned >> 1
    x = (turned & 1) ^ y
    return z * 8 + y * 4 + x * 2 + core


def my_bits():
    index = lax.axis_index("range")
    core = index & 1
    bits = [(index >> (axis + 1)) & 1 for axis in range(4)]
    return core, [
        jnp.where(core == 0, bits[ORDERS[0][i]], bits[ORDERS[1][i]]) for i in range(4)
    ]


def gathered(keep_ref, core_ref, received, core, bits):
    x = jnp.where(core == 0, bits[0], bits[1])
    y = jnp.where(core == 0, bits[1], bits[0])
    z0 = jnp.where(core == 0, bits[2], bits[3])
    z1 = jnp.where(core == 0, bits[3], bits[2])
    e = slot_of(core, x, y, z1 * 2 + z0)
    value = keep_ref[e] + core_ref[e]
    for stage, ref in enumerate(received):
        place = 0
        for bit in bits[stage + 1 :]:
            place = place * 2 + bit
        value = value + ref[place]
    return value


def stage_kernel(stage, keep_ref, core_ref, *refs):
    received, out_ref = refs[:stage], refs[stage]
    core, mine = my_bits()
    free = 3 - stage
    for k in range(1 << free):
        bits = mine[:stage] + [1 - mine[stage]]
        bits += [(k >> (free - 1 - i)) & 1 for i in range(free)]
        out_ref[k] = gathered(keep_ref, core_ref, received, core, bits)


def own_kernel(keep_ref, core_ref, *refs):
    received, (out_ref, packed_ref) = refs[:4], refs[4:]
    core, mine = my_bits()
    value = gathered(keep_ref, core_ref, received, core, mine)
    out_ref[...] = value
    packed_ref[...] = value[: packed_ref.shape[0]]


def summed(kernel, data, shapes):
    return pl.pallas_call(
        kernel,
        out_shape=[jax.ShapeDtypeStruct(shape, F32) for shape in shapes],
        in_specs=[vmem_spec()] * len(data),
        out_specs=[vmem_spec()] * len(shapes),
        compiler_params=params(),
    )(*data)


def bin_sums(keep, core):
    _, rows, wide = keep.shape
    data = [keep, core]
    for stage in range(4):
        kernel = functools.partial(stage_kernel, stage)
        send = summed(kernel, data, [(8 >> stage, rows, wide)])[0]
        data.append(partner(send, [DEVICE_BIT[order[stage]] for order in ORDERS]))
    own, packed = summed(own_kernel, data, [(rows, wide), (rows // 5, wide)])
    bit = 32
    while bit < lax.axis_size("range"):
        own = own + partner(own, (bit, bit))
        packed = packed + partner(packed, (bit, bit))
        bit *= 2
    return own, packed


def from_bin(value, offset):
    count = lax.axis_size("range")
    pairs = []
    for i in range(count):
        target = index_of((bin_of(i) - offset) % 32) | (i & ~31)
        pairs.append((i, target))
    return lax.ppermute(value, "range", pairs)


def turn(value):
    half = value.shape[1] // 2
    rolled = pltpu.roll(value, half, 1)
    return jnp.where(iota(value.shape, 1) < half, -rolled, rolled)


def embed(value):
    return jnp.concatenate([value, turn(value)], axis=0)


def mul(a, b):
    return jnp.dot(a, embed(b), precision=lax.Precision.HIGHEST, preferred_element_type=F32)


def mul_conj(a, b):
    half = a.shape[1] // 2
    stacked = jnp.concatenate([a, -turn(a)], axis=0)
    both = dot_nt(stacked, b, lax.Precision.HIGHEST)
    rows = a.shape[0]
    return jnp.concatenate([both[:rows], both[rows:]], axis=1)


def conj_mul(a, b):
    half = a.shape[1] // 2
    both = lax.dot_general(
        a, b, (((0,), (0,)), ((), ())),
        precision=lax.Precision.HIGHEST, preferred_element_type=F32,
    )
    return both[:half] - turn(both[half:])


def reciprocal(x):
    value = pl.reciprocal(x, approx=True)
    for _ in range(2):
        value = value * (2.0 - x * value)
    return value


def pivot_inverse(p):
    def times(x, y):
        return x[0] * y[0] - x[1] * y[1], x[0] * y[1] + x[1] * y[0]

    def conj(x):
        return x[0], -x[1]

    def plus(x, y):
        return x[0] + y[0], x[1] + y[1]

    def scaled(x, s):
        return x[0] * s, x[1] * s

    def square(x):
        return x[0] * x[0] + x[1] * x[1]

    def two(a, b, d):
        inv = reciprocal(a * d - square(b))
        return d * inv, scaled(b, -inv), a * inv

    a, d = p[0][0], p[1][1]
    b = p[0][1]
    ea, eb, ed = two(a, b, d)
    f = [[p[0][2], p[0][3]], [p[1][2], p[1][3]]]
    w = [
        [plus(scaled(f[0][j], ea), times(eb, f[1][j])) for j in range(2)],
        [plus(times(conj(eb), f[0][j]), scaled(f[1][j], ed)) for j in range(2)],
    ]

    def inner(i, j):
        return plus(times(conj(f[0][i]), w[0][j]), times(conj(f[1][i]), w[1][j]))

    ha = p[2][2] - inner(0, 0)[0]
    hd = p[3][3] - inner(1, 1)[0]
    cross = inner(0, 1)
    hb = (p[2][3][0] - cross[0], p[2][3][1] - cross[1])
    ga, gb, gd = two(ha, hb, hd)
    v = [
        [
            plus(scaled(w[i][0], ga), times(w[i][1], conj(gb))),
            plus(times(w[i][0], gb), scaled(w[i][1], gd)),
        ]
        for i in range(2)
    ]
    top = [
        [plus(times(v[i][0], conj(w[j][0])), times(v[i][1], conj(w[j][1]))) for j in range(2)]
        for i in range(2)
    ]
    zero = None
    out = [[None] * 4 for _ in range(4)]
    out[0][0] = (ea + top[0][0][0], zero)
    out[1][1] = (ed + top[1][1][0], zero)
    out[0][1] = plus(eb, top[0][1])
    out[2][2], out[3][3], out[2][3] = (ga, zero), (gd, zero), gb
    for i in range(2):
        for j in range(2):
            out[i][2 + j] = (-v[i][j][0], -v[i][j][1])
    for i in range(4):
        for j in range(i):
            out[i][j] = conj(out[j][i])
    return out


def invert(matrix):
    chans, width = matrix.shape
    sub = 8
    tiles = [matrix[t * sub : (t + 1) * sub, :] for t in range(chans // sub)]
    lane = iota((sub, width), 1)
    row = iota((sub, width), 0)
    first_half = lane < chans

    def spin(value):
        rolled = pltpu.roll(value, chans, 1)
        return jnp.where(first_half, -rolled, rolled)

    def column(value, k):
        return jnp.broadcast_to(value[:, k : k + 1], (sub, width))

    def combine(terms):
        while len(terms) > 1:
            terms = [
                terms[i] + terms[i + 1] if i + 1 < len(terms) else terms[i]
                for i in range(0, len(terms), 2)
            ]
        return terms[0]

    for k in range(0, chans, 4):
        t, r = divmod(k, sub)
        lines = [jnp.broadcast_to(tiles[t][r + i : r + i + 1, :], (sub, width)) for i in range(4)]
        pivot = [[None] * 4 for _ in range(4)]
        for i in range(4):
            pivot[i][i] = column(lines[i], k + i)
            for j in range(i + 1, 4):
                pivot[i][j] = column(lines[i], k + j), column(lines[i], chans + k + j)
        low = jnp.bitwise_and(lane, chans - 1)
        cleared = (low >= k) & (low < k + 4)
        unit = [
            jnp.where(cleared, jnp.where(lane == k + i, 1.0, 0.0), lines[i]) for i in range(4)
        ]
        spun = [spin(u) for u in unit]
        p = pivot_inverse(pivot)
        fresh_lines, fresh_spun = [], []
        for i in range(4):
            terms, other = [], []
            for j in range(4):
                re, im = p[i][j]
                terms.append(re * unit[j])
                other.append(re * spun[j])
                if im is not None:
                    terms.append(im * spun[j])
                    other.append(-(im * unit[j]))
            fresh_lines.append(combine(terms))
            fresh_spun.append(combine(other))
        fresh = []
        for s, tile in enumerate(tiles):
            terms = []
            for i in range(4):
                terms.append(column(tile, k + i) * fresh_lines[i])
                terms.append(column(tile, chans + k + i) * fresh_spun[i])
            value = jnp.where(cleared, 0.0, tile) - combine(terms)
            if s == t:
                for i in range(4):
                    value = jnp.where(row == r + i, fresh_lines[i], value)
            fresh.append(value)
        tiles = fresh
    return jnp.concatenate(tiles, axis=0)


def unpacked(ref, scale):
    half, wide = ref.shape[0], ref.shape[1]
    piece = ref[...] * scale
    swapped = pltpu.roll(piece, wide // 2, 1)
    return jnp.concatenate([piece, swapped], axis=0)[:, : wide // 2]


def hermitian(mixed, across):
    i, j = iota(mixed.shape, 0), iota(mixed.shape, 1)
    real_part = jnp.where(i >= j, mixed, across)
    imag_part = jnp.where(i < j, mixed, jnp.where(i > j, -across, 0.0))
    return jnp.concatenate([real_part, imag_part], axis=1)


def middle_kernel(total, packed_ref, steer_ref, inv_ref, t_ref):
    chans = inv_ref.shape[0]
    mixed = unpacked(packed_ref, F32(1.0 / total))
    twice = jnp.concatenate([mixed, mixed], axis=1)
    across = jnp.concatenate([twice, twice], axis=0).T[:chans, :chans]
    inverse = invert(hermitian(mixed, across))
    inv_ref[...] = inverse
    t_ref[...] = mul(steer_ref[...], inverse)


def outer_kernel(total, own_ref, left_ref, right_ref, steer_ref, inv_ref, t_ref, out_ref,
                 work, keep):
    chans = inv_ref.shape[0]
    scale = F32(1.0 / total)
    half = chans // 2
    m_left = unpacked(left_ref.at[:half], scale)
    m_right = unpacked(right_ref, scale)
    ml = left_ref[half : half + chans] * scale
    rl = left_ref[half + chans :] * scale
    rm = own_ref[half : half + chans] * scale
    pair = jnp.concatenate([m_left, m_right], axis=1)
    square = jnp.concatenate([pair, pair], axis=0).T
    inv_mid = inv_ref[...]
    t = t_ref[...]
    h = mul(inv_mid, ml)
    g = mul(rm, inv_mid)
    work[...] = hermitian(m_left, square[:chans, :chans]) - conj_mul(ml, h)
    s_rl = rl - mul(rm, h)
    s_rr = hermitian(m_right, square[chans:, :chans]) - mul_conj(g, rm)
    rhs_left = -mul(t, ml)
    rhs_right = -mul_conj(t, rm)
    keep[0] = s_rl
    keep[1] = s_rr
    keep[2] = h
    keep[3] = g
    keep[4, 0:BEAMS] = rhs_left
    keep[4, BEAMS : 2 * BEAMS] = rhs_right

    @pl.loop(0, 2)
    def _(stage):
        work[...] = invert(work[...])

        @pl.when(stage == 0)
        def _():
            inverse = work[...]
            s_rl = keep[0]
            both = mul(jnp.concatenate([s_rl, keep[4, 0:BEAMS]], axis=0), inverse)
            k, y_left = both[:chans], both[chans:]
            work[...] = keep[1] - mul_conj(k, s_rl)
            keep[0] = k
            keep[4, BEAMS : 2 * BEAMS] = keep[4, BEAMS : 2 * BEAMS] - mul_conj(y_left, s_rl)
            keep[4, 0:BEAMS] = y_left
            keep[4, 2 * BEAMS : 3 * BEAMS] = t_ref[...] - mul_conj(y_left, keep[2])
            keep[3] = keep[3] - mul_conj(k, keep[2])

        @pl.when(stage == 1)
        def _():
            y_right = mul(keep[4, BEAMS : 2 * BEAMS], work[...])
            y_left = keep[4, 0:BEAMS] - mul(y_right, keep[0])
            y_mid = keep[4, 2 * BEAMS : 3 * BEAMS] - mul(y_right, keep[3])
            quad = jnp.sum(steer_ref[...] * y_mid, axis=1, keepdims=True)
            y = jnp.concatenate([y_left, y_mid, y_right], axis=1) / jnp.sqrt(quad)
            real_lane = lax.rem(iota(y.shape, 1), 2 * chans) < chans
            mine = jnp.where(real_lane, y, -y).astype(BF16)
            for c in range(out_ref.shape[0]):
                out_ref[c] = mine


def steering(chans):
    index = np.arange(chans)
    sines = -0.8 + 1.6 * np.arange(BEAMS) / (BEAMS - 1)
    angle = math.pi * sines[:, None] * index[None, :]
    return np.concatenate([np.cos(angle), -np.sin(angle)], axis=1).astype(np.float32)


def solve_middle(packed, steer, total):
    half, wide = packed.shape
    return pl.pallas_call(
        functools.partial(middle_kernel, total),
        out_shape=[
            jax.ShapeDtypeStruct((2 * half, wide), F32),
            jax.ShapeDtypeStruct((BEAMS, wide), F32),
        ],
        in_specs=[vmem_spec()] * 2,
        out_specs=[vmem_spec()] * 2,
        compiler_params=params(),
    )(packed, steer)


def solve_outer(own, left, right, steer, inverse, t, total, copies):
    chans, wide = inverse.shape
    return pl.pallas_call(
        functools.partial(outer_kernel, total),
        out_shape=jax.ShapeDtypeStruct((copies, BEAMS, 3 * wide), BF16),
        in_specs=[vmem_spec()] * 6,
        out_specs=vmem_spec(),
        scratch_shapes=[pltpu.VMEM((chans, wide), F32), pltpu.VMEM((5, chans, wide), F32)],
        compiler_params=params(),
    )(own, left, right, steer, inverse, t)


def beam_kernel(bin_ref, block_ref, beam_ref, owner_ref, s0_ref, s1_ref, w_ref, out_ref,
                both_ref, rows_ref, seen_ref):
    bins, wide, gates = s0_ref.shape
    devices = seen_ref.shape[0]
    count = bin_ref.shape[0]
    rows_ref[...] = jnp.zeros_like(rows_ref)

    @pl.loop(0, devices)
    def _(i):
        seen_ref[i] = 0

    w = w_ref[...].astype(F32)
    for k in range(3):
        part = w[:, k * wide : (k + 1) * wide]
        both_ref[:, 0:BEAMS, k * wide : (k + 1) * wide] = part.reshape(bins, BEAMS, wide)
        both_ref[:, BEAMS:, k * wide : (k + 1) * wide] = turn(part).reshape(bins, BEAMS, wide)

    def detection(j, carry):
        bin_id = bin_ref[j]
        beam_id = beam_ref[j]
        owner = owner_ref[j]
        rank = seen_ref[owner]
        seen_ref[owner] = rank + 1
        left = both_ref[index_of(bin_id)].astype(BF16)
        bands = [lax.rem(bin_id + bins - 1 + k, bins) for k in range(3)]
        first = block_ref[j] == 0
        window = jnp.concatenate(
            [jnp.where(first, s0_ref[b], s1_ref[b]) for b in bands], axis=0
        )
        both = dot(left, window)
        line = jnp.concatenate([both[:BEAMS], both[BEAMS:]], axis=1)
        chosen = jnp.where(iota(line.shape, 0) == beam_id, line, 0.0)
        row = owner * CAP + rank
        rows_ref[pl.ds(row, 1), :] = jnp.sum(chosen, axis=0, keepdims=True)
        return carry

    lax.fori_loop(0, count, detection, 0, unroll=16)
    out_ref[...] = rows_ref[...].astype(BF16)


def beam_rows(det_bin, det_block, det_beam, owners, s0, s1, weight, devices):
    bins, wide, gates = s0.shape
    return pl.pallas_call(
        beam_kernel,
        out_shape=jax.ShapeDtypeStruct((devices * CAP, 2 * gates), BF16),
        in_specs=[smem_spec()] * 4 + [vmem_spec()] * 3,
        out_specs=vmem_spec(),
        scratch_shapes=[
            pltpu.VMEM((bins, 2 * BEAMS, 3 * wide), F32),
            pltpu.VMEM((devices * CAP, 2 * gates), F32),
            pltpu.SMEM((devices,), jnp.int32),
        ],
        compiler_params=params(),
    )(det_bin, det_block, det_beam, owners, s0, s1, weight)


def on_device(raw, replica, det_bin, det_block, det_beam, det_owner):
    devices = lax.axis_size("range")
    _, chans, pulses, gates = raw.shape
    bins = pulses
    flat = raw.reshape(2, chans * pulses, gates)
    halo = lax.ppermute(
        first_gates(flat), "range", [(source, source - 1) for source in range(1, devices)]
    )
    table = doppler_matrix(pulses, 8)
    s0, local, matrix = spectra_first(flat, replica, table, pulses)
    first = cross_first(s0)
    s1 = spectra_last(local, halo, matrix, table, pulses)
    core_sum = partner(cross_last(False, s1, first), (1, 1))
    keep = cross_last(True, s1, first)
    own, packed = bin_sums(keep, core_sum)
    total = gates * devices
    steer = steering(chans)
    left = from_bin(own, -1)
    right = from_bin(packed, 1)
    inverse, t = solve_middle(packed, steer, total)
    mine = solve_outer(own, left, right, steer, inverse, t, total, bins)
    groups = [list(range(first, first + bins)) for first in range(0, devices, bins)]
    weight = lax.all_to_all(
        mine, "range", split_axis=0, concat_axis=0, tiled=True,
        axis_index_groups=groups if len(groups) > 1 else None,
    ).reshape(bins * BEAMS, mine.shape[2])
    outgoing = beam_rows(
        det_bin, det_block, det_beam, det_owner[:, 0],
        s0.reshape(bins, 2 * chans, BLOCK), s1.reshape(bins, 2 * chans, BLOCK), weight, devices,
    )
    incoming = lax.all_to_all(
        outgoing.reshape(devices, CAP, 2 * BLOCK), "range", split_axis=0, concat_axis=0, tiled=True
    )
    return incoming.astype(F32).reshape(devices * CAP, 2 * BLOCK)


def solution(mesh):
    in_specs = (
        P(None, None, None, "range"),
        P(),
        P("range"),
        P("range"),
        P("range"),
        P("range", None),
    )
    out_specs = P("range", None)
    return jax.shard_map(
        on_device, mesh=mesh, in_specs=in_specs, out_specs=out_specs, check_vma=False
    )
```

```python
import functools
import math

import jax
import jax.numpy as jnp
import ml_dtypes
import numpy as np
from jax import lax
from jax.experimental import pallas as pl
from jax.experimental.pallas import tpu as pltpu
from jax.sharding import PartitionSpec as P

BLOCK = 128
BEAMS = 8
CAP = 2

F32 = jnp.float32
BF16 = jnp.bfloat16
VMEM = pltpu.VMEM
MIB = 1024 * 1024
NT = (((1,), (1,)), ((), ()))


def vmem_spec():
    return pl.BlockSpec(memory_space=VMEM)


def smem_spec():
    return pl.BlockSpec(memory_space=pltpu.SMEM)


def hbm_spec():
    return pl.BlockSpec(memory_space=pltpu.HBM)


def params(mib=16):
    return pltpu.CompilerParams(vmem_limit_bytes=mib * MIB)


def dot(a, b):
    return jnp.dot(a, b, preferred_element_type=F32)


def dot_nt(a, b, precision=None):
    return lax.dot_general(a, b, NT, precision=precision, preferred_element_type=F32)


def iota(shape, axis):
    return lax.broadcasted_iota(jnp.int32, shape, axis)


def halo_kernel(raw_ref, out_ref, buf, sems):
    parts = sems.shape[0]
    size = out_ref.shape[1] // parts
    copies = []
    for j in range(parts):
        rows = slice(j * size, (j + 1) * size)
        copies.append(
            pltpu.make_async_copy(raw_ref.at[:, rows, :], buf.at[:, rows, :], sems.at[j])
        )
    for copy in copies:
        copy.start()
    for j, copy in enumerate(copies):
        copy.wait()
        rows = slice(j * size, (j + 1) * size)
        out_ref[:, rows, :] = buf[:, rows, :BLOCK]


def first_gates(raw):
    return pl.pallas_call(
        halo_kernel,
        out_shape=jax.ShapeDtypeStruct(raw.shape[:2] + (BLOCK,), BF16),
        in_specs=[hbm_spec()],
        out_specs=vmem_spec(),
        scratch_shapes=[pltpu.VMEM(raw.shape, BF16), pltpu.SemaphoreType.DMA((8,))],
        compiler_params=params(63),
    )(raw)


def correlation_matrix(rep_ref, out_ref):
    taps = rep_ref.shape[1]
    base = rep_ref[...].astype(F32)
    row = iota((taps, 2 * taps), 0)
    parts = []
    for i in range(2):
        line = jnp.concatenate([base[i : i + 1], jnp.zeros((1, taps), F32)], axis=1)
        skew = jnp.broadcast_to(line, (taps, 2 * taps))
        bit = 1
        while bit < taps:
            skew = jnp.where((row & bit) != 0, pltpu.roll(skew, bit, 1), skew)
            bit *= 2
        parts.append(skew.T)
    real_part, imag_part = parts
    out_ref[0] = jnp.concatenate([real_part, -imag_part], axis=1).astype(BF16)
    out_ref[1] = jnp.concatenate([imag_part, real_part], axis=1).astype(BF16)


def doppler_matrix(pulses, group):
    index = np.arange(pulses)
    angle = 2.0 * math.pi / pulses * (index[:, None] * index[None, :] % pulses)
    cosine = np.cos(angle) * pulses**-0.5
    sine = np.sin(angle) * pulses**-0.5
    table = np.stack([np.stack([cosine, -sine], 1), np.stack([sine, cosine], 1)], 0)
    full = np.einsum("ipod,ce->dociep", table, np.eye(group))
    shape = (pulses * 2 * group, 2 * group * pulses)
    return full.reshape(shape).astype(ml_dtypes.bfloat16)


def doppler_rows(total, dft):
    compressed = total.astype(BF16)
    rows, wide = compressed.shape
    half, gates = rows // 2, wide // 2
    stacked = jnp.concatenate(
        [
            jnp.concatenate([compressed[:half, :gates], compressed[half:, :gates]], axis=1),
            jnp.concatenate([compressed[:half, gates:], compressed[half:, gates:]], axis=1),
        ],
        axis=0,
    )
    both = dot(dft, stacked)
    lines = both.shape[0] // 8
    joined = jnp.concatenate(
        [both[:, :gates].reshape(lines, 8, gates), both[:, gates:].reshape(lines, 8, gates)],
        axis=1,
    )
    return joined.astype(BF16)


GROUP = 16


def spectra_first_kernel(raw_ref, rep_ref, dft_ref, s_ref, local_ref, taps_ref, buf, sems):
    bins, _, chans, gates = s_ref.shape
    size = GROUP * bins
    copies = [
        pltpu.make_async_copy(
            raw_ref.at[:, j * size : (j + 1) * size, :],
            buf.at[:, j * size : (j + 1) * size, :],
            sems.at[j],
        )
        for j in range(chans // GROUP)
    ]
    for copy in copies:
        copy.start()
    correlation_matrix(rep_ref, taps_ref)
    for j, copy in enumerate(copies):
        copy.wait()
        rows = slice(j * size, (j + 1) * size)
        total = dot(buf[0, rows, :], taps_ref[0]) + dot(buf[1, rows, :], taps_ref[1])
        out = doppler_rows(total, dft_ref[...])
        s_ref[:, :, j * GROUP : (j + 1) * GROUP, :] = out.reshape(bins, 2, GROUP, gates)
        later = jnp.concatenate([buf[0, rows, gates:], buf[1, rows, gates:]], axis=1)
        near = jnp.concatenate([taps_ref[0, :gates, :], taps_ref[1, :gates, :]], axis=0)
        local_ref[rows, :] = dot(later, near)


def spectra_last_kernel(local_ref, halo_ref, taps_ref, dft_ref, s_ref):
    bins, _, chans, gates = s_ref.shape
    size = GROUP * bins
    for j in range(chans // GROUP):
        rows = slice(j * size, (j + 1) * size)
        later = jnp.concatenate([halo_ref[0, rows, :], halo_ref[1, rows, :]], axis=1)
        far = jnp.concatenate([taps_ref[0, gates:, :], taps_ref[1, gates:, :]], axis=0)
        out = doppler_rows(local_ref[rows, :] + dot(later, far), dft_ref[...])
        s_ref[:, :, j * GROUP : (j + 1) * GROUP, :] = out.reshape(bins, 2, GROUP, gates)


def spectra_first(raw, replica, table, pulses):
    _, rows, gates = raw.shape
    chans = rows // pulses
    taps = replica.shape[1]
    return pl.pallas_call(
        spectra_first_kernel,
        out_shape=[
            jax.ShapeDtypeStruct((pulses, 2, chans, BLOCK), BF16),
            jax.ShapeDtypeStruct((rows, 2 * BLOCK), F32),
            jax.ShapeDtypeStruct((2, 2 * taps, 2 * taps), BF16),
        ],
        in_specs=[hbm_spec(), vmem_spec(), vmem_spec()],
        out_specs=[vmem_spec()] * 3,
        scratch_shapes=[
            pltpu.VMEM(raw.shape, BF16),
            pltpu.SemaphoreType.DMA((chans // GROUP,)),
        ],
        compiler_params=params(),
    )(raw, replica, table)


def spectra_last(local, halo, matrix, table, pulses):
    rows = local.shape[0]
    return pl.pallas_call(
        spectra_last_kernel,
        out_shape=jax.ShapeDtypeStruct((pulses, 2, rows // pulses, BLOCK), BF16),
        in_specs=[vmem_spec()] * 4,
        out_specs=vmem_spec(),
        compiler_params=params(),
    )(local, halo, matrix, table)


def cross_body(base, s_ref, before_ref, out_ref):
    bins, _, chans, gates = s_ref.shape
    lower = iota((chans, chans), 0) >= iota((chans, chans), 1)
    half = chans // 2

    def packed(block):
        swapped = pltpu.roll(block, chans, 1)
        mixed = jnp.where(lower, block[:, :chans], swapped[:, :chans])
        return jnp.concatenate([mixed[:half], mixed[half:]], axis=1)

    def write(e, block):
        value = jnp.concatenate([packed(block[:chans]), block[chans:]], axis=0)
        if before_ref is not None:
            value = value + before_ref[base + e]
        out_ref[e] = value

    @pl.loop(0, out_ref.shape[0] // 2, unroll=2)
    def _(step):
        e = step * 2
        each = []
        for k in range(4):
            where = lax.rem(base + e + k, bins)
            each.append((s_ref[where, 0], s_ref[where, 1]))
        left = jnp.concatenate(
            [jnp.concatenate([re, im], axis=1) for re, im in each], axis=0
        )
        right = jnp.concatenate(
            [
                jnp.concatenate(pieces, axis=1)
                for re, im in each[:2]
                for pieces in ((re, im), (-im, re))
            ],
            axis=0,
        )
        both = dot_nt(left, right)
        write(e, both[: 3 * chans, : 2 * chans])
        write(e + 1, both[chans:, 2 * chans :])


def cross_first_kernel(s_ref, out_ref):
    cross_body(0, s_ref, None, out_ref)


def cross_last_kernel(mine, s_ref, before_ref, out_ref):
    core = lax.axis_index("range") & 1
    base = (core if mine else 1 - core) * out_ref.shape[0]
    cross_body(base, s_ref, before_ref, out_ref)


def cross_first(spectra):
    bins, _, chans, _ = spectra.shape
    return pl.pallas_call(
        cross_first_kernel,
        out_shape=jax.ShapeDtypeStruct((bins, 5 * chans // 2, 2 * chans), F32),
        in_specs=[vmem_spec()],
        out_specs=vmem_spec(),
        compiler_params=params(),
    )(spectra)


def cross_last(mine, spectra, before):
    bins = spectra.shape[0]
    return pl.pallas_call(
        functools.partial(cross_last_kernel, mine),
        out_shape=jax.ShapeDtypeStruct((bins // 2,) + before.shape[1:], F32),
        in_specs=[vmem_spec(), vmem_spec()],
        out_specs=vmem_spec(),
        compiler_params=params(),
    )(spectra, before)


def partner(value, bit):
    count = lax.axis_size("range")
    return lax.ppermute(value, "range", [(i, i ^ bit) for i in range(count)])


def slot_of(core, x, y, z):
    return (4 * z + ((2 * y + (x ^ y)) ^ (3 * (z & 1)))) ^ (15 * core)


def parts_of(index):
    return index & 1, (index >> 1) & 1, (index >> 2) & 1, (index >> 3) & 3


def bin_of(index):
    core, x, y, z = parts_of(index)
    return core * 16 + slot_of(core, x, y, z)


def index_of(bin_id):
    core = bin_id >> 4
    path = (bin_id & 15) ^ (15 * core)
    z = path >> 2
    turned = (path & 3) ^ (3 * (z & 1))
    y = turned >> 1
    x = (turned & 1) ^ y
    return z * 8 + y * 4 + x * 2 + core


def first_kernel(keep_ref, core_ref, a_ref, b_ref):
    core, x, y, z = parts_of(lax.axis_index("range"))
    half = keep_ref.shape[1] // 2
    for k in range(8):
        e = slot_of(core, 1 - x, k // 4, k % 4)
        a_ref[k] = keep_ref[e, :half] + core_ref[e, :half]
        e = slot_of(core, k // 4, 1 - y, k % 4)
        b_ref[k] = keep_ref[e, half:] + core_ref[e, half:]


def second_kernel(keep_ref, core_ref, a1_ref, b1_ref, a_ref, b_ref):
    core, x, y, z = parts_of(lax.axis_index("range"))
    half = keep_ref.shape[1] // 2
    for k in range(4):
        e = slot_of(core, x, 1 - y, k)
        a_ref[k] = keep_ref[e, :half] + core_ref[e, :half] + a1_ref[(1 - y) * 4 + k]
        e = slot_of(core, 1 - x, y, k)
        b_ref[k] = keep_ref[e, half:] + core_ref[e, half:] + b1_ref[(1 - x) * 4 + k]


def line_sum(keep_ref, core_ref, a1_ref, b1_ref, a2_ref, b2_ref, flip):
    core, x, y, z = parts_of(lax.axis_index("range"))
    z = z ^ flip
    half = keep_ref.shape[1] // 2
    e = slot_of(core, x, y, z)
    upper = keep_ref[e, :half] + core_ref[e, :half] + a1_ref[y * 4 + z] + a2_ref[z]
    lower = keep_ref[e, half:] + core_ref[e, half:] + b1_ref[x * 4 + z] + b2_ref[z]
    return upper, lower


def line_kernel(*refs):
    half = refs[0].shape[1] // 2
    for k, out_ref in enumerate(refs[6:]):
        upper, lower = line_sum(*refs[:6], k + 1)
        out_ref[:half] = upper
        out_ref[half:] = lower


def own_kernel(*refs):
    z1_ref, z2_ref, z3_ref, out_ref, packed_ref = refs[6:]
    half = refs[0].shape[1] // 2
    upper, lower = line_sum(*refs[:6], 0)
    upper = upper + z1_ref[:half] + (z2_ref[:half] + z3_ref[:half])
    out_ref[:half] = upper
    packed_ref[...] = upper[: packed_ref.shape[0]]
    out_ref[half:] = lower + z1_ref[half:] + (z2_ref[half:] + z3_ref[half:])


def summed(kernel, data, shapes):
    return pl.pallas_call(
        kernel,
        out_shape=[jax.ShapeDtypeStruct(shape, F32) for shape in shapes],
        in_specs=[vmem_spec()] * len(data),
        out_specs=[vmem_spec()] * len(shapes),
        compiler_params=params(),
    )(*data)


def bin_sums(keep, core):
    _, rows, wide = keep.shape
    half = rows // 2
    data = [keep, core]
    a, b = summed(first_kernel, data, [(8, half, wide)] * 2)
    data += [partner(a, 2), partner(b, 4)]
    a, b = summed(second_kernel, data, [(4, half, wide)] * 2)
    data += [partner(a, 4), partner(b, 2)]
    sends = summed(line_kernel, data, [(rows, wide)] * 3)
    data += [partner(value, (k + 1) * 8) for k, value in enumerate(sends)]
    own, packed = summed(own_kernel, data, [(rows, wide), (rows // 5, wide)])
    bit = 32
    while bit < lax.axis_size("range"):
        own = own + partner(own, bit)
        packed = packed + partner(packed, bit)
        bit *= 2
    return own, packed


def from_bin(value, offset):
    count = lax.axis_size("range")
    pairs = []
    for i in range(count):
        target = index_of((bin_of(i) - offset) % 32) | (i & ~31)
        pairs.append((i, target))
    return lax.ppermute(value, "range", pairs)


def turn(value):
    half = value.shape[1] // 2
    rolled = pltpu.roll(value, half, 1)
    return jnp.where(iota(value.shape, 1) < half, -rolled, rolled)


def embed(value):
    return jnp.concatenate([value, turn(value)], axis=0)


def mul(a, b):
    return jnp.dot(a, embed(b), precision=lax.Precision.HIGHEST, preferred_element_type=F32)


def mul_conj(a, b):
    half = a.shape[1] // 2
    stacked = jnp.concatenate([a, -turn(a)], axis=0)
    both = dot_nt(stacked, b, lax.Precision.HIGHEST)
    rows = a.shape[0]
    return jnp.concatenate([both[:rows], both[rows:]], axis=1)


def conj_mul(a, b):
    half = a.shape[1] // 2
    both = lax.dot_general(
        a, b, (((0,), (0,)), ((), ())),
        precision=lax.Precision.HIGHEST, preferred_element_type=F32,
    )
    return both[:half] - turn(both[half:])


def reciprocal(x):
    value = pl.reciprocal(x, approx=True)
    for _ in range(2):
        value = value * (2.0 - x * value)
    return value


def pivot_inverse(p):
    def times(x, y):
        return x[0] * y[0] - x[1] * y[1], x[0] * y[1] + x[1] * y[0]

    def conj(x):
        return x[0], -x[1]

    def plus(x, y):
        return x[0] + y[0], x[1] + y[1]

    def scaled(x, s):
        return x[0] * s, x[1] * s

    def square(x):
        return x[0] * x[0] + x[1] * x[1]

    def two(a, b, d):
        inv = reciprocal(a * d - square(b))
        return d * inv, scaled(b, -inv), a * inv

    a, d = p[0][0], p[1][1]
    b = p[0][1]
    ea, eb, ed = two(a, b, d)
    f = [[p[0][2], p[0][3]], [p[1][2], p[1][3]]]
    w = [
        [plus(scaled(f[0][j], ea), times(eb, f[1][j])) for j in range(2)],
        [plus(times(conj(eb), f[0][j]), scaled(f[1][j], ed)) for j in range(2)],
    ]

    def inner(i, j):
        return plus(times(conj(f[0][i]), w[0][j]), times(conj(f[1][i]), w[1][j]))

    ha = p[2][2] - inner(0, 0)[0]
    hd = p[3][3] - inner(1, 1)[0]
    cross = inner(0, 1)
    hb = (p[2][3][0] - cross[0], p[2][3][1] - cross[1])
    ga, gb, gd = two(ha, hb, hd)
    v = [
        [
            plus(scaled(w[i][0], ga), times(w[i][1], conj(gb))),
            plus(times(w[i][0], gb), scaled(w[i][1], gd)),
        ]
        for i in range(2)
    ]
    top = [
        [plus(times(v[i][0], conj(w[j][0])), times(v[i][1], conj(w[j][1]))) for j in range(2)]
        for i in range(2)
    ]
    zero = None
    out = [[None] * 4 for _ in range(4)]
    out[0][0] = (ea + top[0][0][0], zero)
    out[1][1] = (ed + top[1][1][0], zero)
    out[0][1] = plus(eb, top[0][1])
    out[2][2], out[3][3], out[2][3] = (ga, zero), (gd, zero), gb
    for i in range(2):
        for j in range(2):
            out[i][2 + j] = (-v[i][j][0], -v[i][j][1])
    for i in range(4):
        for j in range(i):
            out[i][j] = conj(out[j][i])
    return out


def invert(matrix):
    chans, width = matrix.shape
    sub = 8
    tiles = [matrix[t * sub : (t + 1) * sub, :] for t in range(chans // sub)]
    lane = iota((sub, width), 1)
    row = iota((sub, width), 0)
    first_half = lane < chans

    def spin(value):
        rolled = pltpu.roll(value, chans, 1)
        return jnp.where(first_half, -rolled, rolled)

    def column(value, k):
        return jnp.broadcast_to(value[:, k : k + 1], (sub, width))

    def combine(terms):
        while len(terms) > 1:
            terms = [
                terms[i] + terms[i + 1] if i + 1 < len(terms) else terms[i]
                for i in range(0, len(terms), 2)
            ]
        return terms[0]

    for k in range(0, chans, 4):
        t, r = divmod(k, sub)
        lines = [jnp.broadcast_to(tiles[t][r + i : r + i + 1, :], (sub, width)) for i in range(4)]
        pivot = [[None] * 4 for _ in range(4)]
        for i in range(4):
            pivot[i][i] = column(lines[i], k + i)
            for j in range(i + 1, 4):
                pivot[i][j] = column(lines[i], k + j), column(lines[i], chans + k + j)
        low = jnp.bitwise_and(lane, chans - 1)
        cleared = (low >= k) & (low < k + 4)
        unit = [
            jnp.where(cleared, jnp.where(lane == k + i, 1.0, 0.0), lines[i]) for i in range(4)
        ]
        spun = [spin(u) for u in unit]
        p = pivot_inverse(pivot)
        fresh_lines, fresh_spun = [], []
        for i in range(4):
            terms, other = [], []
            for j in range(4):
                re, im = p[i][j]
                terms.append(re * unit[j])
                other.append(re * spun[j])
                if im is not None:
                    terms.append(im * spun[j])
                    other.append(-(im * unit[j]))
            fresh_lines.append(combine(terms))
            fresh_spun.append(combine(other))
        fresh = []
        for s, tile in enumerate(tiles):
            terms = []
            for i in range(4):
                terms.append(column(tile, k + i) * fresh_lines[i])
                terms.append(column(tile, chans + k + i) * fresh_spun[i])
            value = jnp.where(cleared, 0.0, tile) - combine(terms)
            if s == t:
                for i in range(4):
                    value = jnp.where(row == r + i, fresh_lines[i], value)
            fresh.append(value)
        tiles = fresh
    return jnp.concatenate(tiles, axis=0)


def unpacked(ref, scale):
    half, wide = ref.shape[0], ref.shape[1]
    piece = ref[...] * scale
    swapped = pltpu.roll(piece, wide // 2, 1)
    return jnp.concatenate([piece, swapped], axis=0)[:, : wide // 2]


def hermitian(mixed, across):
    i, j = iota(mixed.shape, 0), iota(mixed.shape, 1)
    real_part = jnp.where(i >= j, mixed, across)
    imag_part = jnp.where(i < j, mixed, jnp.where(i > j, -across, 0.0))
    return jnp.concatenate([real_part, imag_part], axis=1)


def middle_kernel(total, packed_ref, steer_ref, inv_ref, t_ref):
    chans = inv_ref.shape[0]
    mixed = unpacked(packed_ref, F32(1.0 / total))
    twice = jnp.concatenate([mixed, mixed], axis=1)
    across = jnp.concatenate([twice, twice], axis=0).T[:chans, :chans]
    inverse = invert(hermitian(mixed, across))
    inv_ref[...] = inverse
    t_ref[...] = mul(steer_ref[...], inverse)


def outer_kernel(total, own_ref, left_ref, right_ref, steer_ref, inv_ref, t_ref, out_ref,
                 work, keep):
    chans = inv_ref.shape[0]
    scale = F32(1.0 / total)
    half = chans // 2
    m_left = unpacked(left_ref.at[:half], scale)
    m_right = unpacked(right_ref, scale)
    ml = left_ref[half : half + chans] * scale
    rl = left_ref[half + chans :] * scale
    rm = own_ref[half : half + chans] * scale
    pair = jnp.concatenate([m_left, m_right], axis=1)
    square = jnp.concatenate([pair, pair], axis=0).T
    inv_mid = inv_ref[...]
    t = t_ref[...]
    h = mul(inv_mid, ml)
    g = mul(rm, inv_mid)
    work[...] = hermitian(m_left, square[:chans, :chans]) - conj_mul(ml, h)
    s_rl = rl - mul(rm, h)
    s_rr = hermitian(m_right, square[chans:, :chans]) - mul_conj(g, rm)
    rhs_left = -mul(t, ml)
    rhs_right = -mul_conj(t, rm)
    keep[0] = s_rl
    keep[1] = s_rr
    keep[2] = h
    keep[3] = g
    keep[4, 0:BEAMS] = rhs_left
    keep[4, BEAMS : 2 * BEAMS] = rhs_right

    @pl.loop(0, 2)
    def _(stage):
        work[...] = invert(work[...])

        @pl.when(stage == 0)
        def _():
            inverse = work[...]
            s_rl = keep[0]
            both = mul(jnp.concatenate([s_rl, keep[4, 0:BEAMS]], axis=0), inverse)
            k, y_left = both[:chans], both[chans:]
            work[...] = keep[1] - mul_conj(k, s_rl)
            keep[0] = k
            keep[4, BEAMS : 2 * BEAMS] = keep[4, BEAMS : 2 * BEAMS] - mul_conj(y_left, s_rl)
            keep[4, 0:BEAMS] = y_left
            keep[4, 2 * BEAMS : 3 * BEAMS] = t_ref[...] - mul_conj(y_left, keep[2])
            keep[3] = keep[3] - mul_conj(k, keep[2])

        @pl.when(stage == 1)
        def _():
            y_right = mul(keep[4, BEAMS : 2 * BEAMS], work[...])
            y_left = keep[4, 0:BEAMS] - mul(y_right, keep[0])
            y_mid = keep[4, 2 * BEAMS : 3 * BEAMS] - mul(y_right, keep[3])
            quad = jnp.sum(steer_ref[...] * y_mid, axis=1, keepdims=True)
            y = jnp.concatenate([y_left, y_mid, y_right], axis=1) / jnp.sqrt(quad)
            real_lane = lax.rem(iota(y.shape, 1), 2 * chans) < chans
            mine = jnp.where(real_lane, y, -y).astype(BF16)
            for c in range(out_ref.shape[0]):
                out_ref[c] = mine


def steering(chans):
    index = np.arange(chans)
    sines = -0.8 + 1.6 * np.arange(BEAMS) / (BEAMS - 1)
    angle = math.pi * sines[:, None] * index[None, :]
    return np.concatenate([np.cos(angle), -np.sin(angle)], axis=1).astype(np.float32)


def solve_middle(packed, steer, total):
    half, wide = packed.shape
    return pl.pallas_call(
        functools.partial(middle_kernel, total),
        out_shape=[
            jax.ShapeDtypeStruct((2 * half, wide), F32),
            jax.ShapeDtypeStruct((BEAMS, wide), F32),
        ],
        in_specs=[vmem_spec()] * 2,
        out_specs=[vmem_spec()] * 2,
        compiler_params=params(),
    )(packed, steer)


def solve_outer(own, left, right, steer, inverse, t, total, copies):
    chans, wide = inverse.shape
    return pl.pallas_call(
        functools.partial(outer_kernel, total),
        out_shape=jax.ShapeDtypeStruct((copies, BEAMS, 3 * wide), BF16),
        in_specs=[vmem_spec()] * 6,
        out_specs=vmem_spec(),
        scratch_shapes=[pltpu.VMEM((chans, wide), F32), pltpu.VMEM((5, chans, wide), F32)],
        compiler_params=params(),
    )(own, left, right, steer, inverse, t)


def beam_kernel(bin_ref, block_ref, beam_ref, owner_ref, s0_ref, s1_ref, same_ref, other_ref,
                out_ref, both_ref, rows_ref, seen_ref):
    bins, wide, gates = s0_ref.shape
    devices = seen_ref.shape[0]
    count = bin_ref.shape[0]
    rows_ref[...] = jnp.zeros_like(rows_ref)

    @pl.loop(0, devices)
    def _(i):
        seen_ref[i] = 0

    core = lax.axis_index("range") & 1
    half = bins // 2
    for h, w_ref in enumerate((same_ref, other_ref)):
        w = w_ref[...].astype(F32).reshape(half * BEAMS, 3 * wide)
        lines = slice(h * half, (h + 1) * half)
        for k in range(3):
            lanes = slice(k * wide, (k + 1) * wide)
            part = w[:, lanes]
            both_ref[lines, 0:BEAMS, lanes] = part.reshape(half, BEAMS, wide)
            both_ref[lines, BEAMS:, lanes] = turn(part).reshape(half, BEAMS, wide)

    def detection(j, carry):
        bin_id = bin_ref[j]
        beam_id = beam_ref[j]
        owner = owner_ref[j]
        rank = seen_ref[owner]
        seen_ref[owner] = rank + 1
        index = index_of(bin_id)
        left = both_ref[(index >> 1) + half * ((index & 1) ^ core)].astype(BF16)
        bands = [lax.rem(bin_id + bins - 1 + k, bins) for k in range(3)]
        first = block_ref[j] == 0
        window = jnp.concatenate(
            [jnp.where(first, s0_ref[b], s1_ref[b]) for b in bands], axis=0
        )
        both = dot(left, window)
        line = jnp.concatenate([both[:BEAMS], both[BEAMS:]], axis=1)
        chosen = jnp.where(iota(line.shape, 0) == beam_id, line, 0.0)
        row = owner * CAP + rank
        rows_ref[pl.ds(row, 1), :] = jnp.sum(chosen, axis=0, keepdims=True)
        return carry

    lax.fori_loop(0, count, detection, 0, unroll=16)
    out_ref[...] = rows_ref[...].astype(BF16)


def beam_rows(det_bin, det_block, det_beam, owners, s0, s1, same, other, devices):
    bins, wide, gates = s0.shape
    return pl.pallas_call(
        beam_kernel,
        out_shape=jax.ShapeDtypeStruct((devices * CAP, 2 * gates), BF16),
        in_specs=[smem_spec()] * 4 + [vmem_spec()] * 4,
        out_specs=vmem_spec(),
        scratch_shapes=[
            pltpu.VMEM((bins, 2 * BEAMS, 3 * wide), F32),
            pltpu.VMEM((devices * CAP, 2 * gates), F32),
            pltpu.SMEM((devices,), jnp.int32),
        ],
        compiler_params=params(),
    )(det_bin, det_block, det_beam, owners, s0, s1, same, other)


def on_device(raw, replica, det_bin, det_block, det_beam, det_owner):
    devices = lax.axis_size("range")
    _, chans, pulses, gates = raw.shape
    bins = pulses
    flat = raw.reshape(2, chans * pulses, gates)
    halo = lax.ppermute(
        first_gates(flat), "range", [(source, source - 1) for source in range(1, devices)]
    )
    table = doppler_matrix(pulses, 8)
    s0, local, matrix = spectra_first(flat, replica, table, pulses)
    first = cross_first(s0)
    s1 = spectra_last(local, halo, matrix, table, pulses)
    core_sum = partner(cross_last(False, s1, first), 1)
    keep = cross_last(True, s1, first)
    own, packed = bin_sums(keep, core_sum)
    total = gates * devices
    steer = steering(chans)
    left = from_bin(own, -1)
    right = from_bin(packed, 1)
    inverse, t = solve_middle(packed, steer, total)
    mine = solve_outer(own, left, right, steer, inverse, t, total, bins // 2)
    groups = [
        [first + 2 * k + c for k in range(bins // 2)]
        for first in range(0, devices, bins) for c in range(2)
    ]
    same = lax.all_to_all(
        mine, "range", split_axis=0, concat_axis=0, tiled=True, axis_index_groups=groups
    )
    other = partner(same, 1)
    outgoing = beam_rows(
        det_bin, det_block, det_beam, det_owner[:, 0],
        s0.reshape(bins, 2 * chans, BLOCK), s1.reshape(bins, 2 * chans, BLOCK), same, other, devices,
    )
    incoming = lax.all_to_all(
        outgoing.reshape(devices, CAP, 2 * BLOCK), "range", split_axis=0, concat_axis=0, tiled=True
    )
    return incoming.astype(F32).reshape(devices * CAP, 2 * BLOCK)


def solution(mesh):
    in_specs = (
        P(None, None, None, "range"),
        P(),
        P("range"),
        P("range"),
        P("range"),
        P("range", None),
    )
    out_specs = P("range", None)
    return jax.shard_map(
        on_device, mesh=mesh, in_specs=in_specs, out_specs=out_specs, check_vma=False
    )
```

```python
import functools
import math

import jax
import jax.numpy as jnp
import ml_dtypes
import numpy as np
from jax import lax
from jax.experimental import pallas as pl
from jax.experimental.pallas import tpu as pltpu
from jax.sharding import PartitionSpec as P

BLOCK = 128
BEAMS = 8
CAP = 2

F32 = jnp.float32
BF16 = jnp.bfloat16
VMEM = pltpu.VMEM
MIB = 1024 * 1024
NT = (((1,), (1,)), ((), ()))


def vmem_spec():
    return pl.BlockSpec(memory_space=VMEM)


def smem_spec():
    return pl.BlockSpec(memory_space=pltpu.SMEM)


def hbm_spec():
    return pl.BlockSpec(memory_space=pltpu.HBM)


def params(mib=16):
    return pltpu.CompilerParams(vmem_limit_bytes=mib * MIB)


def dot(a, b):
    return jnp.dot(a, b, preferred_element_type=F32)


def dot_nt(a, b, precision=None):
    return lax.dot_general(a, b, NT, precision=precision, preferred_element_type=F32)


def iota(shape, axis):
    return lax.broadcasted_iota(jnp.int32, shape, axis)


def halo_kernel(part, parts, raw_ref, out_ref, sems):
    count = sems.shape[0]
    size = out_ref.shape[1] // count
    start = part * (raw_ref.shape[1] // parts)
    copies = [
        pltpu.make_async_copy(
            raw_ref.at[:, start + j * size : start + (j + 1) * size, :BLOCK],
            out_ref.at[:, j * size : (j + 1) * size, :],
            sems.at[j],
        )
        for j in range(count)
    ]
    for copy in copies:
        copy.start()
    for copy in copies:
        copy.wait()


def first_gates(raw, part, parts):
    return pl.pallas_call(
        functools.partial(halo_kernel, part, parts),
        out_shape=jax.ShapeDtypeStruct((2, raw.shape[1] // parts, BLOCK), BF16),
        in_specs=[hbm_spec()],
        out_specs=vmem_spec(),
        scratch_shapes=[pltpu.SemaphoreType.DMA((4,))],
        compiler_params=params(63),
    )(raw)


def correlation_matrix(rep_ref, out_ref):
    taps = rep_ref.shape[1]
    base = rep_ref[...].astype(F32)
    row = iota((taps, 2 * taps), 0)
    parts = []
    for i in range(2):
        line = jnp.concatenate([base[i : i + 1], jnp.zeros((1, taps), F32)], axis=1)
        skew = jnp.broadcast_to(line, (taps, 2 * taps))
        bit = 1
        while bit < taps:
            skew = jnp.where((row & bit) != 0, pltpu.roll(skew, bit, 1), skew)
            bit *= 2
        parts.append(skew.T)
    real_part, imag_part = parts
    out_ref[0] = jnp.concatenate([real_part, -imag_part], axis=1).astype(BF16)
    out_ref[1] = jnp.concatenate([imag_part, real_part], axis=1).astype(BF16)


def doppler_matrix(pulses, group):
    index = np.arange(pulses)
    angle = 2.0 * math.pi / pulses * (index[:, None] * index[None, :] % pulses)
    cosine = np.cos(angle) * pulses**-0.5
    sine = np.sin(angle) * pulses**-0.5
    table = np.stack([np.stack([cosine, -sine], 1), np.stack([sine, cosine], 1)], 0)
    full = np.einsum("ipod,ce->dociep", table, np.eye(group))
    shape = (pulses * 2 * group, 2 * group * pulses)
    return full.reshape(shape).astype(ml_dtypes.bfloat16)


def doppler_rows(total, dft):
    compressed = total.astype(BF16)
    rows, wide = compressed.shape
    half, gates = rows // 2, wide // 2
    stacked = jnp.concatenate(
        [
            jnp.concatenate([compressed[:half, :gates], compressed[half:, :gates]], axis=1),
            jnp.concatenate([compressed[:half, gates:], compressed[half:, gates:]], axis=1),
        ],
        axis=0,
    )
    both = dot(dft, stacked)
    lines = both.shape[0] // 8
    joined = jnp.concatenate(
        [both[:, :gates].reshape(lines, 8, gates), both[:, gates:].reshape(lines, 8, gates)],
        axis=1,
    )
    return joined.astype(BF16)


GROUP = 16


def half_of_bins(bins, mine):
    core = lax.axis_index("range") & 1
    return (core if mine else 1 - core) * (bins // 2)


def sent_bins(bins):
    return bins // 2 + 2


def spectra_first_kernel(raw_ref, rep_ref, dft_ref, s_ref, local_ref, taps_ref, send_ref,
                         buf, sems):
    bins, _, chans, gates = s_ref.shape
    size = GROUP * bins
    copies = [
        pltpu.make_async_copy(
            raw_ref.at[:, j * size : (j + 1) * size, :],
            buf.at[:, j * size : (j + 1) * size, :],
            sems.at[j],
        )
        for j in range(chans // GROUP)
    ]
    for copy in copies:
        copy.start()
    correlation_matrix(rep_ref, taps_ref)
    for j, copy in enumerate(copies):
        copy.wait()
        rows = slice(j * size, (j + 1) * size)
        total = dot(buf[0, rows, :], taps_ref[0]) + dot(buf[1, rows, :], taps_ref[1])
        out = doppler_rows(total, dft_ref[...])
        s_ref[:, :, j * GROUP : (j + 1) * GROUP, :] = out.reshape(bins, 2, GROUP, gates)
        later = jnp.concatenate([buf[0, rows, gates:], buf[1, rows, gates:]], axis=1)
        near = jnp.concatenate([taps_ref[0, :gates, :], taps_ref[1, :gates, :]], axis=0)
        local_ref[rows, :] = dot(later, near)
    base = half_of_bins(bins, False)
    for k in range(send_ref.shape[0]):
        send_ref[k] = s_ref[lax.rem(base + k, bins)]


def spectra_part(part, local_ref, halo_ref, taps_ref, dft_ref, bins, gates, write):
    size = GROUP * bins
    count = halo_ref.shape[1] // size
    far = jnp.concatenate([taps_ref[0, gates:, :], taps_ref[1, gates:, :]], axis=0)
    for j in range(count):
        rows = slice(j * size, (j + 1) * size)
        later = jnp.concatenate([halo_ref[0, rows, :], halo_ref[1, rows, :]], axis=1)
        place = part * count + j
        near = local_ref[place * size : (place + 1) * size, :]
        out = doppler_rows(near + dot(later, far), dft_ref[...])
        write(j, out.reshape(bins, 2, GROUP, gates))


def spectra_upper_kernel(local_ref, halo_ref, taps_ref, dft_ref, _, s_ref):
    bins, _, _, gates = s_ref.shape

    def write(j, value):
        s_ref[:, :, j * GROUP : (j + 1) * GROUP, :] = value

    spectra_part(0, local_ref, halo_ref, taps_ref, dft_ref, bins, gates, write)


def spectra_lower_kernel(upper_ref, local_ref, halo_ref, taps_ref, dft_ref, s_ref, send_ref):
    bins, _, chans, gates = s_ref.shape
    half = upper_ref.shape[2]
    s_ref[:, :, :half, :] = upper_ref[...]

    def write(j, value):
        s_ref[:, :, half + j * GROUP : half + (j + 1) * GROUP, :] = value

    spectra_part(1, local_ref, halo_ref, taps_ref, dft_ref, bins, gates, write)
    base = half_of_bins(bins, False)
    for k in range(send_ref.shape[0]):
        send_ref[k] = s_ref[lax.rem(base + k, bins)]


def spectra_first(raw, replica, table, pulses):
    _, rows, gates = raw.shape
    chans = rows // pulses
    taps = replica.shape[1]
    return pl.pallas_call(
        spectra_first_kernel,
        out_shape=[
            jax.ShapeDtypeStruct((pulses, 2, chans, BLOCK), BF16),
            jax.ShapeDtypeStruct((rows, 2 * BLOCK), F32),
            jax.ShapeDtypeStruct((2, 2 * taps, 2 * taps), BF16),
            jax.ShapeDtypeStruct((sent_bins(pulses), 2, chans, BLOCK), BF16),
        ],
        in_specs=[hbm_spec(), vmem_spec(), vmem_spec()],
        out_specs=[vmem_spec()] * 4,
        scratch_shapes=[
            pltpu.VMEM(raw.shape, BF16),
            pltpu.SemaphoreType.DMA((chans // GROUP,)),
        ],
        compiler_params=params(),
    )(raw, replica, table)


def spectra_last(local, halos, matrix, table, pulses, sums):
    chans = local.shape[0] // pulses
    upper = pl.pallas_call(
        spectra_upper_kernel,
        out_shape=jax.ShapeDtypeStruct((pulses, 2, chans // 2, BLOCK), BF16),
        in_specs=[vmem_spec()] * 4 + [pl.BlockSpec(memory_space=pl.ANY)],
        out_specs=vmem_spec(),
        compiler_params=params(),
    )(local, halos[0], matrix, table, sums)
    return pl.pallas_call(
        spectra_lower_kernel,
        out_shape=[
            jax.ShapeDtypeStruct((pulses, 2, chans, BLOCK), BF16),
            jax.ShapeDtypeStruct((sent_bins(pulses), 2, chans, BLOCK), BF16),
        ],
        in_specs=[vmem_spec()] * 5,
        out_specs=[vmem_spec()] * 2,
        compiler_params=params(),
    )(upper, local, halos[1], matrix, table)


def cross_kernel(s_ref, *refs):
    before_ref = refs[0] if len(refs) == 2 else None
    out_ref = refs[-1]
    held, _, chans, gates = s_ref.shape
    count = out_ref.shape[0]
    base = half_of_bins(held, True) if held == 2 * count else 0
    lower = iota((chans, chans), 0) >= iota((chans, chans), 1)
    half = chans // 2

    def packed(block):
        swapped = pltpu.roll(block, chans, 1)
        mixed = jnp.where(lower, block[:, :chans], swapped[:, :chans])
        return jnp.concatenate([mixed[:half], mixed[half:]], axis=1)

    def write(e, block):
        value = jnp.concatenate([packed(block[:chans]), block[chans:]], axis=0)
        if before_ref is not None:
            value = value + before_ref[e]
        out_ref[e] = value

    @pl.loop(0, count // 2, unroll=2)
    def _(step):
        e = step * 2
        each = []
        for k in range(4):
            where = lax.rem(base + e + k, held)
            each.append((s_ref[where, 0], s_ref[where, 1]))
        left = jnp.concatenate(
            [jnp.concatenate([re, im], axis=1) for re, im in each], axis=0
        )
        right = jnp.concatenate(
            [
                jnp.concatenate(pieces, axis=1)
                for re, im in each[:2]
                for pieces in ((re, im), (-im, re))
            ],
            axis=0,
        )
        both = dot_nt(left, right)
        write(e, both[: 3 * chans, : 2 * chans])
        write(e + 1, both[chans:, 2 * chans :])


def cross(spectra, bins, before=None):
    chans = spectra.shape[2]
    data = [spectra] if before is None else [spectra, before]
    return pl.pallas_call(
        cross_kernel,
        out_shape=jax.ShapeDtypeStruct((bins // 2, 5 * chans // 2, 2 * chans), F32),
        in_specs=[vmem_spec()] * len(data),
        out_specs=vmem_spec(),
        compiler_params=params(),
    )(*data)


def partner(value, bit):
    count = lax.axis_size("range")
    return lax.ppermute(value, "range", [(i, i ^ bit) for i in range(count)])


def slot_of(core, x, y, z):
    return (4 * z + ((2 * y + (x ^ y)) ^ (3 * (z & 1)))) ^ (15 * core)


def parts_of(index):
    return index & 1, (index >> 1) & 1, (index >> 2) & 1, (index >> 3) & 3


def bin_of(index):
    core, x, y, z = parts_of(index)
    return core * 16 + slot_of(core, x, y, z)


def index_of(bin_id):
    core = bin_id >> 4
    path = (bin_id & 15) ^ (15 * core)
    z = path >> 2
    turned = (path & 3) ^ (3 * (z & 1))
    y = turned >> 1
    x = (turned & 1) ^ y
    return z * 8 + y * 4 + x * 2 + core


def first_kernel(keep_ref, a_ref, b_ref):
    core, x, y, z = parts_of(lax.axis_index("range"))
    half = keep_ref.shape[1] // 2
    for k in range(8):
        e = slot_of(core, 1 - x, k // 4, k % 4)
        a_ref[k] = keep_ref[e, :half]
        e = slot_of(core, k // 4, 1 - y, k % 4)
        b_ref[k] = keep_ref[e, half:]


def second_kernel(keep_ref, a1_ref, b1_ref, a_ref, b_ref):
    core, x, y, z = parts_of(lax.axis_index("range"))
    half = keep_ref.shape[1] // 2
    for k in range(4):
        e = slot_of(core, x, 1 - y, k)
        a_ref[k] = keep_ref[e, :half] + a1_ref[(1 - y) * 4 + k]
        e = slot_of(core, 1 - x, y, k)
        b_ref[k] = keep_ref[e, half:] + b1_ref[(1 - x) * 4 + k]


def line_sum(keep_ref, a1_ref, b1_ref, a2_ref, b2_ref, flip):
    core, x, y, z = parts_of(lax.axis_index("range"))
    z = z ^ flip
    half = keep_ref.shape[1] // 2
    e = slot_of(core, x, y, z)
    upper = keep_ref[e, :half] + a1_ref[y * 4 + z] + a2_ref[z]
    lower = keep_ref[e, half:] + b1_ref[x * 4 + z] + b2_ref[z]
    return upper, lower


def line_kernel(*refs):
    half = refs[0].shape[1] // 2
    for k, out_ref in enumerate(refs[5:]):
        upper, lower = line_sum(*refs[:5], k + 1)
        out_ref[:half] = upper
        out_ref[half:] = lower


def own_kernel(*refs):
    z1_ref, z2_ref, z3_ref, out_ref, packed_ref = refs[5:]
    half = refs[0].shape[1] // 2
    upper, lower = line_sum(*refs[:5], 0)
    upper = upper + z1_ref[:half] + (z2_ref[:half] + z3_ref[:half])
    out_ref[:half] = upper
    packed_ref[...] = upper[: packed_ref.shape[0]]
    out_ref[half:] = lower + z1_ref[half:] + (z2_ref[half:] + z3_ref[half:])


def summed(kernel, data, shapes):
    return pl.pallas_call(
        kernel,
        out_shape=[jax.ShapeDtypeStruct(shape, F32) for shape in shapes],
        in_specs=[vmem_spec()] * len(data),
        out_specs=[vmem_spec()] * len(shapes),
        compiler_params=params(),
    )(*data)


def bin_sums(keep):
    _, rows, wide = keep.shape
    half = rows // 2
    data = [keep]
    a, b = summed(first_kernel, data, [(8, half, wide)] * 2)
    data += [partner(a, 2), partner(b, 4)]
    a, b = summed(second_kernel, data, [(4, half, wide)] * 2)
    data += [partner(a, 4), partner(b, 2)]
    sends = summed(line_kernel, data, [(rows, wide)] * 3)
    data += [partner(value, (k + 1) * 8) for k, value in enumerate(sends)]
    own, packed = summed(own_kernel, data, [(rows, wide), (rows // 5, wide)])
    bit = 32
    while bit < lax.axis_size("range"):
        own = own + partner(own, bit)
        packed = packed + partner(packed, bit)
        bit *= 2
    return own, packed


def from_bin(value, offset):
    count = lax.axis_size("range")
    pairs = []
    for i in range(count):
        target = index_of((bin_of(i) - offset) % 32) | (i & ~31)
        pairs.append((i, target))
    return lax.ppermute(value, "range", pairs)


def turn(value):
    half = value.shape[1] // 2
    rolled = pltpu.roll(value, half, 1)
    return jnp.where(iota(value.shape, 1) < half, -rolled, rolled)


def embed(value):
    return jnp.concatenate([value, turn(value)], axis=0)


def mul(a, b):
    return jnp.dot(a, embed(b), precision=lax.Precision.HIGHEST, preferred_element_type=F32)


def mul_conj(a, b):
    half = a.shape[1] // 2
    stacked = jnp.concatenate([a, -turn(a)], axis=0)
    both = dot_nt(stacked, b, lax.Precision.HIGHEST)
    rows = a.shape[0]
    return jnp.concatenate([both[:rows], both[rows:]], axis=1)


def conj_mul(a, b):
    half = a.shape[1] // 2
    both = lax.dot_general(
        a, b, (((0,), (0,)), ((), ())),
        precision=lax.Precision.HIGHEST, preferred_element_type=F32,
    )
    return both[:half] - turn(both[half:])


def reciprocal(x):
    value = pl.reciprocal(x, approx=True)
    for _ in range(2):
        value = value * (2.0 - x * value)
    return value


def pivot_inverse(p):
    def times(x, y):
        return x[0] * y[0] - x[1] * y[1], x[0] * y[1] + x[1] * y[0]

    def conj(x):
        return x[0], -x[1]

    def plus(x, y):
        return x[0] + y[0], x[1] + y[1]

    def scaled(x, s):
        return x[0] * s, x[1] * s

    def square(x):
        return x[0] * x[0] + x[1] * x[1]

    def two(a, b, d):
        inv = reciprocal(a * d - square(b))
        return d * inv, scaled(b, -inv), a * inv

    a, d = p[0][0], p[1][1]
    b = p[0][1]
    ea, eb, ed = two(a, b, d)
    f = [[p[0][2], p[0][3]], [p[1][2], p[1][3]]]
    w = [
        [plus(scaled(f[0][j], ea), times(eb, f[1][j])) for j in range(2)],
        [plus(times(conj(eb), f[0][j]), scaled(f[1][j], ed)) for j in range(2)],
    ]

    def inner(i, j):
        return plus(times(conj(f[0][i]), w[0][j]), times(conj(f[1][i]), w[1][j]))

    ha = p[2][2] - inner(0, 0)[0]
    hd = p[3][3] - inner(1, 1)[0]
    cross = inner(0, 1)
    hb = (p[2][3][0] - cross[0], p[2][3][1] - cross[1])
    ga, gb, gd = two(ha, hb, hd)
    v = [
        [
            plus(scaled(w[i][0], ga), times(w[i][1], conj(gb))),
            plus(times(w[i][0], gb), scaled(w[i][1], gd)),
        ]
        for i in range(2)
    ]
    top = [
        [plus(times(v[i][0], conj(w[j][0])), times(v[i][1], conj(w[j][1]))) for j in range(2)]
        for i in range(2)
    ]
    zero = None
    out = [[None] * 4 for _ in range(4)]
    out[0][0] = (ea + top[0][0][0], zero)
    out[1][1] = (ed + top[1][1][0], zero)
    out[0][1] = plus(eb, top[0][1])
    out[2][2], out[3][3], out[2][3] = (ga, zero), (gd, zero), gb
    for i in range(2):
        for j in range(2):
            out[i][2 + j] = (-v[i][j][0], -v[i][j][1])
    for i in range(4):
        for j in range(i):
            out[i][j] = conj(out[j][i])
    return out


def invert(matrix):
    chans, width = matrix.shape
    sub = 8
    tiles = [matrix[t * sub : (t + 1) * sub, :] for t in range(chans // sub)]
    lane = iota((sub, width), 1)
    row = iota((sub, width), 0)
    first_half = lane < chans

    def spin(value):
        rolled = pltpu.roll(value, chans, 1)
        return jnp.where(first_half, -rolled, rolled)

    def column(value, k):
        return jnp.broadcast_to(value[:, k : k + 1], (sub, width))

    def combine(terms):
        while len(terms) > 1:
            terms = [
                terms[i] + terms[i + 1] if i + 1 < len(terms) else terms[i]
                for i in range(0, len(terms), 2)
            ]
        return terms[0]

    for k in range(0, chans, 4):
        t, r = divmod(k, sub)
        lines = [jnp.broadcast_to(tiles[t][r + i : r + i + 1, :], (sub, width)) for i in range(4)]
        pivot = [[None] * 4 for _ in range(4)]
        for i in range(4):
            pivot[i][i] = column(lines[i], k + i)
            for j in range(i + 1, 4):
                pivot[i][j] = column(lines[i], k + j), column(lines[i], chans + k + j)
        low = jnp.bitwise_and(lane, chans - 1)
        cleared = (low >= k) & (low < k + 4)
        unit = [
            jnp.where(cleared, jnp.where(lane == k + i, 1.0, 0.0), lines[i]) for i in range(4)
        ]
        spun = [spin(u) for u in unit]
        p = pivot_inverse(pivot)
        fresh_lines, fresh_spun = [], []
        for i in range(4):
            terms, other = [], []
            for j in range(4):
                re, im = p[i][j]
                terms.append(re * unit[j])
                other.append(re * spun[j])
                if im is not None:
                    terms.append(im * spun[j])
                    other.append(-(im * unit[j]))
            fresh_lines.append(combine(terms))
            fresh_spun.append(combine(other))
        fresh = []
        for s, tile in enumerate(tiles):
            terms = []
            for i in range(4):
                terms.append(column(tile, k + i) * fresh_lines[i])
                terms.append(column(tile, chans + k + i) * fresh_spun[i])
            value = jnp.where(cleared, 0.0, tile) - combine(terms)
            if s == t:
                for i in range(4):
                    value = jnp.where(row == r + i, fresh_lines[i], value)
            fresh.append(value)
        tiles = fresh
    return jnp.concatenate(tiles, axis=0)


def unpacked(ref, scale):
    half, wide = ref.shape[0], ref.shape[1]
    piece = ref[...] * scale
    swapped = pltpu.roll(piece, wide // 2, 1)
    return jnp.concatenate([piece, swapped], axis=0)[:, : wide // 2]


def hermitian(mixed, across):
    i, j = iota(mixed.shape, 0), iota(mixed.shape, 1)
    real_part = jnp.where(i >= j, mixed, across)
    imag_part = jnp.where(i < j, mixed, jnp.where(i > j, -across, 0.0))
    return jnp.concatenate([real_part, imag_part], axis=1)


def middle_kernel(total, packed_ref, steer_ref, inv_ref, t_ref):
    chans = inv_ref.shape[0]
    mixed = unpacked(packed_ref, F32(1.0 / total))
    twice = jnp.concatenate([mixed, mixed], axis=1)
    across = jnp.concatenate([twice, twice], axis=0).T[:chans, :chans]
    inverse = invert(hermitian(mixed, across))
    inv_ref[...] = inverse
    t_ref[...] = mul(steer_ref[...], inverse)


def outer_kernel(total, own_ref, left_ref, right_ref, steer_ref, inv_ref, t_ref, out_ref,
                 work, keep):
    chans = inv_ref.shape[0]
    scale = F32(1.0 / total)
    half = chans // 2
    m_left = unpacked(left_ref.at[:half], scale)
    m_right = unpacked(right_ref, scale)
    ml = left_ref[half : half + chans] * scale
    rl = left_ref[half + chans :] * scale
    rm = own_ref[half : half + chans] * scale
    pair = jnp.concatenate([m_left, m_right], axis=1)
    square = jnp.concatenate([pair, pair], axis=0).T
    inv_mid = inv_ref[...]
    t = t_ref[...]
    h = mul(inv_mid, ml)
    g = mul(rm, inv_mid)
    work[...] = hermitian(m_left, square[:chans, :chans]) - conj_mul(ml, h)
    s_rl = rl - mul(rm, h)
    s_rr = hermitian(m_right, square[chans:, :chans]) - mul_conj(g, rm)
    rhs_left = -mul(t, ml)
    rhs_right = -mul_conj(t, rm)
    keep[0] = s_rl
    keep[1] = s_rr
    keep[2] = h
    keep[3] = g
    keep[4, 0:BEAMS] = rhs_left
    keep[4, BEAMS : 2 * BEAMS] = rhs_right

    @pl.loop(0, 2)
    def _(stage):
        work[...] = invert(work[...])

        @pl.when(stage == 0)
        def _():
            inverse = work[...]
            s_rl = keep[0]
            both = mul(jnp.concatenate([s_rl, keep[4, 0:BEAMS]], axis=0), inverse)
            k, y_left = both[:chans], both[chans:]
            work[...] = keep[1] - mul_conj(k, s_rl)
            keep[0] = k
            keep[4, BEAMS : 2 * BEAMS] = keep[4, BEAMS : 2 * BEAMS] - mul_conj(y_left, s_rl)
            keep[4, 0:BEAMS] = y_left
            keep[4, 2 * BEAMS : 3 * BEAMS] = t_ref[...] - mul_conj(y_left, keep[2])
            keep[3] = keep[3] - mul_conj(k, keep[2])

        @pl.when(stage == 1)
        def _():
            y_right = mul(keep[4, BEAMS : 2 * BEAMS], work[...])
            y_left = keep[4, 0:BEAMS] - mul(y_right, keep[0])
            y_mid = keep[4, 2 * BEAMS : 3 * BEAMS] - mul(y_right, keep[3])
            quad = jnp.sum(steer_ref[...] * y_mid, axis=1, keepdims=True)
            y = jnp.concatenate([y_left, y_mid, y_right], axis=1) / jnp.sqrt(quad)
            real_lane = lax.rem(iota(y.shape, 1), 2 * chans) < chans
            mine = jnp.where(real_lane, y, -y).astype(BF16)
            for c in range(out_ref.shape[0]):
                out_ref[c] = mine


def steering(chans):
    index = np.arange(chans)
    sines = -0.8 + 1.6 * np.arange(BEAMS) / (BEAMS - 1)
    angle = math.pi * sines[:, None] * index[None, :]
    return np.concatenate([np.cos(angle), -np.sin(angle)], axis=1).astype(np.float32)


def solve_middle(packed, steer, total):
    half, wide = packed.shape
    return pl.pallas_call(
        functools.partial(middle_kernel, total),
        out_shape=[
            jax.ShapeDtypeStruct((2 * half, wide), F32),
            jax.ShapeDtypeStruct((BEAMS, wide), F32),
        ],
        in_specs=[vmem_spec()] * 2,
        out_specs=[vmem_spec()] * 2,
        compiler_params=params(),
    )(packed, steer)


def solve_outer(own, left, right, steer, inverse, t, total, copies):
    chans, wide = inverse.shape
    return pl.pallas_call(
        functools.partial(outer_kernel, total),
        out_shape=jax.ShapeDtypeStruct((copies, BEAMS, 3 * wide), BF16),
        in_specs=[vmem_spec()] * 6,
        out_specs=vmem_spec(),
        scratch_shapes=[pltpu.VMEM((chans, wide), F32), pltpu.VMEM((5, chans, wide), F32)],
        compiler_params=params(),
    )(own, left, right, steer, inverse, t)


def beam_kernel(bin_ref, block_ref, beam_ref, owner_ref, s0_ref, s1_ref, w_ref, out_ref,
                both_ref, rows_ref, seen_ref):
    bins, wide, gates = s0_ref.shape
    devices = seen_ref.shape[0]
    count = bin_ref.shape[0]
    rows_ref[...] = jnp.zeros_like(rows_ref)

    @pl.loop(0, devices)
    def _(i):
        seen_ref[i] = 0

    w = w_ref[...].astype(F32).reshape(bins * BEAMS, 3 * wide)
    for k in range(3):
        lanes = slice(k * wide, (k + 1) * wide)
        part = w[:, lanes]
        both_ref[:, 0:BEAMS, lanes] = part.reshape(bins, BEAMS, wide)
        both_ref[:, BEAMS:, lanes] = turn(part).reshape(bins, BEAMS, wide)

    def detection(j, carry):
        bin_id = bin_ref[j]
        beam_id = beam_ref[j]
        owner = owner_ref[j]
        rank = seen_ref[owner]
        seen_ref[owner] = rank + 1
        left = both_ref[index_of(bin_id)].astype(BF16)
        bands = [lax.rem(bin_id + bins - 1 + k, bins) for k in range(3)]
        first = block_ref[j] == 0
        window = jnp.concatenate(
            [jnp.where(first, s0_ref[b], s1_ref[b]) for b in bands], axis=0
        )
        both = dot(left, window)
        line = jnp.concatenate([both[:BEAMS], both[BEAMS:]], axis=1)
        chosen = jnp.where(iota(line.shape, 0) == beam_id, line, 0.0)
        row = owner * CAP + rank
        rows_ref[pl.ds(row, 1), :] = jnp.sum(chosen, axis=0, keepdims=True)
        return carry

    lax.fori_loop(0, count, detection, 0, unroll=16)
    out_ref[...] = rows_ref[...].astype(BF16)


def beam_rows(det_bin, det_block, det_beam, owners, s0, s1, weight, devices):
    bins, wide, gates = s0.shape
    return pl.pallas_call(
        beam_kernel,
        out_shape=jax.ShapeDtypeStruct((devices * CAP, 2 * gates), BF16),
        in_specs=[smem_spec()] * 4 + [vmem_spec()] * 3,
        out_specs=vmem_spec(),
        scratch_shapes=[
            pltpu.VMEM((bins, 2 * BEAMS, 3 * wide), F32),
            pltpu.VMEM((devices * CAP, 2 * gates), F32),
            pltpu.SMEM((devices,), jnp.int32),
        ],
        compiler_params=params(),
    )(det_bin, det_block, det_beam, owners, s0, s1, weight)


def on_device(raw, replica, det_bin, det_block, det_beam, det_owner):
    devices = lax.axis_size("range")
    _, chans, pulses, gates = raw.shape
    bins = pulses
    flat = raw.reshape(2, chans * pulses, gates)
    before = [(source, source - 1) for source in range(1, devices)]
    halos = [lax.ppermute(first_gates(flat, part, 2), "range", before) for part in range(2)]
    table = doppler_matrix(pulses, 8)
    s0, local, matrix, send0 = spectra_first(flat, replica, table, pulses)
    beside0 = partner(send0, 1)
    sums = cross(s0, bins)
    sums = cross(beside0, bins, sums)
    s1, send1 = spectra_last(local, halos, matrix, table, pulses, sums)
    beside1 = partner(send1, 1)
    sums = cross(s1, bins, sums)
    sums = cross(beside1, bins, sums)
    own, packed = bin_sums(sums)
    total = gates * devices
    steer = steering(chans)
    left = from_bin(own, -1)
    right = from_bin(packed, 1)
    inverse, t = solve_middle(packed, steer, total)
    mine = solve_outer(own, left, right, steer, inverse, t, total, bins)
    groups = [list(range(first, first + bins)) for first in range(0, devices, bins)]
    weight = lax.all_to_all(
        mine, "range", split_axis=0, concat_axis=0, tiled=True,
        axis_index_groups=groups if len(groups) > 1 else None,
    )
    outgoing = beam_rows(
        det_bin, det_block, det_beam, det_owner[:, 0],
        s0.reshape(bins, 2 * chans, BLOCK), s1.reshape(bins, 2 * chans, BLOCK), weight, devices,
    )
    incoming = lax.all_to_all(
        outgoing.reshape(devices, CAP, 2 * BLOCK), "range", split_axis=0, concat_axis=0, tiled=True
    )
    return incoming.astype(F32).reshape(devices * CAP, 2 * BLOCK)


def solution(mesh):
    in_specs = (
        P(None, None, None, "range"),
        P(),
        P("range"),
        P("range"),
        P("range"),
        P("range", None),
    )
    out_specs = P("range", None)
    return jax.shard_map(
        on_device, mesh=mesh, in_specs=in_specs, out_specs=out_specs, check_vma=False
    )
```

```python
import functools
import math

import jax
import jax.numpy as jnp
import ml_dtypes
import numpy as np
from jax import lax
from jax.experimental import pallas as pl
from jax.experimental.pallas import tpu as pltpu
from jax.sharding import PartitionSpec as P

BLOCK = 128
BEAMS = 8
CAP = 2

F32 = jnp.float32
BF16 = jnp.bfloat16
VMEM = pltpu.VMEM
MIB = 1024 * 1024
NT = (((1,), (1,)), ((), ()))


def vmem_spec():
    return pl.BlockSpec(memory_space=VMEM)


def smem_spec():
    return pl.BlockSpec(memory_space=pltpu.SMEM)


def hbm_spec():
    return pl.BlockSpec(memory_space=pltpu.HBM)


def params(mib=16):
    return pltpu.CompilerParams(vmem_limit_bytes=mib * MIB)


def dot(a, b):
    return jnp.dot(a, b, preferred_element_type=F32)


def dot_nt(a, b, precision=None):
    return lax.dot_general(a, b, NT, precision=precision, preferred_element_type=F32)


def iota(shape, axis):
    return lax.broadcasted_iota(jnp.int32, shape, axis)


def halo_kernel(part, parts, raw_ref, out_ref, sems):
    count = sems.shape[0]
    size = out_ref.shape[1] // count
    start = part * (raw_ref.shape[1] // parts)
    copies = [
        pltpu.make_async_copy(
            raw_ref.at[:, start + j * size : start + (j + 1) * size, :BLOCK],
            out_ref.at[:, j * size : (j + 1) * size, :],
            sems.at[j],
        )
        for j in range(count)
    ]
    for copy in copies:
        copy.start()
    for copy in copies:
        copy.wait()


def first_gates(raw, part, parts):
    return pl.pallas_call(
        functools.partial(halo_kernel, part, parts),
        out_shape=jax.ShapeDtypeStruct((2, raw.shape[1] // parts, BLOCK), BF16),
        in_specs=[hbm_spec()],
        out_specs=vmem_spec(),
        scratch_shapes=[pltpu.SemaphoreType.DMA((4,))],
        compiler_params=params(63),
    )(raw)


def correlation_matrix(rep_ref, out_ref):
    taps = rep_ref.shape[1]
    base = rep_ref[...].astype(F32)
    row = iota((taps, 2 * taps), 0)
    parts = []
    for i in range(2):
        line = jnp.concatenate([base[i : i + 1], jnp.zeros((1, taps), F32)], axis=1)
        skew = jnp.broadcast_to(line, (taps, 2 * taps))
        bit = 1
        while bit < taps:
            skew = jnp.where((row & bit) != 0, pltpu.roll(skew, bit, 1), skew)
            bit *= 2
        parts.append(skew.T)
    real_part, imag_part = parts
    out_ref[0] = jnp.concatenate([real_part, -imag_part], axis=1).astype(BF16)
    out_ref[1] = jnp.concatenate([imag_part, real_part], axis=1).astype(BF16)


def doppler_matrix(pulses, group):
    index = np.arange(pulses)
    angle = 2.0 * math.pi / pulses * (index[:, None] * index[None, :] % pulses)
    cosine = np.cos(angle) * pulses**-0.5
    sine = np.sin(angle) * pulses**-0.5
    table = np.stack([np.stack([cosine, -sine], 1), np.stack([sine, cosine], 1)], 0)
    full = np.einsum("ipod,ce->dociep", table, np.eye(group))
    shape = (pulses * 2 * group, 2 * group * pulses)
    return full.reshape(shape).astype(ml_dtypes.bfloat16)


def doppler_rows(total, dft):
    compressed = total.astype(BF16)
    rows, wide = compressed.shape
    half, gates = rows // 2, wide // 2
    stacked = jnp.concatenate(
        [
            jnp.concatenate([compressed[:half, :gates], compressed[half:, :gates]], axis=1),
            jnp.concatenate([compressed[:half, gates:], compressed[half:, gates:]], axis=1),
        ],
        axis=0,
    )
    both = dot(dft, stacked)
    lines = both.shape[0] // 8
    joined = jnp.concatenate(
        [both[:, :gates].reshape(lines, 8, gates), both[:, gates:].reshape(lines, 8, gates)],
        axis=1,
    )
    return joined.astype(BF16)


GROUP = 16


def half_of_bins(bins, mine):
    core = lax.axis_index("range") & 1
    return (core if mine else 1 - core) * (bins // 2)


def sent_bins(bins):
    return bins // 2 + 2


def spectra_first_kernel(raw_ref, rep_ref, dft_ref, _, s_ref, local_ref, taps_ref, send_ref,
                         buf, sems):
    bins, _, chans, gates = s_ref.shape
    size = GROUP * bins
    copies = [
        pltpu.make_async_copy(
            raw_ref.at[:, j * size : (j + 1) * size, :],
            buf.at[:, j * size : (j + 1) * size, :],
            sems.at[j],
        )
        for j in range(chans // GROUP)
    ]
    for copy in copies:
        copy.start()
    correlation_matrix(rep_ref, taps_ref)
    for j, copy in enumerate(copies):
        copy.wait()
        rows = slice(j * size, (j + 1) * size)
        total = dot(buf[0, rows, :], taps_ref[0]) + dot(buf[1, rows, :], taps_ref[1])
        out = doppler_rows(total, dft_ref[...])
        s_ref[:, :, j * GROUP : (j + 1) * GROUP, :] = out.reshape(bins, 2, GROUP, gates)
        later = jnp.concatenate([buf[0, rows, gates:], buf[1, rows, gates:]], axis=1)
        near = jnp.concatenate([taps_ref[0, :gates, :], taps_ref[1, :gates, :]], axis=0)
        local_ref[rows, :] = dot(later, near)
    base = half_of_bins(bins, False)
    for k in range(send_ref.shape[0]):
        send_ref[k] = s_ref[lax.rem(base + k, bins)]


def spectra_part(part, local_ref, halo_ref, taps_ref, dft_ref, bins, gates, write):
    size = GROUP * bins
    count = halo_ref.shape[1] // size
    far = jnp.concatenate([taps_ref[0, gates:, :], taps_ref[1, gates:, :]], axis=0)
    for j in range(count):
        rows = slice(j * size, (j + 1) * size)
        later = jnp.concatenate([halo_ref[0, rows, :], halo_ref[1, rows, :]], axis=1)
        place = part * count + j
        near = local_ref[place * size : (place + 1) * size, :]
        out = doppler_rows(near + dot(later, far), dft_ref[...])
        write(j, out.reshape(bins, 2, GROUP, gates))


def spectra_upper_kernel(local_ref, halo_ref, taps_ref, dft_ref, _, s_ref):
    bins, _, _, gates = s_ref.shape

    def write(j, value):
        s_ref[:, :, j * GROUP : (j + 1) * GROUP, :] = value

    spectra_part(0, local_ref, halo_ref, taps_ref, dft_ref, bins, gates, write)


def spectra_lower_kernel(upper_ref, local_ref, halo_ref, taps_ref, dft_ref, s_ref, send_ref):
    bins, _, chans, gates = s_ref.shape
    half = upper_ref.shape[2]
    s_ref[:, :, :half, :] = upper_ref[...]

    def write(j, value):
        s_ref[:, :, half + j * GROUP : half + (j + 1) * GROUP, :] = value

    spectra_part(1, local_ref, halo_ref, taps_ref, dft_ref, bins, gates, write)
    base = half_of_bins(bins, False)
    for k in range(send_ref.shape[0]):
        send_ref[k] = s_ref[lax.rem(base + k, bins)]


def spectra_first(raw, replica, table, pulses, slices):
    _, rows, gates = raw.shape
    chans = rows // pulses
    taps = replica.shape[1]
    return pl.pallas_call(
        spectra_first_kernel,
        out_shape=[
            jax.ShapeDtypeStruct((pulses, 2, chans, BLOCK), BF16),
            jax.ShapeDtypeStruct((rows, 2 * BLOCK), F32),
            jax.ShapeDtypeStruct((2, 2 * taps, 2 * taps), BF16),
            jax.ShapeDtypeStruct((sent_bins(pulses), 2, chans, BLOCK), BF16),
        ],
        in_specs=[hbm_spec(), vmem_spec(), vmem_spec(), pl.BlockSpec(memory_space=pl.ANY)],
        out_specs=[vmem_spec()] * 4,
        scratch_shapes=[
            pltpu.VMEM(raw.shape, BF16),
            pltpu.SemaphoreType.DMA((chans // GROUP,)),
        ],
        compiler_params=params(),
    )(raw, replica, table, slices)


def spectra_last(local, halos, matrix, table, pulses, sums):
    chans = local.shape[0] // pulses
    upper = pl.pallas_call(
        spectra_upper_kernel,
        out_shape=jax.ShapeDtypeStruct((pulses, 2, chans // 2, BLOCK), BF16),
        in_specs=[vmem_spec()] * 4 + [pl.BlockSpec(memory_space=pl.ANY)],
        out_specs=vmem_spec(),
        compiler_params=params(),
    )(local, halos[0], matrix, table, sums)
    return pl.pallas_call(
        spectra_lower_kernel,
        out_shape=[
            jax.ShapeDtypeStruct((pulses, 2, chans, BLOCK), BF16),
            jax.ShapeDtypeStruct((sent_bins(pulses), 2, chans, BLOCK), BF16),
        ],
        in_specs=[vmem_spec()] * 5,
        out_specs=[vmem_spec()] * 2,
        compiler_params=params(),
    )(upper, local, halos[1], matrix, table)


def cross_kernel(s_ref, *refs):
    before_ref = refs[0] if len(refs) == 2 else None
    out_ref = refs[-1]
    held, _, chans, gates = s_ref.shape
    count = out_ref.shape[0]
    base = half_of_bins(held, True) if held == 2 * count else 0
    lower = iota((chans, chans), 0) >= iota((chans, chans), 1)
    half = chans // 2

    def packed(block):
        swapped = pltpu.roll(block, chans, 1)
        mixed = jnp.where(lower, block[:, :chans], swapped[:, :chans])
        return jnp.concatenate([mixed[:half], mixed[half:]], axis=1)

    def write(e, block):
        value = jnp.concatenate([packed(block[:chans]), block[chans:]], axis=0)
        if before_ref is not None:
            value = value + before_ref[e]
        out_ref[e] = value

    @pl.loop(0, count // 2, unroll=2)
    def _(step):
        e = step * 2
        each = []
        for k in range(4):
            where = lax.rem(base + e + k, held)
            each.append((s_ref[where, 0], s_ref[where, 1]))
        left = jnp.concatenate(
            [jnp.concatenate([re, im], axis=1) for re, im in each], axis=0
        )
        right = jnp.concatenate(
            [
                jnp.concatenate(pieces, axis=1)
                for re, im in each[:2]
                for pieces in ((re, im), (-im, re))
            ],
            axis=0,
        )
        both = dot_nt(left, right)
        write(e, both[: 3 * chans, : 2 * chans])
        write(e + 1, both[chans:, 2 * chans :])


def cross(spectra, bins, before=None):
    chans = spectra.shape[2]
    data = [spectra] if before is None else [spectra, before]
    return pl.pallas_call(
        cross_kernel,
        out_shape=jax.ShapeDtypeStruct((bins // 2, 5 * chans // 2, 2 * chans), F32),
        in_specs=[vmem_spec()] * len(data),
        out_specs=vmem_spec(),
        compiler_params=params(),
    )(*data)


def partner(value, bit):
    count = lax.axis_size("range")
    return lax.ppermute(value, "range", [(i, i ^ bit) for i in range(count)])


def slot_of(core, x, y, z):
    return (4 * z + ((2 * y + (x ^ y)) ^ (3 * (z & 1)))) ^ (15 * core)


def parts_of(index):
    return index & 1, (index >> 1) & 1, (index >> 2) & 1, (index >> 3) & 3


def bin_of(index):
    core, x, y, z = parts_of(index)
    return core * 16 + slot_of(core, x, y, z)


def index_of(bin_id):
    core = bin_id >> 4
    path = (bin_id & 15) ^ (15 * core)
    z = path >> 2
    turned = (path & 3) ^ (3 * (z & 1))
    y = turned >> 1
    x = (turned & 1) ^ y
    return z * 8 + y * 4 + x * 2 + core


def first_kernel(keep_ref, a_ref, b_ref):
    core, x, y, z = parts_of(lax.axis_index("range"))
    half = keep_ref.shape[1] // 2
    for k in range(8):
        e = slot_of(core, 1 - x, k // 4, k % 4)
        a_ref[k] = keep_ref[e, :half]
        e = slot_of(core, k // 4, 1 - y, k % 4)
        b_ref[k] = keep_ref[e, half:]


def second_kernel(keep_ref, a1_ref, b1_ref, a_ref, b_ref):
    core, x, y, z = parts_of(lax.axis_index("range"))
    half = keep_ref.shape[1] // 2
    for k in range(4):
        e = slot_of(core, x, 1 - y, k)
        a_ref[k] = keep_ref[e, :half] + a1_ref[(1 - y) * 4 + k]
        e = slot_of(core, 1 - x, y, k)
        b_ref[k] = keep_ref[e, half:] + b1_ref[(1 - x) * 4 + k]


def line_sum(keep_ref, a1_ref, b1_ref, a2_ref, b2_ref, flip):
    core, x, y, z = parts_of(lax.axis_index("range"))
    z = z ^ flip
    half = keep_ref.shape[1] // 2
    e = slot_of(core, x, y, z)
    upper = keep_ref[e, :half] + a1_ref[y * 4 + z] + a2_ref[z]
    lower = keep_ref[e, half:] + b1_ref[x * 4 + z] + b2_ref[z]
    return upper, lower


def line_kernel(*refs):
    half = refs[0].shape[1] // 2
    for k, out_ref in enumerate(refs[5:]):
        upper, lower = line_sum(*refs[:5], k + 1)
        out_ref[:half] = upper
        out_ref[half:] = lower


def own_kernel(*refs):
    z1_ref, z2_ref, z3_ref, out_ref, packed_ref = refs[5:]
    half = refs[0].shape[1] // 2
    upper, lower = line_sum(*refs[:5], 0)
    upper = upper + z1_ref[:half] + (z2_ref[:half] + z3_ref[:half])
    out_ref[:half] = upper
    packed_ref[...] = upper[: packed_ref.shape[0]]
    out_ref[half:] = lower + z1_ref[half:] + (z2_ref[half:] + z3_ref[half:])


def summed(kernel, data, shapes):
    return pl.pallas_call(
        kernel,
        out_shape=[jax.ShapeDtypeStruct(shape, F32) for shape in shapes],
        in_specs=[vmem_spec()] * len(data),
        out_specs=[vmem_spec()] * len(shapes),
        compiler_params=params(),
    )(*data)


def bin_sums(keep):
    _, rows, wide = keep.shape
    half = rows // 2
    data = [keep]
    a, b = summed(first_kernel, data, [(8, half, wide)] * 2)
    data += [partner(a, 2), partner(b, 4)]
    a, b = summed(second_kernel, data, [(4, half, wide)] * 2)
    data += [partner(a, 4), partner(b, 2)]
    sends = summed(line_kernel, data, [(rows, wide)] * 3)
    data += [partner(value, (k + 1) * 8) for k, value in enumerate(sends)]
    own, packed = summed(own_kernel, data, [(rows, wide), (rows // 5, wide)])
    bit = 32
    while bit < lax.axis_size("range"):
        own = own + partner(own, bit)
        packed = packed + partner(packed, bit)
        bit *= 2
    return own, packed


def from_bin(value, offset):
    count = lax.axis_size("range")
    pairs = []
    for i in range(count):
        target = index_of((bin_of(i) - offset) % 32) | (i & ~31)
        pairs.append((i, target))
    return lax.ppermute(value, "range", pairs)


def turn(value):
    half = value.shape[1] // 2
    rolled = pltpu.roll(value, half, 1)
    return jnp.where(iota(value.shape, 1) < half, -rolled, rolled)


def embed(value):
    return jnp.concatenate([value, turn(value)], axis=0)


def mul(a, b):
    return jnp.dot(a, embed(b), precision=lax.Precision.HIGHEST, preferred_element_type=F32)


def mul_conj(a, b):
    half = a.shape[1] // 2
    stacked = jnp.concatenate([a, -turn(a)], axis=0)
    both = dot_nt(stacked, b, lax.Precision.HIGHEST)
    rows = a.shape[0]
    return jnp.concatenate([both[:rows], both[rows:]], axis=1)


def conj_mul(a, b):
    half = a.shape[1] // 2
    both = lax.dot_general(
        a, b, (((0,), (0,)), ((), ())),
        precision=lax.Precision.HIGHEST, preferred_element_type=F32,
    )
    return both[:half] - turn(both[half:])


def reciprocal(x):
    value = pl.reciprocal(x, approx=True)
    for _ in range(2):
        value = value * (2.0 - x * value)
    return value


def pivot_inverse(p):
    def times(x, y):
        return x[0] * y[0] - x[1] * y[1], x[0] * y[1] + x[1] * y[0]

    def conj(x):
        return x[0], -x[1]

    def plus(x, y):
        return x[0] + y[0], x[1] + y[1]

    def scaled(x, s):
        return x[0] * s, x[1] * s

    def square(x):
        return x[0] * x[0] + x[1] * x[1]

    def two(a, b, d):
        inv = reciprocal(a * d - square(b))
        return d * inv, scaled(b, -inv), a * inv

    a, d = p[0][0], p[1][1]
    b = p[0][1]
    ea, eb, ed = two(a, b, d)
    f = [[p[0][2], p[0][3]], [p[1][2], p[1][3]]]
    w = [
        [plus(scaled(f[0][j], ea), times(eb, f[1][j])) for j in range(2)],
        [plus(times(conj(eb), f[0][j]), scaled(f[1][j], ed)) for j in range(2)],
    ]

    def inner(i, j):
        return plus(times(conj(f[0][i]), w[0][j]), times(conj(f[1][i]), w[1][j]))

    ha = p[2][2] - inner(0, 0)[0]
    hd = p[3][3] - inner(1, 1)[0]
    cross = inner(0, 1)
    hb = (p[2][3][0] - cross[0], p[2][3][1] - cross[1])
    ga, gb, gd = two(ha, hb, hd)
    v = [
        [
            plus(scaled(w[i][0], ga), times(w[i][1], conj(gb))),
            plus(times(w[i][0], gb), scaled(w[i][1], gd)),
        ]
        for i in range(2)
    ]
    top = [
        [plus(times(v[i][0], conj(w[j][0])), times(v[i][1], conj(w[j][1]))) for j in range(2)]
        for i in range(2)
    ]
    zero = None
    out = [[None] * 4 for _ in range(4)]
    out[0][0] = (ea + top[0][0][0], zero)
    out[1][1] = (ed + top[1][1][0], zero)
    out[0][1] = plus(eb, top[0][1])
    out[2][2], out[3][3], out[2][3] = (ga, zero), (gd, zero), gb
    for i in range(2):
        for j in range(2):
            out[i][2 + j] = (-v[i][j][0], -v[i][j][1])
    for i in range(4):
        for j in range(i):
            out[i][j] = conj(out[j][i])
    return out


def invert(matrix):
    chans, width = matrix.shape
    sub = 8
    tiles = [matrix[t * sub : (t + 1) * sub, :] for t in range(chans // sub)]
    lane = iota((sub, width), 1)
    row = iota((sub, width), 0)
    first_half = lane < chans

    def spin(value):
        rolled = pltpu.roll(value, chans, 1)
        return jnp.where(first_half, -rolled, rolled)

    def column(value, k):
        return jnp.broadcast_to(value[:, k : k + 1], (sub, width))

    def combine(terms):
        while len(terms) > 1:
            terms = [
                terms[i] + terms[i + 1] if i + 1 < len(terms) else terms[i]
                for i in range(0, len(terms), 2)
            ]
        return terms[0]

    for k in range(0, chans, 4):
        t, r = divmod(k, sub)
        lines = [jnp.broadcast_to(tiles[t][r + i : r + i + 1, :], (sub, width)) for i in range(4)]
        pivot = [[None] * 4 for _ in range(4)]
        for i in range(4):
            pivot[i][i] = column(lines[i], k + i)
            for j in range(i + 1, 4):
                pivot[i][j] = column(lines[i], k + j), column(lines[i], chans + k + j)
        low = jnp.bitwise_and(lane, chans - 1)
        cleared = (low >= k) & (low < k + 4)
        unit = [
            jnp.where(cleared, jnp.where(lane == k + i, 1.0, 0.0), lines[i]) for i in range(4)
        ]
        spun = [spin(u) for u in unit]
        p = pivot_inverse(pivot)
        fresh_lines, fresh_spun = [], []
        for i in range(4):
            terms, other = [], []
            for j in range(4):
                re, im = p[i][j]
                terms.append(re * unit[j])
                other.append(re * spun[j])
                if im is not None:
                    terms.append(im * spun[j])
                    other.append(-(im * unit[j]))
            fresh_lines.append(combine(terms))
            fresh_spun.append(combine(other))
        fresh = []
        for s, tile in enumerate(tiles):
            terms = []
            for i in range(4):
                terms.append(column(tile, k + i) * fresh_lines[i])
                terms.append(column(tile, chans + k + i) * fresh_spun[i])
            value = jnp.where(cleared, 0.0, tile) - combine(terms)
            if s == t:
                for i in range(4):
                    value = jnp.where(row == r + i, fresh_lines[i], value)
            fresh.append(value)
        tiles = fresh
    return jnp.concatenate(tiles, axis=0)


def unpacked(ref, scale):
    half, wide = ref.shape[0], ref.shape[1]
    piece = ref[...] * scale
    swapped = pltpu.roll(piece, wide // 2, 1)
    return jnp.concatenate([piece, swapped], axis=0)[:, : wide // 2]


def hermitian(mixed, across):
    i, j = iota(mixed.shape, 0), iota(mixed.shape, 1)
    real_part = jnp.where(i >= j, mixed, across)
    imag_part = jnp.where(i < j, mixed, jnp.where(i > j, -across, 0.0))
    return jnp.concatenate([real_part, imag_part], axis=1)


def middle_kernel(total, packed_ref, steer_ref, inv_ref, t_ref):
    chans = inv_ref.shape[0]
    mixed = unpacked(packed_ref, F32(1.0 / total))
    twice = jnp.concatenate([mixed, mixed], axis=1)
    across = jnp.concatenate([twice, twice], axis=0).T[:chans, :chans]
    inverse = invert(hermitian(mixed, across))
    inv_ref[...] = inverse
    t_ref[...] = mul(steer_ref[...], inverse)


def outer_kernel(total, own_ref, left_ref, right_ref, steer_ref, inv_ref, t_ref, out_ref,
                 work, keep):
    chans = inv_ref.shape[0]
    scale = F32(1.0 / total)
    half = chans // 2
    m_left = unpacked(left_ref.at[:half], scale)
    m_right = unpacked(right_ref, scale)
    ml = left_ref[half : half + chans] * scale
    rl = left_ref[half + chans :] * scale
    rm = own_ref[half : half + chans] * scale
    pair = jnp.concatenate([m_left, m_right], axis=1)
    square = jnp.concatenate([pair, pair], axis=0).T
    inv_mid = inv_ref[...]
    t = t_ref[...]
    h = mul(inv_mid, ml)
    g = mul(rm, inv_mid)
    work[...] = hermitian(m_left, square[:chans, :chans]) - conj_mul(ml, h)
    s_rl = rl - mul(rm, h)
    s_rr = hermitian(m_right, square[chans:, :chans]) - mul_conj(g, rm)
    rhs_left = -mul(t, ml)
    rhs_right = -mul_conj(t, rm)
    keep[0] = s_rl
    keep[1] = s_rr
    keep[2] = h
    keep[3] = g
    keep[4, 0:BEAMS] = rhs_left
    keep[4, BEAMS : 2 * BEAMS] = rhs_right

    @pl.loop(0, 2)
    def _(stage):
        work[...] = invert(work[...])

        @pl.when(stage == 0)
        def _():
            inverse = work[...]
            s_rl = keep[0]
            both = mul(jnp.concatenate([s_rl, keep[4, 0:BEAMS]], axis=0), inverse)
            k, y_left = both[:chans], both[chans:]
            work[...] = keep[1] - mul_conj(k, s_rl)
            keep[0] = k
            keep[4, BEAMS : 2 * BEAMS] = keep[4, BEAMS : 2 * BEAMS] - mul_conj(y_left, s_rl)
            keep[4, 0:BEAMS] = y_left
            keep[4, 2 * BEAMS : 3 * BEAMS] = t_ref[...] - mul_conj(y_left, keep[2])
            keep[3] = keep[3] - mul_conj(k, keep[2])

        @pl.when(stage == 1)
        def _():
            y_right = mul(keep[4, BEAMS : 2 * BEAMS], work[...])
            y_left = keep[4, 0:BEAMS] - mul(y_right, keep[0])
            y_mid = keep[4, 2 * BEAMS : 3 * BEAMS] - mul(y_right, keep[3])
            quad = jnp.sum(steer_ref[...] * y_mid, axis=1, keepdims=True)
            y = jnp.concatenate([y_left, y_mid, y_right], axis=1) / jnp.sqrt(quad)
            real_lane = lax.rem(iota(y.shape, 1), 2 * chans) < chans
            mine = jnp.where(real_lane, y, -y).astype(BF16)
            for c in range(out_ref.shape[0]):
                out_ref[c] = mine


def steering(chans):
    index = np.arange(chans)
    sines = -0.8 + 1.6 * np.arange(BEAMS) / (BEAMS - 1)
    angle = math.pi * sines[:, None] * index[None, :]
    return np.concatenate([np.cos(angle), -np.sin(angle)], axis=1).astype(np.float32)


def solve_middle(packed, steer, total):
    half, wide = packed.shape
    return pl.pallas_call(
        functools.partial(middle_kernel, total),
        out_shape=[
            jax.ShapeDtypeStruct((2 * half, wide), F32),
            jax.ShapeDtypeStruct((BEAMS, wide), F32),
        ],
        in_specs=[vmem_spec()] * 2,
        out_specs=[vmem_spec()] * 2,
        compiler_params=params(),
    )(packed, steer)


def solve_outer(own, left, right, steer, inverse, t, total, copies):
    chans, wide = inverse.shape
    return pl.pallas_call(
        functools.partial(outer_kernel, total),
        out_shape=jax.ShapeDtypeStruct((copies, BEAMS, 3 * wide), BF16),
        in_specs=[vmem_spec()] * 6,
        out_specs=vmem_spec(),
        scratch_shapes=[pltpu.VMEM((chans, wide), F32), pltpu.VMEM((5, chans, wide), F32)],
        compiler_params=params(),
    )(own, left, right, steer, inverse, t)


def beam_kernel(bin_ref, block_ref, beam_ref, owner_ref, s0_ref, s1_ref, w_ref, out_ref,
                both_ref, rows_ref, seen_ref):
    bins, wide, gates = s0_ref.shape
    devices = seen_ref.shape[0]
    count = bin_ref.shape[0]
    rows_ref[...] = jnp.zeros_like(rows_ref)

    @pl.loop(0, devices)
    def _(i):
        seen_ref[i] = 0

    w = w_ref[...].astype(F32).reshape(bins * BEAMS, 3 * wide)
    for k in range(3):
        lanes = slice(k * wide, (k + 1) * wide)
        part = w[:, lanes]
        both_ref[:, 0:BEAMS, lanes] = part.reshape(bins, BEAMS, wide)
        both_ref[:, BEAMS:, lanes] = turn(part).reshape(bins, BEAMS, wide)

    def detection(j, carry):
        bin_id = bin_ref[j]
        beam_id = beam_ref[j]
        owner = owner_ref[j]
        rank = seen_ref[owner]
        seen_ref[owner] = rank + 1
        left = both_ref[index_of(bin_id)].astype(BF16)
        bands = [lax.rem(bin_id + bins - 1 + k, bins) for k in range(3)]
        first = block_ref[j] == 0
        window = jnp.concatenate(
            [jnp.where(first, s0_ref[b], s1_ref[b]) for b in bands], axis=0
        )
        both = dot(left, window)
        line = jnp.concatenate([both[:BEAMS], both[BEAMS:]], axis=1)
        chosen = jnp.where(iota(line.shape, 0) == beam_id, line, 0.0)
        row = owner * CAP + rank
        rows_ref[pl.ds(row, 1), :] = jnp.sum(chosen, axis=0, keepdims=True)
        return carry

    lax.fori_loop(0, count, detection, 0, unroll=16)
    out_ref[...] = rows_ref[...].astype(BF16)


def beam_rows(det_bin, det_block, det_beam, owners, s0, s1, weight, devices):
    bins, wide, gates = s0.shape
    return pl.pallas_call(
        beam_kernel,
        out_shape=jax.ShapeDtypeStruct((devices * CAP, 2 * gates), BF16),
        in_specs=[smem_spec()] * 4 + [vmem_spec()] * 3,
        out_specs=vmem_spec(),
        scratch_shapes=[
            pltpu.VMEM((bins, 2 * BEAMS, 3 * wide), F32),
            pltpu.VMEM((devices * CAP, 2 * gates), F32),
            pltpu.SMEM((devices,), jnp.int32),
        ],
        compiler_params=params(),
    )(det_bin, det_block, det_beam, owners, s0, s1, weight)


def on_device(raw, replica, det_bin, det_block, det_beam, det_owner):
    devices = lax.axis_size("range")
    _, chans, pulses, gates = raw.shape
    bins = pulses
    flat = raw.reshape(2, chans * pulses, gates)
    before = [(source, source - 1) for source in range(1, devices)]
    slices = [first_gates(flat, part, 2) for part in range(2)]
    halos = [lax.ppermute(value, "range", before) for value in slices]
    table = doppler_matrix(pulses, 8)
    s0, local, matrix, send0 = spectra_first(flat, replica, table, pulses, slices[1])
    beside0 = partner(send0, 1)
    sums = cross(s0, bins)
    sums = cross(beside0, bins, sums)
    s1, send1 = spectra_last(local, halos, matrix, table, pulses, sums)
    beside1 = partner(send1, 1)
    sums = cross(s1, bins, sums)
    sums = cross(beside1, bins, sums)
    own, packed = bin_sums(sums)
    total = gates * devices
    steer = steering(chans)
    left = from_bin(own, -1)
    right = from_bin(packed, 1)
    inverse, t = solve_middle(packed, steer, total)
    mine = solve_outer(own, left, right, steer, inverse, t, total, bins)
    groups = [list(range(first, first + bins)) for first in range(0, devices, bins)]
    weight = lax.all_to_all(
        mine, "range", split_axis=0, concat_axis=0, tiled=True,
        axis_index_groups=groups if len(groups) > 1 else None,
    )
    outgoing = beam_rows(
        det_bin, det_block, det_beam, det_owner[:, 0],
        s0.reshape(bins, 2 * chans, BLOCK), s1.reshape(bins, 2 * chans, BLOCK), weight, devices,
    )
    incoming = lax.all_to_all(
        outgoing.reshape(devices, CAP, 2 * BLOCK), "range", split_axis=0, concat_axis=0, tiled=True
    )
    return incoming.astype(F32).reshape(devices * CAP, 2 * BLOCK)


def solution(mesh):
    in_specs = (
        P(None, None, None, "range"),
        P(),
        P("range"),
        P("range"),
        P("range"),
        P("range", None),
    )
    out_specs = P("range", None)
    return jax.shard_map(
        on_device, mesh=mesh, in_specs=in_specs, out_specs=out_specs, check_vma=False
    )
```

```python
import functools
import math

import jax
import jax.numpy as jnp
import ml_dtypes
import numpy as np
from jax import lax
from jax.experimental import pallas as pl
from jax.experimental.pallas import tpu as pltpu
from jax.sharding import PartitionSpec as P

BLOCK = 128
BEAMS = 8
CAP = 2

F32 = jnp.float32
BF16 = jnp.bfloat16
VMEM = pltpu.VMEM
MIB = 1024 * 1024
NT = (((1,), (1,)), ((), ()))


def vmem_spec():
    return pl.BlockSpec(memory_space=VMEM)


def smem_spec():
    return pl.BlockSpec(memory_space=pltpu.SMEM)


def hbm_spec():
    return pl.BlockSpec(memory_space=pltpu.HBM)


SHORT = pl.CostEstimate(flops=1, bytes_accessed=1, transcendentals=0)


def params(mib=16):
    return pltpu.CompilerParams(vmem_limit_bytes=mib * MIB)


def dot(a, b):
    return jnp.dot(a, b, preferred_element_type=F32)


def dot_nt(a, b, precision=None):
    return lax.dot_general(a, b, NT, precision=precision, preferred_element_type=F32)


def iota(shape, axis):
    return lax.broadcasted_iota(jnp.int32, shape, axis)


def halo_kernel(raw_ref, out_ref, mark_ref, sems):
    mark_ref[...] = jnp.zeros_like(mark_ref)
    count = sems.shape[0]
    size = out_ref.shape[1] // count
    copies = [
        pltpu.make_async_copy(
            raw_ref.at[:, j * size : (j + 1) * size, :BLOCK],
            out_ref.at[:, j * size : (j + 1) * size, :],
            sems.at[j],
        )
        for j in range(count)
    ]
    for copy in copies:
        copy.start()
    for copy in copies:
        copy.wait()


def first_gates(raw):
    return pl.pallas_call(
        halo_kernel,
        out_shape=[
            jax.ShapeDtypeStruct(raw.shape[:2] + (BLOCK,), BF16),
            jax.ShapeDtypeStruct((8, 128), F32),
        ],
        in_specs=[hbm_spec()],
        out_specs=[vmem_spec()] * 2,
        scratch_shapes=[pltpu.SemaphoreType.DMA((8,))],
        compiler_params=params(63),
    )(raw)


def correlation_matrix(rep_ref, out_ref):
    taps = rep_ref.shape[1]
    base = rep_ref[...].astype(F32)
    row = iota((taps, 2 * taps), 0)
    parts = []
    for i in range(2):
        line = jnp.concatenate([base[i : i + 1], jnp.zeros((1, taps), F32)], axis=1)
        skew = jnp.broadcast_to(line, (taps, 2 * taps))
        bit = 1
        while bit < taps:
            skew = jnp.where((row & bit) != 0, pltpu.roll(skew, bit, 1), skew)
            bit *= 2
        parts.append(skew.T)
    real_part, imag_part = parts
    out_ref[0] = jnp.concatenate([real_part, -imag_part], axis=1).astype(BF16)
    out_ref[1] = jnp.concatenate([imag_part, real_part], axis=1).astype(BF16)


def doppler_matrix(pulses, group):
    index = np.arange(pulses)
    angle = 2.0 * math.pi / pulses * (index[:, None] * index[None, :] % pulses)
    cosine = np.cos(angle) * pulses**-0.5
    sine = np.sin(angle) * pulses**-0.5
    table = np.stack([np.stack([cosine, -sine], 1), np.stack([sine, cosine], 1)], 0)
    full = np.einsum("ipod,ce->dociep", table, np.eye(group))
    shape = (pulses * 2 * group, 2 * group * pulses)
    return full.reshape(shape).astype(ml_dtypes.bfloat16)


def doppler_rows(total, dft):
    compressed = total.astype(BF16)
    rows, wide = compressed.shape
    half, gates = rows // 2, wide // 2
    stacked = jnp.concatenate(
        [
            jnp.concatenate([compressed[:half, :gates], compressed[half:, :gates]], axis=1),
            jnp.concatenate([compressed[:half, gates:], compressed[half:, gates:]], axis=1),
        ],
        axis=0,
    )
    both = dot(dft, stacked)
    lines = both.shape[0] // 8
    joined = jnp.concatenate(
        [both[:, :gates].reshape(lines, 8, gates), both[:, gates:].reshape(lines, 8, gates)],
        axis=1,
    )
    return joined.astype(BF16)


GROUP = 16


def half_of_bins(bins, mine):
    core = lax.axis_index("range") & 1
    return (core if mine else 1 - core) * (bins // 2)


def sent_bins(bins):
    return bins // 2 + 2


def spectra_first_kernel(raw_ref, rep_ref, dft_ref, _, s_ref, local_ref, taps_ref, send_ref,
                         buf, sems):
    bins, _, chans, gates = s_ref.shape
    size = GROUP * bins
    copies = [
        pltpu.make_async_copy(
            raw_ref.at[:, j * size : (j + 1) * size, :],
            buf.at[:, j * size : (j + 1) * size, :],
            sems.at[j],
        )
        for j in range(chans // GROUP)
    ]
    for copy in copies:
        copy.start()
    correlation_matrix(rep_ref, taps_ref)
    for j, copy in enumerate(copies):
        copy.wait()
        rows = slice(j * size, (j + 1) * size)
        total = dot(buf[0, rows, :], taps_ref[0]) + dot(buf[1, rows, :], taps_ref[1])
        out = doppler_rows(total, dft_ref[...])
        s_ref[:, :, j * GROUP : (j + 1) * GROUP, :] = out.reshape(bins, 2, GROUP, gates)
        later = jnp.concatenate([buf[0, rows, gates:], buf[1, rows, gates:]], axis=1)
        near = jnp.concatenate([taps_ref[0, :gates, :], taps_ref[1, :gates, :]], axis=0)
        local_ref[rows, :] = dot(later, near)
    base = half_of_bins(bins, False)
    for k in range(send_ref.shape[0]):
        send_ref[k] = s_ref[lax.rem(base + k, bins)]


def spectra_last_kernel(local_ref, halo_ref, taps_ref, dft_ref, _, s_ref, send_ref):
    bins, _, chans, gates = s_ref.shape
    size = GROUP * bins
    far = jnp.concatenate([taps_ref[0, gates:, :], taps_ref[1, gates:, :]], axis=0)
    for j in range(chans // GROUP):
        rows = slice(j * size, (j + 1) * size)
        later = jnp.concatenate([halo_ref[0, rows, :], halo_ref[1, rows, :]], axis=1)
        out = doppler_rows(local_ref[rows, :] + dot(later, far), dft_ref[...])
        s_ref[:, :, j * GROUP : (j + 1) * GROUP, :] = out.reshape(bins, 2, GROUP, gates)
    base = half_of_bins(bins, False)
    for k in range(send_ref.shape[0]):
        send_ref[k] = s_ref[lax.rem(base + k, bins)]


def spectra_first(raw, replica, table, pulses, mark):
    _, rows, gates = raw.shape
    chans = rows // pulses
    taps = replica.shape[1]
    return pl.pallas_call(
        spectra_first_kernel,
        out_shape=[
            jax.ShapeDtypeStruct((pulses, 2, chans, BLOCK), BF16),
            jax.ShapeDtypeStruct((rows, 2 * BLOCK), F32),
            jax.ShapeDtypeStruct((2, 2 * taps, 2 * taps), BF16),
            jax.ShapeDtypeStruct((sent_bins(pulses), 2, chans, BLOCK), BF16),
        ],
        in_specs=[hbm_spec(), vmem_spec(), vmem_spec(), pl.BlockSpec(memory_space=pl.ANY)],
        out_specs=[vmem_spec()] * 4,
        scratch_shapes=[
            pltpu.VMEM(raw.shape, BF16),
            pltpu.SemaphoreType.DMA((chans // GROUP,)),
        ],
        compiler_params=params(),
        cost_estimate=SHORT,
    )(raw, replica, table, mark)


def spectra_last(local, halo, matrix, table, pulses, sums):
    chans = local.shape[0] // pulses
    return pl.pallas_call(
        spectra_last_kernel,
        out_shape=[
            jax.ShapeDtypeStruct((pulses, 2, chans, BLOCK), BF16),
            jax.ShapeDtypeStruct((sent_bins(pulses), 2, chans, BLOCK), BF16),
        ],
        in_specs=[vmem_spec()] * 4 + [pl.BlockSpec(memory_space=pl.ANY)],
        out_specs=[vmem_spec()] * 2,
        compiler_params=params(),
        cost_estimate=SHORT,
    )(local, halo, matrix, table, sums)


def cross_kernel(s_ref, *refs):
    before_ref = refs[0] if len(refs) == 2 else None
    out_ref = refs[-1]
    held, _, chans, gates = s_ref.shape
    count = out_ref.shape[0]
    base = half_of_bins(held, True) if held == 2 * count else 0
    lower = iota((chans, chans), 0) >= iota((chans, chans), 1)
    half = chans // 2

    def packed(block):
        swapped = pltpu.roll(block, chans, 1)
        mixed = jnp.where(lower, block[:, :chans], swapped[:, :chans])
        return jnp.concatenate([mixed[:half], mixed[half:]], axis=1)

    def write(e, block):
        value = jnp.concatenate([packed(block[:chans]), block[chans:]], axis=0)
        if before_ref is not None:
            value = value + before_ref[e]
        out_ref[e] = value

    @pl.loop(0, count // 2, unroll=2)
    def _(step):
        e = step * 2
        each = []
        for k in range(4):
            where = lax.rem(base + e + k, held)
            each.append((s_ref[where, 0], s_ref[where, 1]))
        left = jnp.concatenate(
            [jnp.concatenate([re, im], axis=1) for re, im in each], axis=0
        )
        right = jnp.concatenate(
            [
                jnp.concatenate(pieces, axis=1)
                for re, im in each[:2]
                for pieces in ((re, im), (-im, re))
            ],
            axis=0,
        )
        both = dot_nt(left, right)
        write(e, both[: 3 * chans, : 2 * chans])
        write(e + 1, both[chans:, 2 * chans :])


def cross(spectra, bins, before=None):
    chans = spectra.shape[2]
    data = [spectra] if before is None else [spectra, before]
    return pl.pallas_call(
        cross_kernel,
        out_shape=jax.ShapeDtypeStruct((bins // 2, 5 * chans // 2, 2 * chans), F32),
        in_specs=[vmem_spec()] * len(data),
        out_specs=vmem_spec(),
        compiler_params=params(),
        cost_estimate=SHORT,
    )(*data)


def partner(value, bit):
    count = lax.axis_size("range")
    return lax.ppermute(value, "range", [(i, i ^ bit) for i in range(count)])


def slot_of(core, x, y, z):
    return (4 * z + ((2 * y + (x ^ y)) ^ (3 * (z & 1)))) ^ (15 * core)


def parts_of(index):
    return index & 1, (index >> 1) & 1, (index >> 2) & 1, (index >> 3) & 3


def bin_of(index):
    core, x, y, z = parts_of(index)
    return core * 16 + slot_of(core, x, y, z)


def index_of(bin_id):
    core = bin_id >> 4
    path = (bin_id & 15) ^ (15 * core)
    z = path >> 2
    turned = (path & 3) ^ (3 * (z & 1))
    y = turned >> 1
    x = (turned & 1) ^ y
    return z * 8 + y * 4 + x * 2 + core


def first_kernel(keep_ref, a_ref, b_ref):
    core, x, y, z = parts_of(lax.axis_index("range"))
    half = keep_ref.shape[1] // 2
    for k in range(8):
        e = slot_of(core, 1 - x, k // 4, k % 4)
        a_ref[k] = keep_ref[e, :half]
        e = slot_of(core, k // 4, 1 - y, k % 4)
        b_ref[k] = keep_ref[e, half:]


def second_kernel(keep_ref, a1_ref, b1_ref, a_ref, b_ref):
    core, x, y, z = parts_of(lax.axis_index("range"))
    half = keep_ref.shape[1] // 2
    for k in range(4):
        e = slot_of(core, x, 1 - y, k)
        a_ref[k] = keep_ref[e, :half] + a1_ref[(1 - y) * 4 + k]
        e = slot_of(core, 1 - x, y, k)
        b_ref[k] = keep_ref[e, half:] + b1_ref[(1 - x) * 4 + k]


def line_sum(keep_ref, a1_ref, b1_ref, a2_ref, b2_ref, flip):
    core, x, y, z = parts_of(lax.axis_index("range"))
    z = z ^ flip
    half = keep_ref.shape[1] // 2
    e = slot_of(core, x, y, z)
    upper = keep_ref[e, :half] + a1_ref[y * 4 + z] + a2_ref[z]
    lower = keep_ref[e, half:] + b1_ref[x * 4 + z] + b2_ref[z]
    return upper, lower


def line_kernel(*refs):
    half = refs[0].shape[1] // 2
    for k, out_ref in enumerate(refs[5:]):
        upper, lower = line_sum(*refs[:5], k + 1)
        out_ref[:half] = upper
        out_ref[half:] = lower


def own_kernel(*refs):
    z1_ref, z2_ref, z3_ref, out_ref, packed_ref = refs[5:]
    half = refs[0].shape[1] // 2
    upper, lower = line_sum(*refs[:5], 0)
    upper = upper + z1_ref[:half] + (z2_ref[:half] + z3_ref[:half])
    out_ref[:half] = upper
    packed_ref[...] = upper[: packed_ref.shape[0]]
    out_ref[half:] = lower + z1_ref[half:] + (z2_ref[half:] + z3_ref[half:])


def summed(kernel, data, shapes):
    return pl.pallas_call(
        kernel,
        out_shape=[jax.ShapeDtypeStruct(shape, F32) for shape in shapes],
        in_specs=[vmem_spec()] * len(data),
        out_specs=[vmem_spec()] * len(shapes),
        compiler_params=params(),
    )(*data)


def bin_sums(keep):
    _, rows, wide = keep.shape
    half = rows // 2
    data = [keep]
    a, b = summed(first_kernel, data, [(8, half, wide)] * 2)
    data += [partner(a, 2), partner(b, 4)]
    a, b = summed(second_kernel, data, [(4, half, wide)] * 2)
    data += [partner(a, 4), partner(b, 2)]
    sends = summed(line_kernel, data, [(rows, wide)] * 3)
    data += [partner(value, (k + 1) * 8) for k, value in enumerate(sends)]
    own, packed = summed(own_kernel, data, [(rows, wide), (rows // 5, wide)])
    bit = 32
    while bit < lax.axis_size("range"):
        own = own + partner(own, bit)
        packed = packed + partner(packed, bit)
        bit *= 2
    return own, packed


def from_bin(value, offset):
    count = lax.axis_size("range")
    pairs = []
    for i in range(count):
        target = index_of((bin_of(i) - offset) % 32) | (i & ~31)
        pairs.append((i, target))
    return lax.ppermute(value, "range", pairs)


def turn(value):
    half = value.shape[1] // 2
    rolled = pltpu.roll(value, half, 1)
    return jnp.where(iota(value.shape, 1) < half, -rolled, rolled)


def embed(value):
    return jnp.concatenate([value, turn(value)], axis=0)


def mul(a, b):
    return jnp.dot(a, embed(b), precision=lax.Precision.HIGHEST, preferred_element_type=F32)


def mul_conj(a, b):
    half = a.shape[1] // 2
    stacked = jnp.concatenate([a, -turn(a)], axis=0)
    both = dot_nt(stacked, b, lax.Precision.HIGHEST)
    rows = a.shape[0]
    return jnp.concatenate([both[:rows], both[rows:]], axis=1)


def conj_mul(a, b):
    half = a.shape[1] // 2
    both = lax.dot_general(
        a, b, (((0,), (0,)), ((), ())),
        precision=lax.Precision.HIGHEST, preferred_element_type=F32,
    )
    return both[:half] - turn(both[half:])


def reciprocal(x):
    value = pl.reciprocal(x, approx=True)
    for _ in range(2):
        value = value * (2.0 - x * value)
    return value


def pivot_inverse(p):
    def times(x, y):
        return x[0] * y[0] - x[1] * y[1], x[0] * y[1] + x[1] * y[0]

    def conj(x):
        return x[0], -x[1]

    def plus(x, y):
        return x[0] + y[0], x[1] + y[1]

    def scaled(x, s):
        return x[0] * s, x[1] * s

    def square(x):
        return x[0] * x[0] + x[1] * x[1]

    def two(a, b, d):
        inv = reciprocal(a * d - square(b))
        return d * inv, scaled(b, -inv), a * inv

    a, d = p[0][0], p[1][1]
    b = p[0][1]
    ea, eb, ed = two(a, b, d)
    f = [[p[0][2], p[0][3]], [p[1][2], p[1][3]]]
    w = [
        [plus(scaled(f[0][j], ea), times(eb, f[1][j])) for j in range(2)],
        [plus(times(conj(eb), f[0][j]), scaled(f[1][j], ed)) for j in range(2)],
    ]

    def inner(i, j):
        return plus(times(conj(f[0][i]), w[0][j]), times(conj(f[1][i]), w[1][j]))

    ha = p[2][2] - inner(0, 0)[0]
    hd = p[3][3] - inner(1, 1)[0]
    cross = inner(0, 1)
    hb = (p[2][3][0] - cross[0], p[2][3][1] - cross[1])
    ga, gb, gd = two(ha, hb, hd)
    v = [
        [
            plus(scaled(w[i][0], ga), times(w[i][1], conj(gb))),
            plus(times(w[i][0], gb), scaled(w[i][1], gd)),
        ]
        for i in range(2)
    ]
    top = [
        [plus(times(v[i][0], conj(w[j][0])), times(v[i][1], conj(w[j][1]))) for j in range(2)]
        for i in range(2)
    ]
    zero = None
    out = [[None] * 4 for _ in range(4)]
    out[0][0] = (ea + top[0][0][0], zero)
    out[1][1] = (ed + top[1][1][0], zero)
    out[0][1] = plus(eb, top[0][1])
    out[2][2], out[3][3], out[2][3] = (ga, zero), (gd, zero), gb
    for i in range(2):
        for j in range(2):
            out[i][2 + j] = (-v[i][j][0], -v[i][j][1])
    for i in range(4):
        for j in range(i):
            out[i][j] = conj(out[j][i])
    return out


def invert(matrix):
    chans, width = matrix.shape
    sub = 8
    tiles = [matrix[t * sub : (t + 1) * sub, :] for t in range(chans // sub)]
    lane = iota((sub, width), 1)
    row = iota((sub, width), 0)
    first_half = lane < chans

    def spin(value):
        rolled = pltpu.roll(value, chans, 1)
        return jnp.where(first_half, -rolled, rolled)

    def column(value, k):
        return jnp.broadcast_to(value[:, k : k + 1], (sub, width))

    def combine(terms):
        while len(terms) > 1:
            terms = [
                terms[i] + terms[i + 1] if i + 1 < len(terms) else terms[i]
                for i in range(0, len(terms), 2)
            ]
        return terms[0]

    for k in range(0, chans, 4):
        t, r = divmod(k, sub)
        lines = [jnp.broadcast_to(tiles[t][r + i : r + i + 1, :], (sub, width)) for i in range(4)]
        pivot = [[None] * 4 for _ in range(4)]
        for i in range(4):
            pivot[i][i] = column(lines[i], k + i)
            for j in range(i + 1, 4):
                pivot[i][j] = column(lines[i], k + j), column(lines[i], chans + k + j)
        low = jnp.bitwise_and(lane, chans - 1)
        cleared = (low >= k) & (low < k + 4)
        unit = [
            jnp.where(cleared, jnp.where(lane == k + i, 1.0, 0.0), lines[i]) for i in range(4)
        ]
        spun = [spin(u) for u in unit]
        p = pivot_inverse(pivot)
        fresh_lines, fresh_spun = [], []
        for i in range(4):
            terms, other = [], []
            for j in range(4):
                re, im = p[i][j]
                terms.append(re * unit[j])
                other.append(re * spun[j])
                if im is not None:
                    terms.append(im * spun[j])
                    other.append(-(im * unit[j]))
            fresh_lines.append(combine(terms))
            fresh_spun.append(combine(other))
        fresh = []
        for s, tile in enumerate(tiles):
            terms = []
            for i in range(4):
                terms.append(column(tile, k + i) * fresh_lines[i])
                terms.append(column(tile, chans + k + i) * fresh_spun[i])
            value = jnp.where(cleared, 0.0, tile) - combine(terms)
            if s == t:
                for i in range(4):
                    value = jnp.where(row == r + i, fresh_lines[i], value)
            fresh.append(value)
        tiles = fresh
    return jnp.concatenate(tiles, axis=0)


def unpacked(ref, scale):
    half, wide = ref.shape[0], ref.shape[1]
    piece = ref[...] * scale
    swapped = pltpu.roll(piece, wide // 2, 1)
    return jnp.concatenate([piece, swapped], axis=0)[:, : wide // 2]


def hermitian(mixed, across):
    i, j = iota(mixed.shape, 0), iota(mixed.shape, 1)
    real_part = jnp.where(i >= j, mixed, across)
    imag_part = jnp.where(i < j, mixed, jnp.where(i > j, -across, 0.0))
    return jnp.concatenate([real_part, imag_part], axis=1)


def middle_kernel(total, packed_ref, steer_ref, inv_ref, t_ref):
    chans = inv_ref.shape[0]
    mixed = unpacked(packed_ref, F32(1.0 / total))
    twice = jnp.concatenate([mixed, mixed], axis=1)
    across = jnp.concatenate([twice, twice], axis=0).T[:chans, :chans]
    inverse = invert(hermitian(mixed, across))
    inv_ref[...] = inverse
    t_ref[...] = mul(steer_ref[...], inverse)


def outer_kernel(total, own_ref, left_ref, right_ref, steer_ref, inv_ref, t_ref, out_ref,
                 work, keep):
    chans = inv_ref.shape[0]
    scale = F32(1.0 / total)
    half = chans // 2
    m_left = unpacked(left_ref.at[:half], scale)
    m_right = unpacked(right_ref, scale)
    ml = left_ref[half : half + chans] * scale
    rl = left_ref[half + chans :] * scale
    rm = own_ref[half : half + chans] * scale
    pair = jnp.concatenate([m_left, m_right], axis=1)
    square = jnp.concatenate([pair, pair], axis=0).T
    inv_mid = inv_ref[...]
    t = t_ref[...]
    h = mul(inv_mid, ml)
    g = mul(rm, inv_mid)
    work[...] = hermitian(m_left, square[:chans, :chans]) - conj_mul(ml, h)
    s_rl = rl - mul(rm, h)
    s_rr = hermitian(m_right, square[chans:, :chans]) - mul_conj(g, rm)
    rhs_left = -mul(t, ml)
    rhs_right = -mul_conj(t, rm)
    keep[0] = s_rl
    keep[1] = s_rr
    keep[2] = h
    keep[3] = g
    keep[4, 0:BEAMS] = rhs_left
    keep[4, BEAMS : 2 * BEAMS] = rhs_right

    @pl.loop(0, 2)
    def _(stage):
        work[...] = invert(work[...])

        @pl.when(stage == 0)
        def _():
            inverse = work[...]
            s_rl = keep[0]
            both = mul(jnp.concatenate([s_rl, keep[4, 0:BEAMS]], axis=0), inverse)
            k, y_left = both[:chans], both[chans:]
            work[...] = keep[1] - mul_conj(k, s_rl)
            keep[0] = k
            keep[4, BEAMS : 2 * BEAMS] = keep[4, BEAMS : 2 * BEAMS] - mul_conj(y_left, s_rl)
            keep[4, 0:BEAMS] = y_left
            keep[4, 2 * BEAMS : 3 * BEAMS] = t_ref[...] - mul_conj(y_left, keep[2])
            keep[3] = keep[3] - mul_conj(k, keep[2])

        @pl.when(stage == 1)
        def _():
            y_right = mul(keep[4, BEAMS : 2 * BEAMS], work[...])
            y_left = keep[4, 0:BEAMS] - mul(y_right, keep[0])
            y_mid = keep[4, 2 * BEAMS : 3 * BEAMS] - mul(y_right, keep[3])
            quad = jnp.sum(steer_ref[...] * y_mid, axis=1, keepdims=True)
            y = jnp.concatenate([y_left, y_mid, y_right], axis=1) / jnp.sqrt(quad)
            real_lane = lax.rem(iota(y.shape, 1), 2 * chans) < chans
            mine = jnp.where(real_lane, y, -y).astype(BF16)
            for c in range(out_ref.shape[0]):
                out_ref[c] = mine


def steering(chans):
    index = np.arange(chans)
    sines = -0.8 + 1.6 * np.arange(BEAMS) / (BEAMS - 1)
    angle = math.pi * sines[:, None] * index[None, :]
    return np.concatenate([np.cos(angle), -np.sin(angle)], axis=1).astype(np.float32)


def solve_middle(packed, steer, total):
    half, wide = packed.shape
    return pl.pallas_call(
        functools.partial(middle_kernel, total),
        out_shape=[
            jax.ShapeDtypeStruct((2 * half, wide), F32),
            jax.ShapeDtypeStruct((BEAMS, wide), F32),
        ],
        in_specs=[vmem_spec()] * 2,
        out_specs=[vmem_spec()] * 2,
        compiler_params=params(),
    )(packed, steer)


def solve_outer(own, left, right, steer, inverse, t, total, copies):
    chans, wide = inverse.shape
    return pl.pallas_call(
        functools.partial(outer_kernel, total),
        out_shape=jax.ShapeDtypeStruct((copies, BEAMS, 3 * wide), BF16),
        in_specs=[vmem_spec()] * 6,
        out_specs=vmem_spec(),
        scratch_shapes=[pltpu.VMEM((chans, wide), F32), pltpu.VMEM((5, chans, wide), F32)],
        compiler_params=params(),
    )(own, left, right, steer, inverse, t)


def beam_kernel(bin_ref, block_ref, beam_ref, owner_ref, s0_ref, s1_ref, w_ref, out_ref,
                both_ref, rows_ref, seen_ref):
    bins, wide, gates = s0_ref.shape
    devices = seen_ref.shape[0]
    count = bin_ref.shape[0]
    rows_ref[...] = jnp.zeros_like(rows_ref)

    @pl.loop(0, devices)
    def _(i):
        seen_ref[i] = 0

    w = w_ref[...].astype(F32).reshape(bins * BEAMS, 3 * wide)
    for k in range(3):
        lanes = slice(k * wide, (k + 1) * wide)
        part = w[:, lanes]
        both_ref[:, 0:BEAMS, lanes] = part.reshape(bins, BEAMS, wide)
        both_ref[:, BEAMS:, lanes] = turn(part).reshape(bins, BEAMS, wide)

    def detection(j, carry):
        bin_id = bin_ref[j]
        beam_id = beam_ref[j]
        owner = owner_ref[j]
        rank = seen_ref[owner]
        seen_ref[owner] = rank + 1
        left = both_ref[index_of(bin_id)].astype(BF16)
        bands = [lax.rem(bin_id + bins - 1 + k, bins) for k in range(3)]
        first = block_ref[j] == 0
        window = jnp.concatenate(
            [jnp.where(first, s0_ref[b], s1_ref[b]) for b in bands], axis=0
        )
        both = dot(left, window)
        line = jnp.concatenate([both[:BEAMS], both[BEAMS:]], axis=1)
        chosen = jnp.where(iota(line.shape, 0) == beam_id, line, 0.0)
        row = owner * CAP + rank
        rows_ref[pl.ds(row, 1), :] = jnp.sum(chosen, axis=0, keepdims=True)
        return carry

    lax.fori_loop(0, count, detection, 0, unroll=16)
    out_ref[...] = rows_ref[...].astype(BF16)


def beam_rows(det_bin, det_block, det_beam, owners, s0, s1, weight, devices):
    bins, wide, gates = s0.shape
    return pl.pallas_call(
        beam_kernel,
        out_shape=jax.ShapeDtypeStruct((devices * CAP, 2 * gates), BF16),
        in_specs=[smem_spec()] * 4 + [vmem_spec()] * 3,
        out_specs=vmem_spec(),
        scratch_shapes=[
            pltpu.VMEM((bins, 2 * BEAMS, 3 * wide), F32),
            pltpu.VMEM((devices * CAP, 2 * gates), F32),
            pltpu.SMEM((devices,), jnp.int32),
        ],
        compiler_params=params(),
    )(det_bin, det_block, det_beam, owners, s0, s1, weight)


def on_device(raw, replica, det_bin, det_block, det_beam, det_owner):
    devices = lax.axis_size("range")
    _, chans, pulses, gates = raw.shape
    bins = pulses
    flat = raw.reshape(2, chans * pulses, gates)
    before = [(source, source - 1) for source in range(1, devices)]
    gates_before, mark = first_gates(flat)
    halo = lax.ppermute(gates_before, "range", before)
    table = doppler_matrix(pulses, 8)
    s0, local, matrix, send0 = spectra_first(flat, replica, table, pulses, mark)
    beside0 = partner(send0, 1)
    sums = cross(s0, bins)
    sums = cross(beside0, bins, sums)
    s1, send1 = spectra_last(local, halo, matrix, table, pulses, sums)
    beside1 = partner(send1, 1)
    sums = cross(s1, bins, sums)
    sums = cross(beside1, bins, sums)
    own, packed = bin_sums(sums)
    total = gates * devices
    steer = steering(chans)
    left = from_bin(own, -1)
    right = from_bin(packed, 1)
    inverse, t = solve_middle(packed, steer, total)
    mine = solve_outer(own, left, right, steer, inverse, t, total, bins)
    groups = [list(range(first, first + bins)) for first in range(0, devices, bins)]
    weight = lax.all_to_all(
        mine, "range", split_axis=0, concat_axis=0, tiled=True,
        axis_index_groups=groups if len(groups) > 1 else None,
    )
    outgoing = beam_rows(
        det_bin, det_block, det_beam, det_owner[:, 0],
        s0.reshape(bins, 2 * chans, BLOCK), s1.reshape(bins, 2 * chans, BLOCK), weight, devices,
    )
    incoming = lax.all_to_all(
        outgoing.reshape(devices, CAP, 2 * BLOCK), "range", split_axis=0, concat_axis=0, tiled=True
    )
    return incoming.astype(F32).reshape(devices * CAP, 2 * BLOCK)


def solution(mesh):
    in_specs = (
        P(None, None, None, "range"),
        P(),
        P("range"),
        P("range"),
        P("range"),
        P("range", None),
    )
    out_specs = P("range", None)
    return jax.shard_map(
        on_device, mesh=mesh, in_specs=in_specs, out_specs=out_specs, check_vma=False
    )
```

```python
import functools
import math

import jax
import jax.numpy as jnp
import ml_dtypes
import numpy as np
from jax import lax
from jax.experimental import pallas as pl
from jax.experimental.pallas import tpu as pltpu
from jax.sharding import PartitionSpec as P

BLOCK = 128
BEAMS = 8
CAP = 2

F32 = jnp.float32
BF16 = jnp.bfloat16
VMEM = pltpu.VMEM
MIB = 1024 * 1024
NT = (((1,), (1,)), ((), ()))


def vmem_spec():
    return pl.BlockSpec(memory_space=VMEM)


def smem_spec():
    return pl.BlockSpec(memory_space=pltpu.SMEM)


def hbm_spec():
    return pl.BlockSpec(memory_space=pltpu.HBM)


SHORT = pl.CostEstimate(flops=1, bytes_accessed=1, transcendentals=0)


def params(mib=16):
    return pltpu.CompilerParams(vmem_limit_bytes=mib * MIB)


def dot(a, b):
    return jnp.dot(a, b, preferred_element_type=F32)


def dot_nt(a, b, precision=None):
    return lax.dot_general(a, b, NT, precision=precision, preferred_element_type=F32)


def iota(shape, axis):
    return lax.broadcasted_iota(jnp.int32, shape, axis)


def halo_kernel(raw_ref, out_ref, mark_ref, sems):
    mark_ref[...] = jnp.zeros_like(mark_ref)
    count = sems.shape[0]
    size = out_ref.shape[1] // count
    copies = [
        pltpu.make_async_copy(
            raw_ref.at[:, j * size : (j + 1) * size, :BLOCK],
            out_ref.at[:, j * size : (j + 1) * size, :],
            sems.at[j],
        )
        for j in range(count)
    ]
    for copy in copies:
        copy.start()
    for copy in copies:
        copy.wait()


def first_gates(raw):
    return pl.pallas_call(
        halo_kernel,
        out_shape=[
            jax.ShapeDtypeStruct(raw.shape[:2] + (BLOCK,), BF16),
            jax.ShapeDtypeStruct((8, 128), F32),
        ],
        in_specs=[hbm_spec()],
        out_specs=[hbm_spec(), vmem_spec()],
        scratch_shapes=[pltpu.SemaphoreType.DMA((8,))],
        compiler_params=params(63),
    )(raw)


def correlation_matrix(rep_ref, out_ref):
    taps = rep_ref.shape[1]
    base = rep_ref[...].astype(F32)
    row = iota((taps, 2 * taps), 0)
    parts = []
    for i in range(2):
        line = jnp.concatenate([base[i : i + 1], jnp.zeros((1, taps), F32)], axis=1)
        skew = jnp.broadcast_to(line, (taps, 2 * taps))
        bit = 1
        while bit < taps:
            skew = jnp.where((row & bit) != 0, pltpu.roll(skew, bit, 1), skew)
            bit *= 2
        parts.append(skew.T)
    real_part, imag_part = parts
    out_ref[0] = jnp.concatenate([real_part, -imag_part], axis=1).astype(BF16)
    out_ref[1] = jnp.concatenate([imag_part, real_part], axis=1).astype(BF16)


def doppler_matrix(pulses, group):
    index = np.arange(pulses)
    angle = 2.0 * math.pi / pulses * (index[:, None] * index[None, :] % pulses)
    cosine = np.cos(angle) * pulses**-0.5
    sine = np.sin(angle) * pulses**-0.5
    table = np.stack([np.stack([cosine, -sine], 1), np.stack([sine, cosine], 1)], 0)
    full = np.einsum("ipod,ce->dociep", table, np.eye(group))
    shape = (pulses * 2 * group, 2 * group * pulses)
    return full.reshape(shape).astype(ml_dtypes.bfloat16)


def doppler_rows(total, dft):
    compressed = total.astype(BF16)
    rows, wide = compressed.shape
    half, gates = rows // 2, wide // 2
    stacked = jnp.concatenate(
        [
            jnp.concatenate([compressed[:half, :gates], compressed[half:, :gates]], axis=1),
            jnp.concatenate([compressed[:half, gates:], compressed[half:, gates:]], axis=1),
        ],
        axis=0,
    )
    both = dot(dft, stacked)
    lines = both.shape[0] // 8
    joined = jnp.concatenate(
        [both[:, :gates].reshape(lines, 8, gates), both[:, gates:].reshape(lines, 8, gates)],
        axis=1,
    )
    return joined.astype(BF16)


GROUP = 16


def half_of_bins(bins, mine):
    core = lax.axis_index("range") & 1
    return (core if mine else 1 - core) * (bins // 2)


def sent_bins(bins):
    return bins // 2 + 2


def spectra_first_kernel(raw_ref, rep_ref, dft_ref, _, s_ref, local_ref, taps_ref, send_ref,
                         buf, sems):
    bins, _, chans, gates = s_ref.shape
    size = GROUP * bins
    copies = [
        pltpu.make_async_copy(
            raw_ref.at[:, j * size : (j + 1) * size, :],
            buf.at[:, j * size : (j + 1) * size, :],
            sems.at[j],
        )
        for j in range(chans // GROUP)
    ]
    for copy in copies:
        copy.start()
    correlation_matrix(rep_ref, taps_ref)
    for j, copy in enumerate(copies):
        copy.wait()
        rows = slice(j * size, (j + 1) * size)
        total = dot(buf[0, rows, :], taps_ref[0]) + dot(buf[1, rows, :], taps_ref[1])
        out = doppler_rows(total, dft_ref[...])
        s_ref[:, :, j * GROUP : (j + 1) * GROUP, :] = out.reshape(bins, 2, GROUP, gates)
        later = jnp.concatenate([buf[0, rows, gates:], buf[1, rows, gates:]], axis=1)
        near = jnp.concatenate([taps_ref[0, :gates, :], taps_ref[1, :gates, :]], axis=0)
        local_ref[rows, :] = dot(later, near)
    base = half_of_bins(bins, False)
    for k in range(send_ref.shape[0]):
        send_ref[k] = s_ref[lax.rem(base + k, bins)]


def spectra_last_kernel(local_ref, halo_ref, taps_ref, dft_ref, _, s_ref, send_ref):
    bins, _, chans, gates = s_ref.shape
    size = GROUP * bins
    far = jnp.concatenate([taps_ref[0, gates:, :], taps_ref[1, gates:, :]], axis=0)
    for j in range(chans // GROUP):
        rows = slice(j * size, (j + 1) * size)
        later = jnp.concatenate([halo_ref[0, rows, :], halo_ref[1, rows, :]], axis=1)
        out = doppler_rows(local_ref[rows, :] + dot(later, far), dft_ref[...])
        s_ref[:, :, j * GROUP : (j + 1) * GROUP, :] = out.reshape(bins, 2, GROUP, gates)
    base = half_of_bins(bins, False)
    for k in range(send_ref.shape[0]):
        send_ref[k] = s_ref[lax.rem(base + k, bins)]


def spectra_first(raw, replica, table, pulses, mark):
    _, rows, gates = raw.shape
    chans = rows // pulses
    taps = replica.shape[1]
    return pl.pallas_call(
        spectra_first_kernel,
        out_shape=[
            jax.ShapeDtypeStruct((pulses, 2, chans, BLOCK), BF16),
            jax.ShapeDtypeStruct((rows, 2 * BLOCK), F32),
            jax.ShapeDtypeStruct((2, 2 * taps, 2 * taps), BF16),
            jax.ShapeDtypeStruct((sent_bins(pulses), 2, chans, BLOCK), BF16),
        ],
        in_specs=[hbm_spec(), vmem_spec(), vmem_spec(), pl.BlockSpec(memory_space=pl.ANY)],
        out_specs=[vmem_spec()] * 4,
        scratch_shapes=[
            pltpu.VMEM(raw.shape, BF16),
            pltpu.SemaphoreType.DMA((chans // GROUP,)),
        ],
        compiler_params=params(),
        cost_estimate=SHORT,
    )(raw, replica, table, mark)


def spectra_last(local, halo, matrix, table, pulses, sums):
    chans = local.shape[0] // pulses
    return pl.pallas_call(
        spectra_last_kernel,
        out_shape=[
            jax.ShapeDtypeStruct((pulses, 2, chans, BLOCK), BF16),
            jax.ShapeDtypeStruct((sent_bins(pulses), 2, chans, BLOCK), BF16),
        ],
        in_specs=[vmem_spec()] * 4 + [pl.BlockSpec(memory_space=pl.ANY)],
        out_specs=[vmem_spec()] * 2,
        compiler_params=params(),
        cost_estimate=SHORT,
    )(local, halo, matrix, table, sums)


def cross_kernel(s_ref, *refs):
    before_ref = refs[0] if len(refs) == 2 else None
    out_ref = refs[-1]
    held, _, chans, gates = s_ref.shape
    count = out_ref.shape[0]
    base = half_of_bins(held, True) if held == 2 * count else 0
    lower = iota((chans, chans), 0) >= iota((chans, chans), 1)
    half = chans // 2

    def packed(block):
        swapped = pltpu.roll(block, chans, 1)
        mixed = jnp.where(lower, block[:, :chans], swapped[:, :chans])
        return jnp.concatenate([mixed[:half], mixed[half:]], axis=1)

    def write(e, block):
        value = jnp.concatenate([packed(block[:chans]), block[chans:]], axis=0)
        if before_ref is not None:
            value = value + before_ref[e]
        out_ref[e] = value

    @pl.loop(0, count // 2, unroll=2)
    def _(step):
        e = step * 2
        each = []
        for k in range(4):
            where = lax.rem(base + e + k, held)
            each.append((s_ref[where, 0], s_ref[where, 1]))
        left = jnp.concatenate(
            [jnp.concatenate([re, im], axis=1) for re, im in each], axis=0
        )
        right = jnp.concatenate(
            [
                jnp.concatenate(pieces, axis=1)
                for re, im in each[:2]
                for pieces in ((re, im), (-im, re))
            ],
            axis=0,
        )
        both = dot_nt(left, right)
        write(e, both[: 3 * chans, : 2 * chans])
        write(e + 1, both[chans:, 2 * chans :])


def cross(spectra, bins, before=None):
    chans = spectra.shape[2]
    data = [spectra] if before is None else [spectra, before]
    return pl.pallas_call(
        cross_kernel,
        out_shape=jax.ShapeDtypeStruct((bins // 2, 5 * chans // 2, 2 * chans), F32),
        in_specs=[vmem_spec()] * len(data),
        out_specs=vmem_spec(),
        compiler_params=params(),
        cost_estimate=SHORT,
    )(*data)


def partner(value, bit):
    count = lax.axis_size("range")
    return lax.ppermute(value, "range", [(i, i ^ bit) for i in range(count)])


def slot_of(core, x, y, z):
    return (4 * z + ((2 * y + (x ^ y)) ^ (3 * (z & 1)))) ^ (15 * core)


def parts_of(index):
    return index & 1, (index >> 1) & 1, (index >> 2) & 1, (index >> 3) & 3


def bin_of(index):
    core, x, y, z = parts_of(index)
    return core * 16 + slot_of(core, x, y, z)


def index_of(bin_id):
    core = bin_id >> 4
    path = (bin_id & 15) ^ (15 * core)
    z = path >> 2
    turned = (path & 3) ^ (3 * (z & 1))
    y = turned >> 1
    x = (turned & 1) ^ y
    return z * 8 + y * 4 + x * 2 + core


def first_kernel(keep_ref, a_ref, b_ref):
    core, x, y, z = parts_of(lax.axis_index("range"))
    half = keep_ref.shape[1] // 2
    for k in range(8):
        e = slot_of(core, 1 - x, k // 4, k % 4)
        a_ref[k] = keep_ref[e, :half]
        e = slot_of(core, k // 4, 1 - y, k % 4)
        b_ref[k] = keep_ref[e, half:]


def second_kernel(keep_ref, a1_ref, b1_ref, a_ref, b_ref):
    core, x, y, z = parts_of(lax.axis_index("range"))
    half = keep_ref.shape[1] // 2
    for k in range(4):
        e = slot_of(core, x, 1 - y, k)
        a_ref[k] = keep_ref[e, :half] + a1_ref[(1 - y) * 4 + k]
        e = slot_of(core, 1 - x, y, k)
        b_ref[k] = keep_ref[e, half:] + b1_ref[(1 - x) * 4 + k]


def line_sum(keep_ref, a1_ref, b1_ref, a2_ref, b2_ref, flip):
    core, x, y, z = parts_of(lax.axis_index("range"))
    z = z ^ flip
    half = keep_ref.shape[1] // 2
    e = slot_of(core, x, y, z)
    upper = keep_ref[e, :half] + a1_ref[y * 4 + z] + a2_ref[z]
    lower = keep_ref[e, half:] + b1_ref[x * 4 + z] + b2_ref[z]
    return upper, lower


def line_kernel(*refs):
    half = refs[0].shape[1] // 2
    for k, out_ref in enumerate(refs[5:]):
        upper, lower = line_sum(*refs[:5], k + 1)
        out_ref[:half] = upper
        out_ref[half:] = lower


def own_kernel(*refs):
    z1_ref, z2_ref, z3_ref, out_ref, packed_ref = refs[5:]
    half = refs[0].shape[1] // 2
    upper, lower = line_sum(*refs[:5], 0)
    upper = upper + z1_ref[:half] + (z2_ref[:half] + z3_ref[:half])
    out_ref[:half] = upper
    packed_ref[...] = upper[: packed_ref.shape[0]]
    out_ref[half:] = lower + z1_ref[half:] + (z2_ref[half:] + z3_ref[half:])


def summed(kernel, data, shapes):
    return pl.pallas_call(
        kernel,
        out_shape=[jax.ShapeDtypeStruct(shape, F32) for shape in shapes],
        in_specs=[vmem_spec()] * len(data),
        out_specs=[vmem_spec()] * len(shapes),
        compiler_params=params(),
    )(*data)


def bin_sums(keep):
    _, rows, wide = keep.shape
    half = rows // 2
    data = [keep]
    a, b = summed(first_kernel, data, [(8, half, wide)] * 2)
    data += [partner(a, 2), partner(b, 4)]
    a, b = summed(second_kernel, data, [(4, half, wide)] * 2)
    data += [partner(a, 4), partner(b, 2)]
    sends = summed(line_kernel, data, [(rows, wide)] * 3)
    data += [partner(value, (k + 1) * 8) for k, value in enumerate(sends)]
    own, packed = summed(own_kernel, data, [(rows, wide), (rows // 5, wide)])
    bit = 32
    while bit < lax.axis_size("range"):
        own = own + partner(own, bit)
        packed = packed + partner(packed, bit)
        bit *= 2
    return own, packed


def from_bin(value, offset):
    count = lax.axis_size("range")
    pairs = []
    for i in range(count):
        target = index_of((bin_of(i) - offset) % 32) | (i & ~31)
        pairs.append((i, target))
    return lax.ppermute(value, "range", pairs)


def turn(value):
    half = value.shape[1] // 2
    rolled = pltpu.roll(value, half, 1)
    return jnp.where(iota(value.shape, 1) < half, -rolled, rolled)


def embed(value):
    return jnp.concatenate([value, turn(value)], axis=0)


def mul(a, b):
    return jnp.dot(a, embed(b), precision=lax.Precision.HIGHEST, preferred_element_type=F32)


def mul_conj(a, b):
    half = a.shape[1] // 2
    stacked = jnp.concatenate([a, -turn(a)], axis=0)
    both = dot_nt(stacked, b, lax.Precision.HIGHEST)
    rows = a.shape[0]
    return jnp.concatenate([both[:rows], both[rows:]], axis=1)


def conj_mul(a, b):
    half = a.shape[1] // 2
    both = lax.dot_general(
        a, b, (((0,), (0,)), ((), ())),
        precision=lax.Precision.HIGHEST, preferred_element_type=F32,
    )
    return both[:half] - turn(both[half:])


def reciprocal(x):
    value = pl.reciprocal(x, approx=True)
    for _ in range(2):
        value = value * (2.0 - x * value)
    return value


def pivot_inverse(p):
    def times(x, y):
        return x[0] * y[0] - x[1] * y[1], x[0] * y[1] + x[1] * y[0]

    def conj(x):
        return x[0], -x[1]

    def plus(x, y):
        return x[0] + y[0], x[1] + y[1]

    def scaled(x, s):
        return x[0] * s, x[1] * s

    def square(x):
        return x[0] * x[0] + x[1] * x[1]

    def two(a, b, d):
        inv = reciprocal(a * d - square(b))
        return d * inv, scaled(b, -inv), a * inv

    a, d = p[0][0], p[1][1]
    b = p[0][1]
    ea, eb, ed = two(a, b, d)
    f = [[p[0][2], p[0][3]], [p[1][2], p[1][3]]]
    w = [
        [plus(scaled(f[0][j], ea), times(eb, f[1][j])) for j in range(2)],
        [plus(times(conj(eb), f[0][j]), scaled(f[1][j], ed)) for j in range(2)],
    ]

    def inner(i, j):
        return plus(times(conj(f[0][i]), w[0][j]), times(conj(f[1][i]), w[1][j]))

    ha = p[2][2] - inner(0, 0)[0]
    hd = p[3][3] - inner(1, 1)[0]
    cross = inner(0, 1)
    hb = (p[2][3][0] - cross[0], p[2][3][1] - cross[1])
    ga, gb, gd = two(ha, hb, hd)
    v = [
        [
            plus(scaled(w[i][0], ga), times(w[i][1], conj(gb))),
            plus(times(w[i][0], gb), scaled(w[i][1], gd)),
        ]
        for i in range(2)
    ]
    top = [
        [plus(times(v[i][0], conj(w[j][0])), times(v[i][1], conj(w[j][1]))) for j in range(2)]
        for i in range(2)
    ]
    zero = None
    out = [[None] * 4 for _ in range(4)]
    out[0][0] = (ea + top[0][0][0], zero)
    out[1][1] = (ed + top[1][1][0], zero)
    out[0][1] = plus(eb, top[0][1])
    out[2][2], out[3][3], out[2][3] = (ga, zero), (gd, zero), gb
    for i in range(2):
        for j in range(2):
            out[i][2 + j] = (-v[i][j][0], -v[i][j][1])
    for i in range(4):
        for j in range(i):
            out[i][j] = conj(out[j][i])
    return out


def invert(matrix):
    chans, width = matrix.shape
    sub = 8
    tiles = [matrix[t * sub : (t + 1) * sub, :] for t in range(chans // sub)]
    lane = iota((sub, width), 1)
    row = iota((sub, width), 0)
    first_half = lane < chans

    def spin(value):
        rolled = pltpu.roll(value, chans, 1)
        return jnp.where(first_half, -rolled, rolled)

    def column(value, k):
        return jnp.broadcast_to(value[:, k : k + 1], (sub, width))

    def combine(terms):
        while len(terms) > 1:
            terms = [
                terms[i] + terms[i + 1] if i + 1 < len(terms) else terms[i]
                for i in range(0, len(terms), 2)
            ]
        return terms[0]

    def rows_at(k):
        t, r = divmod(k, sub)
        return [jnp.broadcast_to(tiles[t][r + i : r + i + 1, :], (sub, width)) for i in range(4)]

    lines = rows_at(0)
    for k in range(0, chans, 4):
        t, r = divmod(k, sub)
        pivot = [[None] * 4 for _ in range(4)]
        for i in range(4):
            pivot[i][i] = column(lines[i], k + i)
            for j in range(i + 1, 4):
                pivot[i][j] = column(lines[i], k + j), column(lines[i], chans + k + j)
        low = jnp.bitwise_and(lane, chans - 1)
        cleared = (low >= k) & (low < k + 4)
        unit = [
            jnp.where(cleared, jnp.where(lane == k + i, 1.0, 0.0), lines[i]) for i in range(4)
        ]
        spun = [spin(u) for u in unit]
        p = pivot_inverse(pivot)
        fresh_lines, fresh_spun = [], []
        for i in range(4):
            terms, other = [], []
            for j in range(4):
                re, im = p[i][j]
                terms.append(re * unit[j])
                other.append(re * spun[j])
                if im is not None:
                    terms.append(im * spun[j])
                    other.append(-(im * unit[j]))
            fresh_lines.append(combine(terms))
            fresh_spun.append(combine(other))

        def updated(value):
            terms = []
            for i in range(4):
                terms.append(column(value, k + i) * fresh_lines[i])
                terms.append(column(value, chans + k + i) * fresh_spun[i])
            return jnp.where(cleared, 0.0, value) - combine(terms)

        if k + 4 < chans:
            lines = [updated(value) for value in rows_at(k + 4)]
        fresh = []
        for s, tile in enumerate(tiles):
            value = updated(tile)
            if s == t:
                for i in range(4):
                    value = jnp.where(row == r + i, fresh_lines[i], value)
            fresh.append(value)
        tiles = fresh
    return jnp.concatenate(tiles, axis=0)


def unpacked(ref, scale):
    half, wide = ref.shape[0], ref.shape[1]
    piece = ref[...] * scale
    swapped = pltpu.roll(piece, wide // 2, 1)
    return jnp.concatenate([piece, swapped], axis=0)[:, : wide // 2]


def hermitian(mixed, across):
    i, j = iota(mixed.shape, 0), iota(mixed.shape, 1)
    real_part = jnp.where(i >= j, mixed, across)
    imag_part = jnp.where(i < j, mixed, jnp.where(i > j, -across, 0.0))
    return jnp.concatenate([real_part, imag_part], axis=1)


def middle_kernel(total, packed_ref, steer_ref, inv_ref, t_ref):
    chans = inv_ref.shape[0]
    mixed = unpacked(packed_ref, F32(1.0 / total))
    twice = jnp.concatenate([mixed, mixed], axis=1)
    across = jnp.concatenate([twice, twice], axis=0).T[:chans, :chans]
    inverse = invert(hermitian(mixed, across))
    inv_ref[...] = inverse
    t_ref[...] = mul(steer_ref[...], inverse)


def outer_kernel(total, own_ref, left_ref, right_ref, steer_ref, inv_ref, t_ref, out_ref,
                 work, keep):
    chans = inv_ref.shape[0]
    scale = F32(1.0 / total)
    half = chans // 2
    m_left = unpacked(left_ref.at[:half], scale)
    m_right = unpacked(right_ref, scale)
    ml = left_ref[half : half + chans] * scale
    rl = left_ref[half + chans :] * scale
    rm = own_ref[half : half + chans] * scale
    pair = jnp.concatenate([m_left, m_right], axis=1)
    square = jnp.concatenate([pair, pair], axis=0).T
    inv_mid = inv_ref[...]
    t = t_ref[...]
    h = mul(inv_mid, ml)
    g = mul(rm, inv_mid)
    work[...] = hermitian(m_left, square[:chans, :chans]) - conj_mul(ml, h)
    s_rl = rl - mul(rm, h)
    s_rr = hermitian(m_right, square[chans:, :chans]) - mul_conj(g, rm)
    rhs_left = -mul(t, ml)
    rhs_right = -mul_conj(t, rm)
    keep[0] = s_rl
    keep[1] = s_rr
    keep[2] = h
    keep[3] = g
    keep[4, 0:BEAMS] = rhs_left
    keep[4, BEAMS : 2 * BEAMS] = rhs_right

    @pl.loop(0, 2)
    def _(stage):
        work[...] = invert(work[...])

        @pl.when(stage == 0)
        def _():
            inverse = work[...]
            s_rl = keep[0]
            both = mul(jnp.concatenate([s_rl, keep[4, 0:BEAMS]], axis=0), inverse)
            k, y_left = both[:chans], both[chans:]
            work[...] = keep[1] - mul_conj(k, s_rl)
            keep[0] = k
            keep[4, BEAMS : 2 * BEAMS] = keep[4, BEAMS : 2 * BEAMS] - mul_conj(y_left, s_rl)
            keep[4, 0:BEAMS] = y_left
            keep[4, 2 * BEAMS : 3 * BEAMS] = t_ref[...] - mul_conj(y_left, keep[2])
            keep[3] = keep[3] - mul_conj(k, keep[2])

        @pl.when(stage == 1)
        def _():
            y_right = mul(keep[4, BEAMS : 2 * BEAMS], work[...])
            y_left = keep[4, 0:BEAMS] - mul(y_right, keep[0])
            y_mid = keep[4, 2 * BEAMS : 3 * BEAMS] - mul(y_right, keep[3])
            quad = jnp.sum(steer_ref[...] * y_mid, axis=1, keepdims=True)
            y = jnp.concatenate([y_left, y_mid, y_right], axis=1) / jnp.sqrt(quad)
            real_lane = lax.rem(iota(y.shape, 1), 2 * chans) < chans
            mine = jnp.where(real_lane, y, -y).astype(BF16)
            for c in range(out_ref.shape[0]):
                out_ref[c] = mine


def steering(chans):
    index = np.arange(chans)
    sines = -0.8 + 1.6 * np.arange(BEAMS) / (BEAMS - 1)
    angle = math.pi * sines[:, None] * index[None, :]
    return np.concatenate([np.cos(angle), -np.sin(angle)], axis=1).astype(np.float32)


def solve_middle(packed, steer, total):
    half, wide = packed.shape
    return pl.pallas_call(
        functools.partial(middle_kernel, total),
        out_shape=[
            jax.ShapeDtypeStruct((2 * half, wide), F32),
            jax.ShapeDtypeStruct((BEAMS, wide), F32),
        ],
        in_specs=[vmem_spec()] * 2,
        out_specs=[vmem_spec()] * 2,
        compiler_params=params(),
    )(packed, steer)


def solve_outer(own, left, right, steer, inverse, t, total, copies):
    chans, wide = inverse.shape
    return pl.pallas_call(
        functools.partial(outer_kernel, total),
        out_shape=jax.ShapeDtypeStruct((copies, BEAMS, 3 * wide), BF16),
        in_specs=[vmem_spec()] * 6,
        out_specs=vmem_spec(),
        scratch_shapes=[pltpu.VMEM((chans, wide), F32), pltpu.VMEM((5, chans, wide), F32)],
        compiler_params=params(),
    )(own, left, right, steer, inverse, t)


def beam_kernel(bin_ref, block_ref, beam_ref, owner_ref, s0_ref, s1_ref, w_ref, out_ref,
                both_ref, rows_ref, seen_ref):
    bins, wide, gates = s0_ref.shape
    devices = seen_ref.shape[0]
    count = bin_ref.shape[0]
    rows_ref[...] = jnp.zeros_like(rows_ref)

    @pl.loop(0, devices)
    def _(i):
        seen_ref[i] = 0

    w = w_ref[...].astype(F32).reshape(bins * BEAMS, 3 * wide)
    for k in range(3):
        lanes = slice(k * wide, (k + 1) * wide)
        part = w[:, lanes]
        both_ref[:, 0:BEAMS, lanes] = part.reshape(bins, BEAMS, wide)
        both_ref[:, BEAMS:, lanes] = turn(part).reshape(bins, BEAMS, wide)

    def detection(j, carry):
        bin_id = bin_ref[j]
        beam_id = beam_ref[j]
        owner = owner_ref[j]
        rank = seen_ref[owner]
        seen_ref[owner] = rank + 1
        left = both_ref[index_of(bin_id)].astype(BF16)
        bands = [lax.rem(bin_id + bins - 1 + k, bins) for k in range(3)]
        first = block_ref[j] == 0
        window = jnp.concatenate(
            [jnp.where(first, s0_ref[b], s1_ref[b]) for b in bands], axis=0
        )
        both = dot(left, window)
        line = jnp.concatenate([both[:BEAMS], both[BEAMS:]], axis=1)
        chosen = jnp.where(iota(line.shape, 0) == beam_id, line, 0.0)
        row = owner * CAP + rank
        rows_ref[pl.ds(row, 1), :] = jnp.sum(chosen, axis=0, keepdims=True)
        return carry

    lax.fori_loop(0, count, detection, 0, unroll=32)
    out_ref[...] = rows_ref[...].astype(BF16)


def beam_rows(det_bin, det_block, det_beam, owners, s0, s1, weight, devices):
    bins, wide, gates = s0.shape
    return pl.pallas_call(
        beam_kernel,
        out_shape=jax.ShapeDtypeStruct((devices * CAP, 2 * gates), BF16),
        in_specs=[smem_spec()] * 4 + [vmem_spec()] * 3,
        out_specs=vmem_spec(),
        scratch_shapes=[
            pltpu.VMEM((bins, 2 * BEAMS, 3 * wide), F32),
            pltpu.VMEM((devices * CAP, 2 * gates), F32),
            pltpu.SMEM((devices,), jnp.int32),
        ],
        compiler_params=params(),
    )(det_bin, det_block, det_beam, owners, s0, s1, weight)


def on_device(raw, replica, det_bin, det_block, det_beam, det_owner):
    devices = lax.axis_size("range")
    _, chans, pulses, gates = raw.shape
    bins = pulses
    flat = raw.reshape(2, chans * pulses, gates)
    before = [(source, source - 1) for source in range(1, devices)]
    gates_before, mark = first_gates(flat)
    halo = lax.ppermute(gates_before, "range", before)
    table = doppler_matrix(pulses, 8)
    s0, local, matrix, send0 = spectra_first(flat, replica, table, pulses, mark)
    beside0 = partner(send0, 1)
    sums = cross(s0, bins)
    sums = cross(beside0, bins, sums)
    s1, send1 = spectra_last(local, halo, matrix, table, pulses, sums)
    beside1 = partner(send1, 1)
    sums = cross(s1, bins, sums)
    sums = cross(beside1, bins, sums)
    own, packed = bin_sums(sums)
    total = gates * devices
    steer = steering(chans)
    left = from_bin(own, -1)
    right = from_bin(packed, 1)
    inverse, t = solve_middle(packed, steer, total)
    mine = solve_outer(own, left, right, steer, inverse, t, total, bins)
    groups = [list(range(first, first + bins)) for first in range(0, devices, bins)]
    weight = lax.all_to_all(
        mine, "range", split_axis=0, concat_axis=0, tiled=True,
        axis_index_groups=groups if len(groups) > 1 else None,
    )
    outgoing = beam_rows(
        det_bin, det_block, det_beam, det_owner[:, 0],
        s0.reshape(bins, 2 * chans, BLOCK), s1.reshape(bins, 2 * chans, BLOCK), weight, devices,
    )
    incoming = lax.all_to_all(
        outgoing.reshape(devices, CAP, 2 * BLOCK), "range", split_axis=0, concat_axis=0, tiled=True
    )
    return incoming.astype(F32).reshape(devices * CAP, 2 * BLOCK)


def solution(mesh):
    in_specs = (
        P(None, None, None, "range"),
        P(),
        P("range"),
        P("range"),
        P("range"),
        P("range", None),
    )
    out_specs = P("range", None)
    return jax.shard_map(
        on_device, mesh=mesh, in_specs=in_specs, out_specs=out_specs, check_vma=False
    )
```

```python
import functools
import math

import jax
import jax.numpy as jnp
import ml_dtypes
import numpy as np
from jax import lax
from jax.experimental import pallas as pl
from jax.experimental.pallas import tpu as pltpu
from jax.sharding import PartitionSpec as P

BLOCK = 128
BEAMS = 8
CAP = 2

F32 = jnp.float32
BF16 = jnp.bfloat16
VMEM = pltpu.VMEM
MIB = 1024 * 1024
NT = (((1,), (1,)), ((), ()))


def vmem_spec():
    return pl.BlockSpec(memory_space=VMEM)


def smem_spec():
    return pl.BlockSpec(memory_space=pltpu.SMEM)


def hbm_spec():
    return pl.BlockSpec(memory_space=pltpu.HBM)


SHORT = pl.CostEstimate(flops=1, bytes_accessed=1, transcendentals=0)


def params(mib=16):
    return pltpu.CompilerParams(vmem_limit_bytes=int(mib * MIB))


def dot(a, b):
    return jnp.dot(a, b, preferred_element_type=F32)


def dot_nt(a, b, precision=None):
    return lax.dot_general(a, b, NT, precision=precision, preferred_element_type=F32)


def iota(shape, axis):
    return lax.broadcasted_iota(jnp.int32, shape, axis)


def halo_kernel(raw_ref, out_ref, mark_ref, buf, in_sems, out_sems):
    mark_ref[...] = jnp.zeros_like(mark_ref)
    count = in_sems.shape[0]
    size = buf.shape[1] // count
    inward, outward = [], []
    for j in range(count):
        rows = slice(j * size, (j + 1) * size)
        inward.append(
            pltpu.make_async_copy(
                raw_ref.at[:, rows, :BLOCK], buf.at[:, rows, :], in_sems.at[j]
            )
        )
        outward.append(
            pltpu.make_async_copy(buf.at[:, rows, :], out_ref.at[:, rows, :], out_sems.at[j])
        )
    for copy in inward:
        copy.start()
    for j in range(count):
        inward[j].wait()
        outward[j].start()
    for copy in outward:
        copy.wait()


def first_gates(raw):
    shape = raw.shape[:2] + (BLOCK,)
    return pl.pallas_call(
        halo_kernel,
        out_shape=[
            jax.ShapeDtypeStruct(shape, BF16),
            jax.ShapeDtypeStruct((8, 128), F32),
        ],
        in_specs=[hbm_spec()],
        out_specs=[hbm_spec(), vmem_spec()],
        scratch_shapes=[
            pltpu.VMEM(shape, BF16),
            pltpu.SemaphoreType.DMA((8,)),
            pltpu.SemaphoreType.DMA((8,)),
        ],
        compiler_params=params(63),
    )(raw)


def correlation_matrix(rep_ref, out_ref):
    taps = rep_ref.shape[1]
    base = rep_ref[...].astype(F32)
    row = iota((taps, 2 * taps), 0)
    parts = []
    for i in range(2):
        line = jnp.concatenate([base[i : i + 1], jnp.zeros((1, taps), F32)], axis=1)
        skew = jnp.broadcast_to(line, (taps, 2 * taps))
        bit = 1
        while bit < taps:
            skew = jnp.where((row & bit) != 0, pltpu.roll(skew, bit, 1), skew)
            bit *= 2
        parts.append(skew.T)
    real_part, imag_part = parts
    out_ref[0] = jnp.concatenate([real_part, -imag_part], axis=1).astype(BF16)
    out_ref[1] = jnp.concatenate([imag_part, real_part], axis=1).astype(BF16)


def doppler_matrix(pulses, group):
    index = np.arange(pulses)
    angle = 2.0 * math.pi / pulses * (index[:, None] * index[None, :] % pulses)
    cosine = np.cos(angle) * pulses**-0.5
    sine = np.sin(angle) * pulses**-0.5
    table = np.stack([np.stack([cosine, -sine], 1), np.stack([sine, cosine], 1)], 0)
    full = np.einsum("ipod,ce->dociep", table, np.eye(group))
    shape = (pulses * 2 * group, 2 * group * pulses)
    return full.reshape(shape).astype(ml_dtypes.bfloat16)


def doppler_rows(total, dft):
    compressed = total.astype(BF16)
    rows, wide = compressed.shape
    half, gates = rows // 2, wide // 2
    stacked = jnp.concatenate(
        [
            jnp.concatenate([compressed[:half, :gates], compressed[half:, :gates]], axis=1),
            jnp.concatenate([compressed[:half, gates:], compressed[half:, gates:]], axis=1),
        ],
        axis=0,
    )
    both = dot(dft, stacked)
    lines = both.shape[0] // 8
    joined = jnp.concatenate(
        [both[:, :gates].reshape(lines, 8, gates), both[:, gates:].reshape(lines, 8, gates)],
        axis=1,
    )
    return joined.astype(BF16)


GROUP = 16


def half_of_bins(bins, mine):
    core = lax.axis_index("range") & 1
    return (core if mine else 1 - core) * (bins // 2)


def sent_bins(bins):
    return bins // 2 + 2


def spectra_first_kernel(raw_ref, rep_ref, dft_ref, _, s_ref, local_ref, taps_ref, send_ref,
                         buf, sems):
    bins, _, chans, gates = s_ref.shape
    size = GROUP * bins
    copies = [
        pltpu.make_async_copy(
            raw_ref.at[:, j * size : (j + 1) * size, :],
            buf.at[:, j * size : (j + 1) * size, :],
            sems.at[j],
        )
        for j in range(chans // GROUP)
    ]
    for copy in copies:
        copy.start()
    correlation_matrix(rep_ref, taps_ref)
    for j, copy in enumerate(copies):
        copy.wait()
        rows = slice(j * size, (j + 1) * size)
        total = dot(buf[0, rows, :], taps_ref[0]) + dot(buf[1, rows, :], taps_ref[1])
        out = doppler_rows(total, dft_ref[...])
        s_ref[:, :, j * GROUP : (j + 1) * GROUP, :] = out.reshape(bins, 2, GROUP, gates)
        later = jnp.concatenate([buf[0, rows, gates:], buf[1, rows, gates:]], axis=1)
        near = jnp.concatenate([taps_ref[0, :gates, :], taps_ref[1, :gates, :]], axis=0)
        local_ref[rows, :] = dot(later, near)
    base = half_of_bins(bins, False)
    for k in range(send_ref.shape[0]):
        send_ref[k] = s_ref[lax.rem(base + k, bins)]


def spectra_last_kernel(local_ref, halo_ref, taps_ref, dft_ref, _, s_ref, send_ref):
    bins, _, chans, gates = s_ref.shape
    size = GROUP * bins
    far = jnp.concatenate([taps_ref[0, gates:, :], taps_ref[1, gates:, :]], axis=0)
    for j in range(chans // GROUP):
        rows = slice(j * size, (j + 1) * size)
        later = jnp.concatenate([halo_ref[0, rows, :], halo_ref[1, rows, :]], axis=1)
        out = doppler_rows(local_ref[rows, :] + dot(later, far), dft_ref[...])
        s_ref[:, :, j * GROUP : (j + 1) * GROUP, :] = out.reshape(bins, 2, GROUP, gates)
    base = half_of_bins(bins, False)
    for k in range(send_ref.shape[0]):
        send_ref[k] = s_ref[lax.rem(base + k, bins)]


def spectra_first(raw, replica, table, pulses, mark):
    _, rows, gates = raw.shape
    chans = rows // pulses
    taps = replica.shape[1]
    return pl.pallas_call(
        spectra_first_kernel,
        out_shape=[
            jax.ShapeDtypeStruct((pulses, 2, chans, BLOCK), BF16),
            jax.ShapeDtypeStruct((rows, 2 * BLOCK), F32),
            jax.ShapeDtypeStruct((2, 2 * taps, 2 * taps), BF16),
            jax.ShapeDtypeStruct((sent_bins(pulses), 2, chans, BLOCK), BF16),
        ],
        in_specs=[hbm_spec(), vmem_spec(), vmem_spec(), pl.BlockSpec(memory_space=pl.ANY)],
        out_specs=[vmem_spec()] * 4,
        scratch_shapes=[
            pltpu.VMEM(raw.shape, BF16),
            pltpu.SemaphoreType.DMA((chans // GROUP,)),
        ],
        compiler_params=params(),
        cost_estimate=SHORT,
    )(raw, replica, table, mark)


def spectra_last(local, halo, matrix, table, pulses, sums):
    chans = local.shape[0] // pulses
    return pl.pallas_call(
        spectra_last_kernel,
        out_shape=[
            jax.ShapeDtypeStruct((pulses, 2, chans, BLOCK), BF16),
            jax.ShapeDtypeStruct((sent_bins(pulses), 2, chans, BLOCK), BF16),
        ],
        in_specs=[vmem_spec()] * 4 + [pl.BlockSpec(memory_space=pl.ANY)],
        out_specs=[vmem_spec()] * 2,
        compiler_params=params(),
        cost_estimate=SHORT,
    )(local, halo, matrix, table, sums)


def cross_kernel(s_ref, *refs):
    before_ref = refs[0] if len(refs) == 2 else None
    out_ref = refs[-1]
    held, _, chans, gates = s_ref.shape
    count = out_ref.shape[0]
    base = half_of_bins(held, True) if held == 2 * count else 0
    lower = iota((chans, chans), 0) >= iota((chans, chans), 1)
    half = chans // 2

    def packed(block):
        swapped = pltpu.roll(block, chans, 1)
        mixed = jnp.where(lower, block[:, :chans], swapped[:, :chans])
        return jnp.concatenate([mixed[:half], mixed[half:]], axis=1)

    def write(e, block):
        value = jnp.concatenate([packed(block[:chans]), block[chans:]], axis=0)
        if before_ref is not None:
            value = value + before_ref[e]
        out_ref[e] = value

    @pl.loop(0, count // 2, unroll=2)
    def _(step):
        e = step * 2
        each = []
        for k in range(4):
            where = lax.rem(base + e + k, held)
            each.append((s_ref[where, 0], s_ref[where, 1]))
        left = jnp.concatenate(
            [jnp.concatenate([re, im], axis=1) for re, im in each], axis=0
        )
        right = jnp.concatenate(
            [
                jnp.concatenate(pieces, axis=1)
                for re, im in each[:2]
                for pieces in ((re, im), (-im, re))
            ],
            axis=0,
        )
        both = dot_nt(left, right)
        write(e, both[: 3 * chans, : 2 * chans])
        write(e + 1, both[chans:, 2 * chans :])


def cross(spectra, bins, before=None):
    chans = spectra.shape[2]
    data = [spectra] if before is None else [spectra, before]
    return pl.pallas_call(
        cross_kernel,
        out_shape=jax.ShapeDtypeStruct((bins // 2, 5 * chans // 2, 2 * chans), F32),
        in_specs=[vmem_spec()] * len(data),
        out_specs=vmem_spec(),
        compiler_params=params(),
        cost_estimate=SHORT,
    )(*data)


U_BITS, V_BITS = (2, 4), (4, 2)


def partner(value, bits):
    count = lax.axis_size("range")
    return lax.ppermute(value, "range", [(i, i ^ bits[i & 1]) for i in range(count)])


def slot_of(core, x, y, z):
    return (4 * z + ((2 * y + (x ^ y)) ^ (3 * (z & 1)))) ^ (15 * core)


def parts_of(index):
    return index & 1, (index >> 1) & 1, (index >> 2) & 1, (index >> 3) & 3


def bin_of(index):
    core, x, y, z = parts_of(index)
    return core * 16 + slot_of(core, x, y, z)


def index_of(bin_id):
    core = bin_id >> 4
    path = (bin_id & 15) ^ (15 * core)
    z = path >> 2
    turned = (path & 3) ^ (3 * (z & 1))
    y = turned >> 1
    x = (turned & 1) ^ y
    return z * 8 + y * 4 + x * 2 + core


def uv_parts():
    core, x, y, z = parts_of(lax.axis_index("range"))
    return core, jnp.where(core == 0, x, y), jnp.where(core == 0, y, x), z


def uv_slot(core, u, v, z):
    return slot_of(core, jnp.where(core == 0, u, v), jnp.where(core == 0, v, u), z)


def first_kernel(keep_ref, a_ref, b_ref):
    core, u, v, z = uv_parts()
    half = keep_ref.shape[1] // 2
    for k in range(8):
        a_ref[k] = keep_ref[uv_slot(core, 1 - u, k // 4, k % 4), :half]
        b_ref[k] = keep_ref[uv_slot(core, k // 4, 1 - v, k % 4), half:]


def second_kernel(keep_ref, a1_ref, b1_ref, a_ref, b_ref):
    core, u, v, z = uv_parts()
    half = keep_ref.shape[1] // 2
    for k in range(4):
        e = uv_slot(core, u, 1 - v, k)
        a_ref[k] = keep_ref[e, :half] + a1_ref[(1 - v) * 4 + k]
        e = uv_slot(core, 1 - u, v, k)
        b_ref[k] = keep_ref[e, half:] + b1_ref[(1 - u) * 4 + k]


def line_sum(keep_ref, a1_ref, b1_ref, a2_ref, b2_ref, flip):
    core, u, v, z = uv_parts()
    z = z ^ flip
    half = keep_ref.shape[1] // 2
    e = uv_slot(core, u, v, z)
    upper = keep_ref[e, :half] + a1_ref[v * 4 + z] + a2_ref[z]
    lower = keep_ref[e, half:] + b1_ref[u * 4 + z] + b2_ref[z]
    return upper, lower


FLIPS = (2, 3, 1)


def line_kernel(*refs):
    half = refs[0].shape[1] // 2
    for flip, out_ref in zip(FLIPS, refs[5:]):
        upper, lower = line_sum(*refs[:5], flip)
        out_ref[:half] = upper
        out_ref[half:] = lower


def own_kernel(*refs):
    z1_ref, z2_ref, z3_ref, out_ref, packed_ref = refs[5:]
    half = refs[0].shape[1] // 2
    upper, lower = line_sum(*refs[:5], 0)
    upper = upper + z1_ref[:half] + (z2_ref[:half] + z3_ref[:half])
    out_ref[:half] = upper
    packed_ref[...] = upper[: packed_ref.shape[0]]
    out_ref[half:] = lower + z1_ref[half:] + (z2_ref[half:] + z3_ref[half:])


def summed(kernel, data, shapes):
    return pl.pallas_call(
        kernel,
        out_shape=[jax.ShapeDtypeStruct(shape, F32) for shape in shapes],
        in_specs=[vmem_spec()] * len(data),
        out_specs=[vmem_spec()] * len(shapes),
        compiler_params=params(),
    )(*data)


def bin_sums(keep):
    _, rows, wide = keep.shape
    half = rows // 2
    data = [keep]
    a, b = summed(first_kernel, data, [(8, half, wide)] * 2)
    data += [partner(a, U_BITS), partner(b, V_BITS)]
    a, b = summed(second_kernel, data, [(4, half, wide)] * 2)
    data += [partner(a, V_BITS), partner(b, U_BITS)]
    sends = summed(line_kernel, data, [(rows, wide)] * 3)
    data += [partner(value, (8 * flip, 8 * flip)) for flip, value in zip(FLIPS, sends)]
    own, packed = summed(own_kernel, data, [(rows, wide), (rows // 5, wide)])
    bit = 32
    while bit < lax.axis_size("range"):
        own = own + partner(own, (bit, bit))
        packed = packed + partner(packed, (bit, bit))
        bit *= 2
    return own, packed


def from_bin(value, offset):
    count = lax.axis_size("range")
    pairs = []
    for i in range(count):
        target = index_of((bin_of(i) - offset) % 32) | (i & ~31)
        pairs.append((i, target))
    return lax.ppermute(value, "range", pairs)


def turn(value):
    half = value.shape[1] // 2
    rolled = pltpu.roll(value, half, 1)
    return jnp.where(iota(value.shape, 1) < half, -rolled, rolled)


def embed(value):
    return jnp.concatenate([value, turn(value)], axis=0)


def mul(a, b):
    return jnp.dot(a, embed(b), precision=lax.Precision.HIGHEST, preferred_element_type=F32)


def mul_conj(a, b):
    half = a.shape[1] // 2
    stacked = jnp.concatenate([a, -turn(a)], axis=0)
    both = dot_nt(stacked, b, lax.Precision.HIGHEST)
    rows = a.shape[0]
    return jnp.concatenate([both[:rows], both[rows:]], axis=1)


def conj_mul(a, b):
    half = a.shape[1] // 2
    both = lax.dot_general(
        a, b, (((0,), (0,)), ((), ())),
        precision=lax.Precision.HIGHEST, preferred_element_type=F32,
    )
    return both[:half] - turn(both[half:])


def reciprocal(x):
    value = pl.reciprocal(x, approx=True)
    for _ in range(2):
        value = value * (2.0 - x * value)
    return value


def pivot_inverse(p):
    def times(x, y):
        return x[0] * y[0] - x[1] * y[1], x[0] * y[1] + x[1] * y[0]

    def conj(x):
        return x[0], -x[1]

    def plus(x, y):
        return x[0] + y[0], x[1] + y[1]

    def scaled(x, s):
        return x[0] * s, x[1] * s

    def square(x):
        return x[0] * x[0] + x[1] * x[1]

    def two(a, b, d):
        inv = reciprocal(a * d - square(b))
        return d * inv, scaled(b, -inv), a * inv

    a, d = p[0][0], p[1][1]
    b = p[0][1]
    ea, eb, ed = two(a, b, d)
    f = [[p[0][2], p[0][3]], [p[1][2], p[1][3]]]
    w = [
        [plus(scaled(f[0][j], ea), times(eb, f[1][j])) for j in range(2)],
        [plus(times(conj(eb), f[0][j]), scaled(f[1][j], ed)) for j in range(2)],
    ]

    def inner(i, j):
        return plus(times(conj(f[0][i]), w[0][j]), times(conj(f[1][i]), w[1][j]))

    ha = p[2][2] - inner(0, 0)[0]
    hd = p[3][3] - inner(1, 1)[0]
    cross = inner(0, 1)
    hb = (p[2][3][0] - cross[0], p[2][3][1] - cross[1])
    ga, gb, gd = two(ha, hb, hd)
    v = [
        [
            plus(scaled(w[i][0], ga), times(w[i][1], conj(gb))),
            plus(times(w[i][0], gb), scaled(w[i][1], gd)),
        ]
        for i in range(2)
    ]
    top = [
        [plus(times(v[i][0], conj(w[j][0])), times(v[i][1], conj(w[j][1]))) for j in range(2)]
        for i in range(2)
    ]
    zero = None
    out = [[None] * 4 for _ in range(4)]
    out[0][0] = (ea + top[0][0][0], zero)
    out[1][1] = (ed + top[1][1][0], zero)
    out[0][1] = plus(eb, top[0][1])
    out[2][2], out[3][3], out[2][3] = (ga, zero), (gd, zero), gb
    for i in range(2):
        for j in range(2):
            out[i][2 + j] = (-v[i][j][0], -v[i][j][1])
    for i in range(4):
        for j in range(i):
            out[i][j] = conj(out[j][i])
    return out


def invert(matrix):
    chans, width = matrix.shape
    sub = 8
    tiles = [matrix[t * sub : (t + 1) * sub, :] for t in range(chans // sub)]
    lane = iota((sub, width), 1)
    row = iota((sub, width), 0)
    first_half = lane < chans

    def spin(value):
        rolled = pltpu.roll(value, chans, 1)
        return jnp.where(first_half, -rolled, rolled)

    def column(value, k):
        return jnp.broadcast_to(value[:, k : k + 1], (sub, width))

    def combine(terms):
        while len(terms) > 1:
            terms = [
                terms[i] + terms[i + 1] if i + 1 < len(terms) else terms[i]
                for i in range(0, len(terms), 2)
            ]
        return terms[0]

    for k in range(0, chans, 4):
        t, r = divmod(k, sub)
        lines = [jnp.broadcast_to(tiles[t][r + i : r + i + 1, :], (sub, width)) for i in range(4)]
        pivot = [[None] * 4 for _ in range(4)]
        for i in range(4):
            pivot[i][i] = column(lines[i], k + i)
            for j in range(i + 1, 4):
                pivot[i][j] = column(lines[i], k + j), column(lines[i], chans + k + j)
        low = jnp.bitwise_and(lane, chans - 1)
        cleared = (low >= k) & (low < k + 4)
        unit = [
            jnp.where(cleared, jnp.where(lane == k + i, 1.0, 0.0), lines[i]) for i in range(4)
        ]
        spun = [spin(u) for u in unit]
        p = pivot_inverse(pivot)
        fresh_lines, fresh_spun = [], []
        for i in range(4):
            terms, other = [], []
            for j in range(4):
                re, im = p[i][j]
                terms.append(re * unit[j])
                other.append(re * spun[j])
                if im is not None:
                    terms.append(im * spun[j])
                    other.append(-(im * unit[j]))
            fresh_lines.append(combine(terms))
            fresh_spun.append(combine(other))
        fresh = []
        for s, tile in enumerate(tiles):
            terms = []
            for i in range(4):
                terms.append(column(tile, k + i) * fresh_lines[i])
                terms.append(column(tile, chans + k + i) * fresh_spun[i])
            value = jnp.where(cleared, 0.0, tile) - combine(terms)
            if s == t:
                for i in range(4):
                    value = jnp.where(row == r + i, fresh_lines[i], value)
            fresh.append(value)
        tiles = fresh
    return jnp.concatenate(tiles, axis=0)


def unpacked(ref, scale):
    half, wide = ref.shape[0], ref.shape[1]
    piece = ref[...] * scale
    swapped = pltpu.roll(piece, wide // 2, 1)
    return jnp.concatenate([piece, swapped], axis=0)[:, : wide // 2]


def hermitian(mixed, across):
    i, j = iota(mixed.shape, 0), iota(mixed.shape, 1)
    real_part = jnp.where(i >= j, mixed, across)
    imag_part = jnp.where(i < j, mixed, jnp.where(i > j, -across, 0.0))
    return jnp.concatenate([real_part, imag_part], axis=1)


def middle_kernel(total, packed_ref, steer_ref, inv_ref, t_ref):
    chans = inv_ref.shape[0]
    mixed = unpacked(packed_ref, F32(1.0 / total))
    twice = jnp.concatenate([mixed, mixed], axis=1)
    across = jnp.concatenate([twice, twice], axis=0).T[:chans, :chans]
    inverse = invert(hermitian(mixed, across))
    inv_ref[...] = inverse
    t_ref[...] = mul(steer_ref[...], inverse)


def outer_kernel(total, own_ref, left_ref, right_ref, steer_ref, inv_ref, t_ref, out_ref,
                 work, keep):
    chans = inv_ref.shape[0]
    scale = F32(1.0 / total)
    half = chans // 2
    m_left = unpacked(left_ref.at[:half], scale)
    m_right = unpacked(right_ref, scale)
    ml = left_ref[half : half + chans] * scale
    rl = left_ref[half + chans :] * scale
    rm = own_ref[half : half + chans] * scale
    pair = jnp.concatenate([m_left, m_right], axis=1)
    square = jnp.concatenate([pair, pair], axis=0).T
    inv_mid = inv_ref[...]
    t = t_ref[...]
    h = mul(inv_mid, ml)
    g = mul(rm, inv_mid)
    work[...] = hermitian(m_left, square[:chans, :chans]) - conj_mul(ml, h)
    s_rl = rl - mul(rm, h)
    s_rr = hermitian(m_right, square[chans:, :chans]) - mul_conj(g, rm)
    rhs_left = -mul(t, ml)
    rhs_right = -mul_conj(t, rm)
    keep[0] = s_rl
    keep[1] = s_rr
    keep[2] = h
    keep[3] = g
    keep[4, 0:BEAMS] = rhs_left
    keep[4, BEAMS : 2 * BEAMS] = rhs_right

    @pl.loop(0, 2)
    def _(stage):
        work[...] = invert(work[...])

        @pl.when(stage == 0)
        def _():
            inverse = work[...]
            s_rl = keep[0]
            both = mul(jnp.concatenate([s_rl, keep[4, 0:BEAMS]], axis=0), inverse)
            k, y_left = both[:chans], both[chans:]
            work[...] = keep[1] - mul_conj(k, s_rl)
            keep[0] = k
            keep[4, BEAMS : 2 * BEAMS] = keep[4, BEAMS : 2 * BEAMS] - mul_conj(y_left, s_rl)
            keep[4, 0:BEAMS] = y_left
            keep[4, 2 * BEAMS : 3 * BEAMS] = t_ref[...] - mul_conj(y_left, keep[2])
            keep[3] = keep[3] - mul_conj(k, keep[2])

        @pl.when(stage == 1)
        def _():
            y_right = mul(keep[4, BEAMS : 2 * BEAMS], work[...])
            y_left = keep[4, 0:BEAMS] - mul(y_right, keep[0])
            y_mid = keep[4, 2 * BEAMS : 3 * BEAMS] - mul(y_right, keep[3])
            quad = jnp.sum(steer_ref[...] * y_mid, axis=1, keepdims=True)
            y = jnp.concatenate([y_left, y_mid, y_right], axis=1) / jnp.sqrt(quad)
            real_lane = lax.rem(iota(y.shape, 1), 2 * chans) < chans
            mine = jnp.where(real_lane, y, -y).astype(BF16)
            for c in range(out_ref.shape[0]):
                out_ref[c] = mine


def steering(chans):
    index = np.arange(chans)
    sines = -0.8 + 1.6 * np.arange(BEAMS) / (BEAMS - 1)
    angle = math.pi * sines[:, None] * index[None, :]
    return np.concatenate([np.cos(angle), -np.sin(angle)], axis=1).astype(np.float32)


def solve_middle(packed, steer, total):
    half, wide = packed.shape
    return pl.pallas_call(
        functools.partial(middle_kernel, total),
        out_shape=[
            jax.ShapeDtypeStruct((2 * half, wide), F32),
            jax.ShapeDtypeStruct((BEAMS, wide), F32),
        ],
        in_specs=[vmem_spec()] * 2,
        out_specs=[vmem_spec()] * 2,
        compiler_params=params(),
    )(packed, steer)


def solve_outer(own, left, right, steer, inverse, t, total, copies):
    chans, wide = inverse.shape
    return pl.pallas_call(
        functools.partial(outer_kernel, total),
        out_shape=jax.ShapeDtypeStruct((copies, BEAMS, 3 * wide), BF16),
        in_specs=[vmem_spec()] * 6,
        out_specs=vmem_spec(),
        scratch_shapes=[pltpu.VMEM((chans, wide), F32), pltpu.VMEM((5, chans, wide), F32)],
        compiler_params=params(),
    )(own, left, right, steer, inverse, t)


def beam_kernel(bin_ref, block_ref, beam_ref, owner_ref, s0_ref, s1_ref, w_ref, out_ref,
                both_ref, rows_ref, seen_ref):
    bins, wide, gates = s0_ref.shape
    devices = seen_ref.shape[0]
    count = bin_ref.shape[0]
    rows_ref[...] = jnp.zeros_like(rows_ref)

    @pl.loop(0, devices)
    def _(i):
        seen_ref[i] = 0

    w = w_ref[...].astype(F32).reshape(bins * BEAMS, 3 * wide)
    for k in range(3):
        lanes = slice(k * wide, (k + 1) * wide)
        part = w[:, lanes]
        both_ref[:, 0:BEAMS, lanes] = part.reshape(bins, BEAMS, wide)
        both_ref[:, BEAMS:, lanes] = turn(part).reshape(bins, BEAMS, wide)

    def detection(j, carry):
        bin_id = bin_ref[j]
        beam_id = beam_ref[j]
        owner = owner_ref[j]
        rank = seen_ref[owner]
        seen_ref[owner] = rank + 1
        left = both_ref[index_of(bin_id)].astype(BF16)
        bands = [lax.rem(bin_id + bins - 1 + k, bins) for k in range(3)]
        first = block_ref[j] == 0
        window = jnp.concatenate(
            [jnp.where(first, s0_ref[b], s1_ref[b]) for b in bands], axis=0
        )
        both = dot(left, window)
        line = jnp.concatenate([both[:BEAMS], both[BEAMS:]], axis=1)
        chosen = jnp.where(iota(line.shape, 0) == beam_id, line, 0.0)
        row = owner * CAP + rank
        rows_ref[pl.ds(row, 1), :] = jnp.sum(chosen, axis=0, keepdims=True)
        return carry

    lax.fori_loop(0, count, detection, 0, unroll=32)
    out_ref[...] = rows_ref[...].astype(BF16)


def beam_rows(det_bin, det_block, det_beam, owners, s0, s1, weight, devices):
    bins, wide, gates = s0.shape
    return pl.pallas_call(
        beam_kernel,
        out_shape=jax.ShapeDtypeStruct((devices * CAP, 2 * gates), BF16),
        in_specs=[smem_spec()] * 4 + [vmem_spec()] * 3,
        out_specs=vmem_spec(),
        scratch_shapes=[
            pltpu.VMEM((bins, 2 * BEAMS, 3 * wide), F32),
            pltpu.VMEM((devices * CAP, 2 * gates), F32),
            pltpu.SMEM((devices,), jnp.int32),
        ],
        compiler_params=params(),
    )(det_bin, det_block, det_beam, owners, s0, s1, weight)


def on_device(raw, replica, det_bin, det_block, det_beam, det_owner):
    devices = lax.axis_size("range")
    _, chans, pulses, gates = raw.shape
    bins = pulses
    flat = raw.reshape(2, chans * pulses, gates)
    before = [(source, source - 1) for source in range(1, devices)]
    gates_before, mark = first_gates(flat)
    halo = lax.ppermute(gates_before, "range", before)
    table = doppler_matrix(pulses, 8)
    s0, local, matrix, send0 = spectra_first(flat, replica, table, pulses, mark)
    beside0 = partner(send0, (1, 1))
    sums = cross(s0, bins)
    sums = cross(beside0, bins, sums)
    s1, send1 = spectra_last(local, halo, matrix, table, pulses, sums)
    beside1 = partner(send1, (1, 1))
    sums = cross(s1, bins, sums)
    sums = cross(beside1, bins, sums)
    own, packed = bin_sums(sums)
    total = gates * devices
    steer = steering(chans)
    left = from_bin(own, -1)
    right = from_bin(packed, 1)
    inverse, t = solve_middle(packed, steer, total)
    mine = solve_outer(own, left, right, steer, inverse, t, total, bins)
    groups = [list(range(first, first + bins)) for first in range(0, devices, bins)]
    weight = lax.all_to_all(
        mine, "range", split_axis=0, concat_axis=0, tiled=True,
        axis_index_groups=groups if len(groups) > 1 else None,
    )
    outgoing = beam_rows(
        det_bin, det_block, det_beam, det_owner[:, 0],
        s0.reshape(bins, 2 * chans, BLOCK), s1.reshape(bins, 2 * chans, BLOCK), weight, devices,
    )
    incoming = lax.all_to_all(
        outgoing.reshape(devices, CAP, 2 * BLOCK), "range", split_axis=0, concat_axis=0, tiled=True
    )
    return incoming.astype(F32).reshape(devices * CAP, 2 * BLOCK)


def solution(mesh):
    in_specs = (
        P(None, None, None, "range"),
        P(),
        P("range"),
        P("range"),
        P("range"),
        P("range", None),
    )
    out_specs = P("range", None)
    return jax.shard_map(
        on_device, mesh=mesh, in_specs=in_specs, out_specs=out_specs, check_vma=False
    )
```

```python
import functools
import math

import jax
import jax.numpy as jnp
import ml_dtypes
import numpy as np
from jax import lax
from jax.experimental import pallas as pl
from jax.experimental.pallas import tpu as pltpu
from jax.sharding import PartitionSpec as P

BLOCK = 128
BEAMS = 8
CAP = 2

F32 = jnp.float32
BF16 = jnp.bfloat16
VMEM = pltpu.VMEM
MIB = 1024 * 1024
NT = (((1,), (1,)), ((), ()))


def vmem_spec():
    return pl.BlockSpec(memory_space=VMEM)


def smem_spec():
    return pl.BlockSpec(memory_space=pltpu.SMEM)


def hbm_spec():
    return pl.BlockSpec(memory_space=pltpu.HBM)


SHORT = pl.CostEstimate(flops=1, bytes_accessed=1, transcendentals=0)


def params(mib=16):
    return pltpu.CompilerParams(vmem_limit_bytes=int(mib * MIB))


def dot(a, b):
    return jnp.dot(a, b, preferred_element_type=F32)


def dot_nt(a, b, precision=None):
    return lax.dot_general(a, b, NT, precision=precision, preferred_element_type=F32)


def iota(shape, axis):
    return lax.broadcasted_iota(jnp.int32, shape, axis)


def halo_kernel(raw_ref, out_ref, mark_ref, sems):
    mark_ref[...] = jnp.zeros_like(mark_ref)
    count = sems.shape[0]
    size = out_ref.shape[1] // count
    copies = [
        pltpu.make_async_copy(
            raw_ref.at[:, j * size : (j + 1) * size, :BLOCK],
            out_ref.at[:, j * size : (j + 1) * size, :],
            sems.at[j],
        )
        for j in range(count)
    ]
    for copy in copies:
        copy.start()
    for copy in copies:
        copy.wait()


def first_gates(raw):
    return pl.pallas_call(
        halo_kernel,
        out_shape=[
            jax.ShapeDtypeStruct(raw.shape[:2] + (BLOCK,), BF16),
            jax.ShapeDtypeStruct((8, 128), F32),
        ],
        in_specs=[hbm_spec()],
        out_specs=[vmem_spec()] * 2,
        scratch_shapes=[pltpu.SemaphoreType.DMA((8,))],
        compiler_params=params(63),
    )(raw)


def correlation_matrix(rep_ref, out_ref):
    taps = rep_ref.shape[1]
    base = rep_ref[...].astype(F32)
    row = iota((taps, 2 * taps), 0)
    parts = []
    for i in range(2):
        line = jnp.concatenate([base[i : i + 1], jnp.zeros((1, taps), F32)], axis=1)
        skew = jnp.broadcast_to(line, (taps, 2 * taps))
        bit = 1
        while bit < taps:
            skew = jnp.where((row & bit) != 0, pltpu.roll(skew, bit, 1), skew)
            bit *= 2
        parts.append(skew.T)
    real_part, imag_part = parts
    out_ref[0] = jnp.concatenate([real_part, -imag_part], axis=1).astype(BF16)
    out_ref[1] = jnp.concatenate([imag_part, real_part], axis=1).astype(BF16)


def doppler_matrix(pulses, group):
    index = np.arange(pulses)
    angle = 2.0 * math.pi / pulses * (index[:, None] * index[None, :] % pulses)
    cosine = np.cos(angle) * pulses**-0.5
    sine = np.sin(angle) * pulses**-0.5
    table = np.stack([np.stack([cosine, -sine], 1), np.stack([sine, cosine], 1)], 0)
    full = np.einsum("ipod,ce->dociep", table, np.eye(group))
    shape = (pulses * 2 * group, 2 * group * pulses)
    return full.reshape(shape).astype(ml_dtypes.bfloat16)


def doppler_rows(total, dft):
    compressed = total.astype(BF16)
    rows, wide = compressed.shape
    half, gates = rows // 2, wide // 2
    stacked = jnp.concatenate(
        [
            jnp.concatenate([compressed[:half, :gates], compressed[half:, :gates]], axis=1),
            jnp.concatenate([compressed[:half, gates:], compressed[half:, gates:]], axis=1),
        ],
        axis=0,
    )
    both = dot(dft, stacked)
    lines = both.shape[0] // 8
    joined = jnp.concatenate(
        [both[:, :gates].reshape(lines, 8, gates), both[:, gates:].reshape(lines, 8, gates)],
        axis=1,
    )
    return joined.astype(BF16)


GROUP = 16


def half_of_bins(bins, mine):
    core = lax.axis_index("range") & 1
    return (core if mine else 1 - core) * (bins // 2)


def sent_bins(bins):
    return bins // 2 + 2


def spectra_first_kernel(raw_ref, rep_ref, dft_ref, _, s_ref, local_ref, taps_ref, send_ref,
                         buf, sems):
    bins, _, chans, gates = s_ref.shape
    size = GROUP * bins
    copies = [
        pltpu.make_async_copy(
            raw_ref.at[:, j * size : (j + 1) * size, :],
            buf.at[:, j * size : (j + 1) * size, :],
            sems.at[j],
        )
        for j in range(chans // GROUP)
    ]
    for copy in copies:
        copy.start()
    correlation_matrix(rep_ref, taps_ref)
    for j, copy in enumerate(copies):
        copy.wait()
        rows = slice(j * size, (j + 1) * size)
        total = dot(buf[0, rows, :], taps_ref[0]) + dot(buf[1, rows, :], taps_ref[1])
        out = doppler_rows(total, dft_ref[...])
        s_ref[:, :, j * GROUP : (j + 1) * GROUP, :] = out.reshape(bins, 2, GROUP, gates)
        later = jnp.concatenate([buf[0, rows, gates:], buf[1, rows, gates:]], axis=1)
        near = jnp.concatenate([taps_ref[0, :gates, :], taps_ref[1, :gates, :]], axis=0)
        local_ref[rows, :] = dot(later, near)
    base = half_of_bins(bins, False)
    for k in range(send_ref.shape[0]):
        send_ref[k] = s_ref[lax.rem(base + k, bins)]


def spectra_last_kernel(local_ref, halo_ref, taps_ref, dft_ref, _, s_ref, send_ref):
    bins, _, chans, gates = s_ref.shape
    size = GROUP * bins
    far = jnp.concatenate([taps_ref[0, gates:, :], taps_ref[1, gates:, :]], axis=0)
    for j in range(chans // GROUP):
        rows = slice(j * size, (j + 1) * size)
        later = jnp.concatenate([halo_ref[0, rows, :], halo_ref[1, rows, :]], axis=1)
        out = doppler_rows(local_ref[rows, :] + dot(later, far), dft_ref[...])
        s_ref[:, :, j * GROUP : (j + 1) * GROUP, :] = out.reshape(bins, 2, GROUP, gates)
    base = half_of_bins(bins, False)
    for k in range(send_ref.shape[0]):
        send_ref[k] = s_ref[lax.rem(base + k, bins)]


def spectra_first(raw, replica, table, pulses, mark):
    _, rows, gates = raw.shape
    chans = rows // pulses
    taps = replica.shape[1]
    return pl.pallas_call(
        spectra_first_kernel,
        out_shape=[
            jax.ShapeDtypeStruct((pulses, 2, chans, BLOCK), BF16),
            jax.ShapeDtypeStruct((rows, 2 * BLOCK), F32),
            jax.ShapeDtypeStruct((2, 2 * taps, 2 * taps), BF16),
            jax.ShapeDtypeStruct((sent_bins(pulses), 2, chans, BLOCK), BF16),
        ],
        in_specs=[hbm_spec(), vmem_spec(), vmem_spec(), pl.BlockSpec(memory_space=pl.ANY)],
        out_specs=[vmem_spec()] * 4,
        scratch_shapes=[
            pltpu.VMEM(raw.shape, BF16),
            pltpu.SemaphoreType.DMA((chans // GROUP,)),
        ],
        compiler_params=params(),
        cost_estimate=SHORT,
    )(raw, replica, table, mark)


def spectra_last(local, halo, matrix, table, pulses, sums):
    chans = local.shape[0] // pulses
    return pl.pallas_call(
        spectra_last_kernel,
        out_shape=[
            jax.ShapeDtypeStruct((pulses, 2, chans, BLOCK), BF16),
            jax.ShapeDtypeStruct((sent_bins(pulses), 2, chans, BLOCK), BF16),
        ],
        in_specs=[vmem_spec()] * 4 + [pl.BlockSpec(memory_space=pl.ANY)],
        out_specs=[vmem_spec()] * 2,
        compiler_params=params(),
        cost_estimate=SHORT,
    )(local, halo, matrix, table, sums)


def cross_kernel(s_ref, *refs):
    before_ref = refs[0] if len(refs) == 2 else None
    out_ref = refs[-1]
    last = out_ref.shape[1] < 3 * s_ref.shape[2]
    held, _, chans, gates = s_ref.shape
    count = out_ref.shape[0]
    base = half_of_bins(held, True) if held == 2 * count else 0
    lower = iota((chans, chans), 0) >= iota((chans, chans), 1)
    half = chans // 2

    def packed(block):
        swapped = pltpu.roll(block, chans, 1)
        mixed = jnp.where(lower, block[:, :chans], swapped[:, :chans])
        return jnp.concatenate([mixed[:half], mixed[half:]], axis=1)

    def write(e, block):
        value = block if before_ref is None else block + before_ref[e]
        if last:
            value = jnp.concatenate([packed(value[:chans]), value[chans:]], axis=0)
        out_ref[e] = value

    @pl.loop(0, count // 2, unroll=2)
    def _(step):
        e = step * 2
        each = []
        for k in range(4):
            where = lax.rem(base + e + k, held)
            each.append((s_ref[where, 0], s_ref[where, 1]))
        left = jnp.concatenate(
            [jnp.concatenate([re, im], axis=1) for re, im in each], axis=0
        )
        right = jnp.concatenate(
            [
                jnp.concatenate(pieces, axis=1)
                for re, im in each[:2]
                for pieces in ((re, im), (-im, re))
            ],
            axis=0,
        )
        both = dot_nt(left, right)
        write(e, both[: 3 * chans, : 2 * chans])
        write(e + 1, both[chans:, 2 * chans :])


def cross(spectra, bins, before=None, last=False):
    chans = spectra.shape[2]
    rows = 5 * chans // 2 if last else 3 * chans
    data = [spectra] if before is None else [spectra, before]
    return pl.pallas_call(
        cross_kernel,
        out_shape=jax.ShapeDtypeStruct((bins // 2, rows, 2 * chans), F32),
        in_specs=[vmem_spec()] * len(data),
        out_specs=vmem_spec(),
        compiler_params=params(),
        cost_estimate=SHORT,
    )(*data)


U_BITS, V_BITS, UV_BITS, Z0_BITS, Z1_BITS = (2, 4), (4, 2), (6, 6), (8, 8), (16, 16)


def spans(rows):
    fifth = rows // 5
    return slice(0, 2 * fifth), slice(2 * fifth, 4 * fifth), slice(4 * fifth, rows)


def partner(value, bits):
    count = lax.axis_size("range")
    return lax.ppermute(value, "range", [(i, i ^ bits[i & 1]) for i in range(count)])


def slot_of(core, x, y, z):
    return (4 * z + ((2 * y + (x ^ y)) ^ (3 * (z & 1)))) ^ (15 * core)


def parts_of(index):
    return index & 1, (index >> 1) & 1, (index >> 2) & 1, (index >> 3) & 3


def bin_of(index):
    core, x, y, z = parts_of(index)
    return core * 16 + slot_of(core, x, y, z)


def index_of(bin_id):
    core = bin_id >> 4
    path = (bin_id & 15) ^ (15 * core)
    z = path >> 2
    turned = (path & 3) ^ (3 * (z & 1))
    y = turned >> 1
    x = (turned & 1) ^ y
    return z * 8 + y * 4 + x * 2 + core


def uv_parts():
    core, x, y, z = parts_of(lax.axis_index("range"))
    return core, jnp.where(core == 0, x, y), jnp.where(core == 0, y, x), z


def uv_slot(core, u, v, z):
    return slot_of(core, jnp.where(core == 0, u, v), jnp.where(core == 0, v, u), z)


def first_kernel(keep_ref, a_ref, b_ref, c_ref):
    core, u, v, z = uv_parts()
    upper, lower, rest = spans(keep_ref.shape[1])
    for k in range(8):
        a_ref[k] = keep_ref[uv_slot(core, 1 - u, k // 4, k % 4), upper]
        b_ref[k] = keep_ref[uv_slot(core, k // 4, 1 - v, k % 4), lower]
        c_ref[k] = keep_ref[uv_slot(core, k // 4, (k // 2) % 2, (k % 2) * 2 + 1 - (z & 1)), rest]


def second_kernel(keep_ref, a1_ref, b1_ref, c1_ref, a_ref, b_ref, c_ref):
    core, u, v, z = uv_parts()
    upper, lower, rest = spans(keep_ref.shape[1])
    for k in range(4):
        e = uv_slot(core, u, 1 - v, k)
        a_ref[k] = keep_ref[e, upper] + a1_ref[(1 - v) * 4 + k]
        e = uv_slot(core, 1 - u, v, k)
        b_ref[k] = keep_ref[e, lower] + b1_ref[(1 - u) * 4 + k]
        e = uv_slot(core, k // 2, k % 2, z ^ 2)
        c_ref[k] = keep_ref[e, rest] + c1_ref[k * 2 + 1 - (z >> 1)]


def line_sum(keep_ref, a1_ref, b1_ref, a2_ref, b2_ref, flip):
    core, u, v, z = uv_parts()
    z = z ^ flip
    upper, lower, _ = spans(keep_ref.shape[1])
    e = uv_slot(core, u, v, z)
    a = keep_ref[e, upper] + a1_ref[v * 4 + z] + a2_ref[z]
    b = keep_ref[e, lower] + b1_ref[u * 4 + z] + b2_ref[z]
    return a, b


def plane_sum(keep_ref, c1_ref, c2_ref, u_flip, v_flip):
    core, u, v, z = uv_parts()
    u, v = u ^ u_flip, v ^ v_flip
    rest = spans(keep_ref.shape[1])[2]
    e = uv_slot(core, u, v, z)
    return keep_ref[e, rest] + c1_ref[u * 4 + v * 2 + (z >> 1)] + c2_ref[u * 2 + v]


FLIPS = (2, 3, 1)
PLANE = ((1, 1, UV_BITS), (1, 0, U_BITS), (0, 1, V_BITS))


def third_kernel(keep_ref, a1_ref, b1_ref, c1_ref, a2_ref, b2_ref, c2_ref, *outs):
    for flip, out_ref in zip(FLIPS, outs[:3]):
        a, b = line_sum(keep_ref, a1_ref, b1_ref, a2_ref, b2_ref, flip)
        out_ref[: a.shape[0]] = a
        out_ref[a.shape[0] :] = b
    for (u_flip, v_flip, _), out_ref in zip(PLANE, outs[3:]):
        out_ref[...] = plane_sum(keep_ref, c1_ref, c2_ref, u_flip, v_flip)


def own_kernel(keep_ref, a1_ref, b1_ref, c1_ref, a2_ref, b2_ref, c2_ref, *refs):
    z1_ref, z2_ref, z3_ref, p1_ref, p2_ref, p3_ref, out_ref, packed_ref = refs
    upper, lower, rest = spans(keep_ref.shape[1])
    a, b = line_sum(keep_ref, a1_ref, b1_ref, a2_ref, b2_ref, 0)
    a = a + z1_ref[upper] + (z2_ref[upper] + z3_ref[upper])
    out_ref[upper] = a
    packed_ref[...] = a[: packed_ref.shape[0]]
    out_ref[lower] = b + z1_ref[lower] + (z2_ref[lower] + z3_ref[lower])
    c = plane_sum(keep_ref, c1_ref, c2_ref, 0, 0)
    out_ref[rest] = c + p1_ref[...] + (p2_ref[...] + p3_ref[...])


def summed(kernel, data, shapes):
    return pl.pallas_call(
        kernel,
        out_shape=[jax.ShapeDtypeStruct(shape, F32) for shape in shapes],
        in_specs=[vmem_spec()] * len(data),
        out_specs=[vmem_spec()] * len(shapes),
        compiler_params=params(),
    )(*data)


def bin_sums(keep):
    _, rows, wide = keep.shape
    fifth = rows // 5
    sizes = (2 * fifth, 2 * fifth, fifth)
    data = [keep]
    a, b, c = summed(first_kernel, data, [(8, size, wide) for size in sizes])
    data += [partner(a, U_BITS), partner(b, V_BITS), partner(c, Z0_BITS)]
    a, b, c = summed(second_kernel, data, [(4, size, wide) for size in sizes])
    data += [partner(a, V_BITS), partner(b, U_BITS), partner(c, Z1_BITS)]
    sends = summed(third_kernel, data, [(4 * fifth, wide)] * 3 + [(fifth, wide)] * 3)
    data += [partner(value, (8 * flip, 8 * flip)) for flip, value in zip(FLIPS, sends)]
    data += [partner(value, bits) for (_, _, bits), value in zip(PLANE, sends[3:])]
    own, packed = summed(own_kernel, data, [(rows, wide), (rows // 5, wide)])
    bit = 32
    while bit < lax.axis_size("range"):
        own = own + partner(own, (bit, bit))
        packed = packed + partner(packed, (bit, bit))
        bit *= 2
    return own, packed


def from_bin(value, offset):
    count = lax.axis_size("range")
    pairs = []
    for i in range(count):
        target = index_of((bin_of(i) - offset) % 32) | (i & ~31)
        pairs.append((i, target))
    return lax.ppermute(value, "range", pairs)


def turn(value):
    half = value.shape[1] // 2
    rolled = pltpu.roll(value, half, 1)
    return jnp.where(iota(value.shape, 1) < half, -rolled, rolled)


def embed(value):
    return jnp.concatenate([value, turn(value)], axis=0)


def mul(a, b):
    return jnp.dot(a, embed(b), precision=lax.Precision.HIGHEST, preferred_element_type=F32)


def mul_conj(a, b):
    half = a.shape[1] // 2
    stacked = jnp.concatenate([a, -turn(a)], axis=0)
    both = dot_nt(stacked, b, lax.Precision.HIGHEST)
    rows = a.shape[0]
    return jnp.concatenate([both[:rows], both[rows:]], axis=1)


def conj_mul(a, b):
    half = a.shape[1] // 2
    both = lax.dot_general(
        a, b, (((0,), (0,)), ((), ())),
        precision=lax.Precision.HIGHEST, preferred_element_type=F32,
    )
    return both[:half] - turn(both[half:])


def reciprocal(x):
    value = pl.reciprocal(x, approx=True)
    for _ in range(2):
        value = value * (2.0 - x * value)
    return value


def pivot_inverse(p):
    def times(x, y):
        return x[0] * y[0] - x[1] * y[1], x[0] * y[1] + x[1] * y[0]

    def conj(x):
        return x[0], -x[1]

    def plus(x, y):
        return x[0] + y[0], x[1] + y[1]

    def scaled(x, s):
        return x[0] * s, x[1] * s

    def square(x):
        return x[0] * x[0] + x[1] * x[1]

    def two(a, b, d):
        inv = reciprocal(a * d - square(b))
        return d * inv, scaled(b, -inv), a * inv

    a, d = p[0][0], p[1][1]
    b = p[0][1]
    ea, eb, ed = two(a, b, d)
    f = [[p[0][2], p[0][3]], [p[1][2], p[1][3]]]
    w = [
        [plus(scaled(f[0][j], ea), times(eb, f[1][j])) for j in range(2)],
        [plus(times(conj(eb), f[0][j]), scaled(f[1][j], ed)) for j in range(2)],
    ]

    def inner(i, j):
        return plus(times(conj(f[0][i]), w[0][j]), times(conj(f[1][i]), w[1][j]))

    ha = p[2][2] - inner(0, 0)[0]
    hd = p[3][3] - inner(1, 1)[0]
    cross = inner(0, 1)
    hb = (p[2][3][0] - cross[0], p[2][3][1] - cross[1])
    ga, gb, gd = two(ha, hb, hd)
    v = [
        [
            plus(scaled(w[i][0], ga), times(w[i][1], conj(gb))),
            plus(times(w[i][0], gb), scaled(w[i][1], gd)),
        ]
        for i in range(2)
    ]
    top = [
        [plus(times(v[i][0], conj(w[j][0])), times(v[i][1], conj(w[j][1]))) for j in range(2)]
        for i in range(2)
    ]
    zero = None
    out = [[None] * 4 for _ in range(4)]
    out[0][0] = (ea + top[0][0][0], zero)
    out[1][1] = (ed + top[1][1][0], zero)
    out[0][1] = plus(eb, top[0][1])
    out[2][2], out[3][3], out[2][3] = (ga, zero), (gd, zero), gb
    for i in range(2):
        for j in range(2):
            out[i][2 + j] = (-v[i][j][0], -v[i][j][1])
    for i in range(4):
        for j in range(i):
            out[i][j] = conj(out[j][i])
    return out


def invert(matrix):
    chans, width = matrix.shape
    sub = 8
    tiles = [matrix[t * sub : (t + 1) * sub, :] for t in range(chans // sub)]
    lane = iota((sub, width), 1)
    row = iota((sub, width), 0)
    first_half = lane < chans

    def spin(value):
        rolled = pltpu.roll(value, chans, 1)
        return jnp.where(first_half, -rolled, rolled)

    def column(value, k):
        return jnp.broadcast_to(value[:, k : k + 1], (sub, width))

    def combine(terms):
        while len(terms) > 1:
            terms = [
                terms[i] + terms[i + 1] if i + 1 < len(terms) else terms[i]
                for i in range(0, len(terms), 2)
            ]
        return terms[0]

    for k in range(0, chans, 4):
        t, r = divmod(k, sub)
        lines = [jnp.broadcast_to(tiles[t][r + i : r + i + 1, :], (sub, width)) for i in range(4)]
        pivot = [[None] * 4 for _ in range(4)]
        for i in range(4):
            pivot[i][i] = column(lines[i], k + i)
            for j in range(i + 1, 4):
                pivot[i][j] = column(lines[i], k + j), column(lines[i], chans + k + j)
        low = jnp.bitwise_and(lane, chans - 1)
        cleared = (low >= k) & (low < k + 4)
        unit = [
            jnp.where(cleared, jnp.where(lane == k + i, 1.0, 0.0), lines[i]) for i in range(4)
        ]
        spun = [spin(u) for u in unit]
        p = pivot_inverse(pivot)
        fresh_lines, fresh_spun = [], []
        for i in range(4):
            terms, other = [], []
            for j in range(4):
                re, im = p[i][j]
                terms.append(re * unit[j])
                other.append(re * spun[j])
                if im is not None:
                    terms.append(im * spun[j])
                    other.append(-(im * unit[j]))
            fresh_lines.append(combine(terms))
            fresh_spun.append(combine(other))
        fresh = []
        for s, tile in enumerate(tiles):
            terms = []
            for i in range(4):
                terms.append(column(tile, k + i) * fresh_lines[i])
                terms.append(column(tile, chans + k + i) * fresh_spun[i])
            value = jnp.where(cleared, 0.0, tile) - combine(terms)
            if s == t:
                for i in range(4):
                    value = jnp.where(row == r + i, fresh_lines[i], value)
            fresh.append(value)
        tiles = fresh
    return jnp.concatenate(tiles, axis=0)


def unpacked(ref, scale):
    half, wide = ref.shape[0], ref.shape[1]
    piece = ref[...] * scale
    swapped = pltpu.roll(piece, wide // 2, 1)
    return jnp.concatenate([piece, swapped], axis=0)[:, : wide // 2]


def hermitian(mixed, across):
    i, j = iota(mixed.shape, 0), iota(mixed.shape, 1)
    real_part = jnp.where(i >= j, mixed, across)
    imag_part = jnp.where(i < j, mixed, jnp.where(i > j, -across, 0.0))
    return jnp.concatenate([real_part, imag_part], axis=1)


def middle_kernel(total, packed_ref, steer_ref, inv_ref, t_ref):
    chans = inv_ref.shape[0]
    mixed = unpacked(packed_ref, F32(1.0 / total))
    twice = jnp.concatenate([mixed, mixed], axis=1)
    across = jnp.concatenate([twice, twice], axis=0).T[:chans, :chans]
    inverse = invert(hermitian(mixed, across))
    inv_ref[...] = inverse
    t_ref[...] = mul(steer_ref[...], inverse)


def outer_kernel(total, own_ref, left_ref, right_ref, steer_ref, inv_ref, t_ref, out_ref,
                 work, keep):
    chans = inv_ref.shape[0]
    scale = F32(1.0 / total)
    half = chans // 2
    m_left = unpacked(left_ref.at[:half], scale)
    m_right = unpacked(right_ref, scale)
    ml = left_ref[half : half + chans] * scale
    rl = left_ref[half + chans :] * scale
    rm = own_ref[half : half + chans] * scale
    pair = jnp.concatenate([m_left, m_right], axis=1)
    square = jnp.concatenate([pair, pair], axis=0).T
    inv_mid = inv_ref[...]
    t = t_ref[...]
    h = mul(inv_mid, ml)
    g = mul(rm, inv_mid)
    work[...] = hermitian(m_left, square[:chans, :chans]) - conj_mul(ml, h)
    s_rl = rl - mul(rm, h)
    s_rr = hermitian(m_right, square[chans:, :chans]) - mul_conj(g, rm)
    rhs_left = -mul(t, ml)
    rhs_right = -mul_conj(t, rm)
    keep[0] = s_rl
    keep[1] = s_rr
    keep[2] = h
    keep[3] = g
    keep[4, 0:BEAMS] = rhs_left
    keep[4, BEAMS : 2 * BEAMS] = rhs_right

    @pl.loop(0, 2)
    def _(stage):
        work[...] = invert(work[...])

        @pl.when(stage == 0)
        def _():
            inverse = work[...]
            s_rl = keep[0]
            both = mul(jnp.concatenate([s_rl, keep[4, 0:BEAMS]], axis=0), inverse)
            k, y_left = both[:chans], both[chans:]
            work[...] = keep[1] - mul_conj(k, s_rl)
            keep[0] = k
            keep[4, BEAMS : 2 * BEAMS] = keep[4, BEAMS : 2 * BEAMS] - mul_conj(y_left, s_rl)
            keep[4, 0:BEAMS] = y_left
            keep[4, 2 * BEAMS : 3 * BEAMS] = t_ref[...] - mul_conj(y_left, keep[2])
            keep[3] = keep[3] - mul_conj(k, keep[2])

        @pl.when(stage == 1)
        def _():
            y_right = mul(keep[4, BEAMS : 2 * BEAMS], work[...])
            y_left = keep[4, 0:BEAMS] - mul(y_right, keep[0])
            y_mid = keep[4, 2 * BEAMS : 3 * BEAMS] - mul(y_right, keep[3])
            quad = jnp.sum(steer_ref[...] * y_mid, axis=1, keepdims=True)
            y = jnp.concatenate([y_left, y_mid, y_right], axis=1) / jnp.sqrt(quad)
            real_lane = lax.rem(iota(y.shape, 1), 2 * chans) < chans
            mine = jnp.where(real_lane, y, -y).astype(BF16)
            for c in range(out_ref.shape[0]):
                out_ref[c] = mine


def steering(chans):
    index = np.arange(chans)
    sines = -0.8 + 1.6 * np.arange(BEAMS) / (BEAMS - 1)
    angle = math.pi * sines[:, None] * index[None, :]
    return np.concatenate([np.cos(angle), -np.sin(angle)], axis=1).astype(np.float32)


def solve_middle(packed, steer, total):
    half, wide = packed.shape
    return pl.pallas_call(
        functools.partial(middle_kernel, total),
        out_shape=[
            jax.ShapeDtypeStruct((2 * half, wide), F32),
            jax.ShapeDtypeStruct((BEAMS, wide), F32),
        ],
        in_specs=[vmem_spec()] * 2,
        out_specs=[vmem_spec()] * 2,
        compiler_params=params(),
    )(packed, steer)


def solve_outer(own, left, right, steer, inverse, t, total, copies):
    chans, wide = inverse.shape
    return pl.pallas_call(
        functools.partial(outer_kernel, total),
        out_shape=jax.ShapeDtypeStruct((copies, BEAMS, 3 * wide), BF16),
        in_specs=[vmem_spec()] * 6,
        out_specs=vmem_spec(),
        scratch_shapes=[pltpu.VMEM((chans, wide), F32), pltpu.VMEM((5, chans, wide), F32)],
        compiler_params=params(),
    )(own, left, right, steer, inverse, t)


def beam_kernel(bin_ref, block_ref, beam_ref, owner_ref, s0_ref, s1_ref, w_ref, out_ref,
                both_ref, rows_ref, seen_ref):
    bins, wide, gates = s0_ref.shape
    devices = seen_ref.shape[0]
    count = bin_ref.shape[0]
    rows_ref[...] = jnp.zeros_like(rows_ref)

    @pl.loop(0, devices)
    def _(i):
        seen_ref[i] = 0

    w = w_ref[...].astype(F32).reshape(bins * BEAMS, 3 * wide)
    for k in range(3):
        lanes = slice(k * wide, (k + 1) * wide)
        part = w[:, lanes]
        both_ref[:, 0:BEAMS, lanes] = part.reshape(bins, BEAMS, wide)
        both_ref[:, BEAMS:, lanes] = turn(part).reshape(bins, BEAMS, wide)

    def detection(j, carry):
        bin_id = bin_ref[j]
        beam_id = beam_ref[j]
        owner = owner_ref[j]
        rank = seen_ref[owner]
        seen_ref[owner] = rank + 1
        left = both_ref[index_of(bin_id)].astype(BF16)
        bands = [lax.rem(bin_id + bins - 1 + k, bins) for k in range(3)]
        first = block_ref[j] == 0
        window = jnp.concatenate(
            [jnp.where(first, s0_ref[b], s1_ref[b]) for b in bands], axis=0
        )
        both = dot(left, window)
        line = jnp.concatenate([both[:BEAMS], both[BEAMS:]], axis=1)
        chosen = jnp.where(iota(line.shape, 0) == beam_id, line, 0.0)
        row = owner * CAP + rank
        rows_ref[pl.ds(row, 1), :] = jnp.sum(chosen, axis=0, keepdims=True)
        return carry

    lax.fori_loop(0, count, detection, 0, unroll=32)
    out_ref[...] = rows_ref[...].astype(BF16)


def beam_rows(det_bin, det_block, det_beam, owners, s0, s1, weight, devices):
    bins, wide, gates = s0.shape
    return pl.pallas_call(
        beam_kernel,
        out_shape=jax.ShapeDtypeStruct((devices * CAP, 2 * gates), BF16),
        in_specs=[smem_spec()] * 4 + [vmem_spec()] * 3,
        out_specs=vmem_spec(),
        scratch_shapes=[
            pltpu.VMEM((bins, 2 * BEAMS, 3 * wide), F32),
            pltpu.VMEM((devices * CAP, 2 * gates), F32),
            pltpu.SMEM((devices,), jnp.int32),
        ],
        compiler_params=params(),
    )(det_bin, det_block, det_beam, owners, s0, s1, weight)


def on_device(raw, replica, det_bin, det_block, det_beam, det_owner):
    devices = lax.axis_size("range")
    _, chans, pulses, gates = raw.shape
    bins = pulses
    flat = raw.reshape(2, chans * pulses, gates)
    before = [(source, source - 1) for source in range(1, devices)]
    gates_before, mark = first_gates(flat)
    halo = lax.ppermute(gates_before, "range", before)
    table = doppler_matrix(pulses, 8)
    s0, local, matrix, send0 = spectra_first(flat, replica, table, pulses, mark)
    beside0 = partner(send0, (1, 1))
    sums = cross(s0, bins)
    sums = cross(beside0, bins, sums)
    s1, send1 = spectra_last(local, halo, matrix, table, pulses, sums)
    beside1 = partner(send1, (1, 1))
    sums = cross(s1, bins, sums)
    sums = cross(beside1, bins, sums, last=True)
    own, packed = bin_sums(sums)
    total = gates * devices
    steer = steering(chans)
    left = from_bin(own, -1)
    right = from_bin(packed, 1)
    inverse, t = solve_middle(packed, steer, total)
    mine = solve_outer(own, left, right, steer, inverse, t, total, bins)
    groups = [list(range(first, first + bins)) for first in range(0, devices, bins)]
    weight = lax.all_to_all(
        mine, "range", split_axis=0, concat_axis=0, tiled=True,
        axis_index_groups=groups if len(groups) > 1 else None,
    )
    outgoing = beam_rows(
        det_bin, det_block, det_beam, det_owner[:, 0],
        s0.reshape(bins, 2 * chans, BLOCK), s1.reshape(bins, 2 * chans, BLOCK), weight, devices,
    )
    incoming = lax.all_to_all(
        outgoing.reshape(devices, CAP, 2 * BLOCK), "range", split_axis=0, concat_axis=0, tiled=True
    )
    return incoming.astype(F32).reshape(devices * CAP, 2 * BLOCK)


def solution(mesh):
    in_specs = (
        P(None, None, None, "range"),
        P(),
        P("range"),
        P("range"),
        P("range"),
        P("range", None),
    )
    out_specs = P("range", None)
    return jax.shard_map(
        on_device, mesh=mesh, in_specs=in_specs, out_specs=out_specs, check_vma=False
    )
```

```python
import functools
import math

import jax
import jax.numpy as jnp
import ml_dtypes
import numpy as np
from jax import lax
from jax.experimental import pallas as pl
from jax.experimental.pallas import tpu as pltpu
from jax.sharding import PartitionSpec as P

BLOCK = 128
BEAMS = 8
CAP = 2

F32 = jnp.float32
BF16 = jnp.bfloat16
VMEM = pltpu.VMEM
MIB = 1024 * 1024
NT = (((1,), (1,)), ((), ()))


def vmem_spec():
    return pl.BlockSpec(memory_space=VMEM)


def smem_spec():
    return pl.BlockSpec(memory_space=pltpu.SMEM)


def hbm_spec():
    return pl.BlockSpec(memory_space=pltpu.HBM)


SHORT = pl.CostEstimate(flops=1, bytes_accessed=1, transcendentals=0)


def params(mib=16):
    return pltpu.CompilerParams(vmem_limit_bytes=int(mib * MIB))


def dot(a, b):
    return jnp.dot(a, b, preferred_element_type=F32)


def dot_nt(a, b, precision=None):
    return lax.dot_general(a, b, NT, precision=precision, preferred_element_type=F32)


def iota(shape, axis):
    return lax.broadcasted_iota(jnp.int32, shape, axis)


def halo_kernel(raw_ref, a_ref, b_ref, mark_ref, sems):
    mark_ref[...] = jnp.zeros_like(mark_ref)
    count = sems.shape[0] // 2
    size = a_ref.shape[1] // count
    copies = []
    for part, out_ref in enumerate((a_ref, b_ref)):
        for j in range(count):
            start = part * a_ref.shape[1] + j * size
            copies.append(
                pltpu.make_async_copy(
                    raw_ref.at[:, start : start + size, :BLOCK],
                    out_ref.at[:, j * size : (j + 1) * size, :],
                    sems.at[part * count + j],
                )
            )
    for copy in copies:
        copy.start()
    for copy in copies:
        copy.wait()


def first_gates(raw):
    half = jax.ShapeDtypeStruct((2, raw.shape[1] // 2, BLOCK), BF16)
    return pl.pallas_call(
        halo_kernel,
        out_shape=[half, half, jax.ShapeDtypeStruct((8, 128), F32)],
        in_specs=[hbm_spec()],
        out_specs=[vmem_spec()] * 3,
        scratch_shapes=[pltpu.SemaphoreType.DMA((8,))],
        compiler_params=params(63),
    )(raw)


def correlation_matrix(rep_ref, out_ref):
    taps = rep_ref.shape[1]
    base = rep_ref[...].astype(F32)
    row = iota((taps, 2 * taps), 0)
    parts = []
    for i in range(2):
        line = jnp.concatenate([base[i : i + 1], jnp.zeros((1, taps), F32)], axis=1)
        skew = jnp.broadcast_to(line, (taps, 2 * taps))
        bit = 1
        while bit < taps:
            skew = jnp.where((row & bit) != 0, pltpu.roll(skew, bit, 1), skew)
            bit *= 2
        parts.append(skew.T)
    real_part, imag_part = parts
    out_ref[0] = jnp.concatenate([real_part, -imag_part], axis=1).astype(BF16)
    out_ref[1] = jnp.concatenate([imag_part, real_part], axis=1).astype(BF16)


def doppler_matrix(pulses, group):
    index = np.arange(pulses)
    angle = 2.0 * math.pi / pulses * (index[:, None] * index[None, :] % pulses)
    cosine = np.cos(angle) * pulses**-0.5
    sine = np.sin(angle) * pulses**-0.5
    table = np.stack([np.stack([cosine, -sine], 1), np.stack([sine, cosine], 1)], 0)
    full = np.einsum("ipod,ce->dociep", table, np.eye(group))
    shape = (pulses * 2 * group, 2 * group * pulses)
    return full.reshape(shape).astype(ml_dtypes.bfloat16)


def doppler_rows(total, dft):
    compressed = total.astype(BF16)
    rows, wide = compressed.shape
    half, gates = rows // 2, wide // 2
    stacked = jnp.concatenate(
        [
            jnp.concatenate([compressed[:half, :gates], compressed[half:, :gates]], axis=1),
            jnp.concatenate([compressed[:half, gates:], compressed[half:, gates:]], axis=1),
        ],
        axis=0,
    )
    both = dot(dft, stacked)
    lines = both.shape[0] // 8
    joined = jnp.concatenate(
        [both[:, :gates].reshape(lines, 8, gates), both[:, gates:].reshape(lines, 8, gates)],
        axis=1,
    )
    return joined.astype(BF16)


GROUP = 16


def half_of_bins(bins, mine):
    core = lax.axis_index("range") & 1
    return (core if mine else 1 - core) * (bins // 2)


def sent_bins(bins):
    return bins // 2 + 2


def spectra_first_kernel(raw_ref, rep_ref, dft_ref, _, s_ref, local_ref, taps_ref, *rest):
    *send_refs, buf, sems = rest
    bins, _, chans, gates = s_ref.shape
    size = GROUP * bins
    copies = [
        pltpu.make_async_copy(
            raw_ref.at[:, j * size : (j + 1) * size, :],
            buf.at[:, j * size : (j + 1) * size, :],
            sems.at[j],
        )
        for j in range(chans // GROUP)
    ]
    for copy in copies:
        copy.start()
    correlation_matrix(rep_ref, taps_ref)
    for j, copy in enumerate(copies):
        copy.wait()
        rows = slice(j * size, (j + 1) * size)
        total = dot(buf[0, rows, :], taps_ref[0]) + dot(buf[1, rows, :], taps_ref[1])
        out = doppler_rows(total, dft_ref[...])
        s_ref[:, :, j * GROUP : (j + 1) * GROUP, :] = out.reshape(bins, 2, GROUP, gates)
        later = jnp.concatenate([buf[0, rows, gates:], buf[1, rows, gates:]], axis=1)
        near = jnp.concatenate([taps_ref[0, :gates, :], taps_ref[1, :gates, :]], axis=0)
        local_ref[rows, :] = dot(later, near)
    base = half_of_bins(bins, False)
    half = chans // 2
    for part, send_ref in enumerate(send_refs):
        for k in range(send_ref.shape[0]):
            send_ref[k] = s_ref[lax.rem(base + k, bins), :, part * half : (part + 1) * half, :]


def spectra_last_kernel(local_ref, a_ref, b_ref, taps_ref, dft_ref, _, s_ref, send_ref):
    bins, _, chans, gates = s_ref.shape
    size = GROUP * bins
    far = jnp.concatenate([taps_ref[0, gates:, :], taps_ref[1, gates:, :]], axis=0)
    for j in range(chans // GROUP):
        rows = slice(j * size, (j + 1) * size)
        ref, first = (a_ref, rows.start) if j < 2 else (b_ref, rows.start - 2 * size)
        later = jnp.concatenate(
            [ref[0, first : first + size, :], ref[1, first : first + size, :]], axis=1
        )
        out = doppler_rows(local_ref[rows, :] + dot(later, far), dft_ref[...])
        s_ref[:, :, j * GROUP : (j + 1) * GROUP, :] = out.reshape(bins, 2, GROUP, gates)
    base = half_of_bins(bins, False)
    for k in range(send_ref.shape[0]):
        send_ref[k] = s_ref[lax.rem(base + k, bins)]


def spectra_first(raw, replica, table, pulses, mark):
    _, rows, gates = raw.shape
    chans = rows // pulses
    taps = replica.shape[1]
    return pl.pallas_call(
        spectra_first_kernel,
        out_shape=[
            jax.ShapeDtypeStruct((pulses, 2, chans, BLOCK), BF16),
            jax.ShapeDtypeStruct((rows, 2 * BLOCK), F32),
            jax.ShapeDtypeStruct((2, 2 * taps, 2 * taps), BF16),
        ]
        + [jax.ShapeDtypeStruct((sent_bins(pulses), 2, chans // 2, BLOCK), BF16)] * 2,
        in_specs=[hbm_spec(), vmem_spec(), vmem_spec(), pl.BlockSpec(memory_space=pl.ANY)],
        out_specs=[vmem_spec()] * 5,
        scratch_shapes=[
            pltpu.VMEM(raw.shape, BF16),
            pltpu.SemaphoreType.DMA((chans // GROUP,)),
        ],
        compiler_params=params(),
        cost_estimate=SHORT,
    )(raw, replica, table, mark)


def spectra_last(local, halos, matrix, table, pulses, sums):
    chans = local.shape[0] // pulses
    return pl.pallas_call(
        spectra_last_kernel,
        out_shape=[
            jax.ShapeDtypeStruct((pulses, 2, chans, BLOCK), BF16),
            jax.ShapeDtypeStruct((sent_bins(pulses), 2, chans, BLOCK), BF16),
        ],
        in_specs=[vmem_spec()] * 5 + [pl.BlockSpec(memory_space=pl.ANY)],
        out_specs=[vmem_spec()] * 2,
        compiler_params=params(),
        cost_estimate=SHORT,
    )(local, *halos, matrix, table, sums)


def cross_kernel(count_refs, *refs):
    s_refs, rest = refs[:count_refs], refs[count_refs:]
    before_ref = rest[0] if len(rest) == 2 else None
    out_ref = rest[-1]
    held, _, _, gates = s_refs[0].shape
    chans = sum(ref.shape[2] for ref in s_refs)
    last = out_ref.shape[1] < 3 * chans
    count = out_ref.shape[0]
    base = half_of_bins(held, True) if held == 2 * count else 0
    lower = iota((chans, chans), 0) >= iota((chans, chans), 1)
    half = chans // 2

    def packed(block):
        swapped = pltpu.roll(block, chans, 1)
        mixed = jnp.where(lower, block[:, :chans], swapped[:, :chans])
        return jnp.concatenate([mixed[:half], mixed[half:]], axis=1)

    def write(e, block):
        value = block if before_ref is None else block + before_ref[e]
        if last:
            value = jnp.concatenate([packed(value[:chans]), value[chans:]], axis=0)
        out_ref[e] = value

    @pl.loop(0, count // 2, unroll=2)
    def _(step):
        e = step * 2
        each = []
        for k in range(4):
            where = lax.rem(base + e + k, held)
            each.append(
                [jnp.concatenate([ref[where, o] for ref in s_refs], axis=0) for o in range(2)]
            )
        left = jnp.concatenate(
            [jnp.concatenate([re, im], axis=1) for re, im in each], axis=0
        )
        right = jnp.concatenate(
            [
                jnp.concatenate(pieces, axis=1)
                for re, im in each[:2]
                for pieces in ((re, im), (-im, re))
            ],
            axis=0,
        )
        both = dot_nt(left, right)
        write(e, both[: 3 * chans, : 2 * chans])
        write(e + 1, both[chans:, 2 * chans :])


def cross(spectra, bins, before=None, last=False):
    chans = sum(value.shape[2] for value in spectra)
    rows = 5 * chans // 2 if last else 3 * chans
    data = spectra if before is None else spectra + [before]
    return pl.pallas_call(
        functools.partial(cross_kernel, len(spectra)),
        out_shape=jax.ShapeDtypeStruct((bins // 2, rows, 2 * chans), F32),
        in_specs=[vmem_spec()] * len(data),
        out_specs=vmem_spec(),
        compiler_params=params(),
        cost_estimate=SHORT,
    )(*data)


U_BITS, V_BITS = (2, 4), (4, 2)


def partner(value, bits):
    count = lax.axis_size("range")
    return lax.ppermute(value, "range", [(i, i ^ bits[i & 1]) for i in range(count)])


def slot_of(core, x, y, z):
    return (4 * z + ((2 * y + (x ^ y)) ^ (3 * (z & 1)))) ^ (15 * core)


def parts_of(index):
    return index & 1, (index >> 1) & 1, (index >> 2) & 1, (index >> 3) & 3


def bin_of(index):
    core, x, y, z = parts_of(index)
    return core * 16 + slot_of(core, x, y, z)


def index_of(bin_id):
    core = bin_id >> 4
    path = (bin_id & 15) ^ (15 * core)
    z = path >> 2
    turned = (path & 3) ^ (3 * (z & 1))
    y = turned >> 1
    x = (turned & 1) ^ y
    return z * 8 + y * 4 + x * 2 + core


def uv_parts():
    core, x, y, z = parts_of(lax.axis_index("range"))
    return core, jnp.where(core == 0, x, y), jnp.where(core == 0, y, x), z


def uv_slot(core, u, v, z):
    return slot_of(core, jnp.where(core == 0, u, v), jnp.where(core == 0, v, u), z)


def first_kernel(keep_ref, a_ref, b_ref):
    core, u, v, z = uv_parts()
    half = keep_ref.shape[1] // 2
    for k in range(8):
        a_ref[k] = keep_ref[uv_slot(core, 1 - u, k // 4, k % 4), :half]
        b_ref[k] = keep_ref[uv_slot(core, k // 4, 1 - v, k % 4), half:]


def second_kernel(keep_ref, a1_ref, b1_ref, a_ref, b_ref):
    core, u, v, z = uv_parts()
    half = keep_ref.shape[1] // 2
    for k in range(4):
        e = uv_slot(core, u, 1 - v, k)
        a_ref[k] = keep_ref[e, :half] + a1_ref[(1 - v) * 4 + k]
        e = uv_slot(core, 1 - u, v, k)
        b_ref[k] = keep_ref[e, half:] + b1_ref[(1 - u) * 4 + k]


def line_sum(keep_ref, a1_ref, b1_ref, a2_ref, b2_ref, flip):
    core, u, v, z = uv_parts()
    z = z ^ flip
    half = keep_ref.shape[1] // 2
    e = uv_slot(core, u, v, z)
    upper = keep_ref[e, :half] + a1_ref[v * 4 + z] + a2_ref[z]
    lower = keep_ref[e, half:] + b1_ref[u * 4 + z] + b2_ref[z]
    return upper, lower


FLIPS = (2, 3, 1)


def line_kernel(*refs):
    half = refs[0].shape[1] // 2
    for flip, out_ref in zip(FLIPS, refs[5:]):
        upper, lower = line_sum(*refs[:5], flip)
        out_ref[:half] = upper
        out_ref[half:] = lower


def own_kernel(*refs):
    z1_ref, z2_ref, z3_ref, out_ref, packed_ref = refs[5:]
    half = refs[0].shape[1] // 2
    upper, lower = line_sum(*refs[:5], 0)
    upper = upper + z1_ref[:half] + (z2_ref[:half] + z3_ref[:half])
    out_ref[:half] = upper
    packed_ref[...] = upper[: packed_ref.shape[0]]
    out_ref[half:] = lower + z1_ref[half:] + (z2_ref[half:] + z3_ref[half:])


def summed(kernel, data, shapes):
    return pl.pallas_call(
        kernel,
        out_shape=[jax.ShapeDtypeStruct(shape, F32) for shape in shapes],
        in_specs=[vmem_spec()] * len(data),
        out_specs=[vmem_spec()] * len(shapes),
        compiler_params=params(),
    )(*data)


def bin_sums(keep):
    _, rows, wide = keep.shape
    half = rows // 2
    data = [keep]
    a, b = summed(first_kernel, data, [(8, half, wide)] * 2)
    data += [partner(a, U_BITS), partner(b, V_BITS)]
    a, b = summed(second_kernel, data, [(4, half, wide)] * 2)
    data += [partner(a, V_BITS), partner(b, U_BITS)]
    sends = summed(line_kernel, data, [(rows, wide)] * 3)
    data += [partner(value, (8 * flip, 8 * flip)) for flip, value in zip(FLIPS, sends)]
    own, packed = summed(own_kernel, data, [(rows, wide), (rows // 5, wide)])
    bit = 32
    while bit < lax.axis_size("range"):
        own = own + partner(own, (bit, bit))
        packed = packed + partner(packed, (bit, bit))
        bit *= 2
    return own, packed


def from_bin(value, offset):
    count = lax.axis_size("range")
    pairs = []
    for i in range(count):
        target = index_of((bin_of(i) - offset) % 32) | (i & ~31)
        pairs.append((i, target))
    return lax.ppermute(value, "range", pairs)


def turn(value):
    half = value.shape[1] // 2
    rolled = pltpu.roll(value, half, 1)
    return jnp.where(iota(value.shape, 1) < half, -rolled, rolled)


def embed(value):
    return jnp.concatenate([value, turn(value)], axis=0)


def mul(a, b):
    return jnp.dot(a, embed(b), precision=lax.Precision.HIGHEST, preferred_element_type=F32)


def mul_conj(a, b):
    half = a.shape[1] // 2
    stacked = jnp.concatenate([a, -turn(a)], axis=0)
    both = dot_nt(stacked, b, lax.Precision.HIGHEST)
    rows = a.shape[0]
    return jnp.concatenate([both[:rows], both[rows:]], axis=1)


def conj_mul(a, b):
    half = a.shape[1] // 2
    both = lax.dot_general(
        a, b, (((0,), (0,)), ((), ())),
        precision=lax.Precision.HIGHEST, preferred_element_type=F32,
    )
    return both[:half] - turn(both[half:])


def reciprocal(x):
    value = pl.reciprocal(x, approx=True)
    for _ in range(2):
        value = value * (2.0 - x * value)
    return value


def pivot_inverse(p):
    def times(x, y):
        return x[0] * y[0] - x[1] * y[1], x[0] * y[1] + x[1] * y[0]

    def conj(x):
        return x[0], -x[1]

    def plus(x, y):
        return x[0] + y[0], x[1] + y[1]

    def scaled(x, s):
        return x[0] * s, x[1] * s

    def square(x):
        return x[0] * x[0] + x[1] * x[1]

    def two(a, b, d):
        inv = reciprocal(a * d - square(b))
        return d * inv, scaled(b, -inv), a * inv

    a, d = p[0][0], p[1][1]
    b = p[0][1]
    ea, eb, ed = two(a, b, d)
    f = [[p[0][2], p[0][3]], [p[1][2], p[1][3]]]
    w = [
        [plus(scaled(f[0][j], ea), times(eb, f[1][j])) for j in range(2)],
        [plus(times(conj(eb), f[0][j]), scaled(f[1][j], ed)) for j in range(2)],
    ]

    def inner(i, j):
        return plus(times(conj(f[0][i]), w[0][j]), times(conj(f[1][i]), w[1][j]))

    ha = p[2][2] - inner(0, 0)[0]
    hd = p[3][3] - inner(1, 1)[0]
    cross = inner(0, 1)
    hb = (p[2][3][0] - cross[0], p[2][3][1] - cross[1])
    ga, gb, gd = two(ha, hb, hd)
    v = [
        [
            plus(scaled(w[i][0], ga), times(w[i][1], conj(gb))),
            plus(times(w[i][0], gb), scaled(w[i][1], gd)),
        ]
        for i in range(2)
    ]
    top = [
        [plus(times(v[i][0], conj(w[j][0])), times(v[i][1], conj(w[j][1]))) for j in range(2)]
        for i in range(2)
    ]
    zero = None
    out = [[None] * 4 for _ in range(4)]
    out[0][0] = (ea + top[0][0][0], zero)
    out[1][1] = (ed + top[1][1][0], zero)
    out[0][1] = plus(eb, top[0][1])
    out[2][2], out[3][3], out[2][3] = (ga, zero), (gd, zero), gb
    for i in range(2):
        for j in range(2):
            out[i][2 + j] = (-v[i][j][0], -v[i][j][1])
    for i in range(4):
        for j in range(i):
            out[i][j] = conj(out[j][i])
    return out


def invert(matrix):
    chans, width = matrix.shape
    sub = 8
    tiles = [matrix[t * sub : (t + 1) * sub, :] for t in range(chans // sub)]
    lane = iota((sub, width), 1)
    row = iota((sub, width), 0)
    first_half = lane < chans

    def spin(value):
        rolled = pltpu.roll(value, chans, 1)
        return jnp.where(first_half, -rolled, rolled)

    def column(value, k):
        return jnp.broadcast_to(value[:, k : k + 1], (sub, width))

    def combine(terms):
        while len(terms) > 1:
            terms = [
                terms[i] + terms[i + 1] if i + 1 < len(terms) else terms[i]
                for i in range(0, len(terms), 2)
            ]
        return terms[0]

    for k in range(0, chans, 4):
        t, r = divmod(k, sub)
        lines = [jnp.broadcast_to(tiles[t][r + i : r + i + 1, :], (sub, width)) for i in range(4)]
        pivot = [[None] * 4 for _ in range(4)]
        for i in range(4):
            pivot[i][i] = column(lines[i], k + i)
            for j in range(i + 1, 4):
                pivot[i][j] = column(lines[i], k + j), column(lines[i], chans + k + j)
        low = jnp.bitwise_and(lane, chans - 1)
        cleared = (low >= k) & (low < k + 4)
        unit = [
            jnp.where(cleared, jnp.where(lane == k + i, 1.0, 0.0), lines[i]) for i in range(4)
        ]
        spun = [spin(u) for u in unit]
        p = pivot_inverse(pivot)
        fresh_lines, fresh_spun = [], []
        for i in range(4):
            terms, other = [], []
            for j in range(4):
                re, im = p[i][j]
                terms.append(re * unit[j])
                other.append(re * spun[j])
                if im is not None:
                    terms.append(im * spun[j])
                    other.append(-(im * unit[j]))
            fresh_lines.append(combine(terms))
            fresh_spun.append(combine(other))
        fresh = []
        for s, tile in enumerate(tiles):
            terms = []
            for i in range(4):
                terms.append(column(tile, k + i) * fresh_lines[i])
                terms.append(column(tile, chans + k + i) * fresh_spun[i])
            value = jnp.where(cleared, 0.0, tile) - combine(terms)
            if s == t:
                for i in range(4):
                    value = jnp.where(row == r + i, fresh_lines[i], value)
            fresh.append(value)
        tiles = fresh
    return jnp.concatenate(tiles, axis=0)


def unpacked(ref, scale):
    half, wide = ref.shape[0], ref.shape[1]
    piece = ref[...] * scale
    swapped = pltpu.roll(piece, wide // 2, 1)
    return jnp.concatenate([piece, swapped], axis=0)[:, : wide // 2]


def hermitian(mixed, across):
    i, j = iota(mixed.shape, 0), iota(mixed.shape, 1)
    real_part = jnp.where(i >= j, mixed, across)
    imag_part = jnp.where(i < j, mixed, jnp.where(i > j, -across, 0.0))
    return jnp.concatenate([real_part, imag_part], axis=1)


def middle_kernel(total, packed_ref, steer_ref, inv_ref, t_ref):
    chans = inv_ref.shape[0]
    mixed = unpacked(packed_ref, F32(1.0 / total))
    twice = jnp.concatenate([mixed, mixed], axis=1)
    across = jnp.concatenate([twice, twice], axis=0).T[:chans, :chans]
    inverse = invert(hermitian(mixed, across))
    inv_ref[...] = inverse
    t_ref[...] = mul(steer_ref[...], inverse)


def outer_kernel(total, own_ref, left_ref, right_ref, steer_ref, inv_ref, t_ref, out_ref,
                 work, keep):
    chans = inv_ref.shape[0]
    scale = F32(1.0 / total)
    half = chans // 2
    m_left = unpacked(left_ref.at[:half], scale)
    m_right = unpacked(right_ref, scale)
    ml = left_ref[half : half + chans] * scale
    rl = left_ref[half + chans :] * scale
    rm = own_ref[half : half + chans] * scale
    pair = jnp.concatenate([m_left, m_right], axis=1)
    square = jnp.concatenate([pair, pair], axis=0).T
    inv_mid = inv_ref[...]
    t = t_ref[...]
    h = mul(inv_mid, ml)
    g = mul(rm, inv_mid)
    work[...] = hermitian(m_left, square[:chans, :chans]) - conj_mul(ml, h)
    s_rl = rl - mul(rm, h)
    s_rr = hermitian(m_right, square[chans:, :chans]) - mul_conj(g, rm)
    rhs_left = -mul(t, ml)
    rhs_right = -mul_conj(t, rm)
    keep[0] = s_rl
    keep[1] = s_rr
    keep[2] = h
    keep[3] = g
    keep[4, 0:BEAMS] = rhs_left
    keep[4, BEAMS : 2 * BEAMS] = rhs_right

    @pl.loop(0, 2)
    def _(stage):
        work[...] = invert(work[...])

        @pl.when(stage == 0)
        def _():
            inverse = work[...]
            s_rl = keep[0]
            both = mul(jnp.concatenate([s_rl, keep[4, 0:BEAMS]], axis=0), inverse)
            k, y_left = both[:chans], both[chans:]
            work[...] = keep[1] - mul_conj(k, s_rl)
            keep[0] = k
            keep[4, BEAMS : 2 * BEAMS] = keep[4, BEAMS : 2 * BEAMS] - mul_conj(y_left, s_rl)
            keep[4, 0:BEAMS] = y_left
            keep[4, 2 * BEAMS : 3 * BEAMS] = t_ref[...] - mul_conj(y_left, keep[2])
            keep[3] = keep[3] - mul_conj(k, keep[2])

        @pl.when(stage == 1)
        def _():
            y_right = mul(keep[4, BEAMS : 2 * BEAMS], work[...])
            y_left = keep[4, 0:BEAMS] - mul(y_right, keep[0])
            y_mid = keep[4, 2 * BEAMS : 3 * BEAMS] - mul(y_right, keep[3])
            quad = jnp.sum(steer_ref[...] * y_mid, axis=1, keepdims=True)
            y = jnp.concatenate([y_left, y_mid, y_right], axis=1) / jnp.sqrt(quad)
            real_lane = lax.rem(iota(y.shape, 1), 2 * chans) < chans
            mine = jnp.where(real_lane, y, -y).astype(BF16)
            for c in range(out_ref.shape[0]):
                out_ref[c] = mine


def steering(chans):
    index = np.arange(chans)
    sines = -0.8 + 1.6 * np.arange(BEAMS) / (BEAMS - 1)
    angle = math.pi * sines[:, None] * index[None, :]
    return np.concatenate([np.cos(angle), -np.sin(angle)], axis=1).astype(np.float32)


def solve_middle(packed, steer, total):
    half, wide = packed.shape
    return pl.pallas_call(
        functools.partial(middle_kernel, total),
        out_shape=[
            jax.ShapeDtypeStruct((2 * half, wide), F32),
            jax.ShapeDtypeStruct((BEAMS, wide), F32),
        ],
        in_specs=[vmem_spec()] * 2,
        out_specs=[vmem_spec()] * 2,
        compiler_params=params(),
    )(packed, steer)


def solve_outer(own, left, right, steer, inverse, t, total, copies):
    chans, wide = inverse.shape
    return pl.pallas_call(
        functools.partial(outer_kernel, total),
        out_shape=jax.ShapeDtypeStruct((copies, BEAMS, 3 * wide), BF16),
        in_specs=[vmem_spec()] * 6,
        out_specs=vmem_spec(),
        scratch_shapes=[pltpu.VMEM((chans, wide), F32), pltpu.VMEM((5, chans, wide), F32)],
        compiler_params=params(),
    )(own, left, right, steer, inverse, t)


def beam_kernel(bin_ref, block_ref, beam_ref, owner_ref, s0_ref, s1_ref, w_ref, out_ref,
                both_ref, rows_ref, seen_ref):
    bins, wide, gates = s0_ref.shape
    devices = seen_ref.shape[0]
    count = bin_ref.shape[0]
    rows_ref[...] = jnp.zeros_like(rows_ref)

    @pl.loop(0, devices)
    def _(i):
        seen_ref[i] = 0

    w = w_ref[...].astype(F32).reshape(bins * BEAMS, 3 * wide)
    for k in range(3):
        lanes = slice(k * wide, (k + 1) * wide)
        part = w[:, lanes]
        both_ref[:, 0:BEAMS, lanes] = part.reshape(bins, BEAMS, wide)
        both_ref[:, BEAMS:, lanes] = turn(part).reshape(bins, BEAMS, wide)

    def detection(j, carry):
        bin_id = bin_ref[j]
        beam_id = beam_ref[j]
        owner = owner_ref[j]
        rank = seen_ref[owner]
        seen_ref[owner] = rank + 1
        left = both_ref[index_of(bin_id)].astype(BF16)
        bands = [lax.rem(bin_id + bins - 1 + k, bins) for k in range(3)]
        first = block_ref[j] == 0
        window = jnp.concatenate(
            [jnp.where(first, s0_ref[b], s1_ref[b]) for b in bands], axis=0
        )
        both = dot(left, window)
        line = jnp.concatenate([both[:BEAMS], both[BEAMS:]], axis=1)
        chosen = jnp.where(iota(line.shape, 0) == beam_id, line, 0.0)
        row = owner * CAP + rank
        rows_ref[pl.ds(row, 1), :] = jnp.sum(chosen, axis=0, keepdims=True)
        return carry

    lax.fori_loop(0, count, detection, 0, unroll=32)
    out_ref[...] = rows_ref[...].astype(BF16)


def beam_rows(det_bin, det_block, det_beam, owners, s0, s1, weight, devices):
    bins, wide, gates = s0.shape
    return pl.pallas_call(
        beam_kernel,
        out_shape=jax.ShapeDtypeStruct((devices * CAP, 2 * gates), BF16),
        in_specs=[smem_spec()] * 4 + [vmem_spec()] * 3,
        out_specs=vmem_spec(),
        scratch_shapes=[
            pltpu.VMEM((bins, 2 * BEAMS, 3 * wide), F32),
            pltpu.VMEM((devices * CAP, 2 * gates), F32),
            pltpu.SMEM((devices,), jnp.int32),
        ],
        compiler_params=params(),
    )(det_bin, det_block, det_beam, owners, s0, s1, weight)


def on_device(raw, replica, det_bin, det_block, det_beam, det_owner):
    devices = lax.axis_size("range")
    _, chans, pulses, gates = raw.shape
    bins = pulses
    flat = raw.reshape(2, chans * pulses, gates)
    before = [(source, source - 1) for source in range(1, devices)]
    *slices, mark = first_gates(flat)
    halos = [lax.ppermute(value, "range", before) for value in slices]
    table = doppler_matrix(pulses, 8)
    s0, local, matrix, *sent = spectra_first(flat, replica, table, pulses, mark)
    beside0 = [partner(value, (1, 1)) for value in sent]
    sums = cross([s0], bins)
    sums = cross(beside0, bins, sums)
    s1, send1 = spectra_last(local, halos, matrix, table, pulses, sums)
    beside1 = partner(send1, (1, 1))
    sums = cross([s1], bins, sums)
    sums = cross([beside1], bins, sums, last=True)
    own, packed = bin_sums(sums)
    total = gates * devices
    steer = steering(chans)
    left = from_bin(own, -1)
    right = from_bin(packed, 1)
    inverse, t = solve_middle(packed, steer, total)
    mine = solve_outer(own, left, right, steer, inverse, t, total, bins)
    groups = [list(range(first, first + bins)) for first in range(0, devices, bins)]
    weight = lax.all_to_all(
        mine, "range", split_axis=0, concat_axis=0, tiled=True,
        axis_index_groups=groups if len(groups) > 1 else None,
    )
    outgoing = beam_rows(
        det_bin, det_block, det_beam, det_owner[:, 0],
        s0.reshape(bins, 2 * chans, BLOCK), s1.reshape(bins, 2 * chans, BLOCK), weight, devices,
    )
    incoming = lax.all_to_all(
        outgoing.reshape(devices, CAP, 2 * BLOCK), "range", split_axis=0, concat_axis=0, tiled=True
    )
    return incoming.astype(F32).reshape(devices * CAP, 2 * BLOCK)


def solution(mesh):
    in_specs = (
        P(None, None, None, "range"),
        P(),
        P("range"),
        P("range"),
        P("range"),
        P("range", None),
    )
    out_specs = P("range", None)
    return jax.shard_map(
        on_device, mesh=mesh, in_specs=in_specs, out_specs=out_specs, check_vma=False
    )
```

```python
import functools
import math

import jax
import jax.numpy as jnp
import ml_dtypes
import numpy as np
from jax import lax
from jax.experimental import pallas as pl
from jax.experimental.pallas import tpu as pltpu
from jax.sharding import PartitionSpec as P

BLOCK = 128
BEAMS = 8
CAP = 2

F32 = jnp.float32
BF16 = jnp.bfloat16
VMEM = pltpu.VMEM
MIB = 1024 * 1024
NT = (((1,), (1,)), ((), ()))


def vmem_spec():
    return pl.BlockSpec(memory_space=VMEM)


def smem_spec():
    return pl.BlockSpec(memory_space=pltpu.SMEM)


def hbm_spec():
    return pl.BlockSpec(memory_space=pltpu.HBM)


SHORT = pl.CostEstimate(flops=1, bytes_accessed=1, transcendentals=0)


def params(mib=16):
    return pltpu.CompilerParams(vmem_limit_bytes=int(mib * MIB))


def dot(a, b):
    return jnp.dot(a, b, preferred_element_type=F32)


def dot_nt(a, b, precision=None):
    return lax.dot_general(a, b, NT, precision=precision, preferred_element_type=F32)


def iota(shape, axis):
    return lax.broadcasted_iota(jnp.int32, shape, axis)


def halo_kernel(raw_ref, a_ref, b_ref, mark_ref, sems):
    mark_ref[...] = jnp.zeros_like(mark_ref)
    count = sems.shape[0] // 2
    size = a_ref.shape[1] // count
    copies = []
    for part, out_ref in enumerate((a_ref, b_ref)):
        for j in range(count):
            start = part * a_ref.shape[1] + j * size
            copies.append(
                pltpu.make_async_copy(
                    raw_ref.at[:, start : start + size, :BLOCK],
                    out_ref.at[:, j * size : (j + 1) * size, :],
                    sems.at[part * count + j],
                )
            )
    for copy in copies:
        copy.start()
    for copy in copies:
        copy.wait()


def first_gates(raw):
    half = jax.ShapeDtypeStruct((2, raw.shape[1] // 2, BLOCK), BF16)
    return pl.pallas_call(
        halo_kernel,
        out_shape=[half, half, jax.ShapeDtypeStruct((8, 128), F32)],
        in_specs=[hbm_spec()],
        out_specs=[vmem_spec()] * 3,
        scratch_shapes=[pltpu.SemaphoreType.DMA((8,))],
        compiler_params=params(63),
    )(raw)


def correlation_matrix(rep_ref, out_ref):
    taps = rep_ref.shape[1]
    base = rep_ref[...].astype(F32)
    row = iota((taps, 2 * taps), 0)
    parts = []
    for i in range(2):
        line = jnp.concatenate([base[i : i + 1], jnp.zeros((1, taps), F32)], axis=1)
        skew = jnp.broadcast_to(line, (taps, 2 * taps))
        bit = 1
        while bit < taps:
            skew = jnp.where((row & bit) != 0, pltpu.roll(skew, bit, 1), skew)
            bit *= 2
        parts.append(skew.T)
    real_part, imag_part = parts
    out_ref[0] = jnp.concatenate([real_part, -imag_part], axis=1).astype(BF16)
    out_ref[1] = jnp.concatenate([imag_part, real_part], axis=1).astype(BF16)


def doppler_matrix(pulses, group):
    index = np.arange(pulses)
    angle = 2.0 * math.pi / pulses * (index[:, None] * index[None, :] % pulses)
    cosine = np.cos(angle) * pulses**-0.5
    sine = np.sin(angle) * pulses**-0.5
    table = np.stack([np.stack([cosine, -sine], 1), np.stack([sine, cosine], 1)], 0)
    full = np.einsum("ipod,ce->dociep", table, np.eye(group))
    shape = (pulses * 2 * group, 2 * group * pulses)
    return full.reshape(shape).astype(ml_dtypes.bfloat16)


def doppler_rows(total, dft):
    compressed = total.astype(BF16)
    rows, wide = compressed.shape
    half, gates = rows // 2, wide // 2
    stacked = jnp.concatenate(
        [
            jnp.concatenate([compressed[:half, :gates], compressed[half:, :gates]], axis=1),
            jnp.concatenate([compressed[:half, gates:], compressed[half:, gates:]], axis=1),
        ],
        axis=0,
    )
    both = dot(dft, stacked)
    lines = both.shape[0] // 8
    joined = jnp.concatenate(
        [both[:, :gates].reshape(lines, 8, gates), both[:, gates:].reshape(lines, 8, gates)],
        axis=1,
    )
    return joined.astype(BF16)


GROUP = 16


def half_of_bins(bins, mine):
    core = lax.axis_index("range") & 1
    return (core if mine else 1 - core) * (bins // 2)


def sent_bins(bins):
    return bins // 2 + 2


def spectra_first_kernel(raw_ref, rep_ref, dft_ref, _, s_ref, local_ref, taps_ref, *rest):
    *send_refs, buf, sems = rest
    bins, _, chans, gates = s_ref.shape
    size = GROUP * bins
    copies = [
        pltpu.make_async_copy(
            raw_ref.at[:, j * size : (j + 1) * size, :],
            buf.at[:, j * size : (j + 1) * size, :],
            sems.at[j],
        )
        for j in range(chans // GROUP)
    ]
    for copy in copies:
        copy.start()
    correlation_matrix(rep_ref, taps_ref)
    for j, copy in enumerate(copies):
        copy.wait()
        rows = slice(j * size, (j + 1) * size)
        total = dot(buf[0, rows, :], taps_ref[0]) + dot(buf[1, rows, :], taps_ref[1])
        out = doppler_rows(total, dft_ref[...])
        s_ref[:, :, j * GROUP : (j + 1) * GROUP, :] = out.reshape(bins, 2, GROUP, gates)
        later = jnp.concatenate([buf[0, rows, gates:], buf[1, rows, gates:]], axis=1)
        near = jnp.concatenate([taps_ref[0, :gates, :], taps_ref[1, :gates, :]], axis=0)
        local_ref[rows, :] = dot(later, near)
    base = half_of_bins(bins, False)
    half = chans // 2
    for part, send_ref in enumerate(send_refs):
        for k in range(send_ref.shape[0]):
            send_ref[k] = s_ref[lax.rem(base + k, bins), :, part * half : (part + 1) * half, :]


def spectra_last_kernel(local_ref, a_ref, b_ref, taps_ref, dft_ref, _, s_ref, send_ref):
    bins, _, chans, gates = s_ref.shape
    size = GROUP * bins
    far = jnp.concatenate([taps_ref[0, gates:, :], taps_ref[1, gates:, :]], axis=0)
    for j in range(chans // GROUP):
        rows = slice(j * size, (j + 1) * size)
        ref, first = (a_ref, rows.start) if j < 2 else (b_ref, rows.start - 2 * size)
        later = jnp.concatenate(
            [ref[0, first : first + size, :], ref[1, first : first + size, :]], axis=1
        )
        out = doppler_rows(local_ref[rows, :] + dot(later, far), dft_ref[...])
        s_ref[:, :, j * GROUP : (j + 1) * GROUP, :] = out.reshape(bins, 2, GROUP, gates)
    base = half_of_bins(bins, False)
    for k in range(send_ref.shape[0]):
        send_ref[k] = s_ref[lax.rem(base + k, bins)]


def spectra_first(raw, replica, table, pulses, mark):
    _, rows, gates = raw.shape
    chans = rows // pulses
    taps = replica.shape[1]
    return pl.pallas_call(
        spectra_first_kernel,
        out_shape=[
            jax.ShapeDtypeStruct((pulses, 2, chans, BLOCK), BF16),
            jax.ShapeDtypeStruct((rows, 2 * BLOCK), F32),
            jax.ShapeDtypeStruct((2, 2 * taps, 2 * taps), BF16),
        ]
        + [jax.ShapeDtypeStruct((sent_bins(pulses), 2, chans // 2, BLOCK), BF16)] * 2,
        in_specs=[hbm_spec(), vmem_spec(), vmem_spec(), pl.BlockSpec(memory_space=pl.ANY)],
        out_specs=[vmem_spec()] * 5,
        scratch_shapes=[
            pltpu.VMEM(raw.shape, BF16),
            pltpu.SemaphoreType.DMA((chans // GROUP,)),
        ],
        compiler_params=params(),
        cost_estimate=SHORT,
    )(raw, replica, table, mark)


def spectra_last(local, halos, matrix, table, pulses, sums):
    chans = local.shape[0] // pulses
    return pl.pallas_call(
        spectra_last_kernel,
        out_shape=[
            jax.ShapeDtypeStruct((pulses, 2, chans, BLOCK), BF16),
            jax.ShapeDtypeStruct((sent_bins(pulses), 2, chans, BLOCK), BF16),
        ],
        in_specs=[vmem_spec()] * 5 + [pl.BlockSpec(memory_space=pl.ANY)],
        out_specs=[vmem_spec()] * 2,
        compiler_params=params(),
        cost_estimate=SHORT,
    )(local, *halos, matrix, table, sums)


def cross_kernel(count_refs, *refs):
    s_refs, rest = refs[:count_refs], refs[count_refs:]
    before_ref = rest[0] if len(rest) == 2 else None
    out_ref = rest[-1]
    held, _, _, gates = s_refs[0].shape
    chans = sum(ref.shape[2] for ref in s_refs)
    last = out_ref.shape[1] < 3 * chans
    count = out_ref.shape[0]
    base = half_of_bins(held, True) if held == 2 * count else 0
    lower = iota((chans, chans), 0) >= iota((chans, chans), 1)
    half = chans // 2

    def packed(block):
        swapped = pltpu.roll(block, chans, 1)
        mixed = jnp.where(lower, block[:, :chans], swapped[:, :chans])
        return jnp.concatenate([mixed[:half], mixed[half:]], axis=1)

    def write(e, block):
        value = block if before_ref is None else block + before_ref[e]
        if last:
            value = jnp.concatenate([packed(value[:chans]), value[chans:]], axis=0)
        out_ref[e] = value

    @pl.loop(0, count // 2, unroll=2)
    def _(step):
        e = step * 2
        each = []
        for k in range(4):
            where = lax.rem(base + e + k, held)
            each.append(
                [jnp.concatenate([ref[where, o] for ref in s_refs], axis=0) for o in range(2)]
            )
        left = jnp.concatenate(
            [jnp.concatenate([re, im], axis=1) for re, im in each], axis=0
        )
        right = jnp.concatenate(
            [
                jnp.concatenate(pieces, axis=1)
                for re, im in each[:2]
                for pieces in ((re, im), (-im, re))
            ],
            axis=0,
        )
        both = dot_nt(left, right)
        write(e, both[: 3 * chans, : 2 * chans])
        write(e + 1, both[chans:, 2 * chans :])


def cross(spectra, bins, before=None, last=False):
    chans = sum(value.shape[2] for value in spectra)
    rows = 5 * chans // 2 if last else 3 * chans
    data = spectra if before is None else spectra + [before]
    return pl.pallas_call(
        functools.partial(cross_kernel, len(spectra)),
        out_shape=jax.ShapeDtypeStruct((bins // 2, rows, 2 * chans), F32),
        in_specs=[vmem_spec()] * len(data),
        out_specs=vmem_spec(),
        compiler_params=params(),
        cost_estimate=SHORT,
    )(*data)


U_BITS, V_BITS = (2, 4), (4, 2)


def partner(value, bits):
    count = lax.axis_size("range")
    return lax.ppermute(value, "range", [(i, i ^ bits[i & 1]) for i in range(count)])


def slot_of(core, x, y, z):
    return (4 * z + ((2 * y + (x ^ y)) ^ (3 * (z & 1)))) ^ (15 * core)


def parts_of(index):
    return index & 1, (index >> 1) & 1, (index >> 2) & 1, (index >> 3) & 3


def bin_of(index):
    core, x, y, z = parts_of(index)
    return core * 16 + slot_of(core, x, y, z)


def index_of(bin_id):
    core = bin_id >> 4
    path = (bin_id & 15) ^ (15 * core)
    z = path >> 2
    turned = (path & 3) ^ (3 * (z & 1))
    y = turned >> 1
    x = (turned & 1) ^ y
    return z * 8 + y * 4 + x * 2 + core


def uv_parts():
    core, x, y, z = parts_of(lax.axis_index("range"))
    return core, jnp.where(core == 0, x, y), jnp.where(core == 0, y, x), z


def uv_slot(core, u, v, z):
    return slot_of(core, jnp.where(core == 0, u, v), jnp.where(core == 0, v, u), z)


def first_kernel(keep_ref, a_ref, b_ref):
    core, u, v, z = uv_parts()
    half = keep_ref.shape[1] // 2
    for k in range(8):
        a_ref[k] = keep_ref[uv_slot(core, 1 - u, k // 4, k % 4), :half]
        b_ref[k] = keep_ref[uv_slot(core, k // 4, 1 - v, k % 4), half:]


def second_kernel(keep_ref, a1_ref, b1_ref, a_ref, b_ref):
    core, u, v, z = uv_parts()
    half = keep_ref.shape[1] // 2
    for k in range(4):
        e = uv_slot(core, u, 1 - v, k)
        a_ref[k] = keep_ref[e, :half] + a1_ref[(1 - v) * 4 + k]
        e = uv_slot(core, 1 - u, v, k)
        b_ref[k] = keep_ref[e, half:] + b1_ref[(1 - u) * 4 + k]


def line_sum(keep_ref, a1_ref, b1_ref, a2_ref, b2_ref, flip):
    core, u, v, z = uv_parts()
    z = z ^ flip
    half = keep_ref.shape[1] // 2
    e = uv_slot(core, u, v, z)
    upper = keep_ref[e, :half] + a1_ref[v * 4 + z] + a2_ref[z]
    lower = keep_ref[e, half:] + b1_ref[u * 4 + z] + b2_ref[z]
    return upper, lower


FLIPS = (2, 3, 1)


def line_kernel(*refs):
    half = refs[0].shape[1] // 2
    for flip, out_ref in zip(FLIPS, refs[5:]):
        upper, lower = line_sum(*refs[:5], flip)
        out_ref[:half] = upper
        out_ref[half:] = lower


def own_kernel(*refs):
    z1_ref, z2_ref, z3_ref, out_ref, packed_ref = refs[5:]
    half = refs[0].shape[1] // 2
    upper, lower = line_sum(*refs[:5], 0)
    upper = upper + z1_ref[:half] + (z2_ref[:half] + z3_ref[:half])
    out_ref[:half] = upper
    packed_ref[...] = upper[: packed_ref.shape[0]]
    out_ref[half:] = lower + z1_ref[half:] + (z2_ref[half:] + z3_ref[half:])


def summed(kernel, data, shapes):
    return pl.pallas_call(
        kernel,
        out_shape=[jax.ShapeDtypeStruct(shape, F32) for shape in shapes],
        in_specs=[vmem_spec()] * len(data),
        out_specs=[vmem_spec()] * len(shapes),
        compiler_params=params(),
    )(*data)


def bin_sums(keep):
    _, rows, wide = keep.shape
    half = rows // 2
    data = [keep]
    a, b = summed(first_kernel, data, [(8, half, wide)] * 2)
    data += [partner(a, U_BITS), partner(b, V_BITS)]
    a, b = summed(second_kernel, data, [(4, half, wide)] * 2)
    data += [partner(a, V_BITS), partner(b, U_BITS)]
    sends = summed(line_kernel, data, [(rows, wide)] * 3)
    data += [partner(value, (8 * flip, 8 * flip)) for flip, value in zip(FLIPS, sends)]
    own, packed = summed(own_kernel, data, [(rows, wide), (rows // 5, wide)])
    bit = 32
    while bit < lax.axis_size("range"):
        own = own + partner(own, (bit, bit))
        packed = packed + partner(packed, (bit, bit))
        bit *= 2
    return own, packed


def from_bin(value, offset):
    count = lax.axis_size("range")
    pairs = []
    for i in range(count):
        target = index_of((bin_of(i) - offset) % 32) | (i & ~31)
        pairs.append((i, target))
    return lax.ppermute(value, "range", pairs)


def turn(value):
    half = value.shape[1] // 2
    rolled = pltpu.roll(value, half, 1)
    return jnp.where(iota(value.shape, 1) < half, -rolled, rolled)


def embed(value):
    return jnp.concatenate([value, turn(value)], axis=0)


def mul(a, b):
    return jnp.dot(a, embed(b), precision=lax.Precision.HIGHEST, preferred_element_type=F32)


def mul_conj(a, b):
    half = a.shape[1] // 2
    stacked = jnp.concatenate([a, -turn(a)], axis=0)
    both = dot_nt(stacked, b, lax.Precision.HIGHEST)
    rows = a.shape[0]
    return jnp.concatenate([both[:rows], both[rows:]], axis=1)


def conj_mul(a, b):
    half = a.shape[1] // 2
    both = lax.dot_general(
        a, b, (((0,), (0,)), ((), ())),
        precision=lax.Precision.HIGHEST, preferred_element_type=F32,
    )
    return both[:half] - turn(both[half:])


def reciprocal(x):
    value = pl.reciprocal(x, approx=True)
    for _ in range(2):
        value = value * (2.0 - x * value)
    return value


def pivot_inverse(p):
    def times(x, y):
        return x[0] * y[0] - x[1] * y[1], x[0] * y[1] + x[1] * y[0]

    def conj(x):
        return x[0], -x[1]

    def plus(x, y):
        return x[0] + y[0], x[1] + y[1]

    def scaled(x, s):
        return x[0] * s, x[1] * s

    def square(x):
        return x[0] * x[0] + x[1] * x[1]

    def two(a, b, d):
        inv = reciprocal(a * d - square(b))
        return d * inv, scaled(b, -inv), a * inv

    a, d = p[0][0], p[1][1]
    b = p[0][1]
    ea, eb, ed = two(a, b, d)
    f = [[p[0][2], p[0][3]], [p[1][2], p[1][3]]]
    w = [
        [plus(scaled(f[0][j], ea), times(eb, f[1][j])) for j in range(2)],
        [plus(times(conj(eb), f[0][j]), scaled(f[1][j], ed)) for j in range(2)],
    ]

    def inner(i, j):
        return plus(times(conj(f[0][i]), w[0][j]), times(conj(f[1][i]), w[1][j]))

    ha = p[2][2] - inner(0, 0)[0]
    hd = p[3][3] - inner(1, 1)[0]
    cross = inner(0, 1)
    hb = (p[2][3][0] - cross[0], p[2][3][1] - cross[1])
    ga, gb, gd = two(ha, hb, hd)
    v = [
        [
            plus(scaled(w[i][0], ga), times(w[i][1], conj(gb))),
            plus(times(w[i][0], gb), scaled(w[i][1], gd)),
        ]
        for i in range(2)
    ]
    top = [
        [plus(times(v[i][0], conj(w[j][0])), times(v[i][1], conj(w[j][1]))) for j in range(2)]
        for i in range(2)
    ]
    zero = None
    out = [[None] * 4 for _ in range(4)]
    out[0][0] = (ea + top[0][0][0], zero)
    out[1][1] = (ed + top[1][1][0], zero)
    out[0][1] = plus(eb, top[0][1])
    out[2][2], out[3][3], out[2][3] = (ga, zero), (gd, zero), gb
    for i in range(2):
        for j in range(2):
            out[i][2 + j] = (-v[i][j][0], -v[i][j][1])
    for i in range(4):
        for j in range(i):
            out[i][j] = conj(out[j][i])
    return out


def invert(matrix):
    chans, width = matrix.shape
    sub = 8
    tiles = [matrix[t * sub : (t + 1) * sub, :] for t in range(chans // sub)]
    lane = iota((sub, width), 1)
    row = iota((sub, width), 0)
    first_half = lane < chans

    def spin(value):
        rolled = pltpu.roll(value, chans, 1)
        return jnp.where(first_half, -rolled, rolled)

    def column(value, k):
        return jnp.broadcast_to(value[:, k : k + 1], (sub, width))

    def combine(terms):
        while len(terms) > 1:
            terms = [
                terms[i] + terms[i + 1] if i + 1 < len(terms) else terms[i]
                for i in range(0, len(terms), 2)
            ]
        return terms[0]

    for k in range(0, chans, 4):
        t, r = divmod(k, sub)
        lines = [jnp.broadcast_to(tiles[t][r + i : r + i + 1, :], (sub, width)) for i in range(4)]
        pivot = [[None] * 4 for _ in range(4)]
        for i in range(4):
            pivot[i][i] = column(lines[i], k + i)
            for j in range(i + 1, 4):
                pivot[i][j] = column(lines[i], k + j), column(lines[i], chans + k + j)
        low = jnp.bitwise_and(lane, chans - 1)
        cleared = (low >= k) & (low < k + 4)
        unit = [
            jnp.where(cleared, jnp.where(lane == k + i, 1.0, 0.0), lines[i]) for i in range(4)
        ]
        spun = [spin(u) for u in unit]
        p = pivot_inverse(pivot)
        fresh_lines, fresh_spun = [], []
        for i in range(4):
            terms, other = [], []
            for j in range(4):
                re, im = p[i][j]
                terms.append(re * unit[j])
                other.append(re * spun[j])
                if im is not None:
                    terms.append(im * spun[j])
                    other.append(-(im * unit[j]))
            fresh_lines.append(combine(terms))
            fresh_spun.append(combine(other))
        fresh = []
        for s, tile in enumerate(tiles):
            terms = []
            for i in range(4):
                terms.append(column(tile, k + i) * fresh_lines[i])
                terms.append(column(tile, chans + k + i) * fresh_spun[i])
            value = jnp.where(cleared, 0.0, tile) - combine(terms)
            if s == t:
                for i in range(4):
                    value = jnp.where(row == r + i, fresh_lines[i], value)
            fresh.append(value)
        tiles = fresh
    return jnp.concatenate(tiles, axis=0)


def unpacked(ref, scale):
    half, wide = ref.shape[0], ref.shape[1]
    piece = ref[...] * scale
    swapped = pltpu.roll(piece, wide // 2, 1)
    return jnp.concatenate([piece, swapped], axis=0)[:, : wide // 2]


def hermitian(mixed, across):
    i, j = iota(mixed.shape, 0), iota(mixed.shape, 1)
    real_part = jnp.where(i >= j, mixed, across)
    imag_part = jnp.where(i < j, mixed, jnp.where(i > j, -across, 0.0))
    return jnp.concatenate([real_part, imag_part], axis=1)


def middle_kernel(total, packed_ref, steer_ref, inv_ref, t_ref):
    chans = inv_ref.shape[0]
    mixed = unpacked(packed_ref, F32(1.0 / total))
    twice = jnp.concatenate([mixed, mixed], axis=1)
    across = jnp.concatenate([twice, twice], axis=0).T[:chans, :chans]
    inverse = invert(hermitian(mixed, across))
    inv_ref[...] = inverse
    t_ref[...] = mul(steer_ref[...], inverse)


def outer_kernel(total, own_ref, left_ref, right_ref, steer_ref, inv_ref, t_ref, out_ref,
                 work, keep):
    chans = inv_ref.shape[0]
    scale = F32(1.0 / total)
    half = chans // 2
    m_left = unpacked(left_ref.at[:half], scale)
    m_right = unpacked(right_ref, scale)
    ml = left_ref[half : half + chans] * scale
    rl = left_ref[half + chans :] * scale
    rm = own_ref[half : half + chans] * scale
    pair = jnp.concatenate([m_left, m_right], axis=1)
    square = jnp.concatenate([pair, pair], axis=0).T
    inv_mid = inv_ref[...]
    t = t_ref[...]
    h = mul(inv_mid, ml)
    g = mul(rm, inv_mid)
    work[...] = hermitian(m_left, square[:chans, :chans]) - conj_mul(ml, h)
    s_rl = rl - mul(rm, h)
    s_rr = hermitian(m_right, square[chans:, :chans]) - mul_conj(g, rm)
    rhs_left = -mul(t, ml)
    rhs_right = -mul_conj(t, rm)
    keep[0] = s_rl
    keep[1] = s_rr
    keep[2] = h
    keep[3] = g
    keep[4, 0:BEAMS] = rhs_left
    keep[4, BEAMS : 2 * BEAMS] = rhs_right

    @pl.loop(0, 2)
    def _(stage):
        work[...] = invert(work[...])

        @pl.when(stage == 0)
        def _():
            inverse = work[...]
            s_rl = keep[0]
            both = mul(jnp.concatenate([s_rl, keep[4, 0:BEAMS]], axis=0), inverse)
            k, y_left = both[:chans], both[chans:]
            work[...] = keep[1] - mul_conj(k, s_rl)
            keep[0] = k
            keep[4, BEAMS : 2 * BEAMS] = keep[4, BEAMS : 2 * BEAMS] - mul_conj(y_left, s_rl)
            keep[4, 0:BEAMS] = y_left
            keep[4, 2 * BEAMS : 3 * BEAMS] = t_ref[...] - mul_conj(y_left, keep[2])
            keep[3] = keep[3] - mul_conj(k, keep[2])

        @pl.when(stage == 1)
        def _():
            y_right = mul(keep[4, BEAMS : 2 * BEAMS], work[...])
            y_left = keep[4, 0:BEAMS] - mul(y_right, keep[0])
            y_mid = keep[4, 2 * BEAMS : 3 * BEAMS] - mul(y_right, keep[3])
            quad = jnp.sum(steer_ref[...] * y_mid, axis=1, keepdims=True)
            y = jnp.concatenate([y_left, y_mid, y_right], axis=1) / jnp.sqrt(quad)
            real_lane = lax.rem(iota(y.shape, 1), 2 * chans) < chans
            mine = jnp.where(real_lane, y, -y).astype(BF16)
            out_ref[...] = mine


def steering(chans):
    index = np.arange(chans)
    sines = -0.8 + 1.6 * np.arange(BEAMS) / (BEAMS - 1)
    angle = math.pi * sines[:, None] * index[None, :]
    return np.concatenate([np.cos(angle), -np.sin(angle)], axis=1).astype(np.float32)


def solve_middle(packed, steer, total):
    half, wide = packed.shape
    return pl.pallas_call(
        functools.partial(middle_kernel, total),
        out_shape=[
            jax.ShapeDtypeStruct((2 * half, wide), F32),
            jax.ShapeDtypeStruct((BEAMS, wide), F32),
        ],
        in_specs=[vmem_spec()] * 2,
        out_specs=[vmem_spec()] * 2,
        compiler_params=params(),
    )(packed, steer)


def solve_outer(own, left, right, steer, inverse, t, total):
    chans, wide = inverse.shape
    return pl.pallas_call(
        functools.partial(outer_kernel, total),
        out_shape=jax.ShapeDtypeStruct((BEAMS, 3 * wide), BF16),
        in_specs=[vmem_spec()] * 6,
        out_specs=vmem_spec(),
        scratch_shapes=[pltpu.VMEM((chans, wide), F32), pltpu.VMEM((5, chans, wide), F32)],
        compiler_params=params(),
    )(own, left, right, steer, inverse, t)


def beam_kernel(bin_ref, block_ref, beam_ref, owner_ref, s0_ref, s1_ref, w_ref, out_ref,
                both_ref, rows_ref, seen_ref):
    bins, wide, gates = s0_ref.shape
    devices = seen_ref.shape[0]
    count = bin_ref.shape[0]
    rows_ref[...] = jnp.zeros_like(rows_ref)

    @pl.loop(0, devices)
    def _(i):
        seen_ref[i] = 0

    w = w_ref[...].astype(F32).reshape(bins * BEAMS, 3 * wide)
    for k in range(3):
        lanes = slice(k * wide, (k + 1) * wide)
        part = w[:, lanes]
        both_ref[:, 0:BEAMS, lanes] = part.reshape(bins, BEAMS, wide)
        both_ref[:, BEAMS:, lanes] = turn(part).reshape(bins, BEAMS, wide)

    def detection(j, carry):
        bin_id = bin_ref[j]
        beam_id = beam_ref[j]
        owner = owner_ref[j]
        rank = seen_ref[owner]
        seen_ref[owner] = rank + 1
        core, x, y, z = parts_of(index_of(bin_id))
        left = both_ref[core * 16 + x * 8 + y * 4 + z].astype(BF16)
        bands = [lax.rem(bin_id + bins - 1 + k, bins) for k in range(3)]
        first = block_ref[j] == 0
        window = jnp.concatenate(
            [jnp.where(first, s0_ref[b], s1_ref[b]) for b in bands], axis=0
        )
        both = dot(left, window)
        line = jnp.concatenate([both[:BEAMS], both[BEAMS:]], axis=1)
        chosen = jnp.where(iota(line.shape, 0) == beam_id, line, 0.0)
        row = owner * CAP + rank
        rows_ref[pl.ds(row, 1), :] = jnp.sum(chosen, axis=0, keepdims=True)
        return carry

    lax.fori_loop(0, count, detection, 0, unroll=32)
    out_ref[...] = rows_ref[...].astype(BF16)


def beam_rows(det_bin, det_block, det_beam, owners, s0, s1, weight, devices):
    bins, wide, gates = s0.shape
    return pl.pallas_call(
        beam_kernel,
        out_shape=jax.ShapeDtypeStruct((devices * CAP, 2 * gates), BF16),
        in_specs=[smem_spec()] * 4 + [vmem_spec()] * 3,
        out_specs=vmem_spec(),
        scratch_shapes=[
            pltpu.VMEM((bins, 2 * BEAMS, 3 * wide), F32),
            pltpu.VMEM((devices * CAP, 2 * gates), F32),
            pltpu.SMEM((devices,), jnp.int32),
        ],
        compiler_params=params(),
    )(det_bin, det_block, det_beam, owners, s0, s1, weight)


def gathered(value, bins):
    count = lax.axis_size("range")
    for members in ((0, 8, 16, 24), (0, 4), (0, 2), (0, 1)):
        groups = []
        for first in range(0, count, bins):
            seen = set()
            for i in range(first, first + bins):
                if i not in seen:
                    group = [i + member for member in members]
                    seen.update(group)
                    groups.append(group)
        value = lax.all_gather(value, "range", axis_index_groups=groups)
    return value


def on_device(raw, replica, det_bin, det_block, det_beam, det_owner):
    devices = lax.axis_size("range")
    _, chans, pulses, gates = raw.shape
    bins = pulses
    flat = raw.reshape(2, chans * pulses, gates)
    before = [(source, source - 1) for source in range(1, devices)]
    *slices, mark = first_gates(flat)
    halos = [lax.ppermute(value, "range", before) for value in slices]
    table = doppler_matrix(pulses, 8)
    s0, local, matrix, *sent = spectra_first(flat, replica, table, pulses, mark)
    beside0 = [partner(value, (1, 1)) for value in sent]
    sums = cross([s0], bins)
    sums = cross(beside0, bins, sums)
    s1, send1 = spectra_last(local, halos, matrix, table, pulses, sums)
    beside1 = partner(send1, (1, 1))
    sums = cross([s1], bins, sums)
    sums = cross([beside1], bins, sums, last=True)
    own, packed = bin_sums(sums)
    total = gates * devices
    steer = steering(chans)
    left = from_bin(own, -1)
    right = from_bin(packed, 1)
    inverse, t = solve_middle(packed, steer, total)
    mine = solve_outer(own, left, right, steer, inverse, t, total)
    weight = gathered(mine, bins).reshape(bins, BEAMS, mine.shape[1])
    outgoing = beam_rows(
        det_bin, det_block, det_beam, det_owner[:, 0],
        s0.reshape(bins, 2 * chans, BLOCK), s1.reshape(bins, 2 * chans, BLOCK), weight, devices,
    )
    incoming = lax.all_to_all(
        outgoing.reshape(devices, CAP, 2 * BLOCK), "range", split_axis=0, concat_axis=0, tiled=True
    )
    return incoming.astype(F32).reshape(devices * CAP, 2 * BLOCK)


def solution(mesh):
    in_specs = (
        P(None, None, None, "range"),
        P(),
        P("range"),
        P("range"),
        P("range"),
        P("range", None),
    )
    out_specs = P("range", None)
    return jax.shard_map(
        on_device, mesh=mesh, in_specs=in_specs, out_specs=out_specs, check_vma=False
    )
```

```python
import functools
import math

import jax
import jax.numpy as jnp
import ml_dtypes
import numpy as np
from jax import lax
from jax.experimental import pallas as pl
from jax.experimental.pallas import tpu as pltpu
from jax.sharding import PartitionSpec as P

BLOCK = 128
BEAMS = 8
CAP = 2

F32 = jnp.float32
BF16 = jnp.bfloat16
VMEM = pltpu.VMEM
MIB = 1024 * 1024
NT = (((1,), (1,)), ((), ()))


def vmem_spec():
    return pl.BlockSpec(memory_space=VMEM)


def smem_spec():
    return pl.BlockSpec(memory_space=pltpu.SMEM)


def hbm_spec():
    return pl.BlockSpec(memory_space=pltpu.HBM)


SHORT = pl.CostEstimate(flops=1, bytes_accessed=1, transcendentals=0)


def params(mib=16):
    return pltpu.CompilerParams(vmem_limit_bytes=int(mib * MIB))


def dot(a, b):
    return jnp.dot(a, b, preferred_element_type=F32)


def dot_nt(a, b, precision=None):
    return lax.dot_general(a, b, NT, precision=precision, preferred_element_type=F32)


def iota(shape, axis):
    return lax.broadcasted_iota(jnp.int32, shape, axis)


def halo_kernel(raw_ref, a_ref, b_ref, mark_ref, sems):
    mark_ref[...] = jnp.zeros_like(mark_ref)
    count = sems.shape[0] // 2
    size = a_ref.shape[1] // count
    copies = []
    for part, out_ref in enumerate((a_ref, b_ref)):
        for j in range(count):
            start = part * a_ref.shape[1] + j * size
            copies.append(
                pltpu.make_async_copy(
                    raw_ref.at[:, start : start + size, :BLOCK],
                    out_ref.at[:, j * size : (j + 1) * size, :],
                    sems.at[part * count + j],
                )
            )
    for copy in copies:
        copy.start()
    for copy in copies:
        copy.wait()


def first_gates(raw):
    half = jax.ShapeDtypeStruct((2, raw.shape[1] // 2, BLOCK), BF16)
    return pl.pallas_call(
        halo_kernel,
        out_shape=[half, half, jax.ShapeDtypeStruct((8, 128), F32)],
        in_specs=[hbm_spec()],
        out_specs=[vmem_spec()] * 3,
        scratch_shapes=[pltpu.SemaphoreType.DMA((8,))],
        compiler_params=params(63),
    )(raw)


def correlation_matrix(rep_ref, out_ref):
    taps = rep_ref.shape[1]
    base = rep_ref[...].astype(F32)
    row = iota((taps, 2 * taps), 0)
    parts = []
    for i in range(2):
        line = jnp.concatenate([base[i : i + 1], jnp.zeros((1, taps), F32)], axis=1)
        skew = jnp.broadcast_to(line, (taps, 2 * taps))
        bit = 1
        while bit < taps:
            skew = jnp.where((row & bit) != 0, pltpu.roll(skew, bit, 1), skew)
            bit *= 2
        parts.append(skew.T)
    real_part, imag_part = parts
    out_ref[0] = jnp.concatenate([real_part, -imag_part], axis=1).astype(BF16)
    out_ref[1] = jnp.concatenate([imag_part, real_part], axis=1).astype(BF16)


def doppler_matrix(pulses, group):
    index = np.arange(pulses)
    angle = 2.0 * math.pi / pulses * (index[:, None] * index[None, :] % pulses)
    cosine = np.cos(angle) * pulses**-0.5
    sine = np.sin(angle) * pulses**-0.5
    table = np.stack([np.stack([cosine, -sine], 1), np.stack([sine, cosine], 1)], 0)
    full = np.einsum("ipod,ce->dociep", table, np.eye(group))
    shape = (pulses * 2 * group, 2 * group * pulses)
    return full.reshape(shape).astype(ml_dtypes.bfloat16)


def doppler_rows(total, dft):
    compressed = total.astype(BF16)
    rows, wide = compressed.shape
    half, gates = rows // 2, wide // 2
    stacked = jnp.concatenate(
        [
            jnp.concatenate([compressed[:half, :gates], compressed[half:, :gates]], axis=1),
            jnp.concatenate([compressed[:half, gates:], compressed[half:, gates:]], axis=1),
        ],
        axis=0,
    )
    both = dot(dft, stacked)
    lines = both.shape[0] // 8
    joined = jnp.concatenate(
        [both[:, :gates].reshape(lines, 8, gates), both[:, gates:].reshape(lines, 8, gates)],
        axis=1,
    )
    return joined.astype(BF16)


GROUP = 16


def half_of_bins(bins, mine):
    core = lax.axis_index("range") & 1
    return (core if mine else 1 - core) * (bins // 2)


def sent_bins(bins):
    return bins // 2 + 2


def spectra_first_kernel(raw_ref, rep_ref, dft_ref, _, s_ref, local_ref, taps_ref, *rest):
    *send_refs, buf, sems = rest
    bins, _, chans, gates = s_ref.shape
    size = GROUP * bins
    copies = [
        pltpu.make_async_copy(
            raw_ref.at[:, j * size : (j + 1) * size, :],
            buf.at[:, j * size : (j + 1) * size, :],
            sems.at[j],
        )
        for j in range(chans // GROUP)
    ]
    for copy in copies:
        copy.start()
    correlation_matrix(rep_ref, taps_ref)
    for j, copy in enumerate(copies):
        copy.wait()
        rows = slice(j * size, (j + 1) * size)
        total = dot(buf[0, rows, :], taps_ref[0]) + dot(buf[1, rows, :], taps_ref[1])
        out = doppler_rows(total, dft_ref[...])
        s_ref[:, :, j * GROUP : (j + 1) * GROUP, :] = out.reshape(bins, 2, GROUP, gates)
        later = jnp.concatenate([buf[0, rows, gates:], buf[1, rows, gates:]], axis=1)
        near = jnp.concatenate([taps_ref[0, :gates, :], taps_ref[1, :gates, :]], axis=0)
        local_ref[rows, :] = dot(later, near)
    base = half_of_bins(bins, False)
    half = chans // 2
    for part, send_ref in enumerate(send_refs):
        for k in range(send_ref.shape[0]):
            send_ref[k] = s_ref[lax.rem(base + k, bins), :, part * half : (part + 1) * half, :]


def spectra_last_kernel(part, local_ref, halo_ref, taps_ref, dft_ref, _, s_ref, send_ref):
    bins, _, chans, gates = s_ref.shape
    size = GROUP * bins
    far = jnp.concatenate([taps_ref[0, gates:, :], taps_ref[1, gates:, :]], axis=0)
    for j in range(chans // GROUP):
        rows = slice(j * size, (j + 1) * size)
        later = jnp.concatenate([halo_ref[0, rows, :], halo_ref[1, rows, :]], axis=1)
        start = part * chans * bins + j * size
        out = doppler_rows(local_ref[start : start + size, :] + dot(later, far), dft_ref[...])
        s_ref[:, :, j * GROUP : (j + 1) * GROUP, :] = out.reshape(bins, 2, GROUP, gates)
    base = half_of_bins(bins, False)
    for k in range(send_ref.shape[0]):
        send_ref[k] = s_ref[lax.rem(base + k, bins)]


def spectra_first(raw, replica, table, pulses, mark):
    _, rows, gates = raw.shape
    chans = rows // pulses
    taps = replica.shape[1]
    return pl.pallas_call(
        spectra_first_kernel,
        out_shape=[
            jax.ShapeDtypeStruct((pulses, 2, chans, BLOCK), BF16),
            jax.ShapeDtypeStruct((rows, 2 * BLOCK), F32),
            jax.ShapeDtypeStruct((2, 2 * taps, 2 * taps), BF16),
        ]
        + [jax.ShapeDtypeStruct((sent_bins(pulses), 2, chans // 2, BLOCK), BF16)] * 2,
        in_specs=[hbm_spec(), vmem_spec(), vmem_spec(), pl.BlockSpec(memory_space=pl.ANY)],
        out_specs=[vmem_spec()] * 5,
        scratch_shapes=[
            pltpu.VMEM(raw.shape, BF16),
            pltpu.SemaphoreType.DMA((chans // GROUP,)),
        ],
        compiler_params=params(),
        cost_estimate=SHORT,
    )(raw, replica, table, mark)


def spectra_last(part, local, halo, matrix, table, pulses, sums):
    chans = halo.shape[1] // pulses
    return pl.pallas_call(
        functools.partial(spectra_last_kernel, part),
        out_shape=[
            jax.ShapeDtypeStruct((pulses, 2, chans, BLOCK), BF16),
            jax.ShapeDtypeStruct((sent_bins(pulses), 2, chans, BLOCK), BF16),
        ],
        in_specs=[vmem_spec()] * 4 + [pl.BlockSpec(memory_space=pl.ANY)],
        out_specs=[vmem_spec()] * 2,
        compiler_params=params(),
        cost_estimate=SHORT,
    )(local, halo, matrix, table, sums)


def cross_kernel(count_refs, *refs):
    s_refs, rest = refs[:count_refs], refs[count_refs:]
    before_ref = rest[0] if len(rest) == 2 else None
    out_ref = rest[-1]
    held, _, _, gates = s_refs[0].shape
    chans = sum(ref.shape[2] for ref in s_refs)
    count = out_ref.shape[0]
    base = half_of_bins(held, True) if held == 2 * count else 0

    def write(e, block):
        out_ref[e] = block if before_ref is None else block + before_ref[e]

    @pl.loop(0, count // 2, unroll=2)
    def _(step):
        e = step * 2
        each = []
        for k in range(4):
            where = lax.rem(base + e + k, held)
            each.append(
                [jnp.concatenate([ref[where, o] for ref in s_refs], axis=0) for o in range(2)]
            )
        left = jnp.concatenate(
            [jnp.concatenate([re, im], axis=1) for re, im in each], axis=0
        )
        right = jnp.concatenate(
            [
                jnp.concatenate(pieces, axis=1)
                for re, im in each[:2]
                for pieces in ((re, im), (-im, re))
            ],
            axis=0,
        )
        both = dot_nt(left, right)
        write(e, both[: 3 * chans, : 2 * chans])
        write(e + 1, both[chans:, 2 * chans :])


def cross(spectra, bins, before=None):
    chans = sum(value.shape[2] for value in spectra)
    data = spectra if before is None else spectra + [before]
    return pl.pallas_call(
        functools.partial(cross_kernel, len(spectra)),
        out_shape=jax.ShapeDtypeStruct((bins // 2, 3 * chans, 2 * chans), F32),
        in_specs=[vmem_spec()] * len(data),
        out_specs=vmem_spec(),
        compiler_params=params(),
        cost_estimate=SHORT,
    )(*data)


U_BITS, V_BITS = (2, 4), (4, 2)


def partner(value, bits):
    count = lax.axis_size("range")
    return lax.ppermute(value, "range", [(i, i ^ bits[i & 1]) for i in range(count)])


def slot_of(core, x, y, z):
    return (4 * z + ((2 * y + (x ^ y)) ^ (3 * (z & 1)))) ^ (15 * core)


def parts_of(index):
    return index & 1, (index >> 1) & 1, (index >> 2) & 1, (index >> 3) & 3


def bin_of(index):
    core, x, y, z = parts_of(index)
    return core * 16 + slot_of(core, x, y, z)


def index_of(bin_id):
    core = bin_id >> 4
    path = (bin_id & 15) ^ (15 * core)
    z = path >> 2
    turned = (path & 3) ^ (3 * (z & 1))
    y = turned >> 1
    x = (turned & 1) ^ y
    return z * 8 + y * 4 + x * 2 + core


def uv_parts():
    core, x, y, z = parts_of(lax.axis_index("range"))
    return core, jnp.where(core == 0, x, y), jnp.where(core == 0, y, x), z


def uv_slot(core, u, v, z):
    return slot_of(core, jnp.where(core == 0, u, v), jnp.where(core == 0, v, u), z)


def packed(block):
    chans = block.shape[0]
    lower = iota((chans, chans), 0) >= iota((chans, chans), 1)
    swapped = pltpu.roll(block, chans, 1)
    mixed = jnp.where(lower, block[:, :chans], swapped[:, :chans])
    return jnp.concatenate([mixed[: chans // 2], mixed[chans // 2 :]], axis=1)


def sent_rows(keep_ref):
    return 5 * keep_ref.shape[1] // 6


def upper_rows(keep_ref, e):
    block = keep_ref.shape[1] // 3
    end = sent_rows(keep_ref) // 2 + block // 2
    return jnp.concatenate([packed(keep_ref[e, :block]), keep_ref[e, block:end]], axis=0)


def lower_rows(keep_ref, e):
    return keep_ref[e, sent_rows(keep_ref) // 2 + keep_ref.shape[1] // 6 :]


def first_kernel(keep_ref, a_ref, b_ref):
    core, u, v, z = uv_parts()
    for k in range(8):
        a_ref[k] = upper_rows(keep_ref, uv_slot(core, 1 - u, k // 4, k % 4))
        b_ref[k] = lower_rows(keep_ref, uv_slot(core, k // 4, 1 - v, k % 4))


def second_kernel(keep_ref, a1_ref, b1_ref, a_ref, b_ref):
    core, u, v, z = uv_parts()
    for k in range(4):
        e = uv_slot(core, u, 1 - v, k)
        a_ref[k] = upper_rows(keep_ref, e) + a1_ref[(1 - v) * 4 + k]
        e = uv_slot(core, 1 - u, v, k)
        b_ref[k] = lower_rows(keep_ref, e) + b1_ref[(1 - u) * 4 + k]


def line_sum(keep_ref, a1_ref, b1_ref, a2_ref, b2_ref, flip):
    core, u, v, z = uv_parts()
    z = z ^ flip
    e = uv_slot(core, u, v, z)
    upper = upper_rows(keep_ref, e) + a1_ref[v * 4 + z] + a2_ref[z]
    lower = lower_rows(keep_ref, e) + b1_ref[u * 4 + z] + b2_ref[z]
    return upper, lower


FLIPS = (2, 3, 1)


def line_kernel(*refs):
    half = sent_rows(refs[0]) // 2
    for flip, out_ref in zip(FLIPS, refs[5:]):
        upper, lower = line_sum(*refs[:5], flip)
        out_ref[:half] = upper
        out_ref[half:] = lower


def own_kernel(*refs):
    z1_ref, z2_ref, z3_ref, out_ref, packed_ref = refs[5:]
    half = sent_rows(refs[0]) // 2
    upper, lower = line_sum(*refs[:5], 0)
    upper = upper + z1_ref[:half] + (z2_ref[:half] + z3_ref[:half])
    out_ref[:half] = upper
    packed_ref[...] = upper[: packed_ref.shape[0]]
    out_ref[half:] = lower + z1_ref[half:] + (z2_ref[half:] + z3_ref[half:])


def summed(kernel, data, shapes):
    return pl.pallas_call(
        kernel,
        out_shape=[jax.ShapeDtypeStruct(shape, F32) for shape in shapes],
        in_specs=[vmem_spec()] * len(data),
        out_specs=[vmem_spec()] * len(shapes),
        compiler_params=params(),
    )(*data)


def bin_sums(keep):
    _, full, wide = keep.shape
    rows = 5 * full // 6
    half = rows // 2
    data = [keep]
    a, b = summed(first_kernel, data, [(8, half, wide)] * 2)
    data += [partner(a, U_BITS), partner(b, V_BITS)]
    a, b = summed(second_kernel, data, [(4, half, wide)] * 2)
    data += [partner(a, V_BITS), partner(b, U_BITS)]
    sends = summed(line_kernel, data, [(rows, wide)] * 3)
    data += [partner(value, (8 * flip, 8 * flip)) for flip, value in zip(FLIPS, sends)]
    own, packed = summed(own_kernel, data, [(rows, wide), (rows // 5, wide)])
    bit = 32
    while bit < lax.axis_size("range"):
        own = own + partner(own, (bit, bit))
        packed = packed + partner(packed, (bit, bit))
        bit *= 2
    return own, packed


def from_bin(value, offset):
    count = lax.axis_size("range")
    pairs = []
    for i in range(count):
        target = index_of((bin_of(i) - offset) % 32) | (i & ~31)
        pairs.append((i, target))
    return lax.ppermute(value, "range", pairs)


def turn(value):
    half = value.shape[1] // 2
    rolled = pltpu.roll(value, half, 1)
    return jnp.where(iota(value.shape, 1) < half, -rolled, rolled)


def embed(value):
    return jnp.concatenate([value, turn(value)], axis=0)


def mul(a, b):
    return jnp.dot(a, embed(b), precision=lax.Precision.HIGHEST, preferred_element_type=F32)


def mul_conj(a, b):
    half = a.shape[1] // 2
    stacked = jnp.concatenate([a, -turn(a)], axis=0)
    both = dot_nt(stacked, b, lax.Precision.HIGHEST)
    rows = a.shape[0]
    return jnp.concatenate([both[:rows], both[rows:]], axis=1)


def conj_mul(a, b):
    half = a.shape[1] // 2
    both = lax.dot_general(
        a, b, (((0,), (0,)), ((), ())),
        precision=lax.Precision.HIGHEST, preferred_element_type=F32,
    )
    return both[:half] - turn(both[half:])


def reciprocal(x):
    value = pl.reciprocal(x, approx=True)
    for _ in range(2):
        value = value * (2.0 - x * value)
    return value


def pivot_inverse(p):
    def times(x, y):
        return x[0] * y[0] - x[1] * y[1], x[0] * y[1] + x[1] * y[0]

    def conj(x):
        return x[0], -x[1]

    def plus(x, y):
        return x[0] + y[0], x[1] + y[1]

    def scaled(x, s):
        return x[0] * s, x[1] * s

    def square(x):
        return x[0] * x[0] + x[1] * x[1]

    def two(a, b, d):
        inv = reciprocal(a * d - square(b))
        return d * inv, scaled(b, -inv), a * inv

    a, d = p[0][0], p[1][1]
    b = p[0][1]
    ea, eb, ed = two(a, b, d)
    f = [[p[0][2], p[0][3]], [p[1][2], p[1][3]]]
    w = [
        [plus(scaled(f[0][j], ea), times(eb, f[1][j])) for j in range(2)],
        [plus(times(conj(eb), f[0][j]), scaled(f[1][j], ed)) for j in range(2)],
    ]

    def inner(i, j):
        return plus(times(conj(f[0][i]), w[0][j]), times(conj(f[1][i]), w[1][j]))

    ha = p[2][2] - inner(0, 0)[0]
    hd = p[3][3] - inner(1, 1)[0]
    cross = inner(0, 1)
    hb = (p[2][3][0] - cross[0], p[2][3][1] - cross[1])
    ga, gb, gd = two(ha, hb, hd)
    v = [
        [
            plus(scaled(w[i][0], ga), times(w[i][1], conj(gb))),
            plus(times(w[i][0], gb), scaled(w[i][1], gd)),
        ]
        for i in range(2)
    ]
    top = [
        [plus(times(v[i][0], conj(w[j][0])), times(v[i][1], conj(w[j][1]))) for j in range(2)]
        for i in range(2)
    ]
    zero = None
    out = [[None] * 4 for _ in range(4)]
    out[0][0] = (ea + top[0][0][0], zero)
    out[1][1] = (ed + top[1][1][0], zero)
    out[0][1] = plus(eb, top[0][1])
    out[2][2], out[3][3], out[2][3] = (ga, zero), (gd, zero), gb
    for i in range(2):
        for j in range(2):
            out[i][2 + j] = (-v[i][j][0], -v[i][j][1])
    for i in range(4):
        for j in range(i):
            out[i][j] = conj(out[j][i])
    return out


def invert(matrix, w_ref, l_ref):
    chans, width = matrix.shape
    sub = 8
    tiles = [matrix[t * sub : (t + 1) * sub, :] for t in range(chans // sub)]
    lane = iota((sub, width), 1)
    low = jnp.bitwise_and(lane, chans - 1)
    first_half = lane < chans

    def spin(value):
        rolled = pltpu.roll(value, chans, 1)
        return jnp.where(first_half, -rolled, rolled)

    def column(value, k):
        return jnp.broadcast_to(value[:, k : k + 1], (sub, width))

    def combine(terms):
        while len(terms) > 1:
            terms = [
                terms[i] + terms[i + 1] if i + 1 < len(terms) else terms[i]
                for i in range(0, len(terms), 2)
            ]
        return terms[0]

    for k in range(0, chans, 4):
        t, r = divmod(k, sub)
        lines = [jnp.broadcast_to(tiles[t][r + i : r + i + 1, :], (sub, width)) for i in range(4)]
        pivot = [[None] * 4 for _ in range(4)]
        for i in range(4):
            pivot[i][i] = column(lines[i], k + i)
            for j in range(i + 1, 4):
                pivot[i][j] = column(lines[i], k + j), column(lines[i], chans + k + j)
        cleared = (low >= k) & (low < k + 4)
        unit = [
            jnp.where(cleared, jnp.where(lane == k + i, 1.0, 0.0), lines[i]) for i in range(4)
        ]
        spun = [spin(u) for u in unit]
        p = pivot_inverse(pivot)
        fresh_lines, fresh_spun = [], []
        for i in range(4):
            terms, other = [], []
            for j in range(4):
                re, im = p[i][j]
                terms.append(re * unit[j])
                other.append(re * spun[j])
                if im is not None:
                    terms.append(im * spun[j])
                    other.append(-(im * unit[j]))
            fresh_lines.append(combine(terms))
            fresh_spun.append(combine(other))
            w_ref[k + i : k + i + 1, :] = fresh_lines[i][:1]
            l_ref[k + i : k + i + 1, :] = unit[i][:1]
        for s in range(t if r == 0 else t + 1, len(tiles)):
            tile = tiles[s]
            terms = []
            for i in range(4):
                terms.append(column(tile, k + i) * fresh_lines[i])
                terms.append(column(tile, chans + k + i) * fresh_spun[i])
            tiles[s] = jnp.where(cleared, 0.0, tile) - combine(terms)
    shape = (chans, width)
    done = jnp.bitwise_and(iota(shape, 1), chans - 1) < (iota(shape, 0) // 4 + 1) * 4
    return conj_mul(jnp.where(done, w_ref[...], 0.0), jnp.where(done, l_ref[...], 0.0))


def unpacked(ref, scale):
    half, wide = ref.shape[0], ref.shape[1]
    piece = ref[...] * scale
    swapped = pltpu.roll(piece, wide // 2, 1)
    return jnp.concatenate([piece, swapped], axis=0)[:, : wide // 2]


def hermitian(mixed, across):
    i, j = iota(mixed.shape, 0), iota(mixed.shape, 1)
    real_part = jnp.where(i >= j, mixed, across)
    imag_part = jnp.where(i < j, mixed, jnp.where(i > j, -across, 0.0))
    return jnp.concatenate([real_part, imag_part], axis=1)


def middle_kernel(total, packed_ref, steer_ref, inv_ref, t_ref, w_ref, l_ref):
    chans = inv_ref.shape[0]
    mixed = unpacked(packed_ref, F32(1.0 / total))
    twice = jnp.concatenate([mixed, mixed], axis=1)
    across = jnp.concatenate([twice, twice], axis=0).T[:chans, :chans]
    inverse = invert(hermitian(mixed, across), w_ref, l_ref)
    inv_ref[...] = inverse
    t_ref[...] = mul(steer_ref[...], inverse)


def outer_kernel(total, own_ref, left_ref, right_ref, steer_ref, inv_ref, t_ref, out_ref,
                 work, keep, w_ref, l_ref):
    chans = inv_ref.shape[0]
    scale = F32(1.0 / total)
    half = chans // 2
    m_left = unpacked(left_ref.at[:half], scale)
    m_right = unpacked(right_ref, scale)
    ml = left_ref[half : half + chans] * scale
    rl = left_ref[half + chans :] * scale
    rm = own_ref[half : half + chans] * scale
    pair = jnp.concatenate([m_left, m_right], axis=1)
    square = jnp.concatenate([pair, pair], axis=0).T
    inv_mid = inv_ref[...]
    t = t_ref[...]
    h = mul(inv_mid, ml)
    g = mul(rm, inv_mid)
    work[...] = hermitian(m_left, square[:chans, :chans]) - conj_mul(ml, h)
    s_rl = rl - mul(rm, h)
    s_rr = hermitian(m_right, square[chans:, :chans]) - mul_conj(g, rm)
    rhs_left = -mul(t, ml)
    rhs_right = -mul_conj(t, rm)
    keep[0] = s_rl
    keep[1] = s_rr
    keep[2] = h
    keep[3] = g
    keep[4, 0:BEAMS] = rhs_left
    keep[4, BEAMS : 2 * BEAMS] = rhs_right

    @pl.loop(0, 2)
    def _(stage):
        work[...] = invert(work[...], w_ref, l_ref)

        @pl.when(stage == 0)
        def _():
            inverse = work[...]
            s_rl = keep[0]
            both = mul(jnp.concatenate([s_rl, keep[4, 0:BEAMS]], axis=0), inverse)
            k, y_left = both[:chans], both[chans:]
            work[...] = keep[1] - mul_conj(k, s_rl)
            keep[0] = k
            keep[4, BEAMS : 2 * BEAMS] = keep[4, BEAMS : 2 * BEAMS] - mul_conj(y_left, s_rl)
            keep[4, 0:BEAMS] = y_left
            keep[4, 2 * BEAMS : 3 * BEAMS] = t_ref[...] - mul_conj(y_left, keep[2])
            keep[3] = keep[3] - mul_conj(k, keep[2])

        @pl.when(stage == 1)
        def _():
            y_right = mul(keep[4, BEAMS : 2 * BEAMS], work[...])
            y_left = keep[4, 0:BEAMS] - mul(y_right, keep[0])
            y_mid = keep[4, 2 * BEAMS : 3 * BEAMS] - mul(y_right, keep[3])
            quad = jnp.sum(steer_ref[...] * y_mid, axis=1, keepdims=True)
            y = jnp.concatenate([y_left, y_mid, y_right], axis=1) / jnp.sqrt(quad)
            real_lane = lax.rem(iota(y.shape, 1), 2 * chans) < chans
            mine = jnp.where(real_lane, y, -y).astype(BF16)
            for c in range(out_ref.shape[0]):
                out_ref[c] = mine


def steering(chans):
    index = np.arange(chans)
    sines = -0.8 + 1.6 * np.arange(BEAMS) / (BEAMS - 1)
    angle = math.pi * sines[:, None] * index[None, :]
    return np.concatenate([np.cos(angle), -np.sin(angle)], axis=1).astype(np.float32)


def solve_middle(packed, steer, total):
    half, wide = packed.shape
    return pl.pallas_call(
        functools.partial(middle_kernel, total),
        out_shape=[
            jax.ShapeDtypeStruct((2 * half, wide), F32),
            jax.ShapeDtypeStruct((BEAMS, wide), F32),
        ],
        in_specs=[vmem_spec()] * 2,
        out_specs=[vmem_spec()] * 2,
        scratch_shapes=[pltpu.VMEM((2 * half, wide), F32)] * 2,
        compiler_params=params(),
    )(packed, steer)


def solve_outer(own, left, right, steer, inverse, t, total, copies):
    chans, wide = inverse.shape
    return pl.pallas_call(
        functools.partial(outer_kernel, total),
        out_shape=jax.ShapeDtypeStruct((copies, BEAMS, 3 * wide), BF16),
        in_specs=[vmem_spec()] * 6,
        out_specs=vmem_spec(),
        scratch_shapes=[
            pltpu.VMEM((chans, wide), F32), pltpu.VMEM((5, chans, wide), F32),
            pltpu.VMEM((chans, wide), F32), pltpu.VMEM((chans, wide), F32),
        ],
        compiler_params=params(),
    )(own, left, right, steer, inverse, t)


def beam_kernel(bin_ref, block_ref, beam_ref, owner_ref, s0_ref, upper_ref, lower_ref, w_ref,
                out_ref, both_ref, rows_ref, seen_ref):
    bins, wide, gates = s0_ref.shape
    devices = seen_ref.shape[0]
    count = bin_ref.shape[0]
    rows_ref[...] = jnp.zeros_like(rows_ref)

    @pl.loop(0, devices)
    def _(i):
        seen_ref[i] = 0

    w = w_ref[...].astype(F32).reshape(bins * BEAMS, 3 * wide)
    for k in range(3):
        lanes = slice(k * wide, (k + 1) * wide)
        part = w[:, lanes]
        both_ref[:, 0:BEAMS, lanes] = part.reshape(bins, BEAMS, wide)
        both_ref[:, BEAMS:, lanes] = turn(part).reshape(bins, BEAMS, wide)

    def detection(j, carry):
        bin_id = bin_ref[j]
        beam_id = beam_ref[j]
        owner = owner_ref[j]
        rank = seen_ref[owner]
        seen_ref[owner] = rank + 1
        left = both_ref[index_of(bin_id)].astype(BF16)
        bands = [lax.rem(bin_id + bins - 1 + k, bins) for k in range(3)]
        first = block_ref[j] == 0
        pieces = []
        for b in bands:
            later = [upper_ref[b, 0], lower_ref[b, 0], upper_ref[b, 1], lower_ref[b, 1]]
            pieces.append(jnp.where(first, s0_ref[b], jnp.concatenate(later, axis=0)))
        window = jnp.concatenate(pieces, axis=0)
        both = dot(left, window)
        line = jnp.concatenate([both[:BEAMS], both[BEAMS:]], axis=1)
        chosen = jnp.where(iota(line.shape, 0) == beam_id, line, 0.0)
        row = owner * CAP + rank
        rows_ref[pl.ds(row, 1), :] = jnp.sum(chosen, axis=0, keepdims=True)
        return carry

    lax.fori_loop(0, count, detection, 0, unroll=32)
    out_ref[...] = rows_ref[...].astype(BF16)


def beam_rows(det_bin, det_block, det_beam, owners, s0, s1, weight, devices):
    bins, wide, gates = s0.shape
    return pl.pallas_call(
        beam_kernel,
        out_shape=jax.ShapeDtypeStruct((devices * CAP, 2 * gates), BF16),
        in_specs=[smem_spec()] * 4 + [vmem_spec()] * 4,
        out_specs=vmem_spec(),
        scratch_shapes=[
            pltpu.VMEM((bins, 2 * BEAMS, 3 * wide), F32),
            pltpu.VMEM((devices * CAP, 2 * gates), F32),
            pltpu.SMEM((devices,), jnp.int32),
        ],
        compiler_params=params(),
    )(det_bin, det_block, det_beam, owners, s0, *s1, weight)


def on_device(raw, replica, det_bin, det_block, det_beam, det_owner):
    devices = lax.axis_size("range")
    _, chans, pulses, gates = raw.shape
    bins = pulses
    flat = raw.reshape(2, chans * pulses, gates)
    before = [(source, source - 1) for source in range(1, devices)]
    *slices, mark = first_gates(flat)
    halos = [lax.ppermute(value, "range", before) for value in slices]
    table = doppler_matrix(pulses, 8)
    s0, local, matrix, *sent = spectra_first(flat, replica, table, pulses, mark)
    beside0 = [partner(value, (1, 1)) for value in sent]
    sums = cross([s0], bins)
    sums = cross(beside0, bins, sums)
    s1, beside1 = [], []
    for part, halo in enumerate(halos):
        value, send = spectra_last(part, local, halo, matrix, table, pulses, sums)
        s1.append(value)
        beside1.append(partner(send, (1, 1)))
    sums = cross(s1, bins, sums)
    sums = cross(beside1, bins, sums)
    own, packed = bin_sums(sums)
    total = gates * devices
    steer = steering(chans)
    left = from_bin(own, -1)
    right = from_bin(packed, 1)
    inverse, t = solve_middle(packed, steer, total)
    mine = solve_outer(own, left, right, steer, inverse, t, total, bins)
    groups = [list(range(first, first + bins)) for first in range(0, devices, bins)]
    weight = lax.all_to_all(
        mine, "range", split_axis=0, concat_axis=0, tiled=True,
        axis_index_groups=groups if len(groups) > 1 else None,
    )
    outgoing = beam_rows(
        det_bin, det_block, det_beam, det_owner[:, 0],
        s0.reshape(bins, 2 * chans, BLOCK), s1, weight, devices,
    )
    incoming = lax.all_to_all(
        outgoing.reshape(devices, CAP, 2 * BLOCK), "range", split_axis=0, concat_axis=0, tiled=True
    )
    return incoming.astype(F32).reshape(devices * CAP, 2 * BLOCK)


def solution(mesh):
    in_specs = (
        P(None, None, None, "range"),
        P(),
        P("range"),
        P("range"),
        P("range"),
        P("range", None),
    )
    out_specs = P("range", None)
    return jax.shard_map(
        on_device, mesh=mesh, in_specs=in_specs, out_specs=out_specs, check_vma=False
    )
```

```python
import functools
import math

import jax
import jax.numpy as jnp
import ml_dtypes
import numpy as np
from jax import lax
from jax.experimental import pallas as pl
from jax.experimental.pallas import tpu as pltpu
from jax.sharding import PartitionSpec as P

BLOCK = 128
BEAMS = 8
CAP = 2

F32 = jnp.float32
BF16 = jnp.bfloat16
VMEM = pltpu.VMEM
MIB = 1024 * 1024
NT = (((1,), (1,)), ((), ()))


def vmem_spec():
    return pl.BlockSpec(memory_space=VMEM)


def smem_spec():
    return pl.BlockSpec(memory_space=pltpu.SMEM)


def hbm_spec():
    return pl.BlockSpec(memory_space=pltpu.HBM)


SHORT = pl.CostEstimate(flops=1, bytes_accessed=1, transcendentals=0)


def params(mib=16):
    return pltpu.CompilerParams(vmem_limit_bytes=int(mib * MIB))


def dot(a, b):
    return jnp.dot(a, b, preferred_element_type=F32)


def dot_nt(a, b, precision=None):
    return lax.dot_general(a, b, NT, precision=precision, preferred_element_type=F32)


def iota(shape, axis):
    return lax.broadcasted_iota(jnp.int32, shape, axis)


def halo_kernel(raw_ref, a_ref, b_ref, mark_ref, sems):
    mark_ref[...] = jnp.zeros_like(mark_ref)
    count = sems.shape[0] // 2
    size = a_ref.shape[1] // count
    copies = []
    for part, out_ref in enumerate((a_ref, b_ref)):
        for j in range(count):
            start = part * a_ref.shape[1] + j * size
            copies.append(
                pltpu.make_async_copy(
                    raw_ref.at[:, start : start + size, :BLOCK],
                    out_ref.at[:, j * size : (j + 1) * size, :],
                    sems.at[part * count + j],
                )
            )
    for copy in copies:
        copy.start()
    for copy in copies:
        copy.wait()


def first_gates(raw):
    half = jax.ShapeDtypeStruct((2, raw.shape[1] // 2, BLOCK), BF16)
    return pl.pallas_call(
        halo_kernel,
        out_shape=[half, half, jax.ShapeDtypeStruct((8, 128), F32)],
        in_specs=[hbm_spec()],
        out_specs=[vmem_spec()] * 3,
        scratch_shapes=[pltpu.SemaphoreType.DMA((8,))],
        compiler_params=params(63),
    )(raw)


def correlation_matrix(rep_ref, out_ref):
    taps = rep_ref.shape[1]
    base = rep_ref[...].astype(F32)
    row = iota((taps, 2 * taps), 0)
    parts = []
    for i in range(2):
        line = jnp.concatenate([base[i : i + 1], jnp.zeros((1, taps), F32)], axis=1)
        skew = jnp.broadcast_to(line, (taps, 2 * taps))
        bit = 1
        while bit < taps:
            skew = jnp.where((row & bit) != 0, pltpu.roll(skew, bit, 1), skew)
            bit *= 2
        parts.append(skew.T)
    real_part, imag_part = parts
    out_ref[0] = jnp.concatenate([real_part, -imag_part], axis=1).astype(BF16)
    out_ref[1] = jnp.concatenate([imag_part, real_part], axis=1).astype(BF16)


def doppler_matrix(pulses, group):
    index = np.arange(pulses)
    angle = 2.0 * math.pi / pulses * (index[:, None] * index[None, :] % pulses)
    cosine = np.cos(angle) * pulses**-0.5
    sine = np.sin(angle) * pulses**-0.5
    table = np.stack([np.stack([cosine, -sine], 1), np.stack([sine, cosine], 1)], 0)
    full = np.einsum("ipod,ce->dociep", table, np.eye(group))
    shape = (pulses * 2 * group, 2 * group * pulses)
    return full.reshape(shape).astype(ml_dtypes.bfloat16)


def doppler_rows(total, dft):
    compressed = total.astype(BF16)
    rows, wide = compressed.shape
    half, gates = rows // 2, wide // 2
    stacked = jnp.concatenate(
        [
            jnp.concatenate([compressed[:half, :gates], compressed[half:, :gates]], axis=1),
            jnp.concatenate([compressed[:half, gates:], compressed[half:, gates:]], axis=1),
        ],
        axis=0,
    )
    both = dot(dft, stacked)
    lines = both.shape[0] // 8
    joined = jnp.concatenate(
        [both[:, :gates].reshape(lines, 8, gates), both[:, gates:].reshape(lines, 8, gates)],
        axis=1,
    )
    return joined.astype(BF16)


GROUP = 16


def half_of_bins(bins, mine):
    core = lax.axis_index("range") & 1
    return (core if mine else 1 - core) * (bins // 2)


def sent_bins(bins):
    return bins // 2 + 2


def spectra_first_kernel(raw_ref, rep_ref, dft_ref, _, s_ref, local_ref, taps_ref, *rest):
    *send_refs, buf, sems = rest
    bins, _, chans, gates = s_ref.shape
    size = GROUP * bins
    copies = [
        pltpu.make_async_copy(
            raw_ref.at[:, j * size : (j + 1) * size, :],
            buf.at[:, j * size : (j + 1) * size, :],
            sems.at[j],
        )
        for j in range(chans // GROUP)
    ]
    for copy in copies:
        copy.start()
    correlation_matrix(rep_ref, taps_ref)
    for j, copy in enumerate(copies):
        copy.wait()
        rows = slice(j * size, (j + 1) * size)
        total = dot(buf[0, rows, :], taps_ref[0]) + dot(buf[1, rows, :], taps_ref[1])
        out = doppler_rows(total, dft_ref[...])
        s_ref[:, :, j * GROUP : (j + 1) * GROUP, :] = out.reshape(bins, 2, GROUP, gates)
        later = jnp.concatenate([buf[0, rows, gates:], buf[1, rows, gates:]], axis=1)
        near = jnp.concatenate([taps_ref[0, :gates, :], taps_ref[1, :gates, :]], axis=0)
        local_ref[rows, :] = dot(later, near)
    base = half_of_bins(bins, False)
    half = chans // 2
    for part, send_ref in enumerate(send_refs):
        for k in range(send_ref.shape[0]):
            send_ref[k] = s_ref[lax.rem(base + k, bins), :, part * half : (part + 1) * half, :]


def spectra_last_kernel(part, local_ref, halo_ref, taps_ref, dft_ref, _, s_ref, send_ref):
    bins, _, chans, gates = s_ref.shape
    size = GROUP * bins
    far = jnp.concatenate([taps_ref[0, gates:, :], taps_ref[1, gates:, :]], axis=0)
    for j in range(chans // GROUP):
        rows = slice(j * size, (j + 1) * size)
        later = jnp.concatenate([halo_ref[0, rows, :], halo_ref[1, rows, :]], axis=1)
        start = part * chans * bins + j * size
        out = doppler_rows(local_ref[start : start + size, :] + dot(later, far), dft_ref[...])
        s_ref[:, :, j * GROUP : (j + 1) * GROUP, :] = out.reshape(bins, 2, GROUP, gates)
    base = half_of_bins(bins, False)
    for k in range(send_ref.shape[0]):
        send_ref[k] = s_ref[lax.rem(base + k, bins)]


def spectra_first(raw, replica, table, pulses, mark):
    _, rows, gates = raw.shape
    chans = rows // pulses
    taps = replica.shape[1]
    return pl.pallas_call(
        spectra_first_kernel,
        out_shape=[
            jax.ShapeDtypeStruct((pulses, 2, chans, BLOCK), BF16),
            jax.ShapeDtypeStruct((rows, 2 * BLOCK), F32),
            jax.ShapeDtypeStruct((2, 2 * taps, 2 * taps), BF16),
        ]
        + [jax.ShapeDtypeStruct((sent_bins(pulses), 2, chans // 2, BLOCK), BF16)] * 2,
        in_specs=[hbm_spec(), vmem_spec(), vmem_spec(), pl.BlockSpec(memory_space=pl.ANY)],
        out_specs=[vmem_spec()] * 5,
        scratch_shapes=[
            pltpu.VMEM(raw.shape, BF16),
            pltpu.SemaphoreType.DMA((chans // GROUP,)),
        ],
        compiler_params=params(),
        cost_estimate=SHORT,
    )(raw, replica, table, mark)


def spectra_last(part, local, halo, matrix, table, pulses, sums):
    chans = halo.shape[1] // pulses
    return pl.pallas_call(
        functools.partial(spectra_last_kernel, part),
        out_shape=[
            jax.ShapeDtypeStruct((pulses, 2, chans, BLOCK), BF16),
            jax.ShapeDtypeStruct((sent_bins(pulses), 2, chans, BLOCK), BF16),
        ],
        in_specs=[vmem_spec()] * 4 + [pl.BlockSpec(memory_space=pl.ANY)],
        out_specs=[vmem_spec()] * 2,
        compiler_params=params(),
        cost_estimate=SHORT,
    )(local, halo, matrix, table, sums)


def cross_kernel(count_refs, *refs):
    s_refs, rest = refs[:count_refs], refs[count_refs:]
    before_ref = rest[0] if len(rest) == 2 else None
    out_ref = rest[-1]
    held, _, _, gates = s_refs[0].shape
    chans = sum(ref.shape[2] for ref in s_refs)
    count = out_ref.shape[0]
    base = half_of_bins(held, True) if held == 2 * count else 0

    def write(e, block):
        out_ref[e] = block if before_ref is None else block + before_ref[e]

    @pl.loop(0, count // 2, unroll=2)
    def _(step):
        e = step * 2
        each = []
        for k in range(4):
            where = lax.rem(base + e + k, held)
            each.append(
                [jnp.concatenate([ref[where, o] for ref in s_refs], axis=0) for o in range(2)]
            )
        left = jnp.concatenate(
            [jnp.concatenate([re, im], axis=1) for re, im in each], axis=0
        )
        right = jnp.concatenate(
            [
                jnp.concatenate(pieces, axis=1)
                for re, im in each[:2]
                for pieces in ((re, im), (-im, re))
            ],
            axis=0,
        )
        both = dot_nt(left, right)
        write(e, both[: 3 * chans, : 2 * chans])
        write(e + 1, both[chans:, 2 * chans :])


def cross(spectra, bins, before=None):
    chans = sum(value.shape[2] for value in spectra)
    data = spectra if before is None else spectra + [before]
    return pl.pallas_call(
        functools.partial(cross_kernel, len(spectra)),
        out_shape=jax.ShapeDtypeStruct((bins // 2, 3 * chans, 2 * chans), F32),
        in_specs=[vmem_spec()] * len(data),
        out_specs=vmem_spec(),
        compiler_params=params(),
        cost_estimate=SHORT,
    )(*data)


U_BITS, V_BITS = (2, 4), (4, 2)


def partner(value, bits):
    count = lax.axis_size("range")
    return lax.ppermute(value, "range", [(i, i ^ bits[i & 1]) for i in range(count)])


def slot_of(core, x, y, z):
    return (4 * z + ((2 * y + (x ^ y)) ^ (3 * (z & 1)))) ^ (15 * core)


def parts_of(index):
    return index & 1, (index >> 1) & 1, (index >> 2) & 1, (index >> 3) & 3


def bin_of(index):
    core, x, y, z = parts_of(index)
    return core * 16 + slot_of(core, x, y, z)


def index_of(bin_id):
    core = bin_id >> 4
    path = (bin_id & 15) ^ (15 * core)
    z = path >> 2
    turned = (path & 3) ^ (3 * (z & 1))
    y = turned >> 1
    x = (turned & 1) ^ y
    return z * 8 + y * 4 + x * 2 + core


def uv_parts():
    core, x, y, z = parts_of(lax.axis_index("range"))
    return core, jnp.where(core == 0, x, y), jnp.where(core == 0, y, x), z


def uv_slot(core, u, v, z):
    return slot_of(core, jnp.where(core == 0, u, v), jnp.where(core == 0, v, u), z)


def packed(block):
    chans = block.shape[0]
    lower = iota((chans, chans), 0) >= iota((chans, chans), 1)
    swapped = pltpu.roll(block, chans, 1)
    mixed = jnp.where(lower, block[:, :chans], swapped[:, :chans])
    return jnp.concatenate([mixed[: chans // 2], mixed[chans // 2 :]], axis=1)


def sent_rows(keep_ref):
    return 5 * keep_ref.shape[1] // 6


def upper_rows(keep_ref, e):
    block = keep_ref.shape[1] // 3
    end = sent_rows(keep_ref) // 2 + block // 2
    return jnp.concatenate([packed(keep_ref[e, :block]), keep_ref[e, block:end]], axis=0)


def lower_rows(keep_ref, e):
    return keep_ref[e, sent_rows(keep_ref) // 2 + keep_ref.shape[1] // 6 :]


def first_kernel(keep_ref, a_ref, b_ref):
    core, u, v, z = uv_parts()
    for k in range(8):
        a_ref[k] = upper_rows(keep_ref, uv_slot(core, 1 - u, k // 4, k % 4))
        b_ref[k] = lower_rows(keep_ref, uv_slot(core, k // 4, 1 - v, k % 4))


def second_kernel(keep_ref, a1_ref, b1_ref, a_ref, b_ref):
    core, u, v, z = uv_parts()
    for k in range(4):
        e = uv_slot(core, u, 1 - v, k)
        a_ref[k] = upper_rows(keep_ref, e) + a1_ref[(1 - v) * 4 + k]
        e = uv_slot(core, 1 - u, v, k)
        b_ref[k] = lower_rows(keep_ref, e) + b1_ref[(1 - u) * 4 + k]


def line_sum(keep_ref, a1_ref, b1_ref, a2_ref, b2_ref, flip):
    core, u, v, z = uv_parts()
    z = z ^ flip
    e = uv_slot(core, u, v, z)
    upper = upper_rows(keep_ref, e) + a1_ref[v * 4 + z] + a2_ref[z]
    lower = lower_rows(keep_ref, e) + b1_ref[u * 4 + z] + b2_ref[z]
    return upper, lower


FLIPS = (2, 3, 1)


def line_kernel(*refs):
    half = sent_rows(refs[0]) // 2
    for flip, out_ref in zip(FLIPS, refs[5:]):
        upper, lower = line_sum(*refs[:5], flip)
        out_ref[:half] = upper
        out_ref[half:] = lower


def own_kernel(*refs):
    z1_ref, z2_ref, z3_ref, out_ref, packed_ref = refs[5:]
    half = sent_rows(refs[0]) // 2
    upper, lower = line_sum(*refs[:5], 0)
    upper = upper + z1_ref[:half] + (z2_ref[:half] + z3_ref[:half])
    out_ref[:half] = upper
    packed_ref[...] = upper[: packed_ref.shape[0]]
    out_ref[half:] = lower + z1_ref[half:] + (z2_ref[half:] + z3_ref[half:])


def summed(kernel, data, shapes):
    return pl.pallas_call(
        kernel,
        out_shape=[jax.ShapeDtypeStruct(shape, F32) for shape in shapes],
        in_specs=[vmem_spec()] * len(data),
        out_specs=[vmem_spec()] * len(shapes),
        compiler_params=params(),
    )(*data)


def bin_sums(keep):
    _, full, wide = keep.shape
    rows = 5 * full // 6
    half = rows // 2
    data = [keep]
    a, b = summed(first_kernel, data, [(8, half, wide)] * 2)
    data += [partner(a, U_BITS), partner(b, V_BITS)]
    a, b = summed(second_kernel, data, [(4, half, wide)] * 2)
    data += [partner(a, V_BITS), partner(b, U_BITS)]
    sends = summed(line_kernel, data, [(rows, wide)] * 3)
    data += [partner(value, (8 * flip, 8 * flip)) for flip, value in zip(FLIPS, sends)]
    own, packed = summed(own_kernel, data, [(rows, wide), (rows // 5, wide)])
    bit = 32
    while bit < lax.axis_size("range"):
        own = own + partner(own, (bit, bit))
        packed = packed + partner(packed, (bit, bit))
        bit *= 2
    return own, packed


def from_bin(value, offset):
    count = lax.axis_size("range")
    pairs = []
    for i in range(count):
        target = index_of((bin_of(i) - offset) % 32) | (i & ~31)
        pairs.append((i, target))
    return lax.ppermute(value, "range", pairs)


def turn(value):
    half = value.shape[1] // 2
    rolled = pltpu.roll(value, half, 1)
    return jnp.where(iota(value.shape, 1) < half, -rolled, rolled)


def embed(value):
    return jnp.concatenate([value, turn(value)], axis=0)


def mul(a, b):
    return jnp.dot(a, embed(b), precision=lax.Precision.HIGHEST, preferred_element_type=F32)


def mul_conj(a, b):
    half = a.shape[1] // 2
    stacked = jnp.concatenate([a, -turn(a)], axis=0)
    both = dot_nt(stacked, b, lax.Precision.HIGHEST)
    rows = a.shape[0]
    return jnp.concatenate([both[:rows], both[rows:]], axis=1)


def reciprocal(x):
    value = pl.reciprocal(x, approx=True)
    for _ in range(2):
        value = value * (2.0 - x * value)
    return value


def pivot_inverse(p):
    def times(x, y):
        return x[0] * y[0] - x[1] * y[1], x[0] * y[1] + x[1] * y[0]

    def conj(x):
        return x[0], -x[1]

    def plus(x, y):
        return x[0] + y[0], x[1] + y[1]

    def scaled(x, s):
        return x[0] * s, x[1] * s

    def square(x):
        return x[0] * x[0] + x[1] * x[1]

    def two(a, b, d):
        inv = reciprocal(a * d - square(b))
        return d * inv, scaled(b, -inv), a * inv

    a, d = p[0][0], p[1][1]
    b = p[0][1]
    ea, eb, ed = two(a, b, d)
    f = [[p[0][2], p[0][3]], [p[1][2], p[1][3]]]
    w = [
        [plus(scaled(f[0][j], ea), times(eb, f[1][j])) for j in range(2)],
        [plus(times(conj(eb), f[0][j]), scaled(f[1][j], ed)) for j in range(2)],
    ]

    def inner(i, j):
        return plus(times(conj(f[0][i]), w[0][j]), times(conj(f[1][i]), w[1][j]))

    ha = p[2][2] - inner(0, 0)[0]
    hd = p[3][3] - inner(1, 1)[0]
    cross = inner(0, 1)
    hb = (p[2][3][0] - cross[0], p[2][3][1] - cross[1])
    ga, gb, gd = two(ha, hb, hd)
    v = [
        [
            plus(scaled(w[i][0], ga), times(w[i][1], conj(gb))),
            plus(times(w[i][0], gb), scaled(w[i][1], gd)),
        ]
        for i in range(2)
    ]
    top = [
        [plus(times(v[i][0], conj(w[j][0])), times(v[i][1], conj(w[j][1]))) for j in range(2)]
        for i in range(2)
    ]
    zero = None
    out = [[None] * 4 for _ in range(4)]
    out[0][0] = (ea + top[0][0][0], zero)
    out[1][1] = (ed + top[1][1][0], zero)
    out[0][1] = plus(eb, top[0][1])
    out[2][2], out[3][3], out[2][3] = (ga, zero), (gd, zero), gb
    for i in range(2):
        for j in range(2):
            out[i][2 + j] = (-v[i][j][0], -v[i][j][1])
    for i in range(4):
        for j in range(i):
            out[i][j] = conj(out[j][i])
    return out


def invert(matrix):
    chans, width = matrix.shape
    sub = 8
    tiles = [matrix[t * sub : (t + 1) * sub, :] for t in range(chans // sub)]
    lane = iota((sub, width), 1)
    row = iota((sub, width), 0)
    first_half = lane < chans

    def spin(value):
        rolled = pltpu.roll(value, chans, 1)
        return jnp.where(first_half, -rolled, rolled)

    def column(value, k):
        return jnp.broadcast_to(value[:, k : k + 1], (sub, width))

    def combine(terms):
        while len(terms) > 1:
            terms = [
                terms[i] + terms[i + 1] if i + 1 < len(terms) else terms[i]
                for i in range(0, len(terms), 2)
            ]
        return terms[0]

    for k in range(0, chans, 4):
        t, r = divmod(k, sub)
        lines = [jnp.broadcast_to(tiles[t][r + i : r + i + 1, :], (sub, width)) for i in range(4)]
        pivot = [[None] * 4 for _ in range(4)]
        for i in range(4):
            pivot[i][i] = column(lines[i], k + i)
            for j in range(i + 1, 4):
                pivot[i][j] = column(lines[i], k + j), column(lines[i], chans + k + j)
        low = jnp.bitwise_and(lane, chans - 1)
        cleared = (low >= k) & (low < k + 4)
        unit = [
            jnp.where(cleared, jnp.where(lane == k + i, 1.0, 0.0), lines[i]) for i in range(4)
        ]
        spun = [spin(u) for u in unit]
        p = pivot_inverse(pivot)
        fresh_lines, fresh_spun = [], []
        for i in range(4):
            terms, other = [], []
            for j in range(4):
                re, im = p[i][j]
                terms.append(re * unit[j])
                other.append(re * spun[j])
                if im is not None:
                    terms.append(im * spun[j])
                    other.append(-(im * unit[j]))
            fresh_lines.append(combine(terms))
            fresh_spun.append(combine(other))
        fresh = []
        for s, tile in enumerate(tiles):
            terms = []
            for i in range(4):
                terms.append(column(tile, k + i) * fresh_lines[i])
                terms.append(column(tile, chans + k + i) * fresh_spun[i])
            value = jnp.where(cleared, 0.0, tile) - combine(terms)
            if s == t:
                for i in range(4):
                    value = jnp.where(row == r + i, fresh_lines[i], value)
            fresh.append(value)
        tiles = fresh
    return jnp.concatenate(tiles, axis=0)


def unpacked(ref, scale):
    half, wide = ref.shape[0], ref.shape[1]
    piece = ref[...] * scale
    swapped = pltpu.roll(piece, wide // 2, 1)
    return jnp.concatenate([piece, swapped], axis=0)[:, : wide // 2]


def hermitian(mixed, across):
    i, j = iota(mixed.shape, 0), iota(mixed.shape, 1)
    real_part = jnp.where(i >= j, mixed, across)
    imag_part = jnp.where(i < j, mixed, jnp.where(i > j, -across, 0.0))
    return jnp.concatenate([real_part, imag_part], axis=1)


def middle_kernel(total, packed_ref, steer_ref, inv_ref, t_ref):
    chans = inv_ref.shape[0]
    mixed = unpacked(packed_ref, F32(1.0 / total))
    twice = jnp.concatenate([mixed, mixed], axis=1)
    across = jnp.concatenate([twice, twice], axis=0).T[:chans, :chans]
    inverse = invert(hermitian(mixed, across))
    inv_ref[...] = inverse
    t_ref[...] = mul(steer_ref[...], inverse)


def outer_kernel(total, own_ref, left_ref, right_ref, steer_ref, inv_ref, t_ref, out_ref,
                 work, keep, small):
    chans = inv_ref.shape[0]
    scale = F32(1.0 / total)
    half = chans // 2
    m_left = unpacked(left_ref.at[:half], scale)
    m_right = unpacked(right_ref, scale)
    ml = left_ref[half : half + chans] * scale
    rl = left_ref[half + chans :] * scale
    rm = own_ref[half : half + chans] * scale
    across = jnp.concatenate([jnp.concatenate([m_left, m_right], axis=1), ml], axis=0).T
    lm = jnp.concatenate([across[:chans, chans:], -across[chans:, chans:]], axis=1)
    t = t_ref[...]
    both = mul(jnp.concatenate([rm, lm], axis=0), inv_ref[...])
    g_right, g_left = both[:chans], both[chans:]
    by_left = mul(jnp.concatenate([g_left, g_right, t], axis=0), ml)
    by_right = mul_conj(jnp.concatenate([g_right, t], axis=0), rm)
    work[...] = hermitian(m_left, across[:chans, :chans]) - by_left[:chans]
    keep[0] = rl - by_left[chans : 2 * chans]
    keep[1] = hermitian(m_right, across[chans:, :chans]) - by_right[:chans]
    keep[2] = g_left
    keep[3] = g_right
    small[0] = -by_left[2 * chans :]
    small[1] = -by_right[chans:]

    @pl.loop(0, 2)
    def _(stage):
        work[...] = invert(work[...])

        @pl.when(stage == 0)
        def _():
            s_rl = keep[0]
            both = mul(jnp.concatenate([s_rl, small[0]], axis=0), work[...])
            back = mul_conj(both, s_rl)
            work[...] = keep[1] - back[:chans]
            small[1] = small[1] - back[chans:]
            middle = mul(both, keep[2])
            keep[0] = both[:chans]
            small[0] = both[chans:]
            keep[3] = keep[3] - middle[:chans]
            small[2] = t_ref[...] - middle[chans:]

        @pl.when(stage == 1)
        def _():
            y_right = mul(small[1], work[...])
            factors = jnp.concatenate([embed(keep[0]), embed(keep[3])], axis=1)
            both = jnp.dot(
                y_right, factors, precision=lax.Precision.HIGHEST, preferred_element_type=F32
            )
            y_left = small[0] - both[:, : 2 * chans]
            y_mid = small[2] - both[:, 2 * chans :]
            quad = jnp.sum(steer_ref[...] * y_mid, axis=1, keepdims=True)
            y = jnp.concatenate([y_left, y_mid, y_right], axis=1) / jnp.sqrt(quad)
            real_lane = lax.rem(iota(y.shape, 1), 2 * chans) < chans
            mine = jnp.where(real_lane, y, -y).astype(BF16)
            for c in range(out_ref.shape[0]):
                out_ref[c] = mine


def steering(chans):
    index = np.arange(chans)
    sines = -0.8 + 1.6 * np.arange(BEAMS) / (BEAMS - 1)
    angle = math.pi * sines[:, None] * index[None, :]
    return np.concatenate([np.cos(angle), -np.sin(angle)], axis=1).astype(np.float32)


def solve_middle(packed, steer, total):
    half, wide = packed.shape
    return pl.pallas_call(
        functools.partial(middle_kernel, total),
        out_shape=[
            jax.ShapeDtypeStruct((2 * half, wide), F32),
            jax.ShapeDtypeStruct((BEAMS, wide), F32),
        ],
        in_specs=[vmem_spec()] * 2,
        out_specs=[vmem_spec()] * 2,
        compiler_params=params(),
    )(packed, steer)


def solve_outer(own, left, right, steer, inverse, t, total, copies):
    chans, wide = inverse.shape
    return pl.pallas_call(
        functools.partial(outer_kernel, total),
        out_shape=jax.ShapeDtypeStruct((copies, BEAMS, 3 * wide), BF16),
        in_specs=[vmem_spec()] * 6,
        out_specs=vmem_spec(),
        scratch_shapes=[
            pltpu.VMEM((chans, wide), F32),
            pltpu.VMEM((4, chans, wide), F32),
            pltpu.VMEM((3, BEAMS, wide), F32),
        ],
        compiler_params=params(),
    )(own, left, right, steer, inverse, t)


def beam_kernel(bin_ref, block_ref, beam_ref, owner_ref, s0_ref, upper_ref, lower_ref, w_ref,
                out_ref, both_ref, rows_ref, seen_ref):
    bins, wide, gates = s0_ref.shape
    devices = seen_ref.shape[0]
    count = bin_ref.shape[0]
    rows_ref[...] = jnp.zeros_like(rows_ref)

    @pl.loop(0, devices)
    def _(i):
        seen_ref[i] = 0

    w = w_ref[...].astype(F32).reshape(bins * BEAMS, 3 * wide)
    for k in range(3):
        lanes = slice(k * wide, (k + 1) * wide)
        part = w[:, lanes]
        both_ref[:, 0:BEAMS, lanes] = part.reshape(bins, BEAMS, wide)
        both_ref[:, BEAMS:, lanes] = turn(part).reshape(bins, BEAMS, wide)

    def detection(j, carry):
        bin_id = bin_ref[j]
        beam_id = beam_ref[j]
        owner = owner_ref[j]
        rank = seen_ref[owner]
        seen_ref[owner] = rank + 1
        left = both_ref[index_of(bin_id)].astype(BF16)
        bands = [lax.rem(bin_id + bins - 1 + k, bins) for k in range(3)]
        first = block_ref[j] == 0
        pieces = []
        for b in bands:
            later = [upper_ref[b, 0], lower_ref[b, 0], upper_ref[b, 1], lower_ref[b, 1]]
            pieces.append(jnp.where(first, s0_ref[b], jnp.concatenate(later, axis=0)))
        window = jnp.concatenate(pieces, axis=0)
        both = dot(left, window)
        line = jnp.concatenate([both[:BEAMS], both[BEAMS:]], axis=1)
        chosen = jnp.where(iota(line.shape, 0) == beam_id, line, 0.0)
        row = owner * CAP + rank
        rows_ref[pl.ds(row, 1), :] = jnp.sum(chosen, axis=0, keepdims=True)
        return carry

    lax.fori_loop(0, count, detection, 0, unroll=32)
    out_ref[...] = rows_ref[...].astype(BF16)


def beam_rows(det_bin, det_block, det_beam, owners, s0, s1, weight, devices):
    bins, wide, gates = s0.shape
    return pl.pallas_call(
        beam_kernel,
        out_shape=jax.ShapeDtypeStruct((devices * CAP, 2 * gates), BF16),
        in_specs=[smem_spec()] * 4 + [vmem_spec()] * 4,
        out_specs=vmem_spec(),
        scratch_shapes=[
            pltpu.VMEM((bins, 2 * BEAMS, 3 * wide), F32),
            pltpu.VMEM((devices * CAP, 2 * gates), F32),
            pltpu.SMEM((devices,), jnp.int32),
        ],
        compiler_params=params(),
    )(det_bin, det_block, det_beam, owners, s0, *s1, weight)


def on_device(raw, replica, det_bin, det_block, det_beam, det_owner):
    devices = lax.axis_size("range")
    _, chans, pulses, gates = raw.shape
    bins = pulses
    flat = raw.reshape(2, chans * pulses, gates)
    before = [(source, source - 1) for source in range(1, devices)]
    *slices, mark = first_gates(flat)
    halos = [lax.ppermute(value, "range", before) for value in slices]
    table = doppler_matrix(pulses, 8)
    s0, local, matrix, *sent = spectra_first(flat, replica, table, pulses, mark)
    beside0 = [partner(value, (1, 1)) for value in sent]
    sums = cross([s0], bins)
    sums = cross(beside0, bins, sums)
    s1, beside1 = [], []
    for part, halo in enumerate(halos):
        value, send = spectra_last(part, local, halo, matrix, table, pulses, sums)
        s1.append(value)
        beside1.append(partner(send, (1, 1)))
    sums = cross(s1, bins, sums)
    sums = cross(beside1, bins, sums)
    own, packed = bin_sums(sums)
    total = gates * devices
    steer = steering(chans)
    left = from_bin(own, -1)
    right = from_bin(packed, 1)
    inverse, t = solve_middle(packed, steer, total)
    mine = solve_outer(own, left, right, steer, inverse, t, total, bins)
    groups = [list(range(first, first + bins)) for first in range(0, devices, bins)]
    weight = lax.all_to_all(
        mine, "range", split_axis=0, concat_axis=0, tiled=True,
        axis_index_groups=groups if len(groups) > 1 else None,
    )
    outgoing = beam_rows(
        det_bin, det_block, det_beam, det_owner[:, 0],
        s0.reshape(bins, 2 * chans, BLOCK), s1, weight, devices,
    )
    incoming = lax.all_to_all(
        outgoing.reshape(devices, CAP, 2 * BLOCK), "range", split_axis=0, concat_axis=0, tiled=True
    )
    return incoming.astype(F32).reshape(devices * CAP, 2 * BLOCK)


def solution(mesh):
    in_specs = (
        P(None, None, None, "range"),
        P(),
        P("range"),
        P("range"),
        P("range"),
        P("range", None),
    )
    out_specs = P("range", None)
    return jax.shard_map(
        on_device, mesh=mesh, in_specs=in_specs, out_specs=out_specs, check_vma=False
    )
```

```python
import functools
import math

import jax
import jax.numpy as jnp
import ml_dtypes
import numpy as np
from jax import lax
from jax.experimental import pallas as pl
from jax.experimental.pallas import tpu as pltpu
from jax.sharding import PartitionSpec as P

BLOCK = 128
BEAMS = 8
CAP = 2

F32 = jnp.float32
BF16 = jnp.bfloat16
VMEM = pltpu.VMEM
MIB = 1024 * 1024
NT = (((1,), (1,)), ((), ()))


def vmem_spec():
    return pl.BlockSpec(memory_space=VMEM)


def smem_spec():
    return pl.BlockSpec(memory_space=pltpu.SMEM)


def hbm_spec():
    return pl.BlockSpec(memory_space=pltpu.HBM)


SHORT = pl.CostEstimate(flops=1, bytes_accessed=1, transcendentals=0)


def params(mib=16):
    return pltpu.CompilerParams(vmem_limit_bytes=int(mib * MIB))


def dot(a, b):
    return jnp.dot(a, b, preferred_element_type=F32)


def dot_nt(a, b, precision=None):
    return lax.dot_general(a, b, NT, precision=precision, preferred_element_type=F32)


def iota(shape, axis):
    return lax.broadcasted_iota(jnp.int32, shape, axis)


def halo_kernel(raw_ref, a_ref, b_ref, mark_ref, sems):
    mark_ref[...] = jnp.zeros_like(mark_ref)
    count = sems.shape[0] // 2
    size = a_ref.shape[1] // count
    copies = []
    for part, out_ref in enumerate((a_ref, b_ref)):
        for j in range(count):
            start = part * a_ref.shape[1] + j * size
            copies.append(
                pltpu.make_async_copy(
                    raw_ref.at[:, start : start + size, :BLOCK],
                    out_ref.at[:, j * size : (j + 1) * size, :],
                    sems.at[part * count + j],
                )
            )
    for copy in copies:
        copy.start()
    for copy in copies:
        copy.wait()


def first_gates(raw):
    half = jax.ShapeDtypeStruct((2, raw.shape[1] // 2, BLOCK), BF16)
    return pl.pallas_call(
        halo_kernel,
        out_shape=[half, half, jax.ShapeDtypeStruct((8, 128), F32)],
        in_specs=[hbm_spec()],
        out_specs=[vmem_spec()] * 3,
        scratch_shapes=[pltpu.SemaphoreType.DMA((8,))],
        compiler_params=params(63),
    )(raw)


def correlation_matrix(rep_ref, out_ref):
    taps = rep_ref.shape[1]
    base = rep_ref[...].astype(F32)
    row = iota((taps, 2 * taps), 0)
    parts = []
    for i in range(2):
        line = jnp.concatenate([base[i : i + 1], jnp.zeros((1, taps), F32)], axis=1)
        skew = jnp.broadcast_to(line, (taps, 2 * taps))
        bit = 1
        while bit < taps:
            skew = jnp.where((row & bit) != 0, pltpu.roll(skew, bit, 1), skew)
            bit *= 2
        parts.append(skew.T)
    real_part, imag_part = parts
    out_ref[0] = jnp.concatenate([real_part, -imag_part], axis=1).astype(BF16)
    out_ref[1] = jnp.concatenate([imag_part, real_part], axis=1).astype(BF16)


def doppler_matrix(pulses, group):
    index = np.arange(pulses)
    angle = 2.0 * math.pi / pulses * (index[:, None] * index[None, :] % pulses)
    cosine = np.cos(angle) * pulses**-0.5
    sine = np.sin(angle) * pulses**-0.5
    table = np.stack([np.stack([cosine, -sine], 1), np.stack([sine, cosine], 1)], 0)
    full = np.einsum("ipod,ce->dociep", table, np.eye(group))
    shape = (pulses * 2 * group, 2 * group * pulses)
    return full.reshape(shape).astype(ml_dtypes.bfloat16)


def doppler_rows(total, dft):
    compressed = total.astype(BF16)
    rows, wide = compressed.shape
    half, gates = rows // 2, wide // 2
    stacked = jnp.concatenate(
        [
            jnp.concatenate([compressed[:half, :gates], compressed[half:, :gates]], axis=1),
            jnp.concatenate([compressed[:half, gates:], compressed[half:, gates:]], axis=1),
        ],
        axis=0,
    )
    both = dot(dft, stacked)
    lines = both.shape[0] // 8
    joined = jnp.concatenate(
        [both[:, :gates].reshape(lines, 8, gates), both[:, gates:].reshape(lines, 8, gates)],
        axis=1,
    )
    return joined.astype(BF16)


GROUP = 16


def half_of_bins(bins, mine):
    core = lax.axis_index("range") & 1
    return (core if mine else 1 - core) * (bins // 2)


def sent_bins(bins):
    return bins // 2 + 2


def spectra_first_kernel(raw_ref, rep_ref, dft_ref, _, s_ref, local_ref, taps_ref, *rest):
    *send_refs, buf, sems = rest
    bins, _, chans, gates = s_ref.shape
    size = GROUP * bins
    copies = [
        pltpu.make_async_copy(
            raw_ref.at[:, j * size : (j + 1) * size, :],
            buf.at[:, j * size : (j + 1) * size, :],
            sems.at[j],
        )
        for j in range(chans // GROUP)
    ]
    for copy in copies:
        copy.start()
    correlation_matrix(rep_ref, taps_ref)
    for j, copy in enumerate(copies):
        copy.wait()
        rows = slice(j * size, (j + 1) * size)
        total = dot(buf[0, rows, :], taps_ref[0]) + dot(buf[1, rows, :], taps_ref[1])
        out = doppler_rows(total, dft_ref[...])
        s_ref[:, :, j * GROUP : (j + 1) * GROUP, :] = out.reshape(bins, 2, GROUP, gates)
        later = jnp.concatenate([buf[0, rows, gates:], buf[1, rows, gates:]], axis=1)
        near = jnp.concatenate([taps_ref[0, :gates, :], taps_ref[1, :gates, :]], axis=0)
        local_ref[rows, :] = dot(later, near)
    base = half_of_bins(bins, False)
    half = chans // 2
    for part, send_ref in enumerate(send_refs):
        for k in range(send_ref.shape[0]):
            send_ref[k] = s_ref[lax.rem(base + k, bins), :, part * half : (part + 1) * half, :]


def spectra_last_kernel(part, local_ref, halo_ref, taps_ref, dft_ref, _, s_ref, send_ref):
    bins, _, chans, gates = s_ref.shape
    size = GROUP * bins
    far = jnp.concatenate([taps_ref[0, gates:, :], taps_ref[1, gates:, :]], axis=0)
    for j in range(chans // GROUP):
        rows = slice(j * size, (j + 1) * size)
        later = jnp.concatenate([halo_ref[0, rows, :], halo_ref[1, rows, :]], axis=1)
        start = part * chans * bins + j * size
        out = doppler_rows(local_ref[start : start + size, :] + dot(later, far), dft_ref[...])
        s_ref[:, :, j * GROUP : (j + 1) * GROUP, :] = out.reshape(bins, 2, GROUP, gates)
    base = half_of_bins(bins, False)
    for k in range(send_ref.shape[0]):
        send_ref[k] = s_ref[lax.rem(base + k, bins)]


def spectra_first(raw, replica, table, pulses, mark):
    _, rows, gates = raw.shape
    chans = rows // pulses
    taps = replica.shape[1]
    return pl.pallas_call(
        spectra_first_kernel,
        out_shape=[
            jax.ShapeDtypeStruct((pulses, 2, chans, BLOCK), BF16),
            jax.ShapeDtypeStruct((rows, 2 * BLOCK), F32),
            jax.ShapeDtypeStruct((2, 2 * taps, 2 * taps), BF16),
        ]
        + [jax.ShapeDtypeStruct((sent_bins(pulses), 2, chans // 2, BLOCK), BF16)] * 2,
        in_specs=[hbm_spec(), vmem_spec(), vmem_spec(), pl.BlockSpec(memory_space=pl.ANY)],
        out_specs=[vmem_spec()] * 5,
        scratch_shapes=[
            pltpu.VMEM(raw.shape, BF16),
            pltpu.SemaphoreType.DMA((chans // GROUP,)),
        ],
        compiler_params=params(),
        cost_estimate=SHORT,
    )(raw, replica, table, mark)


def spectra_last(part, local, halo, matrix, table, pulses, sums):
    chans = halo.shape[1] // pulses
    return pl.pallas_call(
        functools.partial(spectra_last_kernel, part),
        out_shape=[
            jax.ShapeDtypeStruct((pulses, 2, chans, BLOCK), BF16),
            jax.ShapeDtypeStruct((sent_bins(pulses), 2, chans, BLOCK), BF16),
        ],
        in_specs=[vmem_spec()] * 4 + [pl.BlockSpec(memory_space=pl.ANY)],
        out_specs=[vmem_spec()] * 2,
        compiler_params=params(),
        cost_estimate=SHORT,
    )(local, halo, matrix, table, sums)


def cross_kernel(count_refs, *refs):
    s_refs, rest = refs[:count_refs], refs[count_refs:]
    before_ref = rest[0] if len(rest) == 2 else None
    out_ref = rest[-1]
    held, _, _, gates = s_refs[0].shape
    chans = sum(ref.shape[2] for ref in s_refs)
    count = out_ref.shape[0]
    base = half_of_bins(held, True) if held == 2 * count else 0

    def write(e, block):
        out_ref[e] = block if before_ref is None else block + before_ref[e]

    @pl.loop(0, count // 2, unroll=2)
    def _(step):
        e = step * 2
        each = []
        for k in range(4):
            where = lax.rem(base + e + k, held)
            each.append(
                [jnp.concatenate([ref[where, o] for ref in s_refs], axis=0) for o in range(2)]
            )
        left = jnp.concatenate(
            [jnp.concatenate([re, im], axis=1) for re, im in each], axis=0
        )
        right = jnp.concatenate(
            [
                jnp.concatenate(pieces, axis=1)
                for re, im in each[:2]
                for pieces in ((re, im), (-im, re))
            ],
            axis=0,
        )
        both = dot_nt(left, right)
        write(e, both[: 3 * chans, : 2 * chans])
        write(e + 1, both[chans:, 2 * chans :])


def cross(spectra, bins, before=None):
    chans = sum(value.shape[2] for value in spectra)
    data = spectra if before is None else spectra + [before]
    return pl.pallas_call(
        functools.partial(cross_kernel, len(spectra)),
        out_shape=jax.ShapeDtypeStruct((bins // 2, 3 * chans, 2 * chans), F32),
        in_specs=[vmem_spec()] * len(data),
        out_specs=vmem_spec(),
        compiler_params=params(),
        cost_estimate=SHORT,
    )(*data)


U_BITS, V_BITS = (2, 4), (4, 2)


def partner(value, bits):
    count = lax.axis_size("range")
    return lax.ppermute(value, "range", [(i, i ^ bits[i & 1]) for i in range(count)])


def slot_of(core, x, y, z):
    return (4 * z + ((2 * y + (x ^ y)) ^ (3 * (z & 1)))) ^ (15 * core)


def parts_of(index):
    return index & 1, (index >> 1) & 1, (index >> 2) & 1, (index >> 3) & 3


def bin_of(index):
    core, x, y, z = parts_of(index)
    return core * 16 + slot_of(core, x, y, z)


def index_of(bin_id):
    core = bin_id >> 4
    path = (bin_id & 15) ^ (15 * core)
    z = path >> 2
    turned = (path & 3) ^ (3 * (z & 1))
    y = turned >> 1
    x = (turned & 1) ^ y
    return z * 8 + y * 4 + x * 2 + core


def uv_parts():
    core, x, y, z = parts_of(lax.axis_index("range"))
    return core, jnp.where(core == 0, x, y), jnp.where(core == 0, y, x), z


def uv_slot(core, u, v, z):
    return slot_of(core, jnp.where(core == 0, u, v), jnp.where(core == 0, v, u), z)


def packed(block):
    chans = block.shape[0]
    lower = iota((chans, chans), 0) >= iota((chans, chans), 1)
    swapped = pltpu.roll(block, chans, 1)
    mixed = jnp.where(lower, block[:, :chans], swapped[:, :chans])
    return jnp.concatenate([mixed[: chans // 2], mixed[chans // 2 :]], axis=1)


def sent_rows(keep_ref):
    return 5 * keep_ref.shape[1] // 6


def upper_rows(keep_ref, e):
    block = keep_ref.shape[1] // 3
    end = sent_rows(keep_ref) // 2 + block // 2
    return jnp.concatenate([packed(keep_ref[e, :block]), keep_ref[e, block:end]], axis=0)


def lower_rows(keep_ref, e):
    return keep_ref[e, sent_rows(keep_ref) // 2 + keep_ref.shape[1] // 6 :]


def first_kernel(keep_ref, a_ref, b_ref):
    core, u, v, z = uv_parts()
    for k in range(8):
        a_ref[k] = upper_rows(keep_ref, uv_slot(core, 1 - u, k // 4, k % 4))
        b_ref[k] = lower_rows(keep_ref, uv_slot(core, k // 4, 1 - v, k % 4))


def second_kernel(keep_ref, a1_ref, b1_ref, a_ref, b_ref):
    core, u, v, z = uv_parts()
    for k in range(4):
        e = uv_slot(core, u, 1 - v, k)
        a_ref[k] = upper_rows(keep_ref, e) + a1_ref[(1 - v) * 4 + k]
        e = uv_slot(core, 1 - u, v, k)
        b_ref[k] = lower_rows(keep_ref, e) + b1_ref[(1 - u) * 4 + k]


def line_sum(keep_ref, a1_ref, b1_ref, a2_ref, b2_ref, flip):
    core, u, v, z = uv_parts()
    z = z ^ flip
    e = uv_slot(core, u, v, z)
    upper = upper_rows(keep_ref, e) + a1_ref[v * 4 + z] + a2_ref[z]
    lower = lower_rows(keep_ref, e) + b1_ref[u * 4 + z] + b2_ref[z]
    return upper, lower


FLIPS = (2, 3, 1)


def line_kernel(*refs):
    half = sent_rows(refs[0]) // 2
    for flip, out_ref in zip(FLIPS, refs[5:]):
        upper, lower = line_sum(*refs[:5], flip)
        out_ref[:half] = upper
        out_ref[half:] = lower


def own_kernel(*refs):
    z1_ref, z2_ref, z3_ref, out_ref, packed_ref = refs[5:]
    half = sent_rows(refs[0]) // 2
    upper, lower = line_sum(*refs[:5], 0)
    upper = upper + z1_ref[:half] + (z2_ref[:half] + z3_ref[:half])
    out_ref[:half] = upper
    packed_ref[...] = upper[: packed_ref.shape[0]]
    out_ref[half:] = lower + z1_ref[half:] + (z2_ref[half:] + z3_ref[half:])


def summed(kernel, data, shapes):
    return pl.pallas_call(
        kernel,
        out_shape=[jax.ShapeDtypeStruct(shape, F32) for shape in shapes],
        in_specs=[vmem_spec()] * len(data),
        out_specs=[vmem_spec()] * len(shapes),
        compiler_params=params(),
    )(*data)


def bin_sums(keep):
    _, full, wide = keep.shape
    rows = 5 * full // 6
    half = rows // 2
    data = [keep]
    a, b = summed(first_kernel, data, [(8, half, wide)] * 2)
    data += [partner(a, U_BITS), partner(b, V_BITS)]
    a, b = summed(second_kernel, data, [(4, half, wide)] * 2)
    data += [partner(a, V_BITS), partner(b, U_BITS)]
    sends = summed(line_kernel, data, [(rows, wide)] * 3)
    data += [partner(value, (8 * flip, 8 * flip)) for flip, value in zip(FLIPS, sends)]
    own, packed = summed(own_kernel, data, [(rows, wide), (rows // 5, wide)])
    bit = 32
    while bit < lax.axis_size("range"):
        own = own + partner(own, (bit, bit))
        packed = packed + partner(packed, (bit, bit))
        bit *= 2
    return own, packed


def from_bin(value, offset):
    count = lax.axis_size("range")
    pairs = []
    for i in range(count):
        target = index_of((bin_of(i) - offset) % 32) | (i & ~31)
        pairs.append((i, target))
    return lax.ppermute(value, "range", pairs)


def turn(value):
    half = value.shape[1] // 2
    rolled = pltpu.roll(value, half, 1)
    return jnp.where(iota(value.shape, 1) < half, -rolled, rolled)


def embed(value):
    return jnp.concatenate([value, turn(value)], axis=0)


def mul(a, b):
    return jnp.dot(a, embed(b), precision=lax.Precision.HIGHEST, preferred_element_type=F32)


def mul_conj(a, b):
    half = a.shape[1] // 2
    stacked = jnp.concatenate([a, -turn(a)], axis=0)
    both = dot_nt(stacked, b, lax.Precision.HIGHEST)
    rows = a.shape[0]
    return jnp.concatenate([both[:rows], both[rows:]], axis=1)


def reciprocal(x):
    value = pl.reciprocal(x, approx=True)
    for _ in range(2):
        value = value * (2.0 - x * value)
    return value


def pivot_inverse(p):
    def times(x, y):
        return x[0] * y[0] - x[1] * y[1], x[0] * y[1] + x[1] * y[0]

    def conj(x):
        return x[0], -x[1]

    def plus(x, y):
        return x[0] + y[0], x[1] + y[1]

    def scaled(x, s):
        return x[0] * s, x[1] * s

    def square(x):
        return x[0] * x[0] + x[1] * x[1]

    def two(a, b, d):
        inv = reciprocal(a * d - square(b))
        return d * inv, scaled(b, -inv), a * inv

    a, d = p[0][0], p[1][1]
    b = p[0][1]
    ea, eb, ed = two(a, b, d)
    f = [[p[0][2], p[0][3]], [p[1][2], p[1][3]]]
    w = [
        [plus(scaled(f[0][j], ea), times(eb, f[1][j])) for j in range(2)],
        [plus(times(conj(eb), f[0][j]), scaled(f[1][j], ed)) for j in range(2)],
    ]

    def inner(i, j):
        return plus(times(conj(f[0][i]), w[0][j]), times(conj(f[1][i]), w[1][j]))

    ha = p[2][2] - inner(0, 0)[0]
    hd = p[3][3] - inner(1, 1)[0]
    cross = inner(0, 1)
    hb = (p[2][3][0] - cross[0], p[2][3][1] - cross[1])
    ga, gb, gd = two(ha, hb, hd)
    v = [
        [
            plus(scaled(w[i][0], ga), times(w[i][1], conj(gb))),
            plus(times(w[i][0], gb), scaled(w[i][1], gd)),
        ]
        for i in range(2)
    ]
    top = [
        [plus(times(v[i][0], conj(w[j][0])), times(v[i][1], conj(w[j][1]))) for j in range(2)]
        for i in range(2)
    ]
    zero = None
    out = [[None] * 4 for _ in range(4)]
    out[0][0] = (ea + top[0][0][0], zero)
    out[1][1] = (ed + top[1][1][0], zero)
    out[0][1] = plus(eb, top[0][1])
    out[2][2], out[3][3], out[2][3] = (ga, zero), (gd, zero), gb
    for i in range(2):
        for j in range(2):
            out[i][2 + j] = (-v[i][j][0], -v[i][j][1])
    for i in range(4):
        for j in range(i):
            out[i][j] = conj(out[j][i])
    return out


def invert(matrix):
    chans, width = matrix.shape
    sub = 8
    tiles = [matrix[t * sub : (t + 1) * sub, :] for t in range(chans // sub)]
    lane = iota((sub, width), 1)
    row = iota((sub, width), 0)
    first_half = lane < chans

    def spin(value):
        rolled = pltpu.roll(value, chans, 1)
        return jnp.where(first_half, -rolled, rolled)

    def column(value, k):
        return jnp.broadcast_to(value[:, k : k + 1], (sub, width))

    def combine(terms):
        while len(terms) > 1:
            terms = [
                terms[i] + terms[i + 1] if i + 1 < len(terms) else terms[i]
                for i in range(0, len(terms), 2)
            ]
        return terms[0]

    for k in range(0, chans, 4):
        t, r = divmod(k, sub)
        lines = [jnp.broadcast_to(tiles[t][r + i : r + i + 1, :], (sub, width)) for i in range(4)]
        pivot = [[None] * 4 for _ in range(4)]
        for i in range(4):
            pivot[i][i] = column(lines[i], k + i)
            for j in range(i + 1, 4):
                pivot[i][j] = column(lines[i], k + j), column(lines[i], chans + k + j)
        low = jnp.bitwise_and(lane, chans - 1)
        cleared = (low >= k) & (low < k + 4)
        unit = [
            jnp.where(cleared, jnp.where(lane == k + i, 1.0, 0.0), lines[i]) for i in range(4)
        ]
        spun = [spin(u) for u in unit]
        p = pivot_inverse(pivot)
        fresh_lines, fresh_spun = [], []
        for i in range(4):
            terms, other = [], []
            for j in range(4):
                re, im = p[i][j]
                terms.append(re * unit[j])
                other.append(re * spun[j])
                if im is not None:
                    terms.append(im * spun[j])
                    other.append(-(im * unit[j]))
            fresh_lines.append(combine(terms))
            fresh_spun.append(combine(other))
        fresh = []
        for s, tile in enumerate(tiles):
            terms = []
            for i in range(4):
                terms.append(column(tile, k + i) * fresh_lines[i])
                terms.append(column(tile, chans + k + i) * fresh_spun[i])
            value = jnp.where(cleared, 0.0, tile) - combine(terms)
            if s == t:
                for i in range(4):
                    value = jnp.where(row == r + i, fresh_lines[i], value)
            fresh.append(value)
        tiles = fresh
    return jnp.concatenate(tiles, axis=0)


def unpacked(ref, scale):
    half, wide = ref.shape[0], ref.shape[1]
    piece = ref[...] * scale
    swapped = pltpu.roll(piece, wide // 2, 1)
    return jnp.concatenate([piece, swapped], axis=0)[:, : wide // 2]


def hermitian(mixed, across):
    i, j = iota(mixed.shape, 0), iota(mixed.shape, 1)
    real_part = jnp.where(i >= j, mixed, across)
    imag_part = jnp.where(i < j, mixed, jnp.where(i > j, -across, 0.0))
    return jnp.concatenate([real_part, imag_part], axis=1)


def middle_kernel(total, packed_ref, steer_ref, inv_ref, t_ref):
    chans = inv_ref.shape[0]
    mixed = unpacked(packed_ref, F32(1.0 / total))
    twice = jnp.concatenate([mixed, mixed], axis=1)
    across = jnp.concatenate([twice, twice], axis=0).T[:chans, :chans]
    inverse = invert(hermitian(mixed, across))
    inv_ref[...] = inverse
    t_ref[...] = mul(steer_ref[...], inverse)


def outer_kernel(total, own_ref, left_ref, right_ref, steer_ref, inv_ref, t_ref, out_ref,
                 work, keep, small):
    chans = inv_ref.shape[0]
    scale = F32(1.0 / total)
    half = chans // 2
    m_left = unpacked(left_ref.at[:half], scale)
    m_right = unpacked(right_ref, scale)
    ml = left_ref[half : half + chans] * scale
    rl = left_ref[half + chans :] * scale
    rm = own_ref[half : half + chans] * scale
    across = jnp.concatenate([jnp.concatenate([m_left, m_right], axis=1), ml], axis=0).T
    lm = jnp.concatenate([across[:chans, chans:], -across[chans:, chans:]], axis=1)
    t = t_ref[...]
    both = mul(jnp.concatenate([rm, lm], axis=0), inv_ref[...])
    g_right, g_left = both[:chans], both[chans:]
    by_left = mul(jnp.concatenate([g_left, g_right, t], axis=0), ml)
    by_right = mul_conj(jnp.concatenate([g_right, t], axis=0), rm)
    work[...] = hermitian(m_left, across[:chans, :chans]) - by_left[:chans]
    keep[0] = rl - by_left[chans : 2 * chans]
    keep[1] = hermitian(m_right, across[chans:, :chans]) - by_right[:chans]
    keep[2] = g_left
    keep[3] = g_right
    small[0] = -by_left[2 * chans :]
    small[1] = -by_right[chans:]

    @pl.loop(0, 2)
    def _(stage):
        work[...] = invert(work[...])

        @pl.when(stage == 0)
        def _():
            s_rl = keep[0]
            both = mul(jnp.concatenate([s_rl, small[0]], axis=0), work[...])
            back = mul_conj(both, s_rl)
            work[...] = keep[1] - back[:chans]
            small[1] = small[1] - back[chans:]
            middle = mul(both, keep[2])
            keep[0] = both[:chans]
            small[0] = both[chans:]
            keep[3] = keep[3] - middle[:chans]
            small[2] = t_ref[...] - middle[chans:]

        @pl.when(stage == 1)
        def _():
            y_right = mul(small[1], work[...])
            factors = jnp.concatenate([embed(keep[0]), embed(keep[3])], axis=1)
            both = jnp.dot(
                y_right, factors, precision=lax.Precision.HIGHEST, preferred_element_type=F32
            )
            y_left = small[0] - both[:, : 2 * chans]
            y_mid = small[2] - both[:, 2 * chans :]
            quad = jnp.sum(steer_ref[...] * y_mid, axis=1, keepdims=True)
            y = jnp.concatenate([y_left, y_mid, y_right], axis=1) / jnp.sqrt(quad)
            real_lane = lax.rem(iota(y.shape, 1), 2 * chans) < chans
            mine = jnp.where(real_lane, y, -y).astype(BF16)
            for c in range(out_ref.shape[0]):
                out_ref[c] = mine


def steering(chans):
    index = np.arange(chans)
    sines = -0.8 + 1.6 * np.arange(BEAMS) / (BEAMS - 1)
    angle = math.pi * sines[:, None] * index[None, :]
    return np.concatenate([np.cos(angle), -np.sin(angle)], axis=1).astype(np.float32)


def solve_middle(packed, steer, total):
    half, wide = packed.shape
    return pl.pallas_call(
        functools.partial(middle_kernel, total),
        out_shape=[
            jax.ShapeDtypeStruct((2 * half, wide), F32),
            jax.ShapeDtypeStruct((BEAMS, wide), F32),
        ],
        in_specs=[vmem_spec()] * 2,
        out_specs=[vmem_spec()] * 2,
        compiler_params=params(),
    )(packed, steer)


def solve_outer(own, left, right, steer, inverse, t, total, copies):
    chans, wide = inverse.shape
    return pl.pallas_call(
        functools.partial(outer_kernel, total),
        out_shape=jax.ShapeDtypeStruct((copies, BEAMS, 3 * wide), BF16),
        in_specs=[vmem_spec()] * 6,
        out_specs=vmem_spec(),
        scratch_shapes=[
            pltpu.VMEM((chans, wide), F32),
            pltpu.VMEM((4, chans, wide), F32),
            pltpu.VMEM((3, BEAMS, wide), F32),
        ],
        compiler_params=params(),
    )(own, left, right, steer, inverse, t)


def beam_kernel(bin_ref, block_ref, beam_ref, owner_ref, s0_ref, upper_ref, lower_ref, w_ref,
                out_ref, both_ref, rows_ref, seen_ref):
    bins, wide, gates = s0_ref.shape
    devices = seen_ref.shape[0]
    count = bin_ref.shape[0]
    rows_ref[...] = jnp.zeros_like(rows_ref)

    @pl.loop(0, devices)
    def _(i):
        seen_ref[i] = 0

    w = w_ref[...].astype(F32).reshape(bins * BEAMS, 3 * wide)
    for k in range(3):
        lanes = slice(k * wide, (k + 1) * wide)
        part = w[:, lanes]
        both_ref[:, 0:BEAMS, lanes] = part.reshape(bins, BEAMS, wide)
        both_ref[:, BEAMS:, lanes] = turn(part).reshape(bins, BEAMS, wide)

    def window(j):
        bin_id = bin_ref[j]
        first = block_ref[j] == 0
        pieces = []
        for k in range(3):
            band = lax.rem(bin_id + bins - 1 + k, bins)
            later = [upper_ref[band, 0], lower_ref[band, 0], upper_ref[band, 1], lower_ref[band, 1]]
            pieces.append(jnp.where(first, s0_ref[band], jnp.concatenate(later, axis=0)))
        return jnp.concatenate(pieces, axis=0)

    def store(j, block):
        owner = owner_ref[j]
        rank = seen_ref[owner]
        seen_ref[owner] = rank + 1
        line = jnp.concatenate([block[:BEAMS], block[BEAMS:]], axis=1)
        chosen = jnp.where(iota(line.shape, 0) == beam_ref[j], line, 0.0)
        rows_ref[pl.ds(owner * CAP + rank, 1), :] = jnp.sum(chosen, axis=0, keepdims=True)

    def detections(step, carry):
        pair = [step * 2 + k for k in range(2)]
        left = jnp.concatenate([both_ref[index_of(bin_ref[j])] for j in pair], axis=0)
        both = dot(left.astype(BF16), jnp.concatenate([window(j) for j in pair], axis=1))
        for k, j in enumerate(pair):
            rows = slice(k * 2 * BEAMS, (k + 1) * 2 * BEAMS)
            store(j, both[rows, k * gates : (k + 1) * gates])
        return carry

    assert count % 2 == 0
    lax.fori_loop(0, count // 2, detections, 0, unroll=16)
    out_ref[...] = rows_ref[...].astype(BF16)


def beam_rows(det_bin, det_block, det_beam, owners, s0, s1, weight, devices):
    bins, wide, gates = s0.shape
    return pl.pallas_call(
        beam_kernel,
        out_shape=jax.ShapeDtypeStruct((devices * CAP, 2 * gates), BF16),
        in_specs=[smem_spec()] * 4 + [vmem_spec()] * 4,
        out_specs=vmem_spec(),
        scratch_shapes=[
            pltpu.VMEM((bins, 2 * BEAMS, 3 * wide), F32),
            pltpu.VMEM((devices * CAP, 2 * gates), F32),
            pltpu.SMEM((devices,), jnp.int32),
        ],
        compiler_params=params(),
    )(det_bin, det_block, det_beam, owners, s0, *s1, weight)


def on_device(raw, replica, det_bin, det_block, det_beam, det_owner):
    devices = lax.axis_size("range")
    _, chans, pulses, gates = raw.shape
    bins = pulses
    flat = raw.reshape(2, chans * pulses, gates)
    before = [(source, source - 1) for source in range(1, devices)]
    *slices, mark = first_gates(flat)
    halos = [lax.ppermute(value, "range", before) for value in slices]
    table = doppler_matrix(pulses, 8)
    s0, local, matrix, *sent = spectra_first(flat, replica, table, pulses, mark)
    beside0 = [partner(value, (1, 1)) for value in sent]
    sums = cross([s0], bins)
    sums = cross(beside0, bins, sums)
    s1, beside1 = [], []
    for part, halo in enumerate(halos):
        value, send = spectra_last(part, local, halo, matrix, table, pulses, sums)
        s1.append(value)
        beside1.append(partner(send, (1, 1)))
    sums = cross(s1, bins, sums)
    sums = cross(beside1, bins, sums)
    own, packed = bin_sums(sums)
    total = gates * devices
    steer = steering(chans)
    left = from_bin(own, -1)
    right = from_bin(packed, 1)
    inverse, t = solve_middle(packed, steer, total)
    mine = solve_outer(own, left, right, steer, inverse, t, total, bins)
    groups = [list(range(first, first + bins)) for first in range(0, devices, bins)]
    weight = lax.all_to_all(
        mine, "range", split_axis=0, concat_axis=0, tiled=True,
        axis_index_groups=groups if len(groups) > 1 else None,
    )
    outgoing = beam_rows(
        det_bin, det_block, det_beam, det_owner[:, 0],
        s0.reshape(bins, 2 * chans, BLOCK), s1, weight, devices,
    )
    incoming = lax.all_to_all(
        outgoing.reshape(devices, CAP, 2 * BLOCK), "range", split_axis=0, concat_axis=0, tiled=True
    )
    return incoming.astype(F32).reshape(devices * CAP, 2 * BLOCK)


def solution(mesh):
    in_specs = (
        P(None, None, None, "range"),
        P(),
        P("range"),
        P("range"),
        P("range"),
        P("range", None),
    )
    out_specs = P("range", None)
    return jax.shard_map(
        on_device, mesh=mesh, in_specs=in_specs, out_specs=out_specs, check_vma=False
    )
```

```python
import functools
import math

import jax
import jax.numpy as jnp
import ml_dtypes
import numpy as np
from jax import lax
from jax.experimental import pallas as pl
from jax.experimental.pallas import tpu as pltpu
from jax.sharding import PartitionSpec as P

BLOCK = 128
BEAMS = 8
CAP = 2

F32 = jnp.float32
BF16 = jnp.bfloat16
VMEM = pltpu.VMEM
MIB = 1024 * 1024
NT = (((1,), (1,)), ((), ()))


def vmem_spec():
    return pl.BlockSpec(memory_space=VMEM)


def smem_spec():
    return pl.BlockSpec(memory_space=pltpu.SMEM)


def hbm_spec():
    return pl.BlockSpec(memory_space=pltpu.HBM)


SHORT = pl.CostEstimate(flops=1, bytes_accessed=1, transcendentals=0)


def params(mib=16):
    return pltpu.CompilerParams(vmem_limit_bytes=int(mib * MIB))


def dot(a, b):
    return jnp.dot(a, b, preferred_element_type=F32)


def dot_nt(a, b, precision=None):
    return lax.dot_general(a, b, NT, precision=precision, preferred_element_type=F32)


def iota(shape, axis):
    return lax.broadcasted_iota(jnp.int32, shape, axis)


def halo_kernel(raw_ref, a_ref, b_ref, mark_ref, sems):
    mark_ref[...] = jnp.zeros_like(mark_ref)
    count = sems.shape[0] // 2
    size = a_ref.shape[1] // count
    copies = []
    for part, out_ref in enumerate((a_ref, b_ref)):
        for j in range(count):
            start = part * a_ref.shape[1] + j * size
            copies.append(
                pltpu.make_async_copy(
                    raw_ref.at[:, start : start + size, :BLOCK],
                    out_ref.at[:, j * size : (j + 1) * size, :],
                    sems.at[part * count + j],
                )
            )
    for copy in copies:
        copy.start()
    for copy in copies:
        copy.wait()


def first_gates(raw):
    half = jax.ShapeDtypeStruct((2, raw.shape[1] // 2, BLOCK), BF16)
    return pl.pallas_call(
        halo_kernel,
        out_shape=[half, half, jax.ShapeDtypeStruct((8, 128), F32)],
        in_specs=[hbm_spec()],
        out_specs=[vmem_spec()] * 3,
        scratch_shapes=[pltpu.SemaphoreType.DMA((8,))],
        compiler_params=params(61.5),
    )(raw)


def correlation_matrix(rep_ref, out_ref):
    taps = rep_ref.shape[1]
    base = rep_ref[...].astype(F32)
    row = iota((taps, 2 * taps), 0)
    parts = []
    for i in range(2):
        line = jnp.concatenate([base[i : i + 1], jnp.zeros((1, taps), F32)], axis=1)
        skew = jnp.broadcast_to(line, (taps, 2 * taps))
        bit = 1
        while bit < taps:
            skew = jnp.where((row & bit) != 0, pltpu.roll(skew, bit, 1), skew)
            bit *= 2
        parts.append(skew.T)
    real_part, imag_part = parts
    out_ref[0] = jnp.concatenate([real_part, -imag_part], axis=1).astype(BF16)
    out_ref[1] = jnp.concatenate([imag_part, real_part], axis=1).astype(BF16)


def doppler_matrix(pulses, group):
    index = np.arange(pulses)
    angle = 2.0 * math.pi / pulses * (index[:, None] * index[None, :] % pulses)
    cosine = np.cos(angle) * pulses**-0.5
    sine = np.sin(angle) * pulses**-0.5
    table = np.stack([np.stack([cosine, -sine], 1), np.stack([sine, cosine], 1)], 0)
    full = np.einsum("ipod,ce->dociep", table, np.eye(group))
    shape = (pulses * 2 * group, 2 * group * pulses)
    return full.reshape(shape).astype(ml_dtypes.bfloat16)


def doppler_rows(total, dft):
    compressed = total.astype(BF16)
    rows, wide = compressed.shape
    half, gates = rows // 2, wide // 2
    stacked = jnp.concatenate(
        [
            jnp.concatenate([compressed[:half, :gates], compressed[half:, :gates]], axis=1),
            jnp.concatenate([compressed[:half, gates:], compressed[half:, gates:]], axis=1),
        ],
        axis=0,
    )
    both = dot(dft, stacked)
    lines = both.shape[0] // 8
    joined = jnp.concatenate(
        [both[:, :gates].reshape(lines, 8, gates), both[:, gates:].reshape(lines, 8, gates)],
        axis=1,
    )
    return joined.astype(BF16)


GROUP = 16


def half_of_bins(bins, mine):
    core = lax.axis_index("range") & 1
    return (core if mine else 1 - core) * (bins // 2)


def sent_bins(bins):
    return bins // 2 + 2


def spectra_first_kernel(raw_ref, rep_ref, dft_ref, _, s_ref, local_ref, taps_ref, *rest):
    *send_refs, buf, sems = rest
    bins, _, chans, gates = s_ref.shape
    size = GROUP * bins
    copies = [
        pltpu.make_async_copy(
            raw_ref.at[:, j * size : (j + 1) * size, :],
            buf.at[:, j * size : (j + 1) * size, :],
            sems.at[j],
        )
        for j in range(chans // GROUP)
    ]
    for copy in copies:
        copy.start()
    correlation_matrix(rep_ref, taps_ref)
    for j, copy in enumerate(copies):
        copy.wait()
        rows = slice(j * size, (j + 1) * size)
        total = dot(buf[0, rows, :], taps_ref[0]) + dot(buf[1, rows, :], taps_ref[1])
        out = doppler_rows(total, dft_ref[...])
        s_ref[:, :, j * GROUP : (j + 1) * GROUP, :] = out.reshape(bins, 2, GROUP, gates)
        later = jnp.concatenate([buf[0, rows, gates:], buf[1, rows, gates:]], axis=1)
        near = jnp.concatenate([taps_ref[0, :gates, :], taps_ref[1, :gates, :]], axis=0)
        local_ref[rows, :] = dot(later, near)
    base = half_of_bins(bins, False)
    half = chans // 2
    for part, send_ref in enumerate(send_refs):
        for k in range(send_ref.shape[0]):
            send_ref[k] = s_ref[lax.rem(base + k, bins), :, part * half : (part + 1) * half, :]


def spectra_last_kernel(part, local_ref, halo_ref, taps_ref, dft_ref, _, s_ref, send_ref):
    bins, _, chans, gates = s_ref.shape
    size = GROUP * bins
    far = jnp.concatenate([taps_ref[0, gates:, :], taps_ref[1, gates:, :]], axis=0)
    for j in range(chans // GROUP):
        rows = slice(j * size, (j + 1) * size)
        later = jnp.concatenate([halo_ref[0, rows, :], halo_ref[1, rows, :]], axis=1)
        start = part * chans * bins + j * size
        out = doppler_rows(local_ref[start : start + size, :] + dot(later, far), dft_ref[...])
        s_ref[:, :, j * GROUP : (j + 1) * GROUP, :] = out.reshape(bins, 2, GROUP, gates)
    base = half_of_bins(bins, False)
    for k in range(send_ref.shape[0]):
        send_ref[k] = s_ref[lax.rem(base + k, bins)]


def spectra_first(raw, replica, table, pulses, mark):
    _, rows, gates = raw.shape
    chans = rows // pulses
    taps = replica.shape[1]
    return pl.pallas_call(
        spectra_first_kernel,
        out_shape=[
            jax.ShapeDtypeStruct((pulses, 2, chans, BLOCK), BF16),
            jax.ShapeDtypeStruct((rows, 2 * BLOCK), F32),
            jax.ShapeDtypeStruct((2, 2 * taps, 2 * taps), BF16),
        ]
        + [jax.ShapeDtypeStruct((sent_bins(pulses), 2, chans // 2, BLOCK), BF16)] * 2,
        in_specs=[hbm_spec(), vmem_spec(), vmem_spec(), pl.BlockSpec(memory_space=pl.ANY)],
        out_specs=[vmem_spec()] * 5,
        scratch_shapes=[
            pltpu.VMEM(raw.shape, BF16),
            pltpu.SemaphoreType.DMA((chans // GROUP,)),
        ],
        compiler_params=params(),
        cost_estimate=SHORT,
    )(raw, replica, table, mark)


def spectra_last(part, local, halo, matrix, table, pulses, sums):
    chans = halo.shape[1] // pulses
    return pl.pallas_call(
        functools.partial(spectra_last_kernel, part),
        out_shape=[
            jax.ShapeDtypeStruct((pulses, 2, chans, BLOCK), BF16),
            jax.ShapeDtypeStruct((sent_bins(pulses), 2, chans, BLOCK), BF16),
        ],
        in_specs=[vmem_spec()] * 4 + [pl.BlockSpec(memory_space=pl.ANY)],
        out_specs=[vmem_spec()] * 2,
        compiler_params=params(),
        cost_estimate=SHORT,
    )(local, halo, matrix, table, sums)


def cross_kernel(count_refs, *refs):
    s_refs, rest = refs[:count_refs], refs[count_refs:]
    before_ref = rest[0] if len(rest) == 2 else None
    out_ref = rest[-1]
    held, _, _, gates = s_refs[0].shape
    chans = sum(ref.shape[2] for ref in s_refs)
    count = out_ref.shape[0]
    base = half_of_bins(held, True) if held == 2 * count else 0

    def write(e, block):
        out_ref[e] = block if before_ref is None else block + before_ref[e]

    @pl.loop(0, count // 2, unroll=2)
    def _(step):
        e = step * 2
        each = []
        for k in range(4):
            where = lax.rem(base + e + k, held)
            each.append(
                [jnp.concatenate([ref[where, o] for ref in s_refs], axis=0) for o in range(2)]
            )
        left = jnp.concatenate(
            [jnp.concatenate([re, im], axis=1) for re, im in each], axis=0
        )
        right = jnp.concatenate(
            [
                jnp.concatenate(pieces, axis=1)
                for re, im in each[:2]
                for pieces in ((re, im), (-im, re))
            ],
            axis=0,
        )
        both = dot_nt(left, right)
        write(e, both[: 3 * chans, : 2 * chans])
        write(e + 1, both[chans:, 2 * chans :])


def cross(spectra, bins, before=None):
    chans = sum(value.shape[2] for value in spectra)
    data = spectra if before is None else spectra + [before]
    return pl.pallas_call(
        functools.partial(cross_kernel, len(spectra)),
        out_shape=jax.ShapeDtypeStruct((bins // 2, 3 * chans, 2 * chans), F32),
        in_specs=[vmem_spec()] * len(data),
        out_specs=vmem_spec(),
        compiler_params=params(),
        cost_estimate=SHORT,
    )(*data)


U_BITS, V_BITS = (2, 4), (4, 2)


def partner(value, bits):
    count = lax.axis_size("range")
    return lax.ppermute(value, "range", [(i, i ^ bits[i & 1]) for i in range(count)])


def slot_of(core, x, y, z):
    return (4 * z + ((2 * y + (x ^ y)) ^ (3 * (z & 1)))) ^ (15 * core)


def parts_of(index):
    return index & 1, (index >> 1) & 1, (index >> 2) & 1, (index >> 3) & 3


def bin_of(index):
    core, x, y, z = parts_of(index)
    return core * 16 + slot_of(core, x, y, z)


def index_of(bin_id):
    core = bin_id >> 4
    path = (bin_id & 15) ^ (15 * core)
    z = path >> 2
    turned = (path & 3) ^ (3 * (z & 1))
    y = turned >> 1
    x = (turned & 1) ^ y
    return z * 8 + y * 4 + x * 2 + core


def uv_parts():
    core, x, y, z = parts_of(lax.axis_index("range"))
    return core, jnp.where(core == 0, x, y), jnp.where(core == 0, y, x), z


def uv_slot(core, u, v, z):
    return slot_of(core, jnp.where(core == 0, u, v), jnp.where(core == 0, v, u), z)


def packed(block):
    chans = block.shape[0]
    lower = iota((chans, chans), 0) >= iota((chans, chans), 1)
    swapped = pltpu.roll(block, chans, 1)
    mixed = jnp.where(lower, block[:, :chans], swapped[:, :chans])
    return jnp.concatenate([mixed[: chans // 2], mixed[chans // 2 :]], axis=1)


def sent_rows(keep_ref):
    return 5 * keep_ref.shape[1] // 6


def upper_rows(keep_ref, e):
    block = keep_ref.shape[1] // 3
    end = sent_rows(keep_ref) // 2 + block // 2
    return jnp.concatenate([packed(keep_ref[e, :block]), keep_ref[e, block:end]], axis=0)


def lower_rows(keep_ref, e):
    return keep_ref[e, sent_rows(keep_ref) // 2 + keep_ref.shape[1] // 6 :]


def first_kernel(keep_ref, a_ref, b_ref):
    core, u, v, z = uv_parts()
    for k in range(8):
        a_ref[k] = upper_rows(keep_ref, uv_slot(core, 1 - u, k // 4, k % 4))
        b_ref[k] = lower_rows(keep_ref, uv_slot(core, k // 4, 1 - v, k % 4))


def second_kernel(keep_ref, a1_ref, b1_ref, a_ref, b_ref):
    core, u, v, z = uv_parts()
    for k in range(4):
        e = uv_slot(core, u, 1 - v, k)
        a_ref[k] = upper_rows(keep_ref, e) + a1_ref[(1 - v) * 4 + k]
        e = uv_slot(core, 1 - u, v, k)
        b_ref[k] = lower_rows(keep_ref, e) + b1_ref[(1 - u) * 4 + k]


def line_sum(keep_ref, a1_ref, b1_ref, a2_ref, b2_ref, flip):
    core, u, v, z = uv_parts()
    z = z ^ flip
    e = uv_slot(core, u, v, z)
    upper = upper_rows(keep_ref, e) + a1_ref[v * 4 + z] + a2_ref[z]
    lower = lower_rows(keep_ref, e) + b1_ref[u * 4 + z] + b2_ref[z]
    return upper, lower


FLIPS = (2, 3, 1)


def line_kernel(*refs):
    half = sent_rows(refs[0]) // 2
    for flip, out_ref in zip(FLIPS, refs[5:]):
        upper, lower = line_sum(*refs[:5], flip)
        out_ref[:half] = upper
        out_ref[half:] = lower


def own_kernel(*refs):
    z1_ref, z2_ref, z3_ref, out_ref, packed_ref = refs[5:]
    half = sent_rows(refs[0]) // 2
    upper, lower = line_sum(*refs[:5], 0)
    upper = upper + z1_ref[:half] + (z2_ref[:half] + z3_ref[:half])
    out_ref[:half] = upper
    packed_ref[...] = upper[: packed_ref.shape[0]]
    out_ref[half:] = lower + z1_ref[half:] + (z2_ref[half:] + z3_ref[half:])


def summed(kernel, data, shapes):
    return pl.pallas_call(
        kernel,
        out_shape=[jax.ShapeDtypeStruct(shape, F32) for shape in shapes],
        in_specs=[vmem_spec()] * len(data),
        out_specs=[vmem_spec()] * len(shapes),
        compiler_params=params(),
    )(*data)


def bin_sums(keep):
    _, full, wide = keep.shape
    rows = 5 * full // 6
    half = rows // 2
    data = [keep]
    a, b = summed(first_kernel, data, [(8, half, wide)] * 2)
    data += [partner(a, U_BITS), partner(b, V_BITS)]
    a, b = summed(second_kernel, data, [(4, half, wide)] * 2)
    data += [partner(a, V_BITS), partner(b, U_BITS)]
    sends = summed(line_kernel, data, [(rows, wide)] * 3)
    data += [partner(value, (8 * flip, 8 * flip)) for flip, value in zip(FLIPS, sends)]
    own, packed = summed(own_kernel, data, [(rows, wide), (rows // 5, wide)])
    bit = 32
    while bit < lax.axis_size("range"):
        own = own + partner(own, (bit, bit))
        packed = packed + partner(packed, (bit, bit))
        bit *= 2
    return own, packed


def from_bin(value, offset):
    count = lax.axis_size("range")
    pairs = []
    for i in range(count):
        target = index_of((bin_of(i) - offset) % 32) | (i & ~31)
        pairs.append((i, target))
    return lax.ppermute(value, "range", pairs)


def turn(value):
    half = value.shape[1] // 2
    rolled = pltpu.roll(value, half, 1)
    return jnp.where(iota(value.shape, 1) < half, -rolled, rolled)


def embed(value):
    return jnp.concatenate([value, turn(value)], axis=0)


def mul(a, b):
    return jnp.dot(a, embed(b), precision=lax.Precision.HIGHEST, preferred_element_type=F32)


def mul_conj(a, b):
    half = a.shape[1] // 2
    stacked = jnp.concatenate([a, -turn(a)], axis=0)
    both = dot_nt(stacked, b, lax.Precision.HIGHEST)
    rows = a.shape[0]
    return jnp.concatenate([both[:rows], both[rows:]], axis=1)


def reciprocal(x):
    value = pl.reciprocal(x, approx=True)
    for _ in range(2):
        value = value * (2.0 - x * value)
    return value


def pivot_inverse(p):
    def times(x, y):
        return x[0] * y[0] - x[1] * y[1], x[0] * y[1] + x[1] * y[0]

    def conj(x):
        return x[0], -x[1]

    def plus(x, y):
        return x[0] + y[0], x[1] + y[1]

    def scaled(x, s):
        return x[0] * s, x[1] * s

    def square(x):
        return x[0] * x[0] + x[1] * x[1]

    def two(a, b, d):
        inv = reciprocal(a * d - square(b))
        return d * inv, scaled(b, -inv), a * inv

    a, d = p[0][0], p[1][1]
    b = p[0][1]
    ea, eb, ed = two(a, b, d)
    f = [[p[0][2], p[0][3]], [p[1][2], p[1][3]]]
    w = [
        [plus(scaled(f[0][j], ea), times(eb, f[1][j])) for j in range(2)],
        [plus(times(conj(eb), f[0][j]), scaled(f[1][j], ed)) for j in range(2)],
    ]

    def inner(i, j):
        return plus(times(conj(f[0][i]), w[0][j]), times(conj(f[1][i]), w[1][j]))

    ha = p[2][2] - inner(0, 0)[0]
    hd = p[3][3] - inner(1, 1)[0]
    cross = inner(0, 1)
    hb = (p[2][3][0] - cross[0], p[2][3][1] - cross[1])
    ga, gb, gd = two(ha, hb, hd)
    v = [
        [
            plus(scaled(w[i][0], ga), times(w[i][1], conj(gb))),
            plus(times(w[i][0], gb), scaled(w[i][1], gd)),
        ]
        for i in range(2)
    ]
    top = [
        [plus(times(v[i][0], conj(w[j][0])), times(v[i][1], conj(w[j][1]))) for j in range(2)]
        for i in range(2)
    ]
    zero = None
    out = [[None] * 4 for _ in range(4)]
    out[0][0] = (ea + top[0][0][0], zero)
    out[1][1] = (ed + top[1][1][0], zero)
    out[0][1] = plus(eb, top[0][1])
    out[2][2], out[3][3], out[2][3] = (ga, zero), (gd, zero), gb
    for i in range(2):
        for j in range(2):
            out[i][2 + j] = (-v[i][j][0], -v[i][j][1])
    for i in range(4):
        for j in range(i):
            out[i][j] = conj(out[j][i])
    return out


def invert(matrix):
    chans, width = matrix.shape
    sub = 8
    tiles = [matrix[t * sub : (t + 1) * sub, :] for t in range(chans // sub)]
    lane = iota((sub, width), 1)
    row = iota((sub, width), 0)
    first_half = lane < chans

    def spin(value):
        rolled = pltpu.roll(value, chans, 1)
        return jnp.where(first_half, -rolled, rolled)

    def column(value, k):
        return jnp.broadcast_to(value[:, k : k + 1], (sub, width))

    def combine(terms):
        while len(terms) > 1:
            terms = [
                terms[i] + terms[i + 1] if i + 1 < len(terms) else terms[i]
                for i in range(0, len(terms), 2)
            ]
        return terms[0]

    for k in range(0, chans, 4):
        t, r = divmod(k, sub)
        lines = [jnp.broadcast_to(tiles[t][r + i : r + i + 1, :], (sub, width)) for i in range(4)]
        pivot = [[None] * 4 for _ in range(4)]
        for i in range(4):
            pivot[i][i] = column(lines[i], k + i)
            for j in range(i + 1, 4):
                pivot[i][j] = column(lines[i], k + j), column(lines[i], chans + k + j)
        low = jnp.bitwise_and(lane, chans - 1)
        cleared = (low >= k) & (low < k + 4)
        unit = [
            jnp.where(cleared, jnp.where(lane == k + i, 1.0, 0.0), lines[i]) for i in range(4)
        ]
        spun = [spin(u) for u in unit]
        p = pivot_inverse(pivot)
        fresh_lines, fresh_spun = [], []
        for i in range(4):
            terms, other = [], []
            for j in range(4):
                re, im = p[i][j]
                terms.append(re * unit[j])
                other.append(re * spun[j])
                if im is not None:
                    terms.append(im * spun[j])
                    other.append(-(im * unit[j]))
            fresh_lines.append(combine(terms))
            fresh_spun.append(combine(other))
        fresh = []
        for s, tile in enumerate(tiles):
            terms = []
            for i in range(4):
                terms.append(column(tile, k + i) * fresh_lines[i])
                terms.append(column(tile, chans + k + i) * fresh_spun[i])
            value = jnp.where(cleared, 0.0, tile) - combine(terms)
            if s == t:
                for i in range(4):
                    value = jnp.where(row == r + i, fresh_lines[i], value)
            fresh.append(value)
        tiles = fresh
    return jnp.concatenate(tiles, axis=0)


def unpacked(ref, scale):
    half, wide = ref.shape[0], ref.shape[1]
    piece = ref[...] * scale
    swapped = pltpu.roll(piece, wide // 2, 1)
    return jnp.concatenate([piece, swapped], axis=0)[:, : wide // 2]


def hermitian(mixed, across):
    i, j = iota(mixed.shape, 0), iota(mixed.shape, 1)
    real_part = jnp.where(i >= j, mixed, across)
    imag_part = jnp.where(i < j, mixed, jnp.where(i > j, -across, 0.0))
    return jnp.concatenate([real_part, imag_part], axis=1)


def middle_kernel(total, packed_ref, steer_ref, inv_ref, t_ref):
    chans = inv_ref.shape[0]
    mixed = unpacked(packed_ref, F32(1.0 / total))
    twice = jnp.concatenate([mixed, mixed], axis=1)
    across = jnp.concatenate([twice, twice], axis=0).T[:chans, :chans]
    inverse = invert(hermitian(mixed, across))
    inv_ref[...] = inverse
    t_ref[...] = mul(steer_ref[...], inverse)


def outer_kernel(total, own_ref, left_ref, right_ref, steer_ref, inv_ref, t_ref, out_ref,
                 work, keep, small):
    chans = inv_ref.shape[0]
    scale = F32(1.0 / total)
    half = chans // 2
    m_left = unpacked(left_ref.at[:half], scale)
    m_right = unpacked(right_ref, scale)
    ml = left_ref[half : half + chans] * scale
    rl = left_ref[half + chans :] * scale
    rm = own_ref[half : half + chans] * scale
    across = jnp.concatenate([jnp.concatenate([m_left, m_right], axis=1), ml], axis=0).T
    lm = jnp.concatenate([across[:chans, chans:], -across[chans:, chans:]], axis=1)
    t = t_ref[...]
    both = mul(jnp.concatenate([rm, lm], axis=0), inv_ref[...])
    g_right, g_left = both[:chans], both[chans:]
    by_left = mul(jnp.concatenate([g_left, g_right, t], axis=0), ml)
    by_right = mul_conj(jnp.concatenate([g_right, t], axis=0), rm)
    work[...] = hermitian(m_left, across[:chans, :chans]) - by_left[:chans]
    keep[0] = rl - by_left[chans : 2 * chans]
    keep[1] = hermitian(m_right, across[chans:, :chans]) - by_right[:chans]
    keep[2] = g_left
    keep[3] = g_right
    small[0] = -by_left[2 * chans :]
    small[1] = -by_right[chans:]

    @pl.loop(0, 2)
    def _(stage):
        work[...] = invert(work[...])

        @pl.when(stage == 0)
        def _():
            s_rl = keep[0]
            both = mul(jnp.concatenate([s_rl, small[0]], axis=0), work[...])
            back = mul_conj(both, s_rl)
            work[...] = keep[1] - back[:chans]
            small[1] = small[1] - back[chans:]
            middle = mul(both, keep[2])
            keep[0] = both[:chans]
            small[0] = both[chans:]
            keep[3] = keep[3] - middle[:chans]
            small[2] = t_ref[...] - middle[chans:]

        @pl.when(stage == 1)
        def _():
            y_right = mul(small[1], work[...])
            factors = jnp.concatenate([embed(keep[0]), embed(keep[3])], axis=1)
            both = jnp.dot(
                y_right, factors, precision=lax.Precision.HIGHEST, preferred_element_type=F32
            )
            y_left = small[0] - both[:, : 2 * chans]
            y_mid = small[2] - both[:, 2 * chans :]
            quad = jnp.sum(steer_ref[...] * y_mid, axis=1, keepdims=True)
            y = jnp.concatenate([y_left, y_mid, y_right], axis=1) / jnp.sqrt(quad)
            real_lane = lax.rem(iota(y.shape, 1), 2 * chans) < chans
            mine = jnp.where(real_lane, y, -y).astype(BF16)
            for c in range(out_ref.shape[0]):
                out_ref[c] = mine


def steering(chans):
    index = np.arange(chans)
    sines = -0.8 + 1.6 * np.arange(BEAMS) / (BEAMS - 1)
    angle = math.pi * sines[:, None] * index[None, :]
    return np.concatenate([np.cos(angle), -np.sin(angle)], axis=1).astype(np.float32)


def solve_middle(packed, steer, total):
    half, wide = packed.shape
    return pl.pallas_call(
        functools.partial(middle_kernel, total),
        out_shape=[
            jax.ShapeDtypeStruct((2 * half, wide), F32),
            jax.ShapeDtypeStruct((BEAMS, wide), F32),
        ],
        in_specs=[vmem_spec()] * 2,
        out_specs=[vmem_spec()] * 2,
        compiler_params=params(),
    )(packed, steer)


def solve_outer(own, left, right, steer, inverse, t, total, copies):
    chans, wide = inverse.shape
    return pl.pallas_call(
        functools.partial(outer_kernel, total),
        out_shape=jax.ShapeDtypeStruct((copies, BEAMS, 3 * wide), BF16),
        in_specs=[vmem_spec()] * 6,
        out_specs=vmem_spec(),
        scratch_shapes=[
            pltpu.VMEM((chans, wide), F32),
            pltpu.VMEM((4, chans, wide), F32),
            pltpu.VMEM((3, BEAMS, wide), F32),
        ],
        compiler_params=params(),
    )(own, left, right, steer, inverse, t)


def beam_kernel(bin_ref, block_ref, beam_ref, owner_ref, s0_ref, upper_ref, lower_ref, w_ref,
                out_ref, both_ref, rows_ref, seen_ref):
    bins, wide, gates = s0_ref.shape
    devices = seen_ref.shape[0]
    count = bin_ref.shape[0]
    rows_ref[...] = jnp.zeros_like(rows_ref)

    @pl.loop(0, devices)
    def _(i):
        seen_ref[i] = 0

    w = w_ref[...].astype(F32).reshape(bins * BEAMS, 3 * wide)
    for k in range(3):
        lanes = slice(k * wide, (k + 1) * wide)
        part = w[:, lanes]
        both_ref[:, 0:BEAMS, lanes] = part.reshape(bins, BEAMS, wide)
        both_ref[:, BEAMS:, lanes] = turn(part).reshape(bins, BEAMS, wide)

    def detection(j, carry):
        bin_id = bin_ref[j]
        beam_id = beam_ref[j]
        owner = owner_ref[j]
        rank = seen_ref[owner]
        seen_ref[owner] = rank + 1
        left = both_ref[index_of(bin_id)].astype(BF16)
        bands = [lax.rem(bin_id + bins - 1 + k, bins) for k in range(3)]
        first = block_ref[j] == 0
        pieces = []
        for b in bands:
            later = [upper_ref[b, 0], lower_ref[b, 0], upper_ref[b, 1], lower_ref[b, 1]]
            pieces.append(jnp.where(first, s0_ref[b], jnp.concatenate(later, axis=0)))
        window = jnp.concatenate(pieces, axis=0)
        both = dot(left, window)
        line = jnp.concatenate([both[:BEAMS], both[BEAMS:]], axis=1)
        chosen = jnp.where(iota(line.shape, 0) == beam_id, line, 0.0)
        row = owner * CAP + rank
        rows_ref[pl.ds(row, 1), :] = jnp.sum(chosen, axis=0, keepdims=True)
        return carry

    lax.fori_loop(0, count, detection, 0, unroll=32)
    out_ref[...] = rows_ref[...].astype(BF16)


def beam_rows(det_bin, det_block, det_beam, owners, s0, s1, weight, devices):
    bins, wide, gates = s0.shape
    return pl.pallas_call(
        beam_kernel,
        out_shape=jax.ShapeDtypeStruct((devices * CAP, 2 * gates), BF16),
        in_specs=[smem_spec()] * 4 + [vmem_spec()] * 4,
        out_specs=vmem_spec(),
        scratch_shapes=[
            pltpu.VMEM((bins, 2 * BEAMS, 3 * wide), F32),
            pltpu.VMEM((devices * CAP, 2 * gates), F32),
            pltpu.SMEM((devices,), jnp.int32),
        ],
        compiler_params=params(),
    )(det_bin, det_block, det_beam, owners, s0, *s1, weight)


def on_device(raw, replica, det_bin, det_block, det_beam, det_owner):
    devices = lax.axis_size("range")
    _, chans, pulses, gates = raw.shape
    bins = pulses
    flat = raw.reshape(2, chans * pulses, gates)
    before = [(source, source - 1) for source in range(1, devices)]
    *slices, mark = first_gates(flat)
    halos = [lax.ppermute(value, "range", before) for value in slices]
    table = doppler_matrix(pulses, 8)
    s0, local, matrix, *sent = spectra_first(flat, replica, table, pulses, mark)
    beside0 = [partner(value, (1, 1)) for value in sent]
    sums = cross([s0], bins)
    sums = cross(beside0, bins, sums)
    s1, beside1 = [], []
    for part, halo in enumerate(halos):
        value, send = spectra_last(part, local, halo, matrix, table, pulses, sums)
        s1.append(value)
        beside1.append(partner(send, (1, 1)))
    sums = cross(s1, bins, sums)
    sums = cross(beside1, bins, sums)
    own, packed = bin_sums(sums)
    total = gates * devices
    steer = steering(chans)
    left = from_bin(own, -1)
    right = from_bin(packed, 1)
    inverse, t = solve_middle(packed, steer, total)
    mine = solve_outer(own, left, right, steer, inverse, t, total, bins)
    groups = [list(range(first, first + bins)) for first in range(0, devices, bins)]
    weight = lax.all_to_all(
        mine, "range", split_axis=0, concat_axis=0, tiled=True,
        axis_index_groups=groups if len(groups) > 1 else None,
    )
    outgoing = beam_rows(
        det_bin, det_block, det_beam, det_owner[:, 0],
        s0.reshape(bins, 2 * chans, BLOCK), s1, weight, devices,
    )
    incoming = lax.all_to_all(
        outgoing.reshape(devices, CAP, 2 * BLOCK), "range", split_axis=0, concat_axis=0, tiled=True
    )
    return incoming.astype(F32).reshape(devices * CAP, 2 * BLOCK)


def solution(mesh):
    in_specs = (
        P(None, None, None, "range"),
        P(),
        P("range"),
        P("range"),
        P("range"),
        P("range", None),
    )
    out_specs = P("range", None)
    return jax.shard_map(
        on_device, mesh=mesh, in_specs=in_specs, out_specs=out_specs, check_vma=False
    )
```

```python
import functools
import math

import jax
import jax.numpy as jnp
import ml_dtypes
import numpy as np
from jax import lax
from jax.experimental import pallas as pl
from jax.experimental.pallas import tpu as pltpu
from jax.sharding import PartitionSpec as P

BLOCK = 128
BEAMS = 8
CAP = 2

F32 = jnp.float32
BF16 = jnp.bfloat16
VMEM = pltpu.VMEM
MIB = 1024 * 1024
NT = (((1,), (1,)), ((), ()))


def vmem_spec():
    return pl.BlockSpec(memory_space=VMEM)


def smem_spec():
    return pl.BlockSpec(memory_space=pltpu.SMEM)


def hbm_spec():
    return pl.BlockSpec(memory_space=pltpu.HBM)


SHORT = pl.CostEstimate(flops=1, bytes_accessed=1, transcendentals=0)


def params(mib=16):
    return pltpu.CompilerParams(vmem_limit_bytes=int(mib * MIB))


def dot(a, b):
    return jnp.dot(a, b, preferred_element_type=F32)


def dot_nt(a, b, precision=None):
    return lax.dot_general(a, b, NT, precision=precision, preferred_element_type=F32)


def iota(shape, axis):
    return lax.broadcasted_iota(jnp.int32, shape, axis)


def halo_kernel(raw_ref, a_ref, b_ref, mark_ref, sems):
    mark_ref[...] = jnp.zeros_like(mark_ref)
    count = sems.shape[0] // 2
    size = a_ref.shape[1] // count
    copies = []
    for part, out_ref in enumerate((a_ref, b_ref)):
        for j in range(count):
            start = part * a_ref.shape[1] + j * size
            copies.append(
                pltpu.make_async_copy(
                    raw_ref.at[:, start : start + size, :BLOCK],
                    out_ref.at[:, j * size : (j + 1) * size, :],
                    sems.at[part * count + j],
                )
            )
    for copy in copies:
        copy.start()
    for copy in copies:
        copy.wait()


def first_gates(raw):
    half = jax.ShapeDtypeStruct((2, raw.shape[1] // 2, BLOCK), BF16)
    return pl.pallas_call(
        halo_kernel,
        out_shape=[half, half, jax.ShapeDtypeStruct((8, 128), F32)],
        in_specs=[hbm_spec()],
        out_specs=[vmem_spec()] * 3,
        scratch_shapes=[pltpu.SemaphoreType.DMA((8,))],
        compiler_params=params(61.5),
    )(raw)


def correlation_matrix(rep_ref, out_ref):
    taps = rep_ref.shape[1]
    base = rep_ref[...].astype(F32)
    row = iota((taps, 2 * taps), 0)
    parts = []
    for i in range(2):
        line = jnp.concatenate([base[i : i + 1], jnp.zeros((1, taps), F32)], axis=1)
        skew = jnp.broadcast_to(line, (taps, 2 * taps))
        bit = 1
        while bit < taps:
            skew = jnp.where((row & bit) != 0, pltpu.roll(skew, bit, 1), skew)
            bit *= 2
        parts.append(skew.T)
    real_part, imag_part = parts
    out_ref[0] = jnp.concatenate([real_part, -imag_part], axis=1).astype(BF16)
    out_ref[1] = jnp.concatenate([imag_part, real_part], axis=1).astype(BF16)


def doppler_matrix(pulses, group):
    index = np.arange(pulses)
    angle = 2.0 * math.pi / pulses * (index[:, None] * index[None, :] % pulses)
    cosine = np.cos(angle) * pulses**-0.5
    sine = np.sin(angle) * pulses**-0.5
    table = np.stack([np.stack([cosine, -sine], 1), np.stack([sine, cosine], 1)], 0)
    full = np.einsum("ipod,ce->dociep", table, np.eye(group))
    shape = (pulses * 2 * group, 2 * group * pulses)
    return full.reshape(shape).astype(ml_dtypes.bfloat16)


def doppler_rows(total, dft):
    compressed = total.astype(BF16)
    rows, wide = compressed.shape
    half, gates = rows // 2, wide // 2
    stacked = jnp.concatenate(
        [
            jnp.concatenate([compressed[:half, :gates], compressed[half:, :gates]], axis=1),
            jnp.concatenate([compressed[:half, gates:], compressed[half:, gates:]], axis=1),
        ],
        axis=0,
    )
    both = dot(dft, stacked)
    lines = both.shape[0] // 8
    joined = jnp.concatenate(
        [both[:, :gates].reshape(lines, 8, gates), both[:, gates:].reshape(lines, 8, gates)],
        axis=1,
    )
    return joined.astype(BF16)


GROUP = 16


def half_of_bins(bins, mine):
    core = lax.axis_index("range") & 1
    return (core if mine else 1 - core) * (bins // 2)


def sent_bins(bins):
    return bins // 2 + 2


def spectra_first_kernel(raw_ref, rep_ref, dft_ref, _, s_ref, local_ref, taps_ref, *rest):
    *send_refs, buf, sems = rest
    bins, _, chans, gates = s_ref.shape
    size = GROUP * bins
    copies = [
        pltpu.make_async_copy(
            raw_ref.at[:, j * size : (j + 1) * size, :],
            buf.at[:, j * size : (j + 1) * size, :],
            sems.at[j],
        )
        for j in range(chans // GROUP)
    ]
    for copy in copies:
        copy.start()
    correlation_matrix(rep_ref, taps_ref)
    for j, copy in enumerate(copies):
        copy.wait()
        rows = slice(j * size, (j + 1) * size)
        total = dot(buf[0, rows, :], taps_ref[0]) + dot(buf[1, rows, :], taps_ref[1])
        out = doppler_rows(total, dft_ref[...])
        s_ref[:, :, j * GROUP : (j + 1) * GROUP, :] = out.reshape(bins, 2, GROUP, gates)
        later = jnp.concatenate([buf[0, rows, gates:], buf[1, rows, gates:]], axis=1)
        near = jnp.concatenate([taps_ref[0, :gates, :], taps_ref[1, :gates, :]], axis=0)
        local_ref[rows, :] = dot(later, near)
    base = half_of_bins(bins, False)
    half = chans // 2
    for part, send_ref in enumerate(send_refs):
        for k in range(send_ref.shape[0]):
            send_ref[k] = s_ref[lax.rem(base + k, bins), :, part * half : (part + 1) * half, :]


def spectra_last_kernel(part, local_ref, halo_ref, taps_ref, dft_ref, _, s_ref, send_ref):
    bins, _, chans, gates = s_ref.shape
    size = GROUP * bins
    far = jnp.concatenate([taps_ref[0, gates:, :], taps_ref[1, gates:, :]], axis=0)
    for j in range(chans // GROUP):
        rows = slice(j * size, (j + 1) * size)
        later = jnp.concatenate([halo_ref[0, rows, :], halo_ref[1, rows, :]], axis=1)
        start = part * chans * bins + j * size
        out = doppler_rows(local_ref[start : start + size, :] + dot(later, far), dft_ref[...])
        s_ref[:, :, j * GROUP : (j + 1) * GROUP, :] = out.reshape(bins, 2, GROUP, gates)
    base = half_of_bins(bins, False)
    for k in range(send_ref.shape[0]):
        send_ref[k] = s_ref[lax.rem(base + k, bins)]


def spectra_first(raw, replica, table, pulses, mark):
    _, rows, gates = raw.shape
    chans = rows // pulses
    taps = replica.shape[1]
    return pl.pallas_call(
        spectra_first_kernel,
        out_shape=[
            jax.ShapeDtypeStruct((pulses, 2, chans, BLOCK), BF16),
            jax.ShapeDtypeStruct((rows, 2 * BLOCK), F32),
            jax.ShapeDtypeStruct((2, 2 * taps, 2 * taps), BF16),
        ]
        + [jax.ShapeDtypeStruct((sent_bins(pulses), 2, chans // 2, BLOCK), BF16)] * 2,
        in_specs=[hbm_spec(), vmem_spec(), vmem_spec(), pl.BlockSpec(memory_space=pl.ANY)],
        out_specs=[vmem_spec()] * 5,
        scratch_shapes=[
            pltpu.VMEM(raw.shape, BF16),
            pltpu.SemaphoreType.DMA((chans // GROUP,)),
        ],
        compiler_params=params(),
        cost_estimate=SHORT,
    )(raw, replica, table, mark)


def spectra_last(part, local, halo, matrix, table, pulses, sums):
    chans = halo.shape[1] // pulses
    return pl.pallas_call(
        functools.partial(spectra_last_kernel, part),
        out_shape=[
            jax.ShapeDtypeStruct((pulses, 2, chans, BLOCK), BF16),
            jax.ShapeDtypeStruct((sent_bins(pulses), 2, chans, BLOCK), BF16),
        ],
        in_specs=[vmem_spec()] * 4 + [pl.BlockSpec(memory_space=pl.ANY)],
        out_specs=[vmem_spec()] * 2,
        compiler_params=params(),
        cost_estimate=SHORT,
    )(local, halo, matrix, table, sums)


def cross_kernel(count_refs, *refs):
    s_refs, rest = refs[:count_refs], refs[count_refs:]
    before_ref = rest[0] if len(rest) == 2 else None
    out_ref = rest[-1]
    held, _, _, gates = s_refs[0].shape
    chans = sum(ref.shape[2] for ref in s_refs)
    count = out_ref.shape[0]
    base = half_of_bins(held, True) if held == 2 * count else 0

    def write(e, block):
        out_ref[e] = block if before_ref is None else block + before_ref[e]

    @pl.loop(0, count // 2, unroll=8)
    def _(step):
        e = step * 2
        each = []
        for k in range(4):
            where = lax.rem(base + e + k, held)
            each.append(
                [jnp.concatenate([ref[where, o] for ref in s_refs], axis=0) for o in range(2)]
            )
        left = jnp.concatenate(
            [jnp.concatenate([re, im], axis=1) for re, im in each], axis=0
        )
        right = jnp.concatenate(
            [
                jnp.concatenate(pieces, axis=1)
                for re, im in each[:2]
                for pieces in ((re, im), (-im, re))
            ],
            axis=0,
        )
        both = dot_nt(left, right)
        write(e, both[: 3 * chans, : 2 * chans])
        write(e + 1, both[chans:, 2 * chans :])


def cross(spectra, bins, before=None):
    chans = sum(value.shape[2] for value in spectra)
    data = spectra if before is None else spectra + [before]
    return pl.pallas_call(
        functools.partial(cross_kernel, len(spectra)),
        out_shape=jax.ShapeDtypeStruct((bins // 2, 3 * chans, 2 * chans), F32),
        in_specs=[vmem_spec()] * len(data),
        out_specs=vmem_spec(),
        compiler_params=params(),
        cost_estimate=SHORT,
    )(*data)


U_BITS, V_BITS = (2, 4), (4, 2)


def partner(value, bits):
    count = lax.axis_size("range")
    return lax.ppermute(value, "range", [(i, i ^ bits[i & 1]) for i in range(count)])


def slot_of(core, x, y, z):
    return (4 * z + ((2 * y + (x ^ y)) ^ (3 * (z & 1)))) ^ (15 * core)


def parts_of(index):
    return index & 1, (index >> 1) & 1, (index >> 2) & 1, (index >> 3) & 3


def bin_of(index):
    core, x, y, z = parts_of(index)
    return core * 16 + slot_of(core, x, y, z)


def index_of(bin_id):
    core = bin_id >> 4
    path = (bin_id & 15) ^ (15 * core)
    z = path >> 2
    turned = (path & 3) ^ (3 * (z & 1))
    y = turned >> 1
    x = (turned & 1) ^ y
    return z * 8 + y * 4 + x * 2 + core


def uv_parts():
    core, x, y, z = parts_of(lax.axis_index("range"))
    return core, jnp.where(core == 0, x, y), jnp.where(core == 0, y, x), z


def uv_slot(core, u, v, z):
    return slot_of(core, jnp.where(core == 0, u, v), jnp.where(core == 0, v, u), z)


def packed(block):
    chans = block.shape[0]
    lower = iota((chans, chans), 0) >= iota((chans, chans), 1)
    swapped = pltpu.roll(block, chans, 1)
    mixed = jnp.where(lower, block[:, :chans], swapped[:, :chans])
    return jnp.concatenate([mixed[: chans // 2], mixed[chans // 2 :]], axis=1)


def sent_rows(keep_ref):
    return 5 * keep_ref.shape[1] // 6


def upper_rows(keep_ref, e):
    block = keep_ref.shape[1] // 3
    end = sent_rows(keep_ref) // 2 + block // 2
    return jnp.concatenate([packed(keep_ref[e, :block]), keep_ref[e, block:end]], axis=0)


def lower_rows(keep_ref, e):
    return keep_ref[e, sent_rows(keep_ref) // 2 + keep_ref.shape[1] // 6 :]


def first_kernel(keep_ref, a_ref, b_ref):
    core, u, v, z = uv_parts()
    for k in range(8):
        a_ref[k] = upper_rows(keep_ref, uv_slot(core, 1 - u, k // 4, k % 4))
        b_ref[k] = lower_rows(keep_ref, uv_slot(core, k // 4, 1 - v, k % 4))


def second_kernel(keep_ref, a1_ref, b1_ref, a_ref, b_ref):
    core, u, v, z = uv_parts()
    for k in range(4):
        e = uv_slot(core, u, 1 - v, k)
        a_ref[k] = upper_rows(keep_ref, e) + a1_ref[(1 - v) * 4 + k]
        e = uv_slot(core, 1 - u, v, k)
        b_ref[k] = lower_rows(keep_ref, e) + b1_ref[(1 - u) * 4 + k]


def line_sum(keep_ref, a1_ref, b1_ref, a2_ref, b2_ref, flip):
    core, u, v, z = uv_parts()
    z = z ^ flip
    e = uv_slot(core, u, v, z)
    upper = upper_rows(keep_ref, e) + a1_ref[v * 4 + z] + a2_ref[z]
    lower = lower_rows(keep_ref, e) + b1_ref[u * 4 + z] + b2_ref[z]
    return upper, lower


FLIPS = (2, 3, 1)


def line_kernel(*refs):
    half = sent_rows(refs[0]) // 2
    for flip, out_ref in zip(FLIPS, refs[5:]):
        upper, lower = line_sum(*refs[:5], flip)
        out_ref[:half] = upper
        out_ref[half:] = lower


def own_kernel(*refs):
    z1_ref, z2_ref, z3_ref, out_ref, packed_ref = refs[5:]
    half = sent_rows(refs[0]) // 2
    upper, lower = line_sum(*refs[:5], 0)
    upper = upper + z1_ref[:half] + (z2_ref[:half] + z3_ref[:half])
    out_ref[:half] = upper
    packed_ref[...] = upper[: packed_ref.shape[0]]
    out_ref[half:] = lower + z1_ref[half:] + (z2_ref[half:] + z3_ref[half:])


def summed(kernel, data, shapes):
    return pl.pallas_call(
        kernel,
        out_shape=[jax.ShapeDtypeStruct(shape, F32) for shape in shapes],
        in_specs=[vmem_spec()] * len(data),
        out_specs=[vmem_spec()] * len(shapes),
        compiler_params=params(),
    )(*data)


def bin_sums(keep):
    _, full, wide = keep.shape
    rows = 5 * full // 6
    half = rows // 2
    data = [keep]
    a, b = summed(first_kernel, data, [(8, half, wide)] * 2)
    data += [partner(a, U_BITS), partner(b, V_BITS)]
    a, b = summed(second_kernel, data, [(4, half, wide)] * 2)
    data += [partner(a, V_BITS), partner(b, U_BITS)]
    sends = summed(line_kernel, data, [(rows, wide)] * 3)
    data += [partner(value, (8 * flip, 8 * flip)) for flip, value in zip(FLIPS, sends)]
    own, packed = summed(own_kernel, data, [(rows, wide), (rows // 5, wide)])
    bit = 32
    while bit < lax.axis_size("range"):
        own = own + partner(own, (bit, bit))
        packed = packed + partner(packed, (bit, bit))
        bit *= 2
    return own, packed


def from_bin(value, offset):
    count = lax.axis_size("range")
    pairs = []
    for i in range(count):
        target = index_of((bin_of(i) - offset) % 32) | (i & ~31)
        pairs.append((i, target))
    return lax.ppermute(value, "range", pairs)


def turn(value):
    half = value.shape[1] // 2
    rolled = pltpu.roll(value, half, 1)
    return jnp.where(iota(value.shape, 1) < half, -rolled, rolled)


def embed(value):
    return jnp.concatenate([value, turn(value)], axis=0)


def mul(a, b):
    return jnp.dot(a, embed(b), precision=lax.Precision.HIGHEST, preferred_element_type=F32)


def mul_conj(a, b):
    half = a.shape[1] // 2
    stacked = jnp.concatenate([a, -turn(a)], axis=0)
    both = dot_nt(stacked, b, lax.Precision.HIGHEST)
    rows = a.shape[0]
    return jnp.concatenate([both[:rows], both[rows:]], axis=1)


def reciprocal(x):
    value = pl.reciprocal(x, approx=True)
    for _ in range(2):
        value = value * (2.0 - x * value)
    return value


def pivot_inverse(p):
    def times(x, y):
        return x[0] * y[0] - x[1] * y[1], x[0] * y[1] + x[1] * y[0]

    def conj(x):
        return x[0], -x[1]

    def plus(x, y):
        return x[0] + y[0], x[1] + y[1]

    def scaled(x, s):
        return x[0] * s, x[1] * s

    def square(x):
        return x[0] * x[0] + x[1] * x[1]

    def two(a, b, d):
        inv = reciprocal(a * d - square(b))
        return d * inv, scaled(b, -inv), a * inv

    a, d = p[0][0], p[1][1]
    b = p[0][1]
    ea, eb, ed = two(a, b, d)
    f = [[p[0][2], p[0][3]], [p[1][2], p[1][3]]]
    w = [
        [plus(scaled(f[0][j], ea), times(eb, f[1][j])) for j in range(2)],
        [plus(times(conj(eb), f[0][j]), scaled(f[1][j], ed)) for j in range(2)],
    ]

    def inner(i, j):
        return plus(times(conj(f[0][i]), w[0][j]), times(conj(f[1][i]), w[1][j]))

    ha = p[2][2] - inner(0, 0)[0]
    hd = p[3][3] - inner(1, 1)[0]
    cross = inner(0, 1)
    hb = (p[2][3][0] - cross[0], p[2][3][1] - cross[1])
    ga, gb, gd = two(ha, hb, hd)
    v = [
        [
            plus(scaled(w[i][0], ga), times(w[i][1], conj(gb))),
            plus(times(w[i][0], gb), scaled(w[i][1], gd)),
        ]
        for i in range(2)
    ]
    top = [
        [plus(times(v[i][0], conj(w[j][0])), times(v[i][1], conj(w[j][1]))) for j in range(2)]
        for i in range(2)
    ]
    zero = None
    out = [[None] * 4 for _ in range(4)]
    out[0][0] = (ea + top[0][0][0], zero)
    out[1][1] = (ed + top[1][1][0], zero)
    out[0][1] = plus(eb, top[0][1])
    out[2][2], out[3][3], out[2][3] = (ga, zero), (gd, zero), gb
    for i in range(2):
        for j in range(2):
            out[i][2 + j] = (-v[i][j][0], -v[i][j][1])
    for i in range(4):
        for j in range(i):
            out[i][j] = conj(out[j][i])
    return out


def invert(matrix):
    chans, width = matrix.shape
    sub = 8
    tiles = [matrix[t * sub : (t + 1) * sub, :] for t in range(chans // sub)]
    lane = iota((sub, width), 1)
    row = iota((sub, width), 0)
    first_half = lane < chans

    def spin(value):
        rolled = pltpu.roll(value, chans, 1)
        return jnp.where(first_half, -rolled, rolled)

    def column(value, k):
        return jnp.broadcast_to(value[:, k : k + 1], (sub, width))

    def combine(terms):
        while len(terms) > 1:
            terms = [
                terms[i] + terms[i + 1] if i + 1 < len(terms) else terms[i]
                for i in range(0, len(terms), 2)
            ]
        return terms[0]

    for k in range(0, chans, 4):
        t, r = divmod(k, sub)
        lines = [jnp.broadcast_to(tiles[t][r + i : r + i + 1, :], (sub, width)) for i in range(4)]
        pivot = [[None] * 4 for _ in range(4)]
        for i in range(4):
            pivot[i][i] = column(lines[i], k + i)
            for j in range(i + 1, 4):
                pivot[i][j] = column(lines[i], k + j), column(lines[i], chans + k + j)
        low = jnp.bitwise_and(lane, chans - 1)
        cleared = (low >= k) & (low < k + 4)
        unit = [
            jnp.where(cleared, jnp.where(lane == k + i, 1.0, 0.0), lines[i]) for i in range(4)
        ]
        spun = [spin(u) for u in unit]
        p = pivot_inverse(pivot)
        fresh_lines, fresh_spun = [], []
        for i in range(4):
            terms, other = [], []
            for j in range(4):
                re, im = p[i][j]
                terms.append(re * unit[j])
                other.append(re * spun[j])
                if im is not None:
                    terms.append(im * spun[j])
                    other.append(-(im * unit[j]))
            fresh_lines.append(combine(terms))
            fresh_spun.append(combine(other))
        fresh = []
        for s, tile in enumerate(tiles):
            terms = []
            for i in range(4):
                terms.append(column(tile, k + i) * fresh_lines[i])
                terms.append(column(tile, chans + k + i) * fresh_spun[i])
            value = jnp.where(cleared, 0.0, tile) - combine(terms)
            if s == t:
                for i in range(4):
                    value = jnp.where(row == r + i, fresh_lines[i], value)
            fresh.append(value)
        tiles = fresh
    return jnp.concatenate(tiles, axis=0)


def unpacked(ref, scale):
    half, wide = ref.shape[0], ref.shape[1]
    piece = ref[...] * scale
    swapped = pltpu.roll(piece, wide // 2, 1)
    return jnp.concatenate([piece, swapped], axis=0)[:, : wide // 2]


def hermitian(mixed, across):
    i, j = iota(mixed.shape, 0), iota(mixed.shape, 1)
    real_part = jnp.where(i >= j, mixed, across)
    imag_part = jnp.where(i < j, mixed, jnp.where(i > j, -across, 0.0))
    return jnp.concatenate([real_part, imag_part], axis=1)


def middle_kernel(total, packed_ref, steer_ref, inv_ref, t_ref):
    chans = inv_ref.shape[0]
    mixed = unpacked(packed_ref, F32(1.0 / total))
    twice = jnp.concatenate([mixed, mixed], axis=1)
    across = jnp.concatenate([twice, twice], axis=0).T[:chans, :chans]
    inverse = invert(hermitian(mixed, across))
    inv_ref[...] = inverse
    t_ref[...] = mul(steer_ref[...], inverse)


def outer_kernel(total, own_ref, left_ref, right_ref, steer_ref, inv_ref, t_ref, out_ref):
    chans = inv_ref.shape[0]
    scale = F32(1.0 / total)
    half = chans // 2
    m_left = unpacked(left_ref.at[:half], scale)
    m_right = unpacked(right_ref, scale)
    ml = left_ref[half : half + chans] * scale
    rl = left_ref[half + chans :] * scale
    rm = own_ref[half : half + chans] * scale
    across = jnp.concatenate([jnp.concatenate([m_left, m_right], axis=1), ml], axis=0).T
    lm = jnp.concatenate([across[:chans, chans:], -across[chans:, chans:]], axis=1)
    t = t_ref[...]
    both = mul(jnp.concatenate([rm, lm], axis=0), inv_ref[...])
    g_right, g_left = both[:chans], both[chans:]
    by_left = mul(jnp.concatenate([g_left, g_right, t], axis=0), ml)
    by_right = mul_conj(jnp.concatenate([g_right, t], axis=0), rm)
    s_ll = hermitian(m_left, across[:chans, :chans]) - by_left[:chans]
    s_rl = rl - by_left[chans : 2 * chans]
    s_rr = hermitian(m_right, across[chans:, :chans]) - by_right[:chans]

    both = mul(jnp.concatenate([s_rl, -by_left[2 * chans :]], axis=0), invert(s_ll))
    back = mul_conj(both, s_rl)
    middle = mul(both, g_left)
    k, y_left = both[:chans], both[chans:]
    q = g_right - middle[:chans]

    y_right = mul(-by_right[chans:] - back[chans:], invert(s_rr - back[:chans]))
    both = jnp.dot(
        y_right, jnp.concatenate([embed(k), embed(q)], axis=1),
        precision=lax.Precision.HIGHEST, preferred_element_type=F32,
    )
    y_left = y_left - both[:, : 2 * chans]
    y_mid = t - middle[chans:] - both[:, 2 * chans :]
    quad = jnp.sum(steer_ref[...] * y_mid, axis=1, keepdims=True)
    y = jnp.concatenate([y_left, y_mid, y_right], axis=1) / jnp.sqrt(quad)
    real_lane = lax.rem(iota(y.shape, 1), 2 * chans) < chans
    mine = jnp.where(real_lane, y, -y).astype(BF16)
    for c in range(out_ref.shape[0]):
        out_ref[c] = mine


def steering(chans):
    index = np.arange(chans)
    sines = -0.8 + 1.6 * np.arange(BEAMS) / (BEAMS - 1)
    angle = math.pi * sines[:, None] * index[None, :]
    return np.concatenate([np.cos(angle), -np.sin(angle)], axis=1).astype(np.float32)


def solve_middle(packed, steer, total):
    half, wide = packed.shape
    return pl.pallas_call(
        functools.partial(middle_kernel, total),
        out_shape=[
            jax.ShapeDtypeStruct((2 * half, wide), F32),
            jax.ShapeDtypeStruct((BEAMS, wide), F32),
        ],
        in_specs=[vmem_spec()] * 2,
        out_specs=[vmem_spec()] * 2,
        compiler_params=params(),
    )(packed, steer)


def solve_outer(own, left, right, steer, inverse, t, total, copies):
    chans, wide = inverse.shape
    return pl.pallas_call(
        functools.partial(outer_kernel, total),
        out_shape=jax.ShapeDtypeStruct((copies, BEAMS, 3 * wide), BF16),
        in_specs=[vmem_spec()] * 6,
        out_specs=vmem_spec(),
        compiler_params=params(),
    )(own, left, right, steer, inverse, t)


def beam_kernel(bin_ref, block_ref, beam_ref, owner_ref, s0_ref, upper_ref, lower_ref, w_ref,
                out_ref, both_ref, rows_ref, seen_ref):
    bins, wide, gates = s0_ref.shape
    devices = seen_ref.shape[0]
    count = bin_ref.shape[0]
    rows_ref[...] = jnp.zeros_like(rows_ref)

    @pl.loop(0, devices)
    def _(i):
        seen_ref[i] = 0

    w = w_ref[...].astype(F32).reshape(bins * BEAMS, 3 * wide)
    for k in range(3):
        lanes = slice(k * wide, (k + 1) * wide)
        part = w[:, lanes]
        both_ref[:, 0:BEAMS, lanes] = part.reshape(bins, BEAMS, wide)
        both_ref[:, BEAMS:, lanes] = turn(part).reshape(bins, BEAMS, wide)

    def detection(j, carry):
        bin_id = bin_ref[j]
        beam_id = beam_ref[j]
        owner = owner_ref[j]
        rank = seen_ref[owner]
        seen_ref[owner] = rank + 1
        left = both_ref[index_of(bin_id)].astype(BF16)
        bands = [lax.rem(bin_id + bins - 1 + k, bins) for k in range(3)]
        first = block_ref[j] == 0
        pieces = []
        for b in bands:
            later = [upper_ref[b, 0], lower_ref[b, 0], upper_ref[b, 1], lower_ref[b, 1]]
            pieces.append(jnp.where(first, s0_ref[b], jnp.concatenate(later, axis=0)))
        window = jnp.concatenate(pieces, axis=0)
        both = dot(left, window)
        line = jnp.concatenate([both[:BEAMS], both[BEAMS:]], axis=1)
        chosen = jnp.where(iota(line.shape, 0) == beam_id, line, 0.0)
        row = owner * CAP + rank
        rows_ref[pl.ds(row, 1), :] = jnp.sum(chosen, axis=0, keepdims=True)
        return carry

    lax.fori_loop(0, count, detection, 0, unroll=32)
    out_ref[...] = rows_ref[...].astype(BF16)


def beam_rows(det_bin, det_block, det_beam, owners, s0, s1, weight, devices):
    bins, wide, gates = s0.shape
    return pl.pallas_call(
        beam_kernel,
        out_shape=jax.ShapeDtypeStruct((devices * CAP, 2 * gates), BF16),
        in_specs=[smem_spec()] * 4 + [vmem_spec()] * 4,
        out_specs=vmem_spec(),
        scratch_shapes=[
            pltpu.VMEM((bins, 2 * BEAMS, 3 * wide), F32),
            pltpu.VMEM((devices * CAP, 2 * gates), F32),
            pltpu.SMEM((devices,), jnp.int32),
        ],
        compiler_params=params(),
    )(det_bin, det_block, det_beam, owners, s0, *s1, weight)


def on_device(raw, replica, det_bin, det_block, det_beam, det_owner):
    devices = lax.axis_size("range")
    _, chans, pulses, gates = raw.shape
    bins = pulses
    flat = raw.reshape(2, chans * pulses, gates)
    before = [(source, source - 1) for source in range(1, devices)]
    *slices, mark = first_gates(flat)
    halos = [lax.ppermute(value, "range", before) for value in slices]
    table = doppler_matrix(pulses, 8)
    s0, local, matrix, *sent = spectra_first(flat, replica, table, pulses, mark)
    beside0 = [partner(value, (1, 1)) for value in sent]
    sums = cross([s0], bins)
    sums = cross(beside0, bins, sums)
    s1, beside1 = [], []
    for part, halo in enumerate(halos):
        value, send = spectra_last(part, local, halo, matrix, table, pulses, sums)
        s1.append(value)
        beside1.append(partner(send, (1, 1)))
    sums = cross(s1, bins, sums)
    sums = cross(beside1, bins, sums)
    own, packed = bin_sums(sums)
    total = gates * devices
    steer = steering(chans)
    left = from_bin(own, -1)
    right = from_bin(packed, 1)
    inverse, t = solve_middle(packed, steer, total)
    mine = solve_outer(own, left, right, steer, inverse, t, total, bins)
    groups = [list(range(first, first + bins)) for first in range(0, devices, bins)]
    weight = lax.all_to_all(
        mine, "range", split_axis=0, concat_axis=0, tiled=True,
        axis_index_groups=groups if len(groups) > 1 else None,
    )
    outgoing = beam_rows(
        det_bin, det_block, det_beam, det_owner[:, 0],
        s0.reshape(bins, 2 * chans, BLOCK), s1, weight, devices,
    )
    incoming = lax.all_to_all(
        outgoing.reshape(devices, CAP, 2 * BLOCK), "range", split_axis=0, concat_axis=0, tiled=True
    )
    return incoming.astype(F32).reshape(devices * CAP, 2 * BLOCK)


def solution(mesh):
    in_specs = (
        P(None, None, None, "range"),
        P(),
        P("range"),
        P("range"),
        P("range"),
        P("range", None),
    )
    out_specs = P("range", None)
    return jax.shard_map(
        on_device, mesh=mesh, in_specs=in_specs, out_specs=out_specs, check_vma=False
    )
```

```python
import functools
import math

import jax
import jax.numpy as jnp
import ml_dtypes
import numpy as np
from jax import lax
from jax.experimental import pallas as pl
from jax.experimental.pallas import tpu as pltpu
from jax.sharding import PartitionSpec as P

BLOCK = 128
BEAMS = 8
CAP = 2

F32 = jnp.float32
BF16 = jnp.bfloat16
VMEM = pltpu.VMEM
MIB = 1024 * 1024
NT = (((1,), (1,)), ((), ()))


def vmem_spec():
    return pl.BlockSpec(memory_space=VMEM)


def smem_spec():
    return pl.BlockSpec(memory_space=pltpu.SMEM)


def hbm_spec():
    return pl.BlockSpec(memory_space=pltpu.HBM)


SHORT = pl.CostEstimate(flops=1, bytes_accessed=1, transcendentals=0)


def params(mib=16):
    return pltpu.CompilerParams(vmem_limit_bytes=int(mib * MIB))


def dot(a, b):
    return jnp.dot(a, b, preferred_element_type=F32)


def dot_nt(a, b, precision=None):
    return lax.dot_general(a, b, NT, precision=precision, preferred_element_type=F32)


def iota(shape, axis):
    return lax.broadcasted_iota(jnp.int32, shape, axis)


def halo_kernel(raw_ref, a_ref, b_ref, mark_ref, sems):
    mark_ref[...] = jnp.zeros_like(mark_ref)
    count = sems.shape[0] // 2
    size = a_ref.shape[1] // count
    copies = []
    for part, out_ref in enumerate((a_ref, b_ref)):
        for j in range(count):
            start = part * a_ref.shape[1] + j * size
            copies.append(
                pltpu.make_async_copy(
                    raw_ref.at[:, start : start + size, :BLOCK],
                    out_ref.at[:, j * size : (j + 1) * size, :],
                    sems.at[part * count + j],
                )
            )
    for copy in copies:
        copy.start()
    for copy in copies:
        copy.wait()


def first_gates(raw):
    half = jax.ShapeDtypeStruct((2, raw.shape[1] // 2, BLOCK), BF16)
    return pl.pallas_call(
        halo_kernel,
        out_shape=[half, half, jax.ShapeDtypeStruct((8, 128), F32)],
        in_specs=[hbm_spec()],
        out_specs=[vmem_spec()] * 3,
        scratch_shapes=[pltpu.SemaphoreType.DMA((8,))],
        compiler_params=params(61.5),
    )(raw)


def correlation_matrix(rep_ref, out_ref):
    taps = rep_ref.shape[1]
    base = rep_ref[...].astype(F32)
    row = iota((taps, 2 * taps), 0)
    parts = []
    for i in range(2):
        line = jnp.concatenate([base[i : i + 1], jnp.zeros((1, taps), F32)], axis=1)
        skew = jnp.broadcast_to(line, (taps, 2 * taps))
        bit = 1
        while bit < taps:
            skew = jnp.where((row & bit) != 0, pltpu.roll(skew, bit, 1), skew)
            bit *= 2
        parts.append(skew.T)
    real_part, imag_part = parts
    out_ref[0] = jnp.concatenate([real_part, -imag_part], axis=1).astype(BF16)
    out_ref[1] = jnp.concatenate([imag_part, real_part], axis=1).astype(BF16)


def doppler_matrix(pulses, group):
    index = np.arange(pulses)
    angle = 2.0 * math.pi / pulses * (index[:, None] * index[None, :] % pulses)
    cosine = np.cos(angle) * pulses**-0.5
    sine = np.sin(angle) * pulses**-0.5
    table = np.stack([np.stack([cosine, -sine], 1), np.stack([sine, cosine], 1)], 0)
    full = np.einsum("ipod,ce->dociep", table, np.eye(group))
    shape = (pulses * 2 * group, 2 * group * pulses)
    return full.reshape(shape).astype(ml_dtypes.bfloat16)


def doppler_rows(total, dft):
    compressed = total.astype(BF16)
    rows, wide = compressed.shape
    half, gates = rows // 2, wide // 2
    stacked = jnp.concatenate(
        [
            jnp.concatenate([compressed[:half, :gates], compressed[half:, :gates]], axis=1),
            jnp.concatenate([compressed[:half, gates:], compressed[half:, gates:]], axis=1),
        ],
        axis=0,
    )
    both = dot(dft, stacked)
    lines = both.shape[0] // 8
    joined = jnp.concatenate(
        [both[:, :gates].reshape(lines, 8, gates), both[:, gates:].reshape(lines, 8, gates)],
        axis=1,
    )
    return joined.astype(BF16)


GROUP = 16


def half_of_bins(bins, mine):
    core = lax.axis_index("range") & 1
    return (core if mine else 1 - core) * (bins // 2)


def sent_bins(bins):
    return bins // 2 + 2


def spectra_first_kernel(raw_ref, rep_ref, dft_ref, _, s_ref, local_ref, taps_ref, *rest):
    *send_refs, buf, sems = rest
    bins, _, chans, gates = s_ref.shape
    size = GROUP * bins
    copies = [
        pltpu.make_async_copy(
            raw_ref.at[:, j * size : (j + 1) * size, :],
            buf.at[:, j * size : (j + 1) * size, :],
            sems.at[j],
        )
        for j in range(chans // GROUP)
    ]
    for copy in copies:
        copy.start()
    correlation_matrix(rep_ref, taps_ref)
    for j, copy in enumerate(copies):
        copy.wait()
        rows = slice(j * size, (j + 1) * size)
        total = dot(buf[0, rows, :], taps_ref[0]) + dot(buf[1, rows, :], taps_ref[1])
        out = doppler_rows(total, dft_ref[...])
        s_ref[:, :, j * GROUP : (j + 1) * GROUP, :] = out.reshape(bins, 2, GROUP, gates)
        later = jnp.concatenate([buf[0, rows, gates:], buf[1, rows, gates:]], axis=1)
        near = jnp.concatenate([taps_ref[0, :gates, :], taps_ref[1, :gates, :]], axis=0)
        local_ref[rows, :] = dot(later, near)
    base = half_of_bins(bins, False)
    half = chans // 2
    for part, send_ref in enumerate(send_refs):
        for k in range(send_ref.shape[0]):
            send_ref[k] = s_ref[lax.rem(base + k, bins), :, part * half : (part + 1) * half, :]


def spectra_last_kernel(part, local_ref, halo_ref, taps_ref, dft_ref, _, s_ref, send_ref):
    bins, _, chans, gates = s_ref.shape
    size = GROUP * bins
    far = jnp.concatenate([taps_ref[0, gates:, :], taps_ref[1, gates:, :]], axis=0)
    for j in range(chans // GROUP):
        rows = slice(j * size, (j + 1) * size)
        later = jnp.concatenate([halo_ref[0, rows, :], halo_ref[1, rows, :]], axis=1)
        start = part * chans * bins + j * size
        out = doppler_rows(local_ref[start : start + size, :] + dot(later, far), dft_ref[...])
        s_ref[:, :, j * GROUP : (j + 1) * GROUP, :] = out.reshape(bins, 2, GROUP, gates)
    base = half_of_bins(bins, False)
    for k in range(send_ref.shape[0]):
        send_ref[k] = s_ref[lax.rem(base + k, bins)]


def spectra_first(raw, replica, table, pulses, mark):
    _, rows, gates = raw.shape
    chans = rows // pulses
    taps = replica.shape[1]
    return pl.pallas_call(
        spectra_first_kernel,
        out_shape=[
            jax.ShapeDtypeStruct((pulses, 2, chans, BLOCK), BF16),
            jax.ShapeDtypeStruct((rows, 2 * BLOCK), F32),
            jax.ShapeDtypeStruct((2, 2 * taps, 2 * taps), BF16),
        ]
        + [jax.ShapeDtypeStruct((sent_bins(pulses), 2, chans // 2, BLOCK), BF16)] * 2,
        in_specs=[hbm_spec(), vmem_spec(), vmem_spec(), pl.BlockSpec(memory_space=pl.ANY)],
        out_specs=[vmem_spec()] * 5,
        scratch_shapes=[
            pltpu.VMEM(raw.shape, BF16),
            pltpu.SemaphoreType.DMA((chans // GROUP,)),
        ],
        compiler_params=params(),
        cost_estimate=SHORT,
    )(raw, replica, table, mark)


def spectra_last(part, local, halo, matrix, table, pulses, sums):
    chans = halo.shape[1] // pulses
    return pl.pallas_call(
        functools.partial(spectra_last_kernel, part),
        out_shape=[
            jax.ShapeDtypeStruct((pulses, 2, chans, BLOCK), BF16),
            jax.ShapeDtypeStruct((sent_bins(pulses), 2, chans, BLOCK), BF16),
        ],
        in_specs=[vmem_spec()] * 4 + [pl.BlockSpec(memory_space=pl.ANY)],
        out_specs=[vmem_spec()] * 2,
        compiler_params=params(),
        cost_estimate=SHORT,
    )(local, halo, matrix, table, sums)


def cross_kernel(count_refs, *refs):
    s_refs, rest = refs[:count_refs], refs[count_refs:]
    before_ref = rest[0] if len(rest) == 2 else None
    out_ref = rest[-1]
    held, _, _, gates = s_refs[0].shape
    chans = sum(ref.shape[2] for ref in s_refs)
    count = out_ref.shape[0]
    base = half_of_bins(held, True) if held == 2 * count else 0

    def write(e, block):
        out_ref[e] = block if before_ref is None else block + before_ref[e]

    @pl.loop(0, count // 2, unroll=8)
    def _(step):
        e = step * 2
        each = []
        for k in range(4):
            where = lax.rem(base + e + k, held)
            each.append(
                [jnp.concatenate([ref[where, o] for ref in s_refs], axis=0) for o in range(2)]
            )
        left = jnp.concatenate(
            [jnp.concatenate([re, im], axis=1) for re, im in each], axis=0
        )
        right = jnp.concatenate(
            [
                jnp.concatenate(pieces, axis=1)
                for re, im in each[:2]
                for pieces in ((re, im), (-im, re))
            ],
            axis=0,
        )
        both = dot_nt(left, right)
        write(e, both[: 3 * chans, : 2 * chans])
        write(e + 1, both[chans:, 2 * chans :])


def cross(spectra, bins, before=None):
    chans = sum(value.shape[2] for value in spectra)
    data = spectra if before is None else spectra + [before]
    return pl.pallas_call(
        functools.partial(cross_kernel, len(spectra)),
        out_shape=jax.ShapeDtypeStruct((bins // 2, 3 * chans, 2 * chans), F32),
        in_specs=[vmem_spec()] * len(data),
        out_specs=vmem_spec(),
        compiler_params=params(),
        cost_estimate=SHORT,
    )(*data)


U_BITS, V_BITS = (2, 4), (4, 2)


def partner(value, bits):
    count = lax.axis_size("range")
    return lax.ppermute(value, "range", [(i, i ^ bits[i & 1]) for i in range(count)])


def slot_of(core, x, y, z):
    return (4 * z + ((2 * y + (x ^ y)) ^ (3 * (z & 1)))) ^ (15 * core)


def parts_of(index):
    return index & 1, (index >> 1) & 1, (index >> 2) & 1, (index >> 3) & 3


def bin_of(index):
    core, x, y, z = parts_of(index)
    return core * 16 + slot_of(core, x, y, z)


def index_of(bin_id):
    core = bin_id >> 4
    path = (bin_id & 15) ^ (15 * core)
    z = path >> 2
    turned = (path & 3) ^ (3 * (z & 1))
    y = turned >> 1
    x = (turned & 1) ^ y
    return z * 8 + y * 4 + x * 2 + core


def uv_parts():
    core, x, y, z = parts_of(lax.axis_index("range"))
    return core, jnp.where(core == 0, x, y), jnp.where(core == 0, y, x), z


def uv_slot(core, u, v, z):
    return slot_of(core, jnp.where(core == 0, u, v), jnp.where(core == 0, v, u), z)


def packed(block):
    chans = block.shape[0]
    lower = iota((chans, chans), 0) >= iota((chans, chans), 1)
    swapped = pltpu.roll(block, chans, 1)
    mixed = jnp.where(lower, block[:, :chans], swapped[:, :chans])
    return jnp.concatenate([mixed[: chans // 2], mixed[chans // 2 :]], axis=1)


def sent_rows(keep_ref):
    return 5 * keep_ref.shape[1] // 6


def upper_rows(keep_ref, e):
    block = keep_ref.shape[1] // 3
    end = sent_rows(keep_ref) // 2 + block // 2
    return jnp.concatenate([packed(keep_ref[e, :block]), keep_ref[e, block:end]], axis=0)


def lower_rows(keep_ref, e):
    return keep_ref[e, sent_rows(keep_ref) // 2 + keep_ref.shape[1] // 6 :]


def first_kernel(keep_ref, a_ref, b_ref):
    core, u, v, z = uv_parts()
    for k in range(8):
        a_ref[k] = upper_rows(keep_ref, uv_slot(core, 1 - u, k // 4, k % 4))
        b_ref[k] = lower_rows(keep_ref, uv_slot(core, k // 4, 1 - v, k % 4))


def second_kernel(keep_ref, a1_ref, b1_ref, a_ref, b_ref):
    core, u, v, z = uv_parts()
    for k in range(4):
        e = uv_slot(core, u, 1 - v, k)
        a_ref[k] = upper_rows(keep_ref, e) + a1_ref[(1 - v) * 4 + k]
        e = uv_slot(core, 1 - u, v, k)
        b_ref[k] = lower_rows(keep_ref, e) + b1_ref[(1 - u) * 4 + k]


def line_sum(keep_ref, a1_ref, b1_ref, a2_ref, b2_ref, flip):
    core, u, v, z = uv_parts()
    z = z ^ flip
    e = uv_slot(core, u, v, z)
    upper = upper_rows(keep_ref, e) + a1_ref[v * 4 + z] + a2_ref[z]
    lower = lower_rows(keep_ref, e) + b1_ref[u * 4 + z] + b2_ref[z]
    return upper, lower


FLIPS = (2, 3, 1)


def line_kernel(*refs):
    half = sent_rows(refs[0]) // 2
    for flip, out_ref in zip(FLIPS, refs[5:]):
        upper, lower = line_sum(*refs[:5], flip)
        out_ref[:half] = upper
        out_ref[half:] = lower


def own_kernel(*refs):
    z1_ref, z2_ref, z3_ref, out_ref, packed_ref = refs[5:]
    half = sent_rows(refs[0]) // 2
    upper, lower = line_sum(*refs[:5], 0)
    upper = upper + z1_ref[:half] + (z2_ref[:half] + z3_ref[:half])
    out_ref[:half] = upper
    packed_ref[...] = upper[: packed_ref.shape[0]]
    out_ref[half:] = lower + z1_ref[half:] + (z2_ref[half:] + z3_ref[half:])


def summed(kernel, data, shapes):
    return pl.pallas_call(
        kernel,
        out_shape=[jax.ShapeDtypeStruct(shape, F32) for shape in shapes],
        in_specs=[vmem_spec()] * len(data),
        out_specs=[vmem_spec()] * len(shapes),
        compiler_params=params(),
    )(*data)


def bin_sums(keep):
    _, full, wide = keep.shape
    rows = 5 * full // 6
    half = rows // 2
    data = [keep]
    a, b = summed(first_kernel, data, [(8, half, wide)] * 2)
    data += [partner(a, U_BITS), partner(b, V_BITS)]
    a, b = summed(second_kernel, data, [(4, half, wide)] * 2)
    data += [partner(a, V_BITS), partner(b, U_BITS)]
    sends = summed(line_kernel, data, [(rows, wide)] * 3)
    data += [partner(value, (8 * flip, 8 * flip)) for flip, value in zip(FLIPS, sends)]
    own, packed = summed(own_kernel, data, [(rows, wide), (rows // 5, wide)])
    bit = 32
    while bit < lax.axis_size("range"):
        own = own + partner(own, (bit, bit))
        packed = packed + partner(packed, (bit, bit))
        bit *= 2
    return own, packed


def from_bin(value, offset):
    count = lax.axis_size("range")
    pairs = []
    for i in range(count):
        target = index_of((bin_of(i) - offset) % 32) | (i & ~31)
        pairs.append((i, target))
    return lax.ppermute(value, "range", pairs)


def turn(value):
    half = value.shape[1] // 2
    rolled = pltpu.roll(value, half, 1)
    return jnp.where(iota(value.shape, 1) < half, -rolled, rolled)


def embed(value):
    return jnp.concatenate([value, turn(value)], axis=0)


def mul(a, b):
    return jnp.dot(a, embed(b), precision=lax.Precision.HIGHEST, preferred_element_type=F32)


def mul_conj(a, b):
    half = a.shape[1] // 2
    stacked = jnp.concatenate([a, -turn(a)], axis=0)
    both = dot_nt(stacked, b, lax.Precision.HIGHEST)
    rows = a.shape[0]
    return jnp.concatenate([both[:rows], both[rows:]], axis=1)


def reciprocal(x):
    value = pl.reciprocal(x, approx=True)
    for _ in range(2):
        value = value * (2.0 - x * value)
    return value


def pivot_inverse(p):
    def times(x, y):
        return x[0] * y[0] - x[1] * y[1], x[0] * y[1] + x[1] * y[0]

    def conj(x):
        return x[0], -x[1]

    def plus(x, y):
        return x[0] + y[0], x[1] + y[1]

    def scaled(x, s):
        return x[0] * s, x[1] * s

    def square(x):
        return x[0] * x[0] + x[1] * x[1]

    def two(a, b, d):
        inv = reciprocal(a * d - square(b))
        return d * inv, scaled(b, -inv), a * inv

    a, d = p[0][0], p[1][1]
    b = p[0][1]
    ea, eb, ed = two(a, b, d)
    f = [[p[0][2], p[0][3]], [p[1][2], p[1][3]]]
    w = [
        [plus(scaled(f[0][j], ea), times(eb, f[1][j])) for j in range(2)],
        [plus(times(conj(eb), f[0][j]), scaled(f[1][j], ed)) for j in range(2)],
    ]

    def inner(i, j):
        return plus(times(conj(f[0][i]), w[0][j]), times(conj(f[1][i]), w[1][j]))

    ha = p[2][2] - inner(0, 0)[0]
    hd = p[3][3] - inner(1, 1)[0]
    cross = inner(0, 1)
    hb = (p[2][3][0] - cross[0], p[2][3][1] - cross[1])
    ga, gb, gd = two(ha, hb, hd)
    v = [
        [
            plus(scaled(w[i][0], ga), times(w[i][1], conj(gb))),
            plus(times(w[i][0], gb), scaled(w[i][1], gd)),
        ]
        for i in range(2)
    ]
    top = [
        [plus(times(v[i][0], conj(w[j][0])), times(v[i][1], conj(w[j][1]))) for j in range(2)]
        for i in range(2)
    ]
    zero = None
    out = [[None] * 4 for _ in range(4)]
    out[0][0] = (ea + top[0][0][0], zero)
    out[1][1] = (ed + top[1][1][0], zero)
    out[0][1] = plus(eb, top[0][1])
    out[2][2], out[3][3], out[2][3] = (ga, zero), (gd, zero), gb
    for i in range(2):
        for j in range(2):
            out[i][2 + j] = (-v[i][j][0], -v[i][j][1])
    for i in range(4):
        for j in range(i):
            out[i][j] = conj(out[j][i])
    return out


def invert(matrix):
    chans, width = matrix.shape
    sub = 8
    tiles = [matrix[t * sub : (t + 1) * sub, :] for t in range(chans // sub)]
    lane = iota((sub, width), 1)
    row = iota((sub, width), 0)
    first_half = lane < chans

    def spin(value):
        rolled = pltpu.roll(value, chans, 1)
        return jnp.where(first_half, -rolled, rolled)

    def column(value, k):
        return jnp.broadcast_to(value[:, k : k + 1], (sub, width))

    def combine(terms):
        while len(terms) > 1:
            terms = [
                terms[i] + terms[i + 1] if i + 1 < len(terms) else terms[i]
                for i in range(0, len(terms), 2)
            ]
        return terms[0]

    for k in range(0, chans, 4):
        t, r = divmod(k, sub)
        lines = [jnp.broadcast_to(tiles[t][r + i : r + i + 1, :], (sub, width)) for i in range(4)]
        pivot = [[None] * 4 for _ in range(4)]
        for i in range(4):
            pivot[i][i] = column(lines[i], k + i)
            for j in range(i + 1, 4):
                pivot[i][j] = column(lines[i], k + j), column(lines[i], chans + k + j)
        low = jnp.bitwise_and(lane, chans - 1)
        cleared = (low >= k) & (low < k + 4)
        unit = [
            jnp.where(cleared, jnp.where(lane == k + i, 1.0, 0.0), lines[i]) for i in range(4)
        ]
        spun = [spin(u) for u in unit]
        p = pivot_inverse(pivot)
        fresh_lines, fresh_spun = [], []
        for i in range(4):
            terms, other = [], []
            for j in range(4):
                re, im = p[i][j]
                terms.append(re * unit[j])
                other.append(re * spun[j])
                if im is not None:
                    terms.append(im * spun[j])
                    other.append(-(im * unit[j]))
            fresh_lines.append(combine(terms))
            fresh_spun.append(combine(other))
        fresh = []
        for s, tile in enumerate(tiles):
            terms = []
            for i in range(4):
                terms.append(column(tile, k + i) * fresh_lines[i])
                terms.append(column(tile, chans + k + i) * fresh_spun[i])
            value = jnp.where(cleared, 0.0, tile) - combine(terms)
            if s == t:
                for i in range(4):
                    value = jnp.where(row == r + i, fresh_lines[i], value)
            fresh.append(value)
        tiles = fresh
    return jnp.concatenate(tiles, axis=0)


def unpacked(ref, scale):
    half, wide = ref.shape[0], ref.shape[1]
    piece = ref[...] * scale
    swapped = pltpu.roll(piece, wide // 2, 1)
    return jnp.concatenate([piece, swapped], axis=0)[:, : wide // 2]


def hermitian(mixed, across):
    i, j = iota(mixed.shape, 0), iota(mixed.shape, 1)
    real_part = jnp.where(i >= j, mixed, across)
    imag_part = jnp.where(i < j, mixed, jnp.where(i > j, -across, 0.0))
    return jnp.concatenate([real_part, imag_part], axis=1)


def middle_kernel(total, packed_ref, steer_ref, inv_ref, t_ref):
    chans = inv_ref.shape[0]
    mixed = unpacked(packed_ref, F32(1.0 / total))
    twice = jnp.concatenate([mixed, mixed], axis=1)
    across = jnp.concatenate([twice, twice], axis=0).T[:chans, :chans]
    inverse = invert(hermitian(mixed, across))
    inv_ref[...] = inverse
    t_ref[...] = mul(steer_ref[...], inverse)


def outer_kernel(total, own_ref, left_ref, right_ref, steer_ref, inv_ref, t_ref, out_ref,
                 work, keep, small):
    chans = inv_ref.shape[0]
    scale = F32(1.0 / total)
    half = chans // 2
    m_left = unpacked(left_ref.at[:half], scale)
    m_right = unpacked(right_ref, scale)
    ml = left_ref[half : half + chans] * scale
    rl = left_ref[half + chans :] * scale
    rm = own_ref[half : half + chans] * scale
    across = jnp.concatenate([jnp.concatenate([m_left, m_right], axis=1), ml], axis=0).T
    lm = jnp.concatenate([across[:chans, chans:], -across[chans:, chans:]], axis=1)
    t = t_ref[...]
    both = mul(jnp.concatenate([rm, lm], axis=0), inv_ref[...])
    g_right, g_left = both[:chans], both[chans:]
    by_left = mul(jnp.concatenate([g_left, g_right, t], axis=0), ml)
    by_right = mul_conj(jnp.concatenate([g_right, t], axis=0), rm)
    work[...] = hermitian(m_left, across[:chans, :chans]) - by_left[:chans]
    keep[0] = rl - by_left[chans : 2 * chans]
    keep[1] = hermitian(m_right, across[chans:, :chans]) - by_right[:chans]
    keep[2] = g_left
    keep[3] = g_right
    small[0] = -by_left[2 * chans :]
    small[1] = -by_right[chans:]

    @pl.loop(0, 2)
    def _(stage):
        work[...] = invert(work[...])

        @pl.when(stage == 0)
        def _():
            s_rl = keep[0]
            both = mul(jnp.concatenate([s_rl, small[0]], axis=0), work[...])
            back = mul_conj(both, s_rl)
            work[...] = keep[1] - back[:chans]
            small[1] = small[1] - back[chans:]
            middle = mul(both, keep[2])
            keep[0] = both[:chans]
            small[0] = both[chans:]
            keep[3] = keep[3] - middle[:chans]
            small[2] = t_ref[...] - middle[chans:]

        @pl.when(stage == 1)
        def _():
            y_right = mul(small[1], work[...])
            factors = jnp.concatenate([embed(keep[0]), embed(keep[3])], axis=1)
            both = jnp.dot(
                y_right, factors, precision=lax.Precision.HIGHEST, preferred_element_type=F32
            )
            y_left = small[0] - both[:, : 2 * chans]
            y_mid = small[2] - both[:, 2 * chans :]
            quad = jnp.sum(steer_ref[...] * y_mid, axis=1, keepdims=True)
            y = jnp.concatenate([y_left, y_mid, y_right], axis=1) / jnp.sqrt(quad)
            real_lane = lax.rem(iota(y.shape, 1), 2 * chans) < chans
            mine = jnp.where(real_lane, y, -y).astype(BF16)
            for c in range(out_ref.shape[0]):
                out_ref[c] = mine


def steering(chans):
    index = np.arange(chans)
    sines = -0.8 + 1.6 * np.arange(BEAMS) / (BEAMS - 1)
    angle = math.pi * sines[:, None] * index[None, :]
    return np.concatenate([np.cos(angle), -np.sin(angle)], axis=1).astype(np.float32)


def solve_middle(packed, steer, total):
    half, wide = packed.shape
    return pl.pallas_call(
        functools.partial(middle_kernel, total),
        out_shape=[
            jax.ShapeDtypeStruct((2 * half, wide), F32),
            jax.ShapeDtypeStruct((BEAMS, wide), F32),
        ],
        in_specs=[vmem_spec()] * 2,
        out_specs=[vmem_spec()] * 2,
        compiler_params=params(),
    )(packed, steer)


def solve_outer(own, left, right, steer, inverse, t, total, copies):
    chans, wide = inverse.shape
    return pl.pallas_call(
        functools.partial(outer_kernel, total),
        out_shape=jax.ShapeDtypeStruct((copies, BEAMS, 3 * wide), BF16),
        in_specs=[vmem_spec()] * 6,
        out_specs=vmem_spec(),
        scratch_shapes=[
            pltpu.VMEM((chans, wide), F32),
            pltpu.VMEM((4, chans, wide), F32),
            pltpu.VMEM((3, BEAMS, wide), F32),
        ],
        compiler_params=params(),
    )(own, left, right, steer, inverse, t)


def beam_kernel(bin_ref, block_ref, beam_ref, owner_ref, s0_ref, upper_ref, lower_ref, w_ref,
                out_ref, both_ref, rows_ref, seen_ref):
    bins, wide, gates = s0_ref.shape
    devices = seen_ref.shape[0]
    count = bin_ref.shape[0]
    rows_ref[...] = jnp.zeros_like(rows_ref)

    @pl.loop(0, devices)
    def _(i):
        seen_ref[i] = 0

    w = w_ref[...].astype(F32).reshape(bins * BEAMS, 3 * wide)
    for k in range(3):
        lanes = slice(k * wide, (k + 1) * wide)
        part = w[:, lanes]
        both_ref[:, 0:BEAMS, lanes] = part.reshape(bins, BEAMS, wide)
        both_ref[:, BEAMS:, lanes] = turn(part).reshape(bins, BEAMS, wide)

    def detection(j, carry):
        bin_id = bin_ref[j]
        beam_id = beam_ref[j]
        owner = owner_ref[j]
        rank = seen_ref[owner]
        seen_ref[owner] = rank + 1
        left = both_ref[index_of(bin_id)].astype(BF16)
        bands = [lax.rem(bin_id + bins - 1 + k, bins) for k in range(3)]
        first = block_ref[j] == 0
        pieces = []
        for b in bands:
            later = [upper_ref[b, 0], lower_ref[b, 0], upper_ref[b, 1], lower_ref[b, 1]]
            pieces.append(jnp.where(first, s0_ref[b], jnp.concatenate(later, axis=0)))
        window = jnp.concatenate(pieces, axis=0)
        both = dot(left, window)
        line = jnp.concatenate([both[:BEAMS], both[BEAMS:]], axis=1)
        chosen = jnp.where(iota(line.shape, 0) == beam_id, line, 0.0)
        row = owner * CAP + rank
        rows_ref[pl.ds(row, 1), :] = jnp.sum(chosen, axis=0, keepdims=True)
        return carry

    lax.fori_loop(0, count, detection, 0, unroll=32)
    out_ref[...] = rows_ref[...].astype(BF16)


def beam_rows(det_bin, det_block, det_beam, owners, s0, s1, weight, devices):
    bins, wide, gates = s0.shape
    return pl.pallas_call(
        beam_kernel,
        out_shape=jax.ShapeDtypeStruct((devices * CAP, 2 * gates), BF16),
        in_specs=[smem_spec()] * 4 + [vmem_spec()] * 4,
        out_specs=vmem_spec(),
        scratch_shapes=[
            pltpu.VMEM((bins, 2 * BEAMS, 3 * wide), F32),
            pltpu.VMEM((devices * CAP, 2 * gates), F32),
            pltpu.SMEM((devices,), jnp.int32),
        ],
        compiler_params=params(),
    )(det_bin, det_block, det_beam, owners, s0, *s1, weight)


def on_device(raw, replica, det_bin, det_block, det_beam, det_owner):
    devices = lax.axis_size("range")
    _, chans, pulses, gates = raw.shape
    bins = pulses
    flat = raw.reshape(2, chans * pulses, gates)
    before = [(source, source - 1) for source in range(1, devices)]
    *slices, mark = first_gates(flat)
    halos = [lax.ppermute(value, "range", before) for value in slices]
    table = doppler_matrix(pulses, 8)
    s0, local, matrix, *sent = spectra_first(flat, replica, table, pulses, mark)
    beside0 = [partner(value, (1, 1)) for value in sent]
    sums = cross([s0], bins)
    sums = cross(beside0, bins, sums)
    s1, beside1 = [], []
    for part, halo in enumerate(halos):
        value, send = spectra_last(part, local, halo, matrix, table, pulses, sums)
        s1.append(value)
        beside1.append(partner(send, (1, 1)))
    sums = cross(s1, bins, sums)
    sums = cross(beside1, bins, sums)
    own, packed = bin_sums(sums)
    total = gates * devices
    steer = steering(chans)
    left = from_bin(own, -1)
    right = from_bin(packed, 1)
    inverse, t = solve_middle(packed, steer, total)
    mine = solve_outer(own, left, right, steer, inverse, t, total, bins)
    groups = [list(range(first, first + bins)) for first in range(0, devices, bins)]
    weight = lax.all_to_all(
        mine, "range", split_axis=0, concat_axis=0, tiled=True,
        axis_index_groups=groups if len(groups) > 1 else None,
    )
    outgoing = beam_rows(
        det_bin, det_block, det_beam, det_owner[:, 0],
        s0.reshape(bins, 2 * chans, BLOCK), s1, weight, devices,
    )
    incoming = lax.all_to_all(
        outgoing.reshape(devices, CAP, 2 * BLOCK), "range", split_axis=0, concat_axis=0, tiled=True
    )
    return incoming.astype(F32).reshape(devices * CAP, 2 * BLOCK)


def solution(mesh):
    in_specs = (
        P(None, None, None, "range"),
        P(),
        P("range"),
        P("range"),
        P("range"),
        P("range", None),
    )
    out_specs = P("range", None)
    return jax.shard_map(
        on_device, mesh=mesh, in_specs=in_specs, out_specs=out_specs, check_vma=False
    )
```

```python
import functools
import math

import jax
import jax.numpy as jnp
import ml_dtypes
import numpy as np
from jax import lax
from jax.experimental import pallas as pl
from jax.experimental.pallas import tpu as pltpu
from jax.sharding import PartitionSpec as P

BLOCK = 128
BEAMS = 8
CAP = 2

F32 = jnp.float32
BF16 = jnp.bfloat16
VMEM = pltpu.VMEM
MIB = 1024 * 1024
NT = (((1,), (1,)), ((), ()))


def vmem_spec():
    return pl.BlockSpec(memory_space=VMEM)


def smem_spec():
    return pl.BlockSpec(memory_space=pltpu.SMEM)


def hbm_spec():
    return pl.BlockSpec(memory_space=pltpu.HBM)


SHORT = pl.CostEstimate(flops=1, bytes_accessed=1, transcendentals=0)


def params(mib=16):
    return pltpu.CompilerParams(vmem_limit_bytes=int(mib * MIB))


def dot(a, b):
    return jnp.dot(a, b, preferred_element_type=F32)


def dot_nt(a, b, precision=None):
    return lax.dot_general(a, b, NT, precision=precision, preferred_element_type=F32)


def iota(shape, axis):
    return lax.broadcasted_iota(jnp.int32, shape, axis)


def halo_kernel(raw_ref, a_ref, b_ref, mark_ref, sems):
    mark_ref[...] = jnp.zeros_like(mark_ref)
    count = sems.shape[0] // 2
    size = a_ref.shape[1] // count
    copies = []
    for part, out_ref in enumerate((a_ref, b_ref)):
        for j in range(count):
            start = part * a_ref.shape[1] + j * size
            copies.append(
                pltpu.make_async_copy(
                    raw_ref.at[:, start : start + size, :BLOCK],
                    out_ref.at[:, j * size : (j + 1) * size, :],
                    sems.at[part * count + j],
                )
            )
    for copy in copies:
        copy.start()
    for copy in copies:
        copy.wait()


def first_gates(raw):
    half = jax.ShapeDtypeStruct((2, raw.shape[1] // 2, BLOCK), BF16)
    return pl.pallas_call(
        halo_kernel,
        out_shape=[half, half, jax.ShapeDtypeStruct((8, 128), F32)],
        in_specs=[hbm_spec()],
        out_specs=[vmem_spec()] * 3,
        scratch_shapes=[pltpu.SemaphoreType.DMA((8,))],
        compiler_params=params(61.5),
    )(raw)


def correlation_matrix(rep_ref, out_ref):
    taps = rep_ref.shape[1]
    base = rep_ref[...].astype(F32)
    row = iota((taps, 2 * taps), 0)
    parts = []
    for i in range(2):
        line = jnp.concatenate([base[i : i + 1], jnp.zeros((1, taps), F32)], axis=1)
        skew = jnp.broadcast_to(line, (taps, 2 * taps))
        bit = 1
        while bit < taps:
            skew = jnp.where((row & bit) != 0, pltpu.roll(skew, bit, 1), skew)
            bit *= 2
        parts.append(skew.T)
    real_part, imag_part = parts
    out_ref[0] = jnp.concatenate([real_part, -imag_part], axis=1).astype(BF16)
    out_ref[1] = jnp.concatenate([imag_part, real_part], axis=1).astype(BF16)


def doppler_matrix(pulses, group):
    index = np.arange(pulses)
    angle = 2.0 * math.pi / pulses * (index[:, None] * index[None, :] % pulses)
    cosine = np.cos(angle) * pulses**-0.5
    sine = np.sin(angle) * pulses**-0.5
    table = np.stack([np.stack([cosine, -sine], 1), np.stack([sine, cosine], 1)], 0)
    full = np.einsum("ipod,ce->dociep", table, np.eye(group))
    shape = (pulses * 2 * group, 2 * group * pulses)
    return full.reshape(shape).astype(ml_dtypes.bfloat16)


def doppler_rows(total, dft):
    compressed = total.astype(BF16)
    rows, wide = compressed.shape
    half, gates = rows // 2, wide // 2
    stacked = jnp.concatenate(
        [
            jnp.concatenate([compressed[:half, :gates], compressed[half:, :gates]], axis=1),
            jnp.concatenate([compressed[:half, gates:], compressed[half:, gates:]], axis=1),
        ],
        axis=0,
    )
    both = dot(dft, stacked)
    lines = both.shape[0] // 8
    joined = jnp.concatenate(
        [both[:, :gates].reshape(lines, 8, gates), both[:, gates:].reshape(lines, 8, gates)],
        axis=1,
    )
    return joined.astype(BF16)


GROUP = 16


def half_of_bins(bins, mine):
    core = lax.axis_index("range") & 1
    return (core if mine else 1 - core) * (bins // 2)


def sent_bins(bins):
    return bins // 2 + 2


def spectra_first_kernel(raw_ref, rep_ref, dft_ref, _, s_ref, local_ref, taps_ref, *rest):
    *send_refs, buf, sems = rest
    bins, _, chans, gates = s_ref.shape
    size = GROUP * bins
    copies = [
        pltpu.make_async_copy(
            raw_ref.at[:, j * size : (j + 1) * size, :],
            buf.at[:, j * size : (j + 1) * size, :],
            sems.at[j],
        )
        for j in range(chans // GROUP)
    ]
    for copy in copies:
        copy.start()
    correlation_matrix(rep_ref, taps_ref)
    for j, copy in enumerate(copies):
        copy.wait()
        rows = slice(j * size, (j + 1) * size)
        total = dot(buf[0, rows, :], taps_ref[0]) + dot(buf[1, rows, :], taps_ref[1])
        out = doppler_rows(total, dft_ref[...])
        s_ref[:, :, j * GROUP : (j + 1) * GROUP, :] = out.reshape(bins, 2, GROUP, gates)
        later = jnp.concatenate([buf[0, rows, gates:], buf[1, rows, gates:]], axis=1)
        near = jnp.concatenate([taps_ref[0, :gates, :], taps_ref[1, :gates, :]], axis=0)
        local_ref[rows, :] = dot(later, near)
    base = half_of_bins(bins, False)
    half = chans // 2
    for part, send_ref in enumerate(send_refs):
        for k in range(send_ref.shape[0]):
            send_ref[k] = s_ref[lax.rem(base + k, bins), :, part * half : (part + 1) * half, :]


def spectra_last_kernel(part, local_ref, halo_ref, taps_ref, dft_ref, _, s_ref, send_ref):
    bins, _, chans, gates = s_ref.shape
    size = GROUP * bins
    far = jnp.concatenate([taps_ref[0, gates:, :], taps_ref[1, gates:, :]], axis=0)
    for j in range(chans // GROUP):
        rows = slice(j * size, (j + 1) * size)
        later = jnp.concatenate([halo_ref[0, rows, :], halo_ref[1, rows, :]], axis=1)
        start = part * chans * bins + j * size
        out = doppler_rows(local_ref[start : start + size, :] + dot(later, far), dft_ref[...])
        s_ref[:, :, j * GROUP : (j + 1) * GROUP, :] = out.reshape(bins, 2, GROUP, gates)
    base = half_of_bins(bins, False)
    for k in range(send_ref.shape[0]):
        send_ref[k] = s_ref[lax.rem(base + k, bins)]


def spectra_first(raw, replica, table, pulses, mark):
    _, rows, gates = raw.shape
    chans = rows // pulses
    taps = replica.shape[1]
    return pl.pallas_call(
        spectra_first_kernel,
        out_shape=[
            jax.ShapeDtypeStruct((pulses, 2, chans, BLOCK), BF16),
            jax.ShapeDtypeStruct((rows, 2 * BLOCK), F32),
            jax.ShapeDtypeStruct((2, 2 * taps, 2 * taps), BF16),
        ]
        + [jax.ShapeDtypeStruct((sent_bins(pulses), 2, chans // 2, BLOCK), BF16)] * 2,
        in_specs=[hbm_spec(), vmem_spec(), vmem_spec(), pl.BlockSpec(memory_space=pl.ANY)],
        out_specs=[vmem_spec()] * 5,
        scratch_shapes=[
            pltpu.VMEM(raw.shape, BF16),
            pltpu.SemaphoreType.DMA((chans // GROUP,)),
        ],
        compiler_params=params(),
        cost_estimate=SHORT,
    )(raw, replica, table, mark)


def spectra_last(part, local, halo, matrix, table, pulses, sums):
    chans = halo.shape[1] // pulses
    return pl.pallas_call(
        functools.partial(spectra_last_kernel, part),
        out_shape=[
            jax.ShapeDtypeStruct((pulses, 2, chans, BLOCK), BF16),
            jax.ShapeDtypeStruct((sent_bins(pulses), 2, chans, BLOCK), BF16),
        ],
        in_specs=[vmem_spec()] * 4 + [pl.BlockSpec(memory_space=pl.ANY)],
        out_specs=[vmem_spec()] * 2,
        compiler_params=params(),
        cost_estimate=SHORT,
    )(local, halo, matrix, table, sums)


def cross_kernel(count_refs, *refs):
    s_refs, rest = refs[:count_refs], refs[count_refs:]
    before_ref = rest[0] if len(rest) == 2 else None
    out_ref = rest[-1]
    held, _, _, gates = s_refs[0].shape
    chans = sum(ref.shape[2] for ref in s_refs)
    count = out_ref.shape[0]
    base = half_of_bins(held, True) if held == 2 * count else 0

    def write(e, block):
        out_ref[e] = block if before_ref is None else block + before_ref[e]

    @pl.loop(0, count // 2, unroll=8)
    def _(step):
        e = step * 2
        each = []
        for k in range(4):
            where = lax.rem(base + e + k, held)
            each.append(
                [jnp.concatenate([ref[where, o] for ref in s_refs], axis=0) for o in range(2)]
            )
        left = jnp.concatenate(
            [jnp.concatenate([re, im], axis=1) for re, im in each], axis=0
        )
        right = jnp.concatenate(
            [
                jnp.concatenate(pieces, axis=1)
                for re, im in each[:2]
                for pieces in ((re, im), (-im, re))
            ],
            axis=0,
        )
        both = dot_nt(left, right)
        write(e, both[: 3 * chans, : 2 * chans])
        write(e + 1, both[chans:, 2 * chans :])


def cross(spectra, bins, before=None):
    chans = sum(value.shape[2] for value in spectra)
    data = spectra if before is None else spectra + [before]
    return pl.pallas_call(
        functools.partial(cross_kernel, len(spectra)),
        out_shape=jax.ShapeDtypeStruct((bins // 2, 3 * chans, 2 * chans), F32),
        in_specs=[vmem_spec()] * len(data),
        out_specs=vmem_spec(),
        compiler_params=params(),
        cost_estimate=SHORT,
    )(*data)


U_BITS, V_BITS = (2, 4), (4, 2)


def partner(value, bits):
    count = lax.axis_size("range")
    return lax.ppermute(value, "range", [(i, i ^ bits[i & 1]) for i in range(count)])


def slot_of(core, x, y, z):
    return (4 * z + ((2 * y + (x ^ y)) ^ (3 * (z & 1)))) ^ (15 * core)


def parts_of(index):
    return index & 1, (index >> 1) & 1, (index >> 2) & 1, (index >> 3) & 3


def bin_of(index):
    core, x, y, z = parts_of(index)
    return core * 16 + slot_of(core, x, y, z)


def index_of(bin_id):
    core = bin_id >> 4
    path = (bin_id & 15) ^ (15 * core)
    z = path >> 2
    turned = (path & 3) ^ (3 * (z & 1))
    y = turned >> 1
    x = (turned & 1) ^ y
    return z * 8 + y * 4 + x * 2 + core


def uv_parts():
    core, x, y, z = parts_of(lax.axis_index("range"))
    return core, jnp.where(core == 0, x, y), jnp.where(core == 0, y, x), z


def uv_slot(core, u, v, z):
    return slot_of(core, jnp.where(core == 0, u, v), jnp.where(core == 0, v, u), z)


def packed(block):
    chans = block.shape[0]
    lower = iota((chans, chans), 0) >= iota((chans, chans), 1)
    swapped = pltpu.roll(block, chans, 1)
    mixed = jnp.where(lower, block[:, :chans], swapped[:, :chans])
    return jnp.concatenate([mixed[: chans // 2], mixed[chans // 2 :]], axis=1)


def sent_rows(keep_ref):
    return 5 * keep_ref.shape[1] // 6


def upper_rows(keep_ref, e):
    block = keep_ref.shape[1] // 3
    end = sent_rows(keep_ref) // 2 + block // 2
    return jnp.concatenate([packed(keep_ref[e, :block]), keep_ref[e, block:end]], axis=0)


def lower_rows(keep_ref, e):
    return keep_ref[e, sent_rows(keep_ref) // 2 + keep_ref.shape[1] // 6 :]


def first_kernel(keep_ref, a_ref, b_ref):
    core, u, v, z = uv_parts()
    for k in range(8):
        a_ref[k] = upper_rows(keep_ref, uv_slot(core, 1 - u, k // 4, k % 4))
        b_ref[k] = lower_rows(keep_ref, uv_slot(core, k // 4, 1 - v, k % 4))


def second_kernel(keep_ref, a1_ref, b1_ref, a_ref, b_ref):
    core, u, v, z = uv_parts()
    for k in range(4):
        e = uv_slot(core, u, 1 - v, k)
        a_ref[k] = upper_rows(keep_ref, e) + a1_ref[(1 - v) * 4 + k]
        e = uv_slot(core, 1 - u, v, k)
        b_ref[k] = lower_rows(keep_ref, e) + b1_ref[(1 - u) * 4 + k]


def line_sum(keep_ref, a1_ref, b1_ref, a2_ref, b2_ref, flip):
    core, u, v, z = uv_parts()
    z = z ^ flip
    e = uv_slot(core, u, v, z)
    upper = upper_rows(keep_ref, e) + a1_ref[v * 4 + z] + a2_ref[z]
    lower = lower_rows(keep_ref, e) + b1_ref[u * 4 + z] + b2_ref[z]
    return upper, lower


FLIPS = (2, 3, 1)


def line_kernel(*refs):
    half = sent_rows(refs[0]) // 2
    for flip, out_ref in zip(FLIPS, refs[5:]):
        upper, lower = line_sum(*refs[:5], flip)
        out_ref[:half] = upper
        out_ref[half:] = lower


def own_kernel(*refs):
    z1_ref, z2_ref, z3_ref, out_ref, packed_ref = refs[5:]
    half = sent_rows(refs[0]) // 2
    upper, lower = line_sum(*refs[:5], 0)
    upper = upper + z1_ref[:half] + (z2_ref[:half] + z3_ref[:half])
    out_ref[:half] = upper
    packed_ref[...] = upper[: packed_ref.shape[0]]
    out_ref[half:] = lower + z1_ref[half:] + (z2_ref[half:] + z3_ref[half:])


def summed(kernel, data, shapes):
    return pl.pallas_call(
        kernel,
        out_shape=[jax.ShapeDtypeStruct(shape, F32) for shape in shapes],
        in_specs=[vmem_spec()] * len(data),
        out_specs=[vmem_spec()] * len(shapes),
        compiler_params=params(),
    )(*data)


def bin_sums(keep):
    _, full, wide = keep.shape
    rows = 5 * full // 6
    half = rows // 2
    data = [keep]
    a, b = summed(first_kernel, data, [(8, half, wide)] * 2)
    data += [partner(a, U_BITS), partner(b, V_BITS)]
    a, b = summed(second_kernel, data, [(4, half, wide)] * 2)
    data += [partner(a, V_BITS), partner(b, U_BITS)]
    sends = summed(line_kernel, data, [(rows, wide)] * 3)
    data += [partner(value, (8 * flip, 8 * flip)) for flip, value in zip(FLIPS, sends)]
    own, packed = summed(own_kernel, data, [(rows, wide), (rows // 5, wide)])
    bit = 32
    while bit < lax.axis_size("range"):
        own = own + partner(own, (bit, bit))
        packed = packed + partner(packed, (bit, bit))
        bit *= 2
    return own, packed


def from_bin(value, offset):
    count = lax.axis_size("range")
    pairs = []
    for i in range(count):
        target = index_of((bin_of(i) - offset) % 32) | (i & ~31)
        pairs.append((i, target))
    return lax.ppermute(value, "range", pairs)


def turn(value):
    half = value.shape[1] // 2
    rolled = pltpu.roll(value, half, 1)
    return jnp.where(iota(value.shape, 1) < half, -rolled, rolled)


def embed(value):
    return jnp.concatenate([value, turn(value)], axis=0)


def mul(a, b):
    return jnp.dot(a, embed(b), precision=lax.Precision.HIGHEST, preferred_element_type=F32)


def mul_conj(a, b):
    half = a.shape[1] // 2
    stacked = jnp.concatenate([a, -turn(a)], axis=0)
    both = dot_nt(stacked, b, lax.Precision.HIGHEST)
    rows = a.shape[0]
    return jnp.concatenate([both[:rows], both[rows:]], axis=1)


def reciprocal(x):
    value = pl.reciprocal(x, approx=True)
    for _ in range(2):
        value = value * (2.0 - x * value)
    return value


def pivot_inverse(p):
    def times(x, y):
        return x[0] * y[0] - x[1] * y[1], x[0] * y[1] + x[1] * y[0]

    def conj(x):
        return x[0], -x[1]

    def plus(x, y):
        return x[0] + y[0], x[1] + y[1]

    def scaled(x, s):
        return x[0] * s, x[1] * s

    def square(x):
        return x[0] * x[0] + x[1] * x[1]

    def two(a, b, d):
        inv = reciprocal(a * d - square(b))
        return d * inv, scaled(b, -inv), a * inv

    a, d = p[0][0], p[1][1]
    b = p[0][1]
    ea, eb, ed = two(a, b, d)
    f = [[p[0][2], p[0][3]], [p[1][2], p[1][3]]]
    w = [
        [plus(scaled(f[0][j], ea), times(eb, f[1][j])) for j in range(2)],
        [plus(times(conj(eb), f[0][j]), scaled(f[1][j], ed)) for j in range(2)],
    ]

    def inner(i, j):
        return plus(times(conj(f[0][i]), w[0][j]), times(conj(f[1][i]), w[1][j]))

    ha = p[2][2] - inner(0, 0)[0]
    hd = p[3][3] - inner(1, 1)[0]
    cross = inner(0, 1)
    hb = (p[2][3][0] - cross[0], p[2][3][1] - cross[1])
    ga, gb, gd = two(ha, hb, hd)
    v = [
        [
            plus(scaled(w[i][0], ga), times(w[i][1], conj(gb))),
            plus(times(w[i][0], gb), scaled(w[i][1], gd)),
        ]
        for i in range(2)
    ]
    top = [
        [plus(times(v[i][0], conj(w[j][0])), times(v[i][1], conj(w[j][1]))) for j in range(2)]
        for i in range(2)
    ]
    zero = None
    out = [[None] * 4 for _ in range(4)]
    out[0][0] = (ea + top[0][0][0], zero)
    out[1][1] = (ed + top[1][1][0], zero)
    out[0][1] = plus(eb, top[0][1])
    out[2][2], out[3][3], out[2][3] = (ga, zero), (gd, zero), gb
    for i in range(2):
        for j in range(2):
            out[i][2 + j] = (-v[i][j][0], -v[i][j][1])
    for i in range(4):
        for j in range(i):
            out[i][j] = conj(out[j][i])
    return out


def invert(work_ref):
    chans, width = work_ref.shape
    sub = 8
    count = chans // sub
    lane = iota((sub, width), 1)
    row = iota((sub, width), 0)
    low = jnp.bitwise_and(lane, chans - 1)
    first_half = lane < chans

    def spin(value):
        rolled = pltpu.roll(value, chans, 1)
        return jnp.where(first_half, -rolled, rolled)

    def column(value, k):
        return jnp.broadcast_to(value[:, k : k + 1], (sub, width))

    def combine(terms):
        while len(terms) > 1:
            terms = [
                terms[i] + terms[i + 1] if i + 1 < len(terms) else terms[i]
                for i in range(0, len(terms), 2)
            ]
        return terms[0]

    @pl.loop(0, count)
    def _(t):
        here = pl.ds(pl.multiple_of(t * sub, sub), sub)
        for k in (0, 4):
            tile = work_ref[here, :]
            lines = [jnp.broadcast_to(tile[k + i : k + i + 1, :], (sub, width)) for i in range(4)]
            pivot = [[None] * 4 for _ in range(4)]
            for i in range(4):
                pivot[i][i] = column(lines[i], k + i)
                for j in range(i + 1, 4):
                    pivot[i][j] = column(lines[i], k + j), column(lines[i], chans + k + j)
            cleared = (low >= k) & (low < k + 4)
            unit = [
                jnp.where(cleared, jnp.where(lane == k + i, 1.0, 0.0), lines[i])
                for i in range(4)
            ]
            spun = [spin(u) for u in unit]
            p = pivot_inverse(pivot)
            fresh_lines, fresh_spun = [], []
            for i in range(4):
                terms, other = [], []
                for j in range(4):
                    re, im = p[i][j]
                    terms.append(re * unit[j])
                    other.append(re * spun[j])
                    if im is not None:
                        terms.append(im * spun[j])
                        other.append(-(im * unit[j]))
                fresh_lines.append(combine(terms))
                fresh_spun.append(combine(other))
            for s in range(count):
                tile = work_ref[s * sub : (s + 1) * sub, :]
                terms = []
                for i in range(4):
                    terms.append(column(tile, k + i) * fresh_lines[i])
                    terms.append(column(tile, chans + k + i) * fresh_spun[i])
                work_ref[s * sub : (s + 1) * sub, :] = jnp.where(cleared, 0.0, tile) - combine(
                    terms
                )
            tile = work_ref[here, :]
            for i in range(4):
                tile = jnp.where(row == k + i, fresh_lines[i], tile)
            work_ref[here, :] = tile
        for s in range(count):
            tile = work_ref[s * sub : (s + 1) * sub, :]
            ahead = pltpu.roll(tile, width - sub, 1)
            behind = pltpu.roll(tile, chans - sub, 1)
            work_ref[s * sub : (s + 1) * sub, :] = jnp.where(low < chans - sub, ahead, behind)


def unpacked(ref, scale):
    half, wide = ref.shape[0], ref.shape[1]
    piece = ref[...] * scale
    swapped = pltpu.roll(piece, wide // 2, 1)
    return jnp.concatenate([piece, swapped], axis=0)[:, : wide // 2]


def hermitian(mixed, across):
    i, j = iota(mixed.shape, 0), iota(mixed.shape, 1)
    real_part = jnp.where(i >= j, mixed, across)
    imag_part = jnp.where(i < j, mixed, jnp.where(i > j, -across, 0.0))
    return jnp.concatenate([real_part, imag_part], axis=1)


def middle_kernel(total, packed_ref, steer_ref, inv_ref, t_ref):
    chans = inv_ref.shape[0]
    mixed = unpacked(packed_ref, F32(1.0 / total))
    twice = jnp.concatenate([mixed, mixed], axis=1)
    across = jnp.concatenate([twice, twice], axis=0).T[:chans, :chans]
    inv_ref[...] = hermitian(mixed, across)
    invert(inv_ref)
    t_ref[...] = mul(steer_ref[...], inv_ref[...])


def outer_kernel(total, own_ref, left_ref, right_ref, steer_ref, inv_ref, t_ref, out_ref,
                 work, keep, small):
    chans = inv_ref.shape[0]
    scale = F32(1.0 / total)
    half = chans // 2
    m_left = unpacked(left_ref.at[:half], scale)
    m_right = unpacked(right_ref, scale)
    ml = left_ref[half : half + chans] * scale
    rl = left_ref[half + chans :] * scale
    rm = own_ref[half : half + chans] * scale
    across = jnp.concatenate([jnp.concatenate([m_left, m_right], axis=1), ml], axis=0).T
    lm = jnp.concatenate([across[:chans, chans:], -across[chans:, chans:]], axis=1)
    t = t_ref[...]
    both = mul(jnp.concatenate([rm, lm], axis=0), inv_ref[...])
    g_right, g_left = both[:chans], both[chans:]
    by_left = mul(jnp.concatenate([g_left, g_right, t], axis=0), ml)
    by_right = mul_conj(jnp.concatenate([g_right, t], axis=0), rm)
    work[...] = hermitian(m_left, across[:chans, :chans]) - by_left[:chans]
    keep[0] = rl - by_left[chans : 2 * chans]
    keep[1] = hermitian(m_right, across[chans:, :chans]) - by_right[:chans]
    keep[2] = g_left
    keep[3] = g_right
    small[0] = -by_left[2 * chans :]
    small[1] = -by_right[chans:]

    @pl.loop(0, 2)
    def _(stage):
        invert(work)

        @pl.when(stage == 0)
        def _():
            s_rl = keep[0]
            both = mul(jnp.concatenate([s_rl, small[0]], axis=0), work[...])
            back = mul_conj(both, s_rl)
            work[...] = keep[1] - back[:chans]
            small[1] = small[1] - back[chans:]
            middle = mul(both, keep[2])
            keep[0] = both[:chans]
            small[0] = both[chans:]
            keep[3] = keep[3] - middle[:chans]
            small[2] = t_ref[...] - middle[chans:]

        @pl.when(stage == 1)
        def _():
            y_right = mul(small[1], work[...])
            factors = jnp.concatenate([embed(keep[0]), embed(keep[3])], axis=1)
            both = jnp.dot(
                y_right, factors, precision=lax.Precision.HIGHEST, preferred_element_type=F32
            )
            y_left = small[0] - both[:, : 2 * chans]
            y_mid = small[2] - both[:, 2 * chans :]
            quad = jnp.sum(steer_ref[...] * y_mid, axis=1, keepdims=True)
            y = jnp.concatenate([y_left, y_mid, y_right], axis=1) / jnp.sqrt(quad)
            real_lane = lax.rem(iota(y.shape, 1), 2 * chans) < chans
            mine = jnp.where(real_lane, y, -y).astype(BF16)
            for c in range(out_ref.shape[0]):
                out_ref[c] = mine


def steering(chans):
    index = np.arange(chans)
    sines = -0.8 + 1.6 * np.arange(BEAMS) / (BEAMS - 1)
    angle = math.pi * sines[:, None] * index[None, :]
    return np.concatenate([np.cos(angle), -np.sin(angle)], axis=1).astype(np.float32)


def solve_middle(packed, steer, total):
    half, wide = packed.shape
    return pl.pallas_call(
        functools.partial(middle_kernel, total),
        out_shape=[
            jax.ShapeDtypeStruct((2 * half, wide), F32),
            jax.ShapeDtypeStruct((BEAMS, wide), F32),
        ],
        in_specs=[vmem_spec()] * 2,
        out_specs=[vmem_spec()] * 2,
        compiler_params=params(),
    )(packed, steer)


def solve_outer(own, left, right, steer, inverse, t, total, copies):
    chans, wide = inverse.shape
    return pl.pallas_call(
        functools.partial(outer_kernel, total),
        out_shape=jax.ShapeDtypeStruct((copies, BEAMS, 3 * wide), BF16),
        in_specs=[vmem_spec()] * 6,
        out_specs=vmem_spec(),
        scratch_shapes=[
            pltpu.VMEM((chans, wide), F32),
            pltpu.VMEM((4, chans, wide), F32),
            pltpu.VMEM((3, BEAMS, wide), F32),
        ],
        compiler_params=params(),
    )(own, left, right, steer, inverse, t)


def beam_kernel(bin_ref, block_ref, beam_ref, owner_ref, s0_ref, upper_ref, lower_ref, w_ref,
                out_ref, both_ref, rows_ref, seen_ref):
    bins, wide, gates = s0_ref.shape
    devices = seen_ref.shape[0]
    count = bin_ref.shape[0]
    rows_ref[...] = jnp.zeros_like(rows_ref)

    @pl.loop(0, devices)
    def _(i):
        seen_ref[i] = 0

    w = w_ref[...].astype(F32).reshape(bins * BEAMS, 3 * wide)
    for k in range(3):
        lanes = slice(k * wide, (k + 1) * wide)
        part = w[:, lanes]
        both_ref[:, 0:BEAMS, lanes] = part.reshape(bins, BEAMS, wide)
        both_ref[:, BEAMS:, lanes] = turn(part).reshape(bins, BEAMS, wide)

    def detection(j, carry):
        bin_id = bin_ref[j]
        beam_id = beam_ref[j]
        owner = owner_ref[j]
        rank = seen_ref[owner]
        seen_ref[owner] = rank + 1
        left = both_ref[index_of(bin_id)].astype(BF16)
        bands = [lax.rem(bin_id + bins - 1 + k, bins) for k in range(3)]
        first = block_ref[j] == 0
        pieces = []
        for b in bands:
            later = [upper_ref[b, 0], lower_ref[b, 0], upper_ref[b, 1], lower_ref[b, 1]]
            pieces.append(jnp.where(first, s0_ref[b], jnp.concatenate(later, axis=0)))
        window = jnp.concatenate(pieces, axis=0)
        both = dot(left, window)
        line = jnp.concatenate([both[:BEAMS], both[BEAMS:]], axis=1)
        chosen = jnp.where(iota(line.shape, 0) == beam_id, line, 0.0)
        row = owner * CAP + rank
        rows_ref[pl.ds(row, 1), :] = jnp.sum(chosen, axis=0, keepdims=True)
        return carry

    lax.fori_loop(0, count, detection, 0, unroll=32)
    out_ref[...] = rows_ref[...].astype(BF16)


def beam_rows(det_bin, det_block, det_beam, owners, s0, s1, weight, devices):
    bins, wide, gates = s0.shape
    return pl.pallas_call(
        beam_kernel,
        out_shape=jax.ShapeDtypeStruct((devices * CAP, 2 * gates), BF16),
        in_specs=[smem_spec()] * 4 + [vmem_spec()] * 4,
        out_specs=vmem_spec(),
        scratch_shapes=[
            pltpu.VMEM((bins, 2 * BEAMS, 3 * wide), F32),
            pltpu.VMEM((devices * CAP, 2 * gates), F32),
            pltpu.SMEM((devices,), jnp.int32),
        ],
        compiler_params=params(),
    )(det_bin, det_block, det_beam, owners, s0, *s1, weight)


def on_device(raw, replica, det_bin, det_block, det_beam, det_owner):
    devices = lax.axis_size("range")
    _, chans, pulses, gates = raw.shape
    bins = pulses
    flat = raw.reshape(2, chans * pulses, gates)
    before = [(source, source - 1) for source in range(1, devices)]
    *slices, mark = first_gates(flat)
    halos = [lax.ppermute(value, "range", before) for value in slices]
    table = doppler_matrix(pulses, 8)
    s0, local, matrix, *sent = spectra_first(flat, replica, table, pulses, mark)
    beside0 = [partner(value, (1, 1)) for value in sent]
    sums = cross([s0], bins)
    sums = cross(beside0, bins, sums)
    s1, beside1 = [], []
    for part, halo in enumerate(halos):
        value, send = spectra_last(part, local, halo, matrix, table, pulses, sums)
        s1.append(value)
        beside1.append(partner(send, (1, 1)))
    sums = cross(s1, bins, sums)
    sums = cross(beside1, bins, sums)
    own, packed = bin_sums(sums)
    total = gates * devices
    steer = steering(chans)
    left = from_bin(own, -1)
    right = from_bin(packed, 1)
    inverse, t = solve_middle(packed, steer, total)
    mine = solve_outer(own, left, right, steer, inverse, t, total, bins)
    groups = [list(range(first, first + bins)) for first in range(0, devices, bins)]
    weight = lax.all_to_all(
        mine, "range", split_axis=0, concat_axis=0, tiled=True,
        axis_index_groups=groups if len(groups) > 1 else None,
    )
    outgoing = beam_rows(
        det_bin, det_block, det_beam, det_owner[:, 0],
        s0.reshape(bins, 2 * chans, BLOCK), s1, weight, devices,
    )
    incoming = lax.all_to_all(
        outgoing.reshape(devices, CAP, 2 * BLOCK), "range", split_axis=0, concat_axis=0, tiled=True
    )
    return incoming.astype(F32).reshape(devices * CAP, 2 * BLOCK)


def solution(mesh):
    in_specs = (
        P(None, None, None, "range"),
        P(),
        P("range"),
        P("range"),
        P("range"),
        P("range", None),
    )
    out_specs = P("range", None)
    return jax.shard_map(
        on_device, mesh=mesh, in_specs=in_specs, out_specs=out_specs, check_vma=False
    )
```

```python
import functools
import math

import jax
import jax.numpy as jnp
import ml_dtypes
import numpy as np
from jax import lax
from jax.experimental import pallas as pl
from jax.experimental.pallas import tpu as pltpu
from jax.sharding import PartitionSpec as P

BLOCK = 128
BEAMS = 8
CAP = 2

F32 = jnp.float32
BF16 = jnp.bfloat16
VMEM = pltpu.VMEM
MIB = 1024 * 1024
NT = (((1,), (1,)), ((), ()))


def vmem_spec():
    return pl.BlockSpec(memory_space=VMEM)


def smem_spec():
    return pl.BlockSpec(memory_space=pltpu.SMEM)


def hbm_spec():
    return pl.BlockSpec(memory_space=pltpu.HBM)


SHORT = pl.CostEstimate(flops=1, bytes_accessed=1, transcendentals=0)


def params(mib=16):
    return pltpu.CompilerParams(vmem_limit_bytes=int(mib * MIB))


def dot(a, b):
    return jnp.dot(a, b, preferred_element_type=F32)


def dot_nt(a, b, precision=None):
    return lax.dot_general(a, b, NT, precision=precision, preferred_element_type=F32)


def iota(shape, axis):
    return lax.broadcasted_iota(jnp.int32, shape, axis)


def halo_kernel(raw_ref, a_ref, b_ref, mark_ref, sems):
    mark_ref[...] = jnp.zeros_like(mark_ref)
    count = sems.shape[0] // 2
    size = a_ref.shape[1] // count
    copies = []
    for part, out_ref in enumerate((a_ref, b_ref)):
        for j in range(count):
            start = part * a_ref.shape[1] + j * size
            copies.append(
                pltpu.make_async_copy(
                    raw_ref.at[:, start : start + size, :BLOCK],
                    out_ref.at[:, j * size : (j + 1) * size, :],
                    sems.at[part * count + j],
                )
            )
    for copy in copies:
        copy.start()
    for copy in copies:
        copy.wait()


def first_gates(raw):
    half = jax.ShapeDtypeStruct((2, raw.shape[1] // 2, BLOCK), BF16)
    return pl.pallas_call(
        halo_kernel,
        out_shape=[half, half, jax.ShapeDtypeStruct((8, 128), F32)],
        in_specs=[hbm_spec()],
        out_specs=[vmem_spec()] * 3,
        scratch_shapes=[pltpu.SemaphoreType.DMA((2,))],
        compiler_params=params(63),
    )(raw)


def correlation_matrix(rep_ref, out_ref):
    taps = rep_ref.shape[1]
    base = rep_ref[...].astype(F32)
    row = iota((taps, 2 * taps), 0)
    parts = []
    for i in range(2):
        line = jnp.concatenate([base[i : i + 1], jnp.zeros((1, taps), F32)], axis=1)
        skew = jnp.broadcast_to(line, (taps, 2 * taps))
        bit = 1
        while bit < taps:
            skew = jnp.where((row & bit) != 0, pltpu.roll(skew, bit, 1), skew)
            bit *= 2
        parts.append(skew.T)
    real_part, imag_part = parts
    out_ref[0] = jnp.concatenate([real_part, -imag_part], axis=1).astype(BF16)
    out_ref[1] = jnp.concatenate([imag_part, real_part], axis=1).astype(BF16)


def doppler_matrix(pulses, group):
    index = np.arange(pulses)
    angle = 2.0 * math.pi / pulses * (index[:, None] * index[None, :] % pulses)
    cosine = np.cos(angle) * pulses**-0.5
    sine = np.sin(angle) * pulses**-0.5
    table = np.stack([np.stack([cosine, -sine], 1), np.stack([sine, cosine], 1)], 0)
    full = np.einsum("ipod,ce->dociep", table, np.eye(group))
    shape = (pulses * 2 * group, 2 * group * pulses)
    return full.reshape(shape).astype(ml_dtypes.bfloat16)


def doppler_rows(total, dft):
    compressed = total.astype(BF16)
    rows, wide = compressed.shape
    half, gates = rows // 2, wide // 2
    stacked = jnp.concatenate(
        [
            jnp.concatenate([compressed[:half, :gates], compressed[half:, :gates]], axis=1),
            jnp.concatenate([compressed[:half, gates:], compressed[half:, gates:]], axis=1),
        ],
        axis=0,
    )
    both = dot(dft, stacked)
    lines = both.shape[0] // 8
    joined = jnp.concatenate(
        [both[:, :gates].reshape(lines, 8, gates), both[:, gates:].reshape(lines, 8, gates)],
        axis=1,
    )
    return joined.astype(BF16)


GROUP = 16


def half_of_bins(bins, mine):
    core = lax.axis_index("range") & 1
    return (core if mine else 1 - core) * (bins // 2)


def sent_bins(bins):
    return bins // 2 + 2


def spectra_first_kernel(raw_ref, rep_ref, dft_ref, _, s_ref, local_ref, taps_ref, *rest):
    *send_refs, buf, sems = rest
    bins, _, chans, gates = s_ref.shape
    size = GROUP * bins
    copies = [
        pltpu.make_async_copy(
            raw_ref.at[:, j * size : (j + 1) * size, :],
            buf.at[:, j * size : (j + 1) * size, :],
            sems.at[j],
        )
        for j in range(chans // GROUP)
    ]
    for copy in copies:
        copy.start()
    correlation_matrix(rep_ref, taps_ref)
    for j, copy in enumerate(copies):
        copy.wait()
        rows = slice(j * size, (j + 1) * size)
        total = dot(buf[0, rows, :], taps_ref[0]) + dot(buf[1, rows, :], taps_ref[1])
        out = doppler_rows(total, dft_ref[...])
        s_ref[:, :, j * GROUP : (j + 1) * GROUP, :] = out.reshape(bins, 2, GROUP, gates)
        later = jnp.concatenate([buf[0, rows, gates:], buf[1, rows, gates:]], axis=1)
        near = jnp.concatenate([taps_ref[0, :gates, :], taps_ref[1, :gates, :]], axis=0)
        local_ref[rows, :] = dot(later, near)
    base = half_of_bins(bins, False)
    half = chans // 2
    for part, send_ref in enumerate(send_refs):
        for k in range(send_ref.shape[0]):
            send_ref[k] = s_ref[lax.rem(base + k, bins), :, part * half : (part + 1) * half, :]


def spectra_last_kernel(part, local_ref, halo_ref, taps_ref, dft_ref, _, s_ref, send_ref):
    bins, _, chans, gates = s_ref.shape
    size = GROUP * bins
    far = jnp.concatenate([taps_ref[0, gates:, :], taps_ref[1, gates:, :]], axis=0)
    for j in range(chans // GROUP):
        rows = slice(j * size, (j + 1) * size)
        later = jnp.concatenate([halo_ref[0, rows, :], halo_ref[1, rows, :]], axis=1)
        start = part * chans * bins + j * size
        out = doppler_rows(local_ref[start : start + size, :] + dot(later, far), dft_ref[...])
        s_ref[:, :, j * GROUP : (j + 1) * GROUP, :] = out.reshape(bins, 2, GROUP, gates)
    base = half_of_bins(bins, False)
    for k in range(send_ref.shape[0]):
        send_ref[k] = s_ref[lax.rem(base + k, bins)]


def spectra_first(raw, replica, table, pulses, mark):
    _, rows, gates = raw.shape
    chans = rows // pulses
    taps = replica.shape[1]
    return pl.pallas_call(
        spectra_first_kernel,
        out_shape=[
            jax.ShapeDtypeStruct((pulses, 2, chans, BLOCK), BF16),
            jax.ShapeDtypeStruct((rows, 2 * BLOCK), F32),
            jax.ShapeDtypeStruct((2, 2 * taps, 2 * taps), BF16),
        ]
        + [jax.ShapeDtypeStruct((sent_bins(pulses), 2, chans // 2, BLOCK), BF16)] * 2,
        in_specs=[hbm_spec(), vmem_spec(), vmem_spec(), pl.BlockSpec(memory_space=pl.ANY)],
        out_specs=[vmem_spec()] * 5,
        scratch_shapes=[
            pltpu.VMEM(raw.shape, BF16),
            pltpu.SemaphoreType.DMA((chans // GROUP,)),
        ],
        compiler_params=params(),
        cost_estimate=SHORT,
    )(raw, replica, table, mark)


def spectra_last(part, local, halo, matrix, table, pulses, sums):
    chans = halo.shape[1] // pulses
    return pl.pallas_call(
        functools.partial(spectra_last_kernel, part),
        out_shape=[
            jax.ShapeDtypeStruct((pulses, 2, chans, BLOCK), BF16),
            jax.ShapeDtypeStruct((sent_bins(pulses), 2, chans, BLOCK), BF16),
        ],
        in_specs=[vmem_spec()] * 4 + [pl.BlockSpec(memory_space=pl.ANY)],
        out_specs=[vmem_spec()] * 2,
        compiler_params=params(),
        cost_estimate=SHORT,
    )(local, halo, matrix, table, sums)


def cross_kernel(count_refs, *refs):
    s_refs, rest = refs[:count_refs], refs[count_refs:]
    before_ref = rest[0] if len(rest) == 2 else None
    out_ref = rest[-1]
    held, _, _, gates = s_refs[0].shape
    chans = sum(ref.shape[2] for ref in s_refs)
    count = out_ref.shape[0]
    base = half_of_bins(held, True) if held == 2 * count else 0

    def write(e, block):
        out_ref[e] = block if before_ref is None else block + before_ref[e]

    @pl.loop(0, count // 2, unroll=8)
    def _(step):
        e = step * 2
        each = []
        for k in range(4):
            where = lax.rem(base + e + k, held)
            each.append(
                [jnp.concatenate([ref[where, o] for ref in s_refs], axis=0) for o in range(2)]
            )
        left = jnp.concatenate(
            [jnp.concatenate([re, im], axis=1) for re, im in each], axis=0
        )
        right = jnp.concatenate(
            [
                jnp.concatenate(pieces, axis=1)
                for re, im in each[:2]
                for pieces in ((re, im), (-im, re))
            ],
            axis=0,
        )
        both = dot_nt(left, right)
        write(e, both[: 3 * chans, : 2 * chans])
        write(e + 1, both[chans:, 2 * chans :])


def cross(spectra, bins, before=None):
    chans = sum(value.shape[2] for value in spectra)
    data = spectra if before is None else spectra + [before]
    return pl.pallas_call(
        functools.partial(cross_kernel, len(spectra)),
        out_shape=jax.ShapeDtypeStruct((bins // 2, 3 * chans, 2 * chans), F32),
        in_specs=[vmem_spec()] * len(data),
        out_specs=vmem_spec(),
        compiler_params=params(),
        cost_estimate=SHORT,
    )(*data)


U_BITS, V_BITS = (2, 4), (4, 2)


def partner(value, bits):
    count = lax.axis_size("range")
    return lax.ppermute(value, "range", [(i, i ^ bits[i & 1]) for i in range(count)])


def slot_of(core, x, y, z):
    return (4 * z + ((2 * y + (x ^ y)) ^ (3 * (z & 1)))) ^ (15 * core)


def parts_of(index):
    return index & 1, (index >> 1) & 1, (index >> 2) & 1, (index >> 3) & 3


def bin_of(index):
    core, x, y, z = parts_of(index)
    return core * 16 + slot_of(core, x, y, z)


def index_of(bin_id):
    core = bin_id >> 4
    path = (bin_id & 15) ^ (15 * core)
    z = path >> 2
    turned = (path & 3) ^ (3 * (z & 1))
    y = turned >> 1
    x = (turned & 1) ^ y
    return z * 8 + y * 4 + x * 2 + core


def uv_parts():
    core, x, y, z = parts_of(lax.axis_index("range"))
    return core, jnp.where(core == 0, x, y), jnp.where(core == 0, y, x), z


def uv_slot(core, u, v, z):
    return slot_of(core, jnp.where(core == 0, u, v), jnp.where(core == 0, v, u), z)


def packed(block):
    chans = block.shape[0]
    lower = iota((chans, chans), 0) >= iota((chans, chans), 1)
    swapped = pltpu.roll(block, chans, 1)
    mixed = jnp.where(lower, block[:, :chans], swapped[:, :chans])
    return jnp.concatenate([mixed[: chans // 2], mixed[chans // 2 :]], axis=1)


def sent_rows(keep_ref):
    return 5 * keep_ref.shape[1] // 6


def upper_rows(keep_ref, e):
    block = keep_ref.shape[1] // 3
    end = sent_rows(keep_ref) // 2 + block // 2
    return jnp.concatenate([packed(keep_ref[e, :block]), keep_ref[e, block:end]], axis=0)


def lower_rows(keep_ref, e):
    return keep_ref[e, sent_rows(keep_ref) // 2 + keep_ref.shape[1] // 6 :]


def first_kernel(keep_ref, a_ref, b_ref):
    core, u, v, z = uv_parts()
    for k in range(8):
        a_ref[k] = upper_rows(keep_ref, uv_slot(core, 1 - u, k // 4, k % 4))
        b_ref[k] = lower_rows(keep_ref, uv_slot(core, k // 4, 1 - v, k % 4))


def second_kernel(keep_ref, a1_ref, b1_ref, a_ref, b_ref):
    core, u, v, z = uv_parts()
    for k in range(4):
        e = uv_slot(core, u, 1 - v, k)
        a_ref[k] = upper_rows(keep_ref, e) + a1_ref[(1 - v) * 4 + k]
        e = uv_slot(core, 1 - u, v, k)
        b_ref[k] = lower_rows(keep_ref, e) + b1_ref[(1 - u) * 4 + k]


def line_sum(keep_ref, a1_ref, b1_ref, a2_ref, b2_ref, flip):
    core, u, v, z = uv_parts()
    z = z ^ flip
    e = uv_slot(core, u, v, z)
    upper = upper_rows(keep_ref, e) + a1_ref[v * 4 + z] + a2_ref[z]
    lower = lower_rows(keep_ref, e) + b1_ref[u * 4 + z] + b2_ref[z]
    return upper, lower


FLIPS = (2, 3, 1)


def line_kernel(*refs):
    half = sent_rows(refs[0]) // 2
    for flip, out_ref in zip(FLIPS, refs[5:]):
        upper, lower = line_sum(*refs[:5], flip)
        out_ref[:half] = upper
        out_ref[half:] = lower


def own_kernel(*refs):
    z1_ref, z2_ref, z3_ref, out_ref, packed_ref = refs[5:]
    half = sent_rows(refs[0]) // 2
    upper, lower = line_sum(*refs[:5], 0)
    upper = upper + z1_ref[:half] + (z2_ref[:half] + z3_ref[:half])
    out_ref[:half] = upper
    packed_ref[...] = upper[: packed_ref.shape[0]]
    out_ref[half:] = lower + z1_ref[half:] + (z2_ref[half:] + z3_ref[half:])


def summed(kernel, data, shapes):
    return pl.pallas_call(
        kernel,
        out_shape=[jax.ShapeDtypeStruct(shape, F32) for shape in shapes],
        in_specs=[vmem_spec()] * len(data),
        out_specs=[vmem_spec()] * len(shapes),
        compiler_params=params(),
    )(*data)


def bin_sums(keep):
    _, full, wide = keep.shape
    rows = 5 * full // 6
    half = rows // 2
    data = [keep]
    a, b = summed(first_kernel, data, [(8, half, wide)] * 2)
    data += [partner(a, U_BITS), partner(b, V_BITS)]
    a, b = summed(second_kernel, data, [(4, half, wide)] * 2)
    data += [partner(a, V_BITS), partner(b, U_BITS)]
    sends = summed(line_kernel, data, [(rows, wide)] * 3)
    data += [partner(value, (8 * flip, 8 * flip)) for flip, value in zip(FLIPS, sends)]
    own, packed = summed(own_kernel, data, [(rows, wide), (rows // 5, wide)])
    bit = 32
    while bit < lax.axis_size("range"):
        own = own + partner(own, (bit, bit))
        packed = packed + partner(packed, (bit, bit))
        bit *= 2
    return own, packed


def from_bin(value, offset):
    count = lax.axis_size("range")
    pairs = []
    for i in range(count):
        target = index_of((bin_of(i) - offset) % 32) | (i & ~31)
        pairs.append((i, target))
    return lax.ppermute(value, "range", pairs)


def turn(value):
    half = value.shape[1] // 2
    rolled = pltpu.roll(value, half, 1)
    return jnp.where(iota(value.shape, 1) < half, -rolled, rolled)


def embed(value):
    return jnp.concatenate([value, turn(value)], axis=0)


def mul(a, b):
    return jnp.dot(a, embed(b), precision=lax.Precision.HIGHEST, preferred_element_type=F32)


def mul_conj(a, b):
    half = a.shape[1] // 2
    stacked = jnp.concatenate([a, -turn(a)], axis=0)
    both = dot_nt(stacked, b, lax.Precision.HIGHEST)
    rows = a.shape[0]
    return jnp.concatenate([both[:rows], both[rows:]], axis=1)


def reciprocal(x):
    value = pl.reciprocal(x, approx=True)
    for _ in range(2):
        value = value * (2.0 - x * value)
    return value


def pivot_inverse(p):
    def times(x, y):
        return x[0] * y[0] - x[1] * y[1], x[0] * y[1] + x[1] * y[0]

    def conj(x):
        return x[0], -x[1]

    def plus(x, y):
        return x[0] + y[0], x[1] + y[1]

    def scaled(x, s):
        return x[0] * s, x[1] * s

    def square(x):
        return x[0] * x[0] + x[1] * x[1]

    def two(a, b, d):
        inv = reciprocal(a * d - square(b))
        return d * inv, scaled(b, -inv), a * inv

    a, d = p[0][0], p[1][1]
    b = p[0][1]
    ea, eb, ed = two(a, b, d)
    f = [[p[0][2], p[0][3]], [p[1][2], p[1][3]]]
    w = [
        [plus(scaled(f[0][j], ea), times(eb, f[1][j])) for j in range(2)],
        [plus(times(conj(eb), f[0][j]), scaled(f[1][j], ed)) for j in range(2)],
    ]

    def inner(i, j):
        return plus(times(conj(f[0][i]), w[0][j]), times(conj(f[1][i]), w[1][j]))

    ha = p[2][2] - inner(0, 0)[0]
    hd = p[3][3] - inner(1, 1)[0]
    cross = inner(0, 1)
    hb = (p[2][3][0] - cross[0], p[2][3][1] - cross[1])
    ga, gb, gd = two(ha, hb, hd)
    v = [
        [
            plus(scaled(w[i][0], ga), times(w[i][1], conj(gb))),
            plus(times(w[i][0], gb), scaled(w[i][1], gd)),
        ]
        for i in range(2)
    ]
    top = [
        [plus(times(v[i][0], conj(w[j][0])), times(v[i][1], conj(w[j][1]))) for j in range(2)]
        for i in range(2)
    ]
    zero = None
    out = [[None] * 4 for _ in range(4)]
    out[0][0] = (ea + top[0][0][0], zero)
    out[1][1] = (ed + top[1][1][0], zero)
    out[0][1] = plus(eb, top[0][1])
    out[2][2], out[3][3], out[2][3] = (ga, zero), (gd, zero), gb
    for i in range(2):
        for j in range(2):
            out[i][2 + j] = (-v[i][j][0], -v[i][j][1])
    for i in range(4):
        for j in range(i):
            out[i][j] = conj(out[j][i])
    return out


def invert(matrix):
    chans, width = matrix.shape
    sub = 8
    tiles = [matrix[t * sub : (t + 1) * sub, :] for t in range(chans // sub)]
    lane = iota((sub, width), 1)
    row = iota((sub, width), 0)
    first_half = lane < chans

    def spin(value):
        rolled = pltpu.roll(value, chans, 1)
        return jnp.where(first_half, -rolled, rolled)

    def column(value, k):
        return jnp.broadcast_to(value[:, k : k + 1], (sub, width))

    def combine(terms):
        while len(terms) > 1:
            terms = [
                terms[i] + terms[i + 1] if i + 1 < len(terms) else terms[i]
                for i in range(0, len(terms), 2)
            ]
        return terms[0]

    for k in range(0, chans, 4):
        t, r = divmod(k, sub)
        lines = [jnp.broadcast_to(tiles[t][r + i : r + i + 1, :], (sub, width)) for i in range(4)]
        pivot = [[None] * 4 for _ in range(4)]
        for i in range(4):
            pivot[i][i] = column(lines[i], k + i)
            for j in range(i + 1, 4):
                pivot[i][j] = column(lines[i], k + j), column(lines[i], chans + k + j)
        low = jnp.bitwise_and(lane, chans - 1)
        cleared = (low >= k) & (low < k + 4)
        unit = [
            jnp.where(cleared, jnp.where(lane == k + i, 1.0, 0.0), lines[i]) for i in range(4)
        ]
        spun = [spin(u) for u in unit]
        p = pivot_inverse(pivot)
        fresh_lines, fresh_spun = [], []
        for i in range(4):
            terms, other = [], []
            for j in range(4):
                re, im = p[i][j]
                terms.append(re * unit[j])
                other.append(re * spun[j])
                if im is not None:
                    terms.append(im * spun[j])
                    other.append(-(im * unit[j]))
            fresh_lines.append(combine(terms))
            fresh_spun.append(combine(other))
        fresh = []
        for s, tile in enumerate(tiles):
            terms = []
            for i in range(4):
                terms.append(column(tile, k + i) * fresh_lines[i])
                terms.append(column(tile, chans + k + i) * fresh_spun[i])
            value = jnp.where(cleared, 0.0, tile) - combine(terms)
            if s == t:
                for i in range(4):
                    value = jnp.where(row == r + i, fresh_lines[i], value)
            fresh.append(value)
        tiles = fresh
    return jnp.concatenate(tiles, axis=0)


def unpacked(ref, scale):
    half, wide = ref.shape[0], ref.shape[1]
    piece = ref[...] * scale
    swapped = pltpu.roll(piece, wide // 2, 1)
    return jnp.concatenate([piece, swapped], axis=0)[:, : wide // 2]


def hermitian(mixed, across):
    i, j = iota(mixed.shape, 0), iota(mixed.shape, 1)
    real_part = jnp.where(i >= j, mixed, across)
    imag_part = jnp.where(i < j, mixed, jnp.where(i > j, -across, 0.0))
    return jnp.concatenate([real_part, imag_part], axis=1)


def middle_kernel(total, packed_ref, steer_ref, inv_ref, t_ref):
    chans = inv_ref.shape[0]
    mixed = unpacked(packed_ref, F32(1.0 / total))
    twice = jnp.concatenate([mixed, mixed], axis=1)
    across = jnp.concatenate([twice, twice], axis=0).T[:chans, :chans]
    inverse = invert(hermitian(mixed, across))
    inv_ref[...] = inverse
    t_ref[...] = mul(steer_ref[...], inverse)


def outer_kernel(total, own_ref, left_ref, right_ref, steer_ref, inv_ref, t_ref, out_ref,
                 work, keep, small):
    chans = inv_ref.shape[0]
    scale = F32(1.0 / total)
    half = chans // 2
    m_left = unpacked(left_ref.at[:half], scale)
    m_right = unpacked(right_ref, scale)
    ml = left_ref[half : half + chans] * scale
    rl = left_ref[half + chans :] * scale
    rm = own_ref[half : half + chans] * scale
    across = jnp.concatenate([jnp.concatenate([m_left, m_right], axis=1), ml], axis=0).T
    lm = jnp.concatenate([across[:chans, chans:], -across[chans:, chans:]], axis=1)
    t = t_ref[...]
    both = mul(jnp.concatenate([rm, lm], axis=0), inv_ref[...])
    g_right, g_left = both[:chans], both[chans:]
    by_left = mul(jnp.concatenate([g_left, g_right, t], axis=0), ml)
    by_right = mul_conj(jnp.concatenate([g_right, t], axis=0), rm)
    work[...] = hermitian(m_left, across[:chans, :chans]) - by_left[:chans]
    keep[0] = rl - by_left[chans : 2 * chans]
    keep[1] = hermitian(m_right, across[chans:, :chans]) - by_right[:chans]
    keep[2] = g_left
    keep[3] = g_right
    small[0] = -by_left[2 * chans :]
    small[1] = -by_right[chans:]

    @pl.loop(0, 2)
    def _(stage):
        work[...] = invert(work[...])

        @pl.when(stage == 0)
        def _():
            s_rl = keep[0]
            both = mul(jnp.concatenate([s_rl, small[0]], axis=0), work[...])
            back = mul_conj(both, s_rl)
            work[...] = keep[1] - back[:chans]
            small[1] = small[1] - back[chans:]
            middle = mul(both, keep[2])
            keep[0] = both[:chans]
            small[0] = both[chans:]
            keep[3] = keep[3] - middle[:chans]
            small[2] = t_ref[...] - middle[chans:]

        @pl.when(stage == 1)
        def _():
            y_right = mul(small[1], work[...])
            factors = jnp.concatenate([embed(keep[0]), embed(keep[3])], axis=1)
            both = jnp.dot(
                y_right, factors, precision=lax.Precision.HIGHEST, preferred_element_type=F32
            )
            y_left = small[0] - both[:, : 2 * chans]
            y_mid = small[2] - both[:, 2 * chans :]
            quad = jnp.sum(steer_ref[...] * y_mid, axis=1, keepdims=True)
            y = jnp.concatenate([y_left, y_mid, y_right], axis=1) / jnp.sqrt(quad)
            real_lane = lax.rem(iota(y.shape, 1), 2 * chans) < chans
            mine = jnp.where(real_lane, y, -y).astype(BF16)
            for c in range(out_ref.shape[0]):
                out_ref[c] = mine


def steering(chans):
    index = np.arange(chans)
    sines = -0.8 + 1.6 * np.arange(BEAMS) / (BEAMS - 1)
    angle = math.pi * sines[:, None] * index[None, :]
    return np.concatenate([np.cos(angle), -np.sin(angle)], axis=1).astype(np.float32)


def solve_middle(packed, steer, total):
    half, wide = packed.shape
    return pl.pallas_call(
        functools.partial(middle_kernel, total),
        out_shape=[
            jax.ShapeDtypeStruct((2 * half, wide), F32),
            jax.ShapeDtypeStruct((BEAMS, wide), F32),
        ],
        in_specs=[vmem_spec()] * 2,
        out_specs=[vmem_spec()] * 2,
        compiler_params=params(),
    )(packed, steer)


def solve_outer(own, left, right, steer, inverse, t, total, copies):
    chans, wide = inverse.shape
    return pl.pallas_call(
        functools.partial(outer_kernel, total),
        out_shape=jax.ShapeDtypeStruct((copies, BEAMS, 3 * wide), BF16),
        in_specs=[vmem_spec()] * 6,
        out_specs=vmem_spec(),
        scratch_shapes=[
            pltpu.VMEM((chans, wide), F32),
            pltpu.VMEM((4, chans, wide), F32),
            pltpu.VMEM((3, BEAMS, wide), F32),
        ],
        compiler_params=params(),
    )(own, left, right, steer, inverse, t)


def beam_kernel(bin_ref, block_ref, beam_ref, owner_ref, s0_ref, upper_ref, lower_ref, w_ref,
                out_ref, both_ref, rows_ref, seen_ref):
    bins, wide, gates = s0_ref.shape
    devices = seen_ref.shape[0]
    count = bin_ref.shape[0]
    rows_ref[...] = jnp.zeros_like(rows_ref)

    @pl.loop(0, devices)
    def _(i):
        seen_ref[i] = 0

    w = w_ref[...].astype(F32).reshape(bins * BEAMS, 3 * wide)
    for k in range(3):
        lanes = slice(k * wide, (k + 1) * wide)
        part = w[:, lanes]
        both_ref[:, 0:BEAMS, lanes] = part.reshape(bins, BEAMS, wide)
        both_ref[:, BEAMS:, lanes] = turn(part).reshape(bins, BEAMS, wide)

    def detection(j, carry):
        bin_id = bin_ref[j]
        beam_id = beam_ref[j]
        owner = owner_ref[j]
        rank = seen_ref[owner]
        seen_ref[owner] = rank + 1
        left = both_ref[index_of(bin_id)].astype(BF16)
        bands = [lax.rem(bin_id + bins - 1 + k, bins) for k in range(3)]
        first = block_ref[j] == 0
        pieces = []
        for b in bands:
            later = [upper_ref[b, 0], lower_ref[b, 0], upper_ref[b, 1], lower_ref[b, 1]]
            pieces.append(jnp.where(first, s0_ref[b], jnp.concatenate(later, axis=0)))
        window = jnp.concatenate(pieces, axis=0)
        both = dot(left, window)
        line = jnp.concatenate([both[:BEAMS], both[BEAMS:]], axis=1)
        chosen = jnp.where(iota(line.shape, 0) == beam_id, line, 0.0)
        row = owner * CAP + rank
        rows_ref[pl.ds(row, 1), :] = jnp.sum(chosen, axis=0, keepdims=True)
        return carry

    lax.fori_loop(0, count, detection, 0, unroll=32)
    out_ref[...] = rows_ref[...].astype(BF16)


def beam_rows(det_bin, det_block, det_beam, owners, s0, s1, weight, devices):
    bins, wide, gates = s0.shape
    return pl.pallas_call(
        beam_kernel,
        out_shape=jax.ShapeDtypeStruct((devices * CAP, 2 * gates), BF16),
        in_specs=[smem_spec()] * 4 + [vmem_spec()] * 4,
        out_specs=vmem_spec(),
        scratch_shapes=[
            pltpu.VMEM((bins, 2 * BEAMS, 3 * wide), F32),
            pltpu.VMEM((devices * CAP, 2 * gates), F32),
            pltpu.SMEM((devices,), jnp.int32),
        ],
        compiler_params=params(),
    )(det_bin, det_block, det_beam, owners, s0, *s1, weight)


def on_device(raw, replica, det_bin, det_block, det_beam, det_owner):
    devices = lax.axis_size("range")
    _, chans, pulses, gates = raw.shape
    bins = pulses
    flat = raw.reshape(2, chans * pulses, gates)
    before = [(source, source - 1) for source in range(1, devices)]
    *slices, mark = first_gates(flat)
    halos = [lax.ppermute(value, "range", before) for value in slices]
    table = doppler_matrix(pulses, 8)
    s0, local, matrix, *sent = spectra_first(flat, replica, table, pulses, mark)
    beside0 = [partner(value, (1, 1)) for value in sent]
    sums = cross([s0], bins)
    sums = cross(beside0, bins, sums)
    s1, beside1 = [], []
    for part, halo in enumerate(halos):
        value, send = spectra_last(part, local, halo, matrix, table, pulses, sums)
        s1.append(value)
        beside1.append(partner(send, (1, 1)))
    sums = cross(s1, bins, sums)
    sums = cross(beside1, bins, sums)
    own, packed = bin_sums(sums)
    total = gates * devices
    steer = steering(chans)
    left = from_bin(own, -1)
    right = from_bin(packed, 1)
    inverse, t = solve_middle(packed, steer, total)
    mine = solve_outer(own, left, right, steer, inverse, t, total, bins)
    groups = [list(range(first, first + bins)) for first in range(0, devices, bins)]
    weight = lax.all_to_all(
        mine, "range", split_axis=0, concat_axis=0, tiled=True,
        axis_index_groups=groups if len(groups) > 1 else None,
    )
    outgoing = beam_rows(
        det_bin, det_block, det_beam, det_owner[:, 0],
        s0.reshape(bins, 2 * chans, BLOCK), s1, weight, devices,
    )
    incoming = lax.all_to_all(
        outgoing.reshape(devices, CAP, 2 * BLOCK), "range", split_axis=0, concat_axis=0, tiled=True
    )
    return incoming.astype(F32).reshape(devices * CAP, 2 * BLOCK)


def solution(mesh):
    in_specs = (
        P(None, None, None, "range"),
        P(),
        P("range"),
        P("range"),
        P("range"),
        P("range", None),
    )
    out_specs = P("range", None)
    return jax.shard_map(
        on_device, mesh=mesh, in_specs=in_specs, out_specs=out_specs, check_vma=False
    )
```

```python
import functools
import math

import jax
import jax.numpy as jnp
import ml_dtypes
import numpy as np
from jax import lax
from jax.experimental import pallas as pl
from jax.experimental.pallas import tpu as pltpu
from jax.sharding import PartitionSpec as P

BLOCK = 128
BEAMS = 8
CAP = 2

F32 = jnp.float32
BF16 = jnp.bfloat16
VMEM = pltpu.VMEM
MIB = 1024 * 1024
NT = (((1,), (1,)), ((), ()))


def vmem_spec():
    return pl.BlockSpec(memory_space=VMEM)


def smem_spec():
    return pl.BlockSpec(memory_space=pltpu.SMEM)


def hbm_spec():
    return pl.BlockSpec(memory_space=pltpu.HBM)


SHORT = pl.CostEstimate(flops=1, bytes_accessed=1, transcendentals=0)


def params(mib=16):
    return pltpu.CompilerParams(vmem_limit_bytes=int(mib * MIB))


def dot(a, b):
    return jnp.dot(a, b, preferred_element_type=F32)


def dot_nt(a, b, precision=None):
    return lax.dot_general(a, b, NT, precision=precision, preferred_element_type=F32)


def iota(shape, axis):
    return lax.broadcasted_iota(jnp.int32, shape, axis)


def halo_kernel(raw_ref, a_ref, b_ref, mark_ref, sems):
    mark_ref[...] = jnp.zeros_like(mark_ref)
    count = sems.shape[0] // 2
    size = a_ref.shape[1] // count
    copies = []
    for part, out_ref in enumerate((a_ref, b_ref)):
        for j in range(count):
            start = part * a_ref.shape[1] + j * size
            copies.append(
                pltpu.make_async_copy(
                    raw_ref.at[:, start : start + size, :BLOCK],
                    out_ref.at[:, j * size : (j + 1) * size, :],
                    sems.at[part * count + j],
                )
            )
    for copy in copies:
        copy.start()
    for copy in copies:
        copy.wait()


def first_gates(raw):
    half = jax.ShapeDtypeStruct((2, raw.shape[1] // 2, BLOCK), BF16)
    return pl.pallas_call(
        halo_kernel,
        out_shape=[half, half, jax.ShapeDtypeStruct((8, 128), F32)],
        in_specs=[hbm_spec()],
        out_specs=[vmem_spec()] * 3,
        scratch_shapes=[pltpu.SemaphoreType.DMA((2,))],
        compiler_params=params(63),
    )(raw)


def correlation_matrix(rep_ref, out_ref):
    taps = rep_ref.shape[1]
    base = rep_ref[...].astype(F32)
    row = iota((taps, 2 * taps), 0)
    parts = []
    for i in range(2):
        line = jnp.concatenate([base[i : i + 1], jnp.zeros((1, taps), F32)], axis=1)
        skew = jnp.broadcast_to(line, (taps, 2 * taps))
        bit = 1
        while bit < taps:
            skew = jnp.where((row & bit) != 0, pltpu.roll(skew, bit, 1), skew)
            bit *= 2
        parts.append(skew.T)
    real_part, imag_part = parts
    out_ref[0] = jnp.concatenate([real_part, -imag_part], axis=1).astype(BF16)
    out_ref[1] = jnp.concatenate([imag_part, real_part], axis=1).astype(BF16)


def doppler_matrix(pulses, group):
    index = np.arange(pulses)
    angle = 2.0 * math.pi / pulses * (index[:, None] * index[None, :] % pulses)
    cosine = np.cos(angle) * pulses**-0.5
    sine = np.sin(angle) * pulses**-0.5
    table = np.stack([np.stack([cosine, -sine], 1), np.stack([sine, cosine], 1)], 0)
    full = np.einsum("ipod,ce->dociep", table, np.eye(group))
    shape = (pulses * 2 * group, 2 * group * pulses)
    return full.reshape(shape).astype(ml_dtypes.bfloat16)


def doppler_rows(total, dft):
    compressed = total.astype(BF16)
    rows, wide = compressed.shape
    half, gates = rows // 2, wide // 2
    stacked = jnp.concatenate(
        [
            jnp.concatenate([compressed[:half, :gates], compressed[half:, :gates]], axis=1),
            jnp.concatenate([compressed[:half, gates:], compressed[half:, gates:]], axis=1),
        ],
        axis=0,
    )
    both = dot(dft, stacked)
    lines = both.shape[0] // 8
    joined = jnp.concatenate(
        [both[:, :gates].reshape(lines, 8, gates), both[:, gates:].reshape(lines, 8, gates)],
        axis=1,
    )
    return joined.astype(BF16)


GROUP = 16


def half_of_bins(bins, mine):
    core = lax.axis_index("range") & 1
    return (core if mine else 1 - core) * (bins // 2)


def sent_bins(bins):
    return bins // 2 + 2


def spectra_first_kernel(raw_ref, rep_ref, dft_ref, _, s_ref, local_ref, taps_ref, *rest):
    *send_refs, buf, sems = rest
    bins, _, chans, gates = s_ref.shape
    size = GROUP * bins
    copies = [
        pltpu.make_async_copy(
            raw_ref.at[:, j * size : (j + 1) * size, :],
            buf.at[:, j * size : (j + 1) * size, :],
            sems.at[j],
        )
        for j in range(chans // GROUP)
    ]
    for copy in copies:
        copy.start()
    correlation_matrix(rep_ref, taps_ref)
    for j, copy in enumerate(copies):
        copy.wait()
        rows = slice(j * size, (j + 1) * size)
        total = dot(buf[0, rows, :], taps_ref[0]) + dot(buf[1, rows, :], taps_ref[1])
        out = doppler_rows(total, dft_ref[...])
        s_ref[:, :, j * GROUP : (j + 1) * GROUP, :] = out.reshape(bins, 2, GROUP, gates)
        later = jnp.concatenate([buf[0, rows, gates:], buf[1, rows, gates:]], axis=1)
        near = jnp.concatenate([taps_ref[0, :gates, :], taps_ref[1, :gates, :]], axis=0)
        local_ref[rows, :] = dot(later, near)
    base = half_of_bins(bins, False)
    half = chans // 2
    for part, send_ref in enumerate(send_refs):
        for k in range(send_ref.shape[0]):
            send_ref[k] = s_ref[lax.rem(base + k, bins), :, part * half : (part + 1) * half, :]


def spectra_last_kernel(part, local_ref, halo_ref, taps_ref, dft_ref, _, s_ref, send_ref):
    bins, _, chans, gates = s_ref.shape
    size = GROUP * bins
    far = jnp.concatenate([taps_ref[0, gates:, :], taps_ref[1, gates:, :]], axis=0)
    for j in range(chans // GROUP):
        rows = slice(j * size, (j + 1) * size)
        later = jnp.concatenate([halo_ref[0, rows, :], halo_ref[1, rows, :]], axis=1)
        start = part * chans * bins + j * size
        out = doppler_rows(local_ref[start : start + size, :] + dot(later, far), dft_ref[...])
        s_ref[:, :, j * GROUP : (j + 1) * GROUP, :] = out.reshape(bins, 2, GROUP, gates)
    base = half_of_bins(bins, False)
    for k in range(send_ref.shape[0]):
        send_ref[k] = s_ref[lax.rem(base + k, bins)]


def spectra_first(raw, replica, table, pulses, mark):
    _, rows, gates = raw.shape
    chans = rows // pulses
    taps = replica.shape[1]
    return pl.pallas_call(
        spectra_first_kernel,
        out_shape=[
            jax.ShapeDtypeStruct((pulses, 2, chans, BLOCK), BF16),
            jax.ShapeDtypeStruct((rows, 2 * BLOCK), F32),
            jax.ShapeDtypeStruct((2, 2 * taps, 2 * taps), BF16),
        ]
        + [jax.ShapeDtypeStruct((sent_bins(pulses), 2, chans // 2, BLOCK), BF16)] * 2,
        in_specs=[hbm_spec(), vmem_spec(), vmem_spec(), pl.BlockSpec(memory_space=pl.ANY)],
        out_specs=[vmem_spec()] * 5,
        scratch_shapes=[
            pltpu.VMEM(raw.shape, BF16),
            pltpu.SemaphoreType.DMA((chans // GROUP,)),
        ],
        compiler_params=params(),
        cost_estimate=SHORT,
    )(raw, replica, table, mark)


def spectra_last(part, local, halo, matrix, table, pulses, sums):
    chans = halo.shape[1] // pulses
    return pl.pallas_call(
        functools.partial(spectra_last_kernel, part),
        out_shape=[
            jax.ShapeDtypeStruct((pulses, 2, chans, BLOCK), BF16),
            jax.ShapeDtypeStruct((sent_bins(pulses), 2, chans, BLOCK), BF16),
        ],
        in_specs=[vmem_spec()] * 4 + [pl.BlockSpec(memory_space=pl.ANY)],
        out_specs=[vmem_spec()] * 2,
        compiler_params=params(),
        cost_estimate=SHORT,
    )(local, halo, matrix, table, sums)


def cross_kernel(count_refs, *refs):
    s_refs, rest = refs[:count_refs], refs[count_refs:]
    before_ref = rest[0] if len(rest) == 2 else None
    out_ref = rest[-1]
    held, _, _, gates = s_refs[0].shape
    chans = sum(ref.shape[2] for ref in s_refs)
    count = out_ref.shape[0]
    base = half_of_bins(held, True) if held == 2 * count else 0

    def write(e, block):
        out_ref[e] = block if before_ref is None else block + before_ref[e]

    @pl.loop(0, count // 2, unroll=8)
    def _(step):
        e = step * 2
        each = []
        for k in range(4):
            where = lax.rem(base + e + k, held)
            each.append(
                [jnp.concatenate([ref[where, o] for ref in s_refs], axis=0) for o in range(2)]
            )
        left = jnp.concatenate(
            [jnp.concatenate([re, im], axis=1) for re, im in each], axis=0
        )
        right = jnp.concatenate(
            [
                jnp.concatenate(pieces, axis=1)
                for re, im in each[:2]
                for pieces in ((re, im), (-im, re))
            ],
            axis=0,
        )
        both = dot_nt(left, right)
        write(e, both[: 3 * chans, : 2 * chans])
        write(e + 1, both[chans:, 2 * chans :])


def cross(spectra, bins, before=None):
    chans = sum(value.shape[2] for value in spectra)
    data = spectra if before is None else spectra + [before]
    return pl.pallas_call(
        functools.partial(cross_kernel, len(spectra)),
        out_shape=jax.ShapeDtypeStruct((bins // 2, 3 * chans, 2 * chans), F32),
        in_specs=[vmem_spec()] * len(data),
        out_specs=vmem_spec(),
        compiler_params=params(),
        cost_estimate=SHORT,
    )(*data)


U_BITS, V_BITS = (2, 4), (4, 2)


def partner(value, bits):
    count = lax.axis_size("range")
    return lax.ppermute(value, "range", [(i, i ^ bits[i & 1]) for i in range(count)])


def slot_of(core, x, y, z):
    return (4 * z + ((2 * y + (x ^ y)) ^ (3 * (z & 1)))) ^ (15 * core)


def parts_of(index):
    return index & 1, (index >> 1) & 1, (index >> 2) & 1, (index >> 3) & 3


def bin_of(index):
    core, x, y, z = parts_of(index)
    return core * 16 + slot_of(core, x, y, z)


def index_of(bin_id):
    core = bin_id >> 4
    path = (bin_id & 15) ^ (15 * core)
    z = path >> 2
    turned = (path & 3) ^ (3 * (z & 1))
    y = turned >> 1
    x = (turned & 1) ^ y
    return z * 8 + y * 4 + x * 2 + core


def uv_parts():
    core, x, y, z = parts_of(lax.axis_index("range"))
    return core, jnp.where(core == 0, x, y), jnp.where(core == 0, y, x), z


def uv_slot(core, u, v, z):
    return slot_of(core, jnp.where(core == 0, u, v), jnp.where(core == 0, v, u), z)


def packed(block):
    chans = block.shape[0]
    lower = iota((chans, chans), 0) >= iota((chans, chans), 1)
    swapped = pltpu.roll(block, chans, 1)
    mixed = jnp.where(lower, block[:, :chans], swapped[:, :chans])
    return jnp.concatenate([mixed[: chans // 2], mixed[chans // 2 :]], axis=1)


def sent_rows(keep_ref):
    return 5 * keep_ref.shape[1] // 6


def upper_rows(keep_ref, e):
    block = keep_ref.shape[1] // 3
    end = sent_rows(keep_ref) // 2 + block // 2
    return jnp.concatenate([packed(keep_ref[e, :block]), keep_ref[e, block:end]], axis=0)


def lower_rows(keep_ref, e):
    return keep_ref[e, sent_rows(keep_ref) // 2 + keep_ref.shape[1] // 6 :]


def first_upper_kernel(keep_ref, a_ref):
    core, u, v, z = uv_parts()
    for k in range(8):
        a_ref[k] = upper_rows(keep_ref, uv_slot(core, 1 - u, k // 4, k % 4))


def first_lower_kernel(keep_ref, b_ref):
    core, u, v, z = uv_parts()
    for k in range(8):
        b_ref[k] = lower_rows(keep_ref, uv_slot(core, k // 4, 1 - v, k % 4))


def second_kernel(keep_ref, a1_ref, b1_ref, a_ref, b_ref):
    core, u, v, z = uv_parts()
    for k in range(4):
        e = uv_slot(core, u, 1 - v, k)
        a_ref[k] = upper_rows(keep_ref, e) + a1_ref[(1 - v) * 4 + k]
        e = uv_slot(core, 1 - u, v, k)
        b_ref[k] = lower_rows(keep_ref, e) + b1_ref[(1 - u) * 4 + k]


def line_sum(keep_ref, a1_ref, b1_ref, a2_ref, b2_ref, flip):
    core, u, v, z = uv_parts()
    z = z ^ flip
    e = uv_slot(core, u, v, z)
    upper = upper_rows(keep_ref, e) + a1_ref[v * 4 + z] + a2_ref[z]
    lower = lower_rows(keep_ref, e) + b1_ref[u * 4 + z] + b2_ref[z]
    return upper, lower


FLIPS = (2, 3, 1)


def line_kernel(*refs):
    half = sent_rows(refs[0]) // 2
    for flip, out_ref in zip(FLIPS, refs[5:]):
        upper, lower = line_sum(*refs[:5], flip)
        out_ref[:half] = upper
        out_ref[half:] = lower


def own_kernel(*refs):
    z1_ref, z2_ref, z3_ref, out_ref, packed_ref = refs[5:]
    half = sent_rows(refs[0]) // 2
    upper, lower = line_sum(*refs[:5], 0)
    upper = upper + z1_ref[:half] + (z2_ref[:half] + z3_ref[:half])
    out_ref[:half] = upper
    packed_ref[...] = upper[: packed_ref.shape[0]]
    out_ref[half:] = lower + z1_ref[half:] + (z2_ref[half:] + z3_ref[half:])


def summed(kernel, data, shapes):
    return pl.pallas_call(
        kernel,
        out_shape=[jax.ShapeDtypeStruct(shape, F32) for shape in shapes],
        in_specs=[vmem_spec()] * len(data),
        out_specs=[vmem_spec()] * len(shapes),
        compiler_params=params(),
    )(*data)


def bin_sums(keep):
    _, full, wide = keep.shape
    rows = 5 * full // 6
    half = rows // 2
    data = [keep]
    b1 = partner(summed(first_lower_kernel, data, [(8, half, wide)])[0], V_BITS)
    a1 = partner(summed(first_upper_kernel, data, [(8, half, wide)])[0], U_BITS)
    data += [a1, b1]
    a, b = summed(second_kernel, data, [(4, half, wide)] * 2)
    data += [partner(a, V_BITS), partner(b, U_BITS)]
    sends = summed(line_kernel, data, [(rows, wide)] * 3)
    data += [partner(value, (8 * flip, 8 * flip)) for flip, value in zip(FLIPS, sends)]
    own, packed = summed(own_kernel, data, [(rows, wide), (rows // 5, wide)])
    bit = 32
    while bit < lax.axis_size("range"):
        own = own + partner(own, (bit, bit))
        packed = packed + partner(packed, (bit, bit))
        bit *= 2
    return own, packed


def from_bin(value, offset):
    count = lax.axis_size("range")
    pairs = []
    for i in range(count):
        target = index_of((bin_of(i) - offset) % 32) | (i & ~31)
        pairs.append((i, target))
    return lax.ppermute(value, "range", pairs)


def turn(value):
    half = value.shape[1] // 2
    rolled = pltpu.roll(value, half, 1)
    return jnp.where(iota(value.shape, 1) < half, -rolled, rolled)


def embed(value):
    return jnp.concatenate([value, turn(value)], axis=0)


def mul(a, b):
    return jnp.dot(a, embed(b), precision=lax.Precision.HIGHEST, preferred_element_type=F32)


def mul_conj(a, b):
    half = a.shape[1] // 2
    stacked = jnp.concatenate([a, -turn(a)], axis=0)
    both = dot_nt(stacked, b, lax.Precision.HIGHEST)
    rows = a.shape[0]
    return jnp.concatenate([both[:rows], both[rows:]], axis=1)


def reciprocal(x):
    value = pl.reciprocal(x, approx=True)
    for _ in range(2):
        value = value * (2.0 - x * value)
    return value


def pivot_inverse(p):
    def times(x, y):
        return x[0] * y[0] - x[1] * y[1], x[0] * y[1] + x[1] * y[0]

    def conj(x):
        return x[0], -x[1]

    def plus(x, y):
        return x[0] + y[0], x[1] + y[1]

    def scaled(x, s):
        return x[0] * s, x[1] * s

    def square(x):
        return x[0] * x[0] + x[1] * x[1]

    def two(a, b, d):
        inv = reciprocal(a * d - square(b))
        return d * inv, scaled(b, -inv), a * inv

    a, d = p[0][0], p[1][1]
    b = p[0][1]
    ea, eb, ed = two(a, b, d)
    f = [[p[0][2], p[0][3]], [p[1][2], p[1][3]]]
    w = [
        [plus(scaled(f[0][j], ea), times(eb, f[1][j])) for j in range(2)],
        [plus(times(conj(eb), f[0][j]), scaled(f[1][j], ed)) for j in range(2)],
    ]

    def inner(i, j):
        return plus(times(conj(f[0][i]), w[0][j]), times(conj(f[1][i]), w[1][j]))

    ha = p[2][2] - inner(0, 0)[0]
    hd = p[3][3] - inner(1, 1)[0]
    cross = inner(0, 1)
    hb = (p[2][3][0] - cross[0], p[2][3][1] - cross[1])
    ga, gb, gd = two(ha, hb, hd)
    v = [
        [
            plus(scaled(w[i][0], ga), times(w[i][1], conj(gb))),
            plus(times(w[i][0], gb), scaled(w[i][1], gd)),
        ]
        for i in range(2)
    ]
    top = [
        [plus(times(v[i][0], conj(w[j][0])), times(v[i][1], conj(w[j][1]))) for j in range(2)]
        for i in range(2)
    ]
    zero = None
    out = [[None] * 4 for _ in range(4)]
    out[0][0] = (ea + top[0][0][0], zero)
    out[1][1] = (ed + top[1][1][0], zero)
    out[0][1] = plus(eb, top[0][1])
    out[2][2], out[3][3], out[2][3] = (ga, zero), (gd, zero), gb
    for i in range(2):
        for j in range(2):
            out[i][2 + j] = (-v[i][j][0], -v[i][j][1])
    for i in range(4):
        for j in range(i):
            out[i][j] = conj(out[j][i])
    return out


def invert(matrix):
    chans, width = matrix.shape
    sub = 8
    tiles = [matrix[t * sub : (t + 1) * sub, :] for t in range(chans // sub)]
    lane = iota((sub, width), 1)
    row = iota((sub, width), 0)
    first_half = lane < chans

    def spin(value):
        rolled = pltpu.roll(value, chans, 1)
        return jnp.where(first_half, -rolled, rolled)

    def column(value, k):
        return jnp.broadcast_to(value[:, k : k + 1], (sub, width))

    def combine(terms):
        while len(terms) > 1:
            terms = [
                terms[i] + terms[i + 1] if i + 1 < len(terms) else terms[i]
                for i in range(0, len(terms), 2)
            ]
        return terms[0]

    for k in range(0, chans, 4):
        t, r = divmod(k, sub)
        lines = [jnp.broadcast_to(tiles[t][r + i : r + i + 1, :], (sub, width)) for i in range(4)]
        pivot = [[None] * 4 for _ in range(4)]
        for i in range(4):
            pivot[i][i] = column(lines[i], k + i)
            for j in range(i + 1, 4):
                pivot[i][j] = column(lines[i], k + j), column(lines[i], chans + k + j)
        low = jnp.bitwise_and(lane, chans - 1)
        cleared = (low >= k) & (low < k + 4)
        unit = [
            jnp.where(cleared, jnp.where(lane == k + i, 1.0, 0.0), lines[i]) for i in range(4)
        ]
        spun = [spin(u) for u in unit]
        p = pivot_inverse(pivot)
        fresh_lines, fresh_spun = [], []
        for i in range(4):
            terms, other = [], []
            for j in range(4):
                re, im = p[i][j]
                terms.append(re * unit[j])
                other.append(re * spun[j])
                if im is not None:
                    terms.append(im * spun[j])
                    other.append(-(im * unit[j]))
            fresh_lines.append(combine(terms))
            fresh_spun.append(combine(other))
        fresh = []
        for s, tile in enumerate(tiles):
            terms = []
            for i in range(4):
                terms.append(column(tile, k + i) * fresh_lines[i])
                terms.append(column(tile, chans + k + i) * fresh_spun[i])
            value = jnp.where(cleared, 0.0, tile) - combine(terms)
            if s == t:
                for i in range(4):
                    value = jnp.where(row == r + i, fresh_lines[i], value)
            fresh.append(value)
        tiles = fresh
    return jnp.concatenate(tiles, axis=0)


def unpacked(ref, scale):
    half, wide = ref.shape[0], ref.shape[1]
    piece = ref[...] * scale
    swapped = pltpu.roll(piece, wide // 2, 1)
    return jnp.concatenate([piece, swapped], axis=0)[:, : wide // 2]


def hermitian(mixed, across):
    i, j = iota(mixed.shape, 0), iota(mixed.shape, 1)
    real_part = jnp.where(i >= j, mixed, across)
    imag_part = jnp.where(i < j, mixed, jnp.where(i > j, -across, 0.0))
    return jnp.concatenate([real_part, imag_part], axis=1)


def middle_kernel(total, packed_ref, steer_ref, inv_ref, t_ref):
    chans = inv_ref.shape[0]
    mixed = unpacked(packed_ref, F32(1.0 / total))
    twice = jnp.concatenate([mixed, mixed], axis=1)
    across = jnp.concatenate([twice, twice], axis=0).T[:chans, :chans]
    inverse = invert(hermitian(mixed, across))
    inv_ref[...] = inverse
    t_ref[...] = mul(steer_ref[...], inverse)


def outer_kernel(total, own_ref, left_ref, right_ref, steer_ref, inv_ref, t_ref, out_ref,
                 work, keep, small):
    chans = inv_ref.shape[0]
    scale = F32(1.0 / total)
    half = chans // 2
    m_left = unpacked(left_ref.at[:half], scale)
    m_right = unpacked(right_ref, scale)
    ml = left_ref[half : half + chans] * scale
    rl = left_ref[half + chans :] * scale
    rm = own_ref[half : half + chans] * scale
    across = jnp.concatenate([jnp.concatenate([m_left, m_right], axis=1), ml], axis=0).T
    lm = jnp.concatenate([across[:chans, chans:], -across[chans:, chans:]], axis=1)
    t = t_ref[...]
    both = mul(jnp.concatenate([rm, lm], axis=0), inv_ref[...])
    g_right, g_left = both[:chans], both[chans:]
    by_left = mul(jnp.concatenate([g_left, g_right, t], axis=0), ml)
    by_right = mul_conj(jnp.concatenate([g_right, t], axis=0), rm)
    work[...] = hermitian(m_left, across[:chans, :chans]) - by_left[:chans]
    keep[0] = rl - by_left[chans : 2 * chans]
    keep[1] = hermitian(m_right, across[chans:, :chans]) - by_right[:chans]
    keep[2] = g_left
    keep[3] = g_right
    small[0] = -by_left[2 * chans :]
    small[1] = -by_right[chans:]

    @pl.loop(0, 2)
    def _(stage):
        work[...] = invert(work[...])

        @pl.when(stage == 0)
        def _():
            s_rl = keep[0]
            both = mul(jnp.concatenate([s_rl, small[0]], axis=0), work[...])
            back = mul_conj(both, s_rl)
            work[...] = keep[1] - back[:chans]
            small[1] = small[1] - back[chans:]
            middle = mul(both, keep[2])
            keep[0] = both[:chans]
            small[0] = both[chans:]
            keep[3] = keep[3] - middle[:chans]
            small[2] = t_ref[...] - middle[chans:]

        @pl.when(stage == 1)
        def _():
            y_right = mul(small[1], work[...])
            factors = jnp.concatenate([embed(keep[0]), embed(keep[3])], axis=1)
            both = jnp.dot(
                y_right, factors, precision=lax.Precision.HIGHEST, preferred_element_type=F32
            )
            y_left = small[0] - both[:, : 2 * chans]
            y_mid = small[2] - both[:, 2 * chans :]
            quad = jnp.sum(steer_ref[...] * y_mid, axis=1, keepdims=True)
            y = jnp.concatenate([y_left, y_mid, y_right], axis=1) / jnp.sqrt(quad)
            real_lane = lax.rem(iota(y.shape, 1), 2 * chans) < chans
            mine = jnp.where(real_lane, y, -y).astype(BF16)
            for c in range(out_ref.shape[0]):
                out_ref[c] = mine


def steering(chans):
    index = np.arange(chans)
    sines = -0.8 + 1.6 * np.arange(BEAMS) / (BEAMS - 1)
    angle = math.pi * sines[:, None] * index[None, :]
    return np.concatenate([np.cos(angle), -np.sin(angle)], axis=1).astype(np.float32)


def solve_middle(packed, steer, total):
    half, wide = packed.shape
    return pl.pallas_call(
        functools.partial(middle_kernel, total),
        out_shape=[
            jax.ShapeDtypeStruct((2 * half, wide), F32),
            jax.ShapeDtypeStruct((BEAMS, wide), F32),
        ],
        in_specs=[vmem_spec()] * 2,
        out_specs=[vmem_spec()] * 2,
        compiler_params=params(),
    )(packed, steer)


def solve_outer(own, left, right, steer, inverse, t, total, copies):
    chans, wide = inverse.shape
    return pl.pallas_call(
        functools.partial(outer_kernel, total),
        out_shape=jax.ShapeDtypeStruct((copies, BEAMS, 3 * wide), BF16),
        in_specs=[vmem_spec()] * 6,
        out_specs=vmem_spec(),
        scratch_shapes=[
            pltpu.VMEM((chans, wide), F32),
            pltpu.VMEM((4, chans, wide), F32),
            pltpu.VMEM((3, BEAMS, wide), F32),
        ],
        compiler_params=params(),
    )(own, left, right, steer, inverse, t)


def beam_kernel(bin_ref, block_ref, beam_ref, owner_ref, s0_ref, upper_ref, lower_ref, w_ref,
                out_ref, both_ref, rows_ref, seen_ref):
    bins, wide, gates = s0_ref.shape
    devices = seen_ref.shape[0]
    count = bin_ref.shape[0]
    rows_ref[...] = jnp.zeros_like(rows_ref)

    @pl.loop(0, devices)
    def _(i):
        seen_ref[i] = 0

    w = w_ref[...].astype(F32).reshape(bins * BEAMS, 3 * wide)
    for k in range(3):
        lanes = slice(k * wide, (k + 1) * wide)
        part = w[:, lanes]
        both_ref[:, 0:BEAMS, lanes] = part.reshape(bins, BEAMS, wide)
        both_ref[:, BEAMS:, lanes] = turn(part).reshape(bins, BEAMS, wide)

    def detection(j, carry):
        bin_id = bin_ref[j]
        beam_id = beam_ref[j]
        owner = owner_ref[j]
        rank = seen_ref[owner]
        seen_ref[owner] = rank + 1
        left = both_ref[index_of(bin_id)].astype(BF16)
        bands = [lax.rem(bin_id + bins - 1 + k, bins) for k in range(3)]
        first = block_ref[j] == 0
        pieces = []
        for b in bands:
            later = [upper_ref[b, 0], lower_ref[b, 0], upper_ref[b, 1], lower_ref[b, 1]]
            pieces.append(jnp.where(first, s0_ref[b], jnp.concatenate(later, axis=0)))
        window = jnp.concatenate(pieces, axis=0)
        both = dot(left, window)
        line = jnp.concatenate([both[:BEAMS], both[BEAMS:]], axis=1)
        chosen = jnp.where(iota(line.shape, 0) == beam_id, line, 0.0)
        row = owner * CAP + rank
        rows_ref[pl.ds(row, 1), :] = jnp.sum(chosen, axis=0, keepdims=True)
        return carry

    lax.fori_loop(0, count, detection, 0, unroll=32)
    out_ref[...] = rows_ref[...].astype(BF16)


def beam_rows(det_bin, det_block, det_beam, owners, s0, s1, weight, devices):
    bins, wide, gates = s0.shape
    return pl.pallas_call(
        beam_kernel,
        out_shape=jax.ShapeDtypeStruct((devices * CAP, 2 * gates), BF16),
        in_specs=[smem_spec()] * 4 + [vmem_spec()] * 4,
        out_specs=vmem_spec(),
        scratch_shapes=[
            pltpu.VMEM((bins, 2 * BEAMS, 3 * wide), F32),
            pltpu.VMEM((devices * CAP, 2 * gates), F32),
            pltpu.SMEM((devices,), jnp.int32),
        ],
        compiler_params=params(),
    )(det_bin, det_block, det_beam, owners, s0, *s1, weight)


def on_device(raw, replica, det_bin, det_block, det_beam, det_owner):
    devices = lax.axis_size("range")
    _, chans, pulses, gates = raw.shape
    bins = pulses
    flat = raw.reshape(2, chans * pulses, gates)
    before = [(source, source - 1) for source in range(1, devices)]
    *slices, mark = first_gates(flat)
    halos = [lax.ppermute(value, "range", before) for value in slices]
    table = doppler_matrix(pulses, 8)
    s0, local, matrix, *sent = spectra_first(flat, replica, table, pulses, mark)
    beside0 = [partner(value, (1, 1)) for value in sent]
    sums = cross([s0], bins)
    sums = cross(beside0, bins, sums)
    s1, beside1 = [], []
    for part, halo in enumerate(halos):
        value, send = spectra_last(part, local, halo, matrix, table, pulses, sums)
        s1.append(value)
        beside1.append(partner(send, (1, 1)))
    sums = cross(s1, bins, sums)
    sums = cross(beside1, bins, sums)
    own, packed = bin_sums(sums)
    total = gates * devices
    steer = steering(chans)
    left = from_bin(own, -1)
    right = from_bin(packed, 1)
    inverse, t = solve_middle(packed, steer, total)
    mine = solve_outer(own, left, right, steer, inverse, t, total, bins)
    groups = [list(range(first, first + bins)) for first in range(0, devices, bins)]
    weight = lax.all_to_all(
        mine, "range", split_axis=0, concat_axis=0, tiled=True,
        axis_index_groups=groups if len(groups) > 1 else None,
    )
    outgoing = beam_rows(
        det_bin, det_block, det_beam, det_owner[:, 0],
        s0.reshape(bins, 2 * chans, BLOCK), s1, weight, devices,
    )
    incoming = lax.all_to_all(
        outgoing.reshape(devices, CAP, 2 * BLOCK), "range", split_axis=0, concat_axis=0, tiled=True
    )
    return incoming.astype(F32).reshape(devices * CAP, 2 * BLOCK)


def solution(mesh):
    in_specs = (
        P(None, None, None, "range"),
        P(),
        P("range"),
        P("range"),
        P("range"),
        P("range", None),
    )
    out_specs = P("range", None)
    return jax.shard_map(
        on_device, mesh=mesh, in_specs=in_specs, out_specs=out_specs, check_vma=False
    )
```
